32 devices in a mesh: seq: 8 (over z, x), mp: 4 (over y, core).
Axes of the slice: x: 2, y: 2, z: 4, core: 2. Of those that a mesh axis runs over, the one named last changes fastest.
Arguments:
- tokens_in: float32 [1024, 2048], P('seq'), may hold values from -6 to 6
- cotangent: float32 [1024, 2048], P('seq'), may hold values from -6 to 6
- lengths: int32 [4], replicated, may hold values from 8 to 960, as said below
- lower_bound: float32 [2048], P('mp'), may hold values from 0.94 to 1, as said below
- query_weight: float32 [2048, 2048], P(None, 'mp'), may hold values from -0.125 to 0.125
- forget_weight: float32 [2048, 2048], P(None, 'mp'), may hold values from -0.125 to 0.125
- input_weight: float32 [2048, 2048], P(None, 'mp'), may hold values from -0.125 to 0.125
- gate_weight: float32 [2048, 2048], P(None, 'mp'), may hold values from -0.125 to 0.125
- out_weight: float32 [2048, 2048], P('mp'), may hold values from -0.25 to 0.25
- swiglu_gate: float32 [2048, 5632], P(None, 'mp'), may hold values from -0.125 to 0.125
- swiglu_up: float32 [2048, 5632], P(None, 'mp'), may hold values from -0.125 to 0.125
- swiglu_down: float32 [5632, 2048], P('mp'), may hold values from -0.15625 to 0.15625
- first_gain: float32 [2048], replicated, may hold values from 0.5 to 1.5
- group_gain: float32 [2048], P('mp'), may hold values from 0.5 to 1.5
- second_gain: float32 [2048], replicated, may hold values from 0.5 to 1.5
Outputs:
- output: float32 [1024, 2048], P(('seq', 'mp'))
- grad_tokens: float32 [1024, 2048], P(('seq', 'mp'))
- grad_query: float32 [2048, 2048], P('seq', 'mp')
- grad_forget: float32 [2048, 2048], P('seq', 'mp')
- grad_inputs: float32 [2048, 2048], P('seq', 'mp')
- grad_gate: float32 [2048, 2048], P('seq', 'mp')
- grad_out: float32 [2048, 2048], P('mp', 'seq')
- grad_swiglu_gate: float32 [2048, 5632], P('seq', 'mp')
- grad_swiglu_up: float32 [2048, 5632], P('seq', 'mp')
- grad_swiglu_down: float32 [5632, 2048], P('mp', 'seq')
- grad_first_gain: float32 [2048], P('seq')
- grad_group_gain: float32 [2048], P(('mp', 'seq'))
- grad_second_gain: float32 [2048], P('seq')
The draws below stay inside these ranges and needn't reach their ends.
Inputs may be any that keep to these rules, and one draw needn't show every extreme that they name: 4 sequences packed in order, their lengths summing to 1024; one of them, at a seed-drawn place, is exactly 960 long; every other is at least max(1, 8) long. `lower_bound`: the same within each head's channels up to a factor of two.
All inputs are finite; a program needn't handle non-finite values.
Results may differ from the reference program's by a relative error of at most 0.0003.
Values sent between devices are 32-bit elements; how exact they have to be, the bound alone decides.
A program may use at most 256 MiB of HBM per device.

```python
import math
import jax
import jax.numpy as jnp
from jax import lax

D = 2048
HEADS = 16
HDIM = 128
FF = 5632
TOK_DEV = 128
NSEQ = 4
TOKENS = 1024


def draw_lengths(key, part):
    key = jax.random.fold_in(key, 5)
    key_cut, key_place = jax.random.split(key)
    others = TOK_DEV // 2
    least = max(1, TOK_DEV // 16)
    spare = others - (NSEQ - 1) * least
    cuts = jnp.sort(jax.random.randint(key_cut, (NSEQ - 2,), 0, spare + 1)).astype(jnp.int32)
    edges = jnp.concatenate([jnp.zeros((1,), jnp.int32), cuts, jnp.full((1,), spare, jnp.int32)])
    pieces = jnp.diff(edges) + least
    place = jax.random.randint(key_place, (), 0, NSEQ)
    indices = jnp.arange(NSEQ, dtype=jnp.int32)
    shifted = jnp.minimum(jnp.where(indices > place, indices - 1, indices), NSEQ - 2)
    return jnp.where(indices == place, TOKENS - others, pieces[shifted]).astype(jnp.int32)


def draw_lower_bound(key, part):
    key = jax.random.fold_in(key, 11)
    key_head, key_chan = jax.random.split(key)
    lowest = math.log(0.5 / TOKENS)
    highest = math.log(0.05)
    head_rate = jnp.exp(jax.random.uniform(key_head, (HEADS, 1), jnp.float32, lowest, highest))
    jitter = jax.random.uniform(key_chan, (HEADS, HDIM), jnp.float32, 0.7, 1.4)
    rate = jnp.minimum(head_rate * jitter, 0.06).reshape(-1)
    return 1.0 - rate


def block_scale(own_key, extent, shards, low, largest):
    level = 1.0
    for position, blocks in shards:
        steps = jax.random.uniform(jax.random.fold_in(jax.random.fold_in(own_key, 6), position), (blocks,), jnp.float32, low / len(shards), largest / len(shards))
        level = level * jnp.repeat(jnp.exp(steps), extent[position] // blocks).reshape((-1,) + (1,) * (len(extent) - 1 - position))
    return level


def gaussian(rng, shape, scale, most, cuts=(), kind=jnp.bfloat16):
    values = jax.random.normal(rng, shape, jnp.float32) * scale
    if len(cuts) > 0:
        values = block_scale(rng, shape, cuts, -0.22, 0.18) * values
    return jnp.clip(values, min=-most, max=most).astype(kind)


def setup_inputs(seed: int = 0) -> dict:
    keys = jax.random.split(jax.random.key(seed), 16)
    return {
        "tokens_in": gaussian(keys[0], (TOKENS, D), 1.0, 6.0, ((0, 8),), jnp.float32),
        "cotangent": gaussian(keys[1], (TOKENS, D), 1.0, 6.0, ((0, 8),), jnp.float32),
        "lengths": draw_lengths(jax.random.fold_in(keys[15], 71), 0),
        "lower_bound": draw_lower_bound(jax.random.fold_in(keys[15], 71), 0),
        "query_weight": gaussian(keys[4], (D, D), D ** -0.5, 0.125, ((1, 4),), jnp.float32),
        "forget_weight": gaussian(keys[5], (D, D), D ** -0.5, 0.125, ((1, 4),), jnp.float32),
        "input_weight": gaussian(keys[6], (D, D), D ** -0.5, 0.125, ((1, 4),), jnp.float32),
        "gate_weight": gaussian(keys[7], (D, D), D ** -0.5, 0.125, ((1, 4),), jnp.float32),
        "out_weight": gaussian(keys[8], (D, D), (D // 4) ** -0.5, 0.25, ((0, 4),), jnp.float32),
        "swiglu_gate": gaussian(keys[9], (D, FF), D ** -0.5, 0.125, ((1, 4),), jnp.float32),
        "swiglu_up": gaussian(keys[10], (D, FF), D ** -0.5, 0.125, ((1, 4),), jnp.float32),
        "swiglu_down": gaussian(keys[11], (FF, D), (FF // 4) ** -0.5, 0.15625, ((0, 4),), jnp.float32),
        "first_gain": jnp.clip(1.0 + 0.1 * jax.random.normal(keys[12], (D,), jnp.float32), 0.5, 1.5),
        "group_gain": jnp.clip(1.0 + 0.1 * jax.random.normal(keys[13], (D,), jnp.float32), 0.5, 1.5),
        "second_gain": jnp.clip(1.0 + 0.1 * jax.random.normal(keys[14], (D,), jnp.float32), 0.5, 1.5),
    }


@jax.custom_vjp
def low(v):
    return lax.optimization_barrier(v.astype(jnp.bfloat16)).astype(jnp.float32)

@jax.custom_vjp
def low_back(v):
    return v

def low_keep(v):
    return (low(v), None)

def low_pass(kept, grad):
    return (grad,)

def back_keep(v):
    return (v, None)

def back_low(kept, grad):
    return (low(grad),)
low.defvjp(low_keep, low_pass)
low_back.defvjp(back_keep, back_low)
TOP_PRECISION = lax.Precision.HIGHEST
norm_eps = 1e-06
group_eps = 1e-05

def matmul(left, right):
    return jnp.dot(left, right, precision=TOP_PRECISION)

def rms_norm(entries, gain):
    return entries * lax.rsqrt(lax.optimization_barrier(jnp.mean(entries * entries, -1, keepdims=True)) + norm_eps) * gain

def end_update(carried_state, key_vecs, value_rows, segment, carry_marker, log_decay):
    trailing_decay = jnp.exp(log_decay[-1])
    in_last = (segment == segment[-1]).astype(key_vecs.dtype)
    weighted_terms = key_vecs * jnp.exp(log_decay[-1][None] - log_decay) * in_last[:, None, None]
    return carried_state * (trailing_decay * carry_marker[-1])[:, :, None] + jnp.einsum('bef,bey->efy', weighted_terms, value_rows, precision=TOP_PRECISION)

def out_step(carried_state, pieces):
    query_rows, key_vecs, value_rows, segment, flag_bool = pieces
    carry_marker = flag_bool.astype(key_vecs.dtype)
    log_decay = jnp.cumsum(jnp.log1p(-key_vecs), 0)
    growth_factor = jnp.exp(log_decay)
    scores = jnp.einsum('thk,shk->hts', query_rows * growth_factor, key_vecs * jnp.exp(-log_decay), precision=TOP_PRECISION)
    places = jnp.arange(key_vecs.shape[0])
    allowed = (places[:, None] >= places[None, :]) & (segment[:, None] == segment[None, :])
    scores = jnp.where(allowed[None], scores, 0.0)
    output_rows = jnp.einsum('hts,shv->thv', scores, value_rows, precision=TOP_PRECISION)
    output_rows = output_rows + jnp.einsum('dsj,sjp->dsp', query_rows * growth_factor * carry_marker[:, None, None], carried_state, precision=TOP_PRECISION)
    return (end_update(carried_state, key_vecs, value_rows, segment, carry_marker, log_decay), output_rows)

def block_flags(segment, segment_before, block_size):
    block_count = segment.shape[0] // block_size
    shifted = jnp.concatenate([jnp.reshape(segment_before, (1,)).astype(jnp.int32), segment[:-1]])
    first_segs = shifted.reshape(block_count, block_size)[:, 0]
    blocked = segment.reshape(block_count, block_size)
    return (blocked, blocked == first_segs[:, None])

def run_blocks(query_rows, key_vecs, value_rows, segment, block_size):
    token_count, head_count, width = query_rows.shape
    block_count = token_count // block_size
    blocked, flags = block_flags(segment, jnp.array(-1, jnp.int32), block_size)

    def split(entries):
        return entries.reshape(block_count, block_size, head_count, width)
    start = jnp.zeros((head_count, width, width), query_rows.dtype)
    _, output_rows = lax.scan(jax.checkpoint(out_step), start, (split(query_rows), split(key_vecs), split(value_rows), blocked, flags))
    return output_rows.reshape(token_count, head_count, width)

def reference(tokens_in, cotangent, lengths, lower_bound, query_weight, forget_weight, input_weight, gate_weight, out_weight, swiglu_gate, swiglu_up, swiglu_down, first_gain, group_gain, second_gain):
    positions = jnp.arange(TOKENS, dtype=jnp.int32)
    offsets = (jnp.cumsum(lengths) - lengths).astype(jnp.int32)
    segment = (lax.optimization_barrier(jnp.sum((positions[:, None] >= offsets[None, :]).astype(jnp.int32), 1)) - 1).astype(jnp.int32)

    def forward(tokens, w_query, w_forget, w_input, w_gate, w_out, w_sgate, w_sup, w_sdown, gain_one, gain_group, gain_two):
        normed_one = rms_norm(tokens, gain_one)
        query_rows = jax.nn.silu(matmul(normed_one, w_query)).reshape(TOKENS, HEADS, HDIM)
        key_vecs = ((1.0 - lower_bound) * jax.nn.sigmoid(-matmul(normed_one, w_forget))).reshape(TOKENS, HEADS, HDIM)
        value_rows = matmul(normed_one, w_input).reshape(TOKENS, HEADS, HDIM)
        gate_in = matmul(normed_one, w_gate)
        raw = run_blocks(query_rows, key_vecs, value_rows, segment, min(64, TOKENS))
        normed_raw = raw * lax.rsqrt(lax.optimization_barrier(jnp.mean(raw * raw, -1, keepdims=True)) + group_eps)
        mixer = normed_raw.reshape(TOKENS, D) * gain_group * jax.nn.silu(gate_in)
        residual = tokens + matmul(mixer, w_out)
        normed_two = rms_norm(residual, gain_two)
        hidden = jax.nn.silu(matmul(normed_two, w_sgate)) * matmul(normed_two, w_sup)
        return residual + matmul(hidden, w_sdown)
    output, back = jax.vjp(forward, tokens_in, query_weight, forget_weight, input_weight, gate_weight, out_weight, swiglu_gate, swiglu_up, swiglu_down, first_gain, group_gain, second_gain)
    grads = back(cotangent)
    return (output, grads[0], grads[1], grads[2], grads[3], grads[4], grads[5], grads[6], grads[7], grads[8], grads[9], grads[10], grads[11])
```

```python
from functools import partial

import jax
import jax.numpy as jnp
from jax import lax
from jax.sharding import PartitionSpec as P

HDIM = 128
CHUNK = 128
HIGH = lax.Precision.HIGH
HIGHEST = lax.Precision.HIGHEST
norm_eps = 1e-06
group_eps = 1e-05


def dot(left, right, contract_left, contract_right, precision=HIGH):
    return lax.dot_general(
        left,
        right,
        (((contract_left,), (contract_right,)), ((), ())),
        precision=precision,
        preferred_element_type=jnp.float32,
    )


def rms(entries):
    return lax.rsqrt(jnp.mean(entries * entries, -1, keepdims=True) + norm_eps)


def silu_grad(entries):
    gate = jax.nn.sigmoid(entries)
    return gate * (1.0 + entries * (1.0 - gate))


def gather_tokens(block):
    return lax.all_gather(block, "seq", axis=0, tiled=True)


def recurrence(query_rows, key_vecs, value_rows, segment):
    token_count, width = query_rows.shape
    heads = width // HDIM
    chunks = token_count // CHUNK

    def split(entries):
        return entries.reshape(chunks, CHUNK, heads, HDIM)

    blocked = segment.reshape(chunks, CHUNK)
    last_seg = blocked[:, -1]
    first_segs = jnp.concatenate([jnp.full((1,), -1, segment.dtype), last_seg[:-1]])
    carry = (blocked == first_segs[:, None]).astype(jnp.float32)
    in_last = (blocked == last_seg[:, None]).astype(jnp.float32)
    places = jnp.arange(CHUNK)
    allowed = (places[None, :, None] >= places[None, None, :]) & (
        blocked[:, :, None] == blocked[:, None, :]
    )
    lower = (places[:, None] >= places[None, :]).astype(jnp.float32)
    queries, keys, values = split(query_rows), split(key_vecs), split(value_rows)
    log_decay = jnp.einsum("ts,cshk->cthk", lower, jnp.log1p(-keys), precision=HIGHEST)
    growth = jnp.exp(log_decay)
    grown = queries * growth
    last = log_decay[:, -1]
    scores = jnp.einsum("cthk,cshk->chts", grown, keys * jnp.exp(-log_decay), precision=HIGH)
    scores = jnp.where(allowed[:, None], scores, 0.0)
    inner = jnp.einsum("chts,cshv->cthv", scores, values, precision=HIGH)
    weighted = keys * jnp.exp(last[:, None] - log_decay) * in_last[:, :, None, None]
    updates = jnp.einsum("cshk,cshv->chkv", weighted, values, precision=HIGH)
    through = jnp.exp(last) * carry[:, -1][:, None, None]
    state = jnp.zeros_like(updates[0])
    states = []
    for chunk in range(chunks):
        states.append(state)
        state = state * through[chunk][:, :, None] + updates[chunk]
    outer = jnp.einsum(
        "cthk,chkv->cthv", grown * carry[:, :, None, None], jnp.stack(states), precision=HIGH
    )
    return (inner + outer).reshape(token_count, width)


def mixer_all(pre_query, pre_forget, value_rows, gate_in, group_gain, lower_bound, segment):
    key_vecs = (1.0 - lower_bound) * jax.nn.sigmoid(-pre_forget)
    raw = recurrence(jax.nn.silu(pre_query), key_vecs, value_rows, segment)
    heads = raw.reshape(raw.shape[0], -1, HDIM)
    scale = lax.rsqrt(jnp.mean(heads * heads, -1, keepdims=True) + group_eps)
    normed = (heads * scale).reshape(raw.shape)
    return normed * group_gain * jax.nn.silu(gate_in)


def shards(
    tokens_in,
    cotangent,
    lengths,
    lower_bound,
    query_weight,
    forget_weight,
    input_weight,
    gate_weight,
    out_weight,
    swiglu_gate,
    swiglu_up,
    swiglu_down,
    first_gain,
    group_gain,
    second_gain,
):
    seq_count = lax.axis_size("seq")
    seq_place = lax.axis_index("seq")
    own_rows, model = tokens_in.shape
    token_count = own_rows * seq_count
    share_rows = own_rows // lax.axis_size("mp")
    share_start = lax.axis_index("mp") * share_rows
    start_row = seq_place * own_rows
    own_cols = model // seq_count
    start_col = seq_place * own_cols

    def own(entries):
        return lax.dynamic_slice_in_dim(entries, start_row, own_rows, 0)

    def columns(entries):
        return lax.dynamic_slice_in_dim(entries, start_col, own_cols, 1)

    def share(entries):
        return lax.dynamic_slice_in_dim(entries, share_start, share_rows, 0)

    positions = jnp.arange(token_count, dtype=jnp.int32)
    offsets = jnp.cumsum(lengths) - lengths
    segment = jnp.sum((positions[:, None] >= offsets[None, :]).astype(jnp.int32), 1) - 1

    all_tokens = gather_tokens(tokens_in)
    all_cotangent = gather_tokens(cotangent)
    normed_one = all_tokens * rms(all_tokens) * first_gain
    pre_query = dot(normed_one, query_weight, 1, 0)
    pre_forget = dot(normed_one, forget_weight, 1, 0)
    value_rows = dot(normed_one, input_weight, 1, 0)
    gate_in = dot(normed_one, gate_weight, 1, 0)
    mixer, mixer_back = jax.vjp(
        partial(mixer_all, lower_bound=lower_bound, segment=segment),
        pre_query,
        pre_forget,
        value_rows,
        gate_in,
        group_gain,
    )
    residual = tokens_in + lax.psum(dot(own(mixer), out_weight, 1, 0), "mp")
    scale_two = rms(residual)
    normed_two = residual * scale_two * second_gain
    grad_hidden_all = dot(all_cotangent, swiglu_down, 1, 1)
    a = dot(normed_two, swiglu_gate, 1, 0)
    b = dot(normed_two, swiglu_up, 1, 0)
    silu_a = jax.nn.silu(a)
    ffn_part = dot(silu_a * b, swiglu_down, 1, 0)
    output = share(residual) + lax.psum_scatter(ffn_part, "mp", scatter_dimension=0, tiled=True)
    e = own(grad_hidden_all)
    grad_a = e * b * silu_grad(a)
    grad_b = e * silu_a
    grad_normed_two = lax.psum(
        dot(grad_a, swiglu_gate, 1, 1) + dot(grad_b, swiglu_up, 1, 1), "mp"
    )
    pulled = grad_normed_two * second_gain
    grad_residual = (
        cotangent
        + scale_two * pulled
        - residual * scale_two**3 * jnp.mean(pulled * residual, -1, keepdims=True)
    )
    all_normed_two = gather_tokens(normed_two)
    a_all = dot(all_normed_two, swiglu_gate, 1, 0)
    b_all = dot(all_normed_two, swiglu_up, 1, 0)
    silu_all = jax.nn.silu(a_all)
    hidden_all = silu_all * b_all
    grad_a_all = grad_hidden_all * b_all * silu_grad(a_all)
    grad_b_all = grad_hidden_all * silu_all
    normed_two_cols = columns(all_normed_two)
    grad_sgate = dot(normed_two_cols, grad_a_all, 0, 0)
    grad_sup = dot(normed_two_cols, grad_b_all, 0, 0)
    grad_sdown = dot(hidden_all, columns(all_cotangent), 0, 0)

    grad_mixer = gather_tokens(dot(grad_residual, out_weight, 1, 1))
    residual_cols = lax.all_to_all(grad_residual, "seq", 1, 0, tiled=True)
    grad_outw = dot(mixer, residual_cols, 0, 0)
    grad_query_rows, grad_forget_rows, grad_value_rows, grad_gate_rows, grad_group = mixer_back(
        grad_mixer
    )
    grad_group = lax.dynamic_slice_in_dim(
        grad_group, seq_place * (group_gain.shape[0] // seq_count), group_gain.shape[0] // seq_count
    )
    normed_one_cols = columns(normed_one)
    pairs = (
        (grad_query_rows, query_weight),
        (grad_forget_rows, forget_weight),
        (grad_value_rows, input_weight),
        (grad_gate_rows, gate_weight),
    )
    weight_grads = []
    normed_part = 0.0
    first_sum = 0.0
    for grad_rows, weight in pairs:
        weight_grad = dot(normed_one_cols, grad_rows, 0, 0)
        weight_grads.append(weight_grad)
        normed_part = normed_part + dot(own(grad_rows), weight, 1, 1)
        own_weight = lax.dynamic_slice_in_dim(weight, start_col, own_cols, 0)
        first_sum = first_sum + jnp.sum(own_weight * weight_grad, 1)
    second_sum = jnp.sum(
        lax.dynamic_slice_in_dim(swiglu_gate, start_col, own_cols, 0) * grad_sgate
        + lax.dynamic_slice_in_dim(swiglu_up, start_col, own_cols, 0) * grad_sup,
        1,
    )
    gains = jnp.stack(
        [
            lax.dynamic_slice_in_dim(first_gain, start_col, own_cols),
            lax.dynamic_slice_in_dim(second_gain, start_col, own_cols),
        ]
    )
    gain_grads = lax.psum(jnp.stack([first_sum, second_sum]), "mp") / gains
    grad_normed_one = lax.psum_scatter(normed_part, "mp", scatter_dimension=0, tiled=True)
    tokens_share = share(tokens_in)
    scale_one = rms(tokens_share)
    pulled_one = grad_normed_one * first_gain
    grad_tokens = (
        share(grad_residual)
        + scale_one * pulled_one
        - tokens_share * scale_one**3 * jnp.mean(pulled_one * tokens_share, -1, keepdims=True)
    )
    return (
        output,
        grad_tokens,
        weight_grads[0],
        weight_grads[1],
        weight_grads[2],
        weight_grads[3],
        grad_outw,
        grad_sgate,
        grad_sup,
        grad_sdown,
        gain_grads[0],
        grad_group,
        gain_grads[1],
    )


def solution(mesh):
    in_specs = (
        P("seq", None),
        P("seq", None),
        P(),
        P("mp"),
        P(None, "mp"),
        P(None, "mp"),
        P(None, "mp"),
        P(None, "mp"),
        P("mp", None),
        P(None, "mp"),
        P(None, "mp"),
        P("mp", None),
        P(),
        P("mp"),
        P(),
    )
    out_specs = (
        P(("seq", "mp"), None),
        P(("seq", "mp"), None),
        P("seq", "mp"),
        P("seq", "mp"),
        P("seq", "mp"),
        P("seq", "mp"),
        P("mp", "seq"),
        P("seq", "mp"),
        P("seq", "mp"),
        P("mp", "seq"),
        P("seq"),
        P(("mp", "seq")),
        P("seq"),
    )
    return jax.shard_map(shards, mesh=mesh, in_specs=in_specs, out_specs=out_specs, check_vma=False)
```

```python
from functools import partial

import jax
import jax.numpy as jnp
from jax import lax
from jax.experimental import pallas as pl
from jax.experimental.pallas import tpu as pltpu
from jax.sharding import PartitionSpec as P

HDIM = 128
CHUNK = 128
HIGH = lax.Precision.HIGH
HIGHEST = lax.Precision.HIGHEST
norm_eps = 1e-06
group_eps = 1e-05


def dot(left, right, contract_left, contract_right, precision=HIGH):
    return lax.dot_general(
        left,
        right,
        (((contract_left,), (contract_right,)), ((), ())),
        precision=precision,
        preferred_element_type=jnp.float32,
    )


def rms(entries):
    return lax.rsqrt(jnp.mean(entries * entries, -1, keepdims=True) + norm_eps)


def silu_grad(entries):
    gate = jax.nn.sigmoid(entries)
    return gate * (1.0 + entries * (1.0 - gate))


def gather_tokens(block):
    return lax.all_gather(block, "seq", axis=0, tiled=True)


def recurrence(query_rows, key_vecs, value_rows, segment):
    token_count, width = query_rows.shape
    heads = width // HDIM
    chunks = token_count // CHUNK

    def split(entries):
        return entries.reshape(chunks, CHUNK, heads, HDIM)

    blocked = segment.reshape(chunks, CHUNK)
    last_seg = blocked[:, -1]
    first_segs = jnp.concatenate([jnp.full((1,), -1, segment.dtype), last_seg[:-1]])
    carry = (blocked == first_segs[:, None]).astype(jnp.float32)
    in_last = (blocked == last_seg[:, None]).astype(jnp.float32)
    places = jnp.arange(CHUNK)
    allowed = (places[None, :, None] >= places[None, None, :]) & (
        blocked[:, :, None] == blocked[:, None, :]
    )
    lower = (places[:, None] >= places[None, :]).astype(jnp.float32)
    queries, keys, values = split(query_rows), split(key_vecs), split(value_rows)
    log_decay = jnp.einsum("ts,cshk->cthk", lower, jnp.log1p(-keys), precision=HIGHEST)
    growth = jnp.exp(log_decay)
    grown = queries * growth
    last = log_decay[:, -1]
    scores = jnp.einsum("cthk,cshk->chts", grown, keys * jnp.exp(-log_decay), precision=HIGH)
    scores = jnp.where(allowed[:, None], scores, 0.0)
    inner = jnp.einsum("chts,cshv->cthv", scores, values, precision=HIGH)
    weighted = keys * jnp.exp(last[:, None] - log_decay) * in_last[:, :, None, None]
    updates = jnp.einsum("cshk,cshv->chkv", weighted, values, precision=HIGH)
    through = jnp.exp(last) * carry[:, -1][:, None, None]
    state = jnp.zeros_like(updates[0])
    states = []
    for chunk in range(chunks):
        states.append(state)
        state = state * through[chunk][:, :, None] + updates[chunk]
    outer = jnp.einsum(
        "cthk,chkv->cthv", grown * carry[:, :, None, None], jnp.stack(states), precision=HIGH
    )
    return (inner + outer).reshape(token_count, width)


def mixer_all(pre_query, pre_forget, value_rows, gate_in, group_gain, lower_bound, segment):
    key_vecs = (1.0 - lower_bound) * jax.nn.sigmoid(-pre_forget)
    raw = recurrence(jax.nn.silu(pre_query), key_vecs, value_rows, segment)
    heads = raw.reshape(raw.shape[0], -1, HDIM)
    scale = lax.rsqrt(jnp.mean(heads * heads, -1, keepdims=True) + group_eps)
    normed = (heads * scale).reshape(raw.shape)
    return normed * group_gain * jax.nn.silu(gate_in)


def shards(
    tokens_in,
    cotangent,
    lengths,
    lower_bound,
    query_weight,
    forget_weight,
    input_weight,
    gate_weight,
    out_weight,
    swiglu_gate,
    swiglu_up,
    swiglu_down,
    first_gain,
    group_gain,
    second_gain,
):
    seq_count = lax.axis_size("seq")
    seq_place = lax.axis_index("seq")
    own_rows, model = tokens_in.shape
    token_count = own_rows * seq_count
    share_rows = own_rows // lax.axis_size("mp")
    share_start = lax.axis_index("mp") * share_rows
    start_row = seq_place * own_rows
    own_cols = model // seq_count
    start_col = seq_place * own_cols

    def own(entries):
        return lax.dynamic_slice_in_dim(entries, start_row, own_rows, 0)

    def columns(entries):
        return lax.dynamic_slice_in_dim(entries, start_col, own_cols, 1)

    def share(entries):
        return lax.dynamic_slice_in_dim(entries, share_start, share_rows, 0)

    positions = jnp.arange(token_count, dtype=jnp.int32)
    offsets = jnp.cumsum(lengths) - lengths
    segment = jnp.sum((positions[:, None] >= offsets[None, :]).astype(jnp.int32), 1) - 1

    all_tokens = gather_tokens(tokens_in)
    all_cotangent = gather_tokens(cotangent)
    normed_one = all_tokens * rms(all_tokens) * first_gain
    pre_query = dot(normed_one, query_weight, 1, 0)
    pre_forget = dot(normed_one, forget_weight, 1, 0)
    value_rows = dot(normed_one, input_weight, 1, 0)
    gate_in = dot(normed_one, gate_weight, 1, 0)
    mixer, mixer_back = jax.vjp(
        partial(mixer_all, lower_bound=lower_bound, segment=segment),
        pre_query,
        pre_forget,
        value_rows,
        gate_in,
        group_gain,
    )
    residual = tokens_in + lax.psum(dot(own(mixer), out_weight, 1, 0), "mp")
    scale_two = rms(residual)
    normed_two = residual * scale_two * second_gain
    grad_hidden_all = dot(all_cotangent, swiglu_down, 1, 1)
    a = dot(normed_two, swiglu_gate, 1, 0)
    b = dot(normed_two, swiglu_up, 1, 0)
    silu_a = jax.nn.silu(a)
    ffn_part = dot(silu_a * b, swiglu_down, 1, 0)
    output = share(residual) + lax.psum_scatter(ffn_part, "mp", scatter_dimension=0, tiled=True)
    e = own(grad_hidden_all)
    grad_a = e * b * silu_grad(a)
    grad_b = e * silu_a
    grad_normed_two = lax.psum(
        dot(grad_a, swiglu_gate, 1, 1) + dot(grad_b, swiglu_up, 1, 1), "mp"
    )
    pulled = grad_normed_two * second_gain
    grad_residual = (
        cotangent
        + scale_two * pulled
        - residual * scale_two**3 * jnp.mean(pulled * residual, -1, keepdims=True)
    )
    all_normed_two = gather_tokens(normed_two)
    a_all = dot(all_normed_two, swiglu_gate, 1, 0)
    b_all = dot(all_normed_two, swiglu_up, 1, 0)
    silu_all = jax.nn.silu(a_all)
    hidden_all = silu_all * b_all
    grad_a_all = grad_hidden_all * b_all * silu_grad(a_all)
    grad_b_all = grad_hidden_all * silu_all
    normed_two_cols = columns(all_normed_two)
    grad_sgate = dot(normed_two_cols, grad_a_all, 0, 0)
    grad_sup = dot(normed_two_cols, grad_b_all, 0, 0)
    grad_sdown = dot(hidden_all, columns(all_cotangent), 0, 0)

    grad_mixer = gather_tokens(dot(grad_residual, out_weight, 1, 1))
    residual_cols = lax.all_to_all(grad_residual, "seq", 1, 0, tiled=True)
    grad_outw = dot(mixer, residual_cols, 0, 0)
    grad_query_rows, grad_forget_rows, grad_value_rows, grad_gate_rows, grad_group = mixer_back(
        grad_mixer
    )
    grad_group = lax.dynamic_slice_in_dim(
        grad_group, seq_place * (group_gain.shape[0] // seq_count), group_gain.shape[0] // seq_count
    )
    normed_one_cols = columns(normed_one)
    pairs = (
        (grad_query_rows, query_weight),
        (grad_forget_rows, forget_weight),
        (grad_value_rows, input_weight),
        (grad_gate_rows, gate_weight),
    )
    weight_grads = []
    normed_part = 0.0
    first_sum = 0.0
    for grad_rows, weight in pairs:
        weight_grad = dot(normed_one_cols, grad_rows, 0, 0)
        weight_grads.append(weight_grad)
        normed_part = normed_part + dot(own(grad_rows), weight, 1, 1)
        own_weight = lax.dynamic_slice_in_dim(weight, start_col, own_cols, 0)
        first_sum = first_sum + jnp.sum(own_weight * weight_grad, 1)
    second_sum = jnp.sum(
        lax.dynamic_slice_in_dim(swiglu_gate, start_col, own_cols, 0) * grad_sgate
        + lax.dynamic_slice_in_dim(swiglu_up, start_col, own_cols, 0) * grad_sup,
        1,
    )
    gains = jnp.stack(
        [
            lax.dynamic_slice_in_dim(first_gain, start_col, own_cols),
            lax.dynamic_slice_in_dim(second_gain, start_col, own_cols),
        ]
    )
    gain_grads = lax.psum(jnp.stack([first_sum, second_sum]), "mp") / gains
    grad_normed_one = lax.psum_scatter(normed_part, "mp", scatter_dimension=0, tiled=True)
    tokens_share = share(tokens_in)
    scale_one = rms(tokens_share)
    pulled_one = grad_normed_one * first_gain
    grad_tokens = (
        share(grad_residual)
        + scale_one * pulled_one
        - tokens_share * scale_one**3 * jnp.mean(pulled_one * tokens_share, -1, keepdims=True)
    )
    return (
        output,
        grad_tokens,
        weight_grads[0],
        weight_grads[1],
        weight_grads[2],
        weight_grads[3],
        grad_outw,
        grad_sgate,
        grad_sup,
        grad_sdown,
        gain_grads[0],
        grad_group,
        gain_grads[1],
    )


Z, X = 4, 2


def z_shift(array, distance):
    steps = [(z * X + x, (z + distance) % Z * X + x) for z in range(Z) for x in range(X)]
    return lax.ppermute(array, "seq", steps)


def x_swap(array):
    return lax.ppermute(array, "seq", [(s, s ^ 1) for s in range(Z * X)])


def core_swap(array):
    return lax.ppermute(array, "mp", [(m, m ^ 1) for m in range(4)])


def y_swap(array):
    return lax.ppermute(array, "mp", [(m, m ^ 2) for m in range(4)])


def cut(array, place, size, axis):
    return lax.dynamic_slice_in_dim(array, place * size, size, axis)


def in_order(first, mine, other, axis):
    return jnp.where(
        first, jnp.concatenate([mine, other], axis), jnp.concatenate([other, mine], axis)
    )


def in_place(shifted, z):
    return [lax.select_n((z - here) % Z, *shifted) for here in range(Z)]


def core_place():
    return lax.axis_index("mp") % 2


def scatter_over_mp(part):
    rows = part.shape[0] // 4
    core = core_place()
    place = lax.axis_index("mp") // 2
    pieces = part.reshape(2, 2, rows, part.shape[1])

    def of_core(index):
        return lax.dynamic_index_in_dim(pieces, index, 1, False)

    mine = of_core(core) + core_swap(of_core(1 - core))

    def of_y(index):
        return lax.dynamic_index_in_dim(mine, index, 0, False)

    return of_y(place) + y_swap(of_y(1 - place))


F32, BF16 = jnp.float32, jnp.bfloat16
MESH = pl.DeviceIdType.MESH
ANY = pl.BlockSpec(memory_space=pl.ANY)
TILE = 256
VMEM_BYTES = 60 << 20


def halves(entries):
    high = entries.astype(BF16)
    return high, (entries - high.astype(F32)).astype(BF16)


def product(left, right, contract_left, contract_right):
    return lax.dot_general(
        left,
        right,
        (((contract_left,), (contract_right,)), ((), ())),
        preferred_element_type=F32,
    )


def three_pass(left, right, contract_left, contract_right):
    (left_high, left_low), (right_high, right_low) = left, right
    return product(left_high, right_high, contract_left, contract_right) + (
        product(left_high, right_low, contract_left, contract_right)
        + product(left_low, right_high, contract_left, contract_right)
    )


def remote(src, dst, sems, index, device):
    return pltpu.make_async_remote_copy(
        src_ref=src,
        dst_ref=dst,
        send_sem=sems[0].at[index],
        recv_sem=sems[1].at[index],
        device_id=device,
        device_id_type=MESH,
    )


def where_am_i():
    place, part = lax.axis_index("seq"), lax.axis_index("mp")
    return place // X, place % X, part // 2, part % 2


class Gather:
    spec = pl.BlockSpec(memory_space=pl.ANY)

    def shape(block):
        return (Z * X * block.shape[0], block.shape[1])

    def scratch(block):
        return [
            pltpu.SemaphoreType.DMA((26,)),
            pltpu.SemaphoreType.DMA((26,)),
            pltpu.SemaphoreType.DMA((1,)),
        ]

    def __init__(self, block_ref, out_ref, send, recv, local):
        self.block, self.out, self.sems_here, self.local = block_ref, out_ref, (send, recv), local
        self.z, self.x, self.y, self.core = where_am_i()
        self.rows, self.half = block_ref.shape[0], block_ref.shape[1] // 2

    def device(self, z, x, core):
        return (z * X + x, self.y * 2 + core)

    def region(self, z, x, core):
        return self.out.at[
            pl.ds(pl.multiple_of((z * X + x) * self.rows, self.rows), self.rows),
            pl.ds(pl.multiple_of(core * self.half, self.half), self.half),
        ]

    def own(self):
        return self.block.at[:, pl.ds(pl.multiple_of(self.core * self.half, self.half), self.half)]

    def along(self, way, step, arriving):
        source = self.z - way * (step if arriving else step - 1)
        src = self.own() if step == 1 and not arriving else self.region(source, self.x, self.core)
        return remote(
            src,
            self.region(source, self.x, self.core),
            self.sems_here,
            (0 if way > 0 else 3) + step - 1,
            self.device(self.z + way, self.x, self.core),
        )

    def across(self, way, step, arriving):
        source = self.z - way * step
        x = 1 - self.x if arriving else self.x
        src = self.own() if step == 0 and not arriving else self.region(source, x, self.core)
        return remote(
            src,
            self.region(source, x, self.core),
            self.sems_here,
            6 + (0 if step == 0 else (0 if way > 0 else 3) + step),
            self.device(self.z, 1 - self.x, self.core),
        )

    def inside(self, way, step, other_x, arriving):
        source = self.z - way * step
        x = 1 - self.x if other_x else self.x
        core = 1 - self.core if arriving else self.core
        region = self.region(source, x, core)
        index = (0 if way > 0 else 3) + step
        return remote(
            region,
            region,
            self.sems_here,
            13 + index if other_x else 13 + 6 + index,
            self.device(self.z, self.x, 1 - self.core),
        )

    def holds(self, way, step):
        source = self.z - way * step
        return (source >= 0) & (source < Z)

    def goes_on(self, way, step):
        return self.holds(way, step - 1) & (self.z + way >= 0) & (self.z + way < Z)

    def when_holds(self, way, step, action):
        if step == 0:
            action()
        else:
            pl.when(self.holds(way, step))(action)

    def greet(self):
        barrier = pltpu.get_barrier_semaphore()

        def signal(device):
            pl.semaphore_signal(barrier, inc=1, device_id=device, device_id_type=MESH)

        signal(self.device(self.z, 1 - self.x, self.core))
        signal(self.device(self.z, self.x, 1 - self.core))
        for way in (1, -1):
            ahead = (self.z + way >= 0) & (self.z + way < Z)
            pl.when(ahead)(lambda way=way: signal(self.device(self.z + way, self.x, self.core)))
        neighbours = jnp.where(self.z > 0, 1, 0) + jnp.where(self.z < Z - 1, 1, 0)
        pl.semaphore_wait(barrier, 2 + neighbours)

    def own_copy(self):
        row = pl.multiple_of((self.z * X + self.x) * self.rows, self.rows)
        return pltpu.make_async_copy(
            self.block, self.out.at[pl.ds(row, self.rows), :], self.local.at[0]
        )

    def begin(self):
        self.greet()
        self.own_copy().start()
        for way in (1, -1):
            pl.when(self.goes_on(way, 1))(lambda way=way: self.along(way, 1, False).start())
        self.across(1, 0, False).start()

    def arrive_along(self, step):
        for way in (1, -1):

            def action(way=way):
                self.along(way, step, True).wait_recv()
                if step < Z - 1:
                    pl.when(self.goes_on(way, step + 1))(
                        lambda: self.along(way, step + 1, False).start()
                    )
                self.across(way, step, False).start()
                self.inside(way, step, False, False).start()

            self.when_holds(way, step, action)

    def arrive_across(self, step):
        for way in (1, -1) if step else (1,):

            def action(way=way):
                self.across(way, step, True).wait_recv()
                self.inside(way, step, True, False).start()

            self.when_holds(way, step, action)

    def finish(self):
        self.own_copy().wait()
        for way in (1, -1):
            for step in range(1, Z):
                pl.when(self.goes_on(way, step))(
                    lambda way=way, step=step: self.along(way, step, False).wait_send()
                )
        for step in range(Z):
            for way in (1, -1) if step else (1,):

                def action(way=way, step=step):
                    self.across(way, step, False).wait_send()
                    self.inside(way, step, True, False).wait_send()
                    self.inside(way, step, True, True).wait_recv()
                    if step:
                        self.inside(way, step, False, False).wait_send()
                        self.inside(way, step, False, True).wait_recv()

                self.when_holds(way, step, action)

    def events(self):
        def round_of(step):
            def event():
                self.arrive_along(step)
                self.arrive_across(step - 1)

            return event

        return [round_of(step) for step in range(1, Z)] + [
            lambda: self.arrive_across(Z - 1),
            self.finish,
        ]


def move_only(kind, array, collective_id):
    def kernel(array_ref, out_ref, *scratch):
        move = kind(array_ref, out_ref, *scratch)
        move.begin()
        for event in move.events():
            event()

    return pl.pallas_call(
        kernel,
        out_shape=jax.ShapeDtypeStruct(kind.shape(array), F32),
        in_specs=[kind.spec],
        out_specs=kind.spec,
        scratch_shapes=kind.scratch(array),
        compiler_params=pltpu.CompilerParams(collective_id=collective_id, has_side_effects=True),
        cost_estimate=pl.CostEstimate(flops=0, bytes_accessed=16 << 20, transcendentals=0),
    )(array)


def load_halves(src_ref, high_ref, low_ref, stage_ref, sem):
    rows = stage_ref.shape[1]
    count = src_ref.shape[0] // rows

    def fetch(index):
        return pltpu.make_async_copy(
            src_ref.at[pl.ds(index * rows, rows), :], stage_ref.at[index % 2], sem.at[index % 2]
        )

    fetch(0).start()
    for index in range(count):
        if index + 1 < count:
            fetch(index + 1).start()
        fetch(index).wait()
        high, low = halves(stage_ref[index % 2])
        high_ref[index * rows : (index + 1) * rows, :] = high
        low_ref[index * rows : (index + 1) * rows, :] = low


def at_steps(events, steps):
    step = pl.program_id(0)
    for event, when in zip(events, steps, strict=True):
        pl.when(step == when)(event)


def beside_product(kind, array, left, weights, by_rows, collective_id, steps):
    rows, inner = left.shape
    count = len(weights)
    if count > 1:
        tiles, columns = count, count * TILE
    else:
        columns = weights[0].shape[0 if by_rows else 1]
        tiles = pl.cdiv(columns, TILE)

    def kernel(array_ref, left_ref, *refs):
        weight_refs, refs = refs[:count], refs[count:]
        out_ref, product_ref, high_ref, low_ref, stage_ref, stage_sem, weight_buf, weight_sem, *scratch = refs
        move = kind(array_ref, out_ref, *scratch)
        step = pl.program_id(0)
        pl.when(step == 0)(move.begin)
        if count > 1:
            start = pl.multiple_of((lax.axis_index("seq") % X) * TILE, TILE)

            def fetch(index):
                return pltpu.make_async_copy(
                    weight_refs[index].at[:, pl.ds(start, TILE)],
                    weight_buf.at[index % 2],
                    weight_sem.at[index % 2],
                )

            pl.when(step == 0)(fetch(0).start)
            for index in range(count - 1):
                pl.when(step == index)(fetch(index + 1).start)
        pl.when(step == 0)(
            lambda: load_halves(left_ref, high_ref, low_ref, stage_ref, stage_sem)
        )
        if count > 1:
            for index in range(count):
                pl.when(step == index)(fetch(index).wait)
            weight = weight_buf[lax.rem(step, 2)]
        else:
            weight = weight_refs[0][...]
        product_ref[...] = three_pass(
            (high_ref[...], low_ref[...]), halves(weight), 1, 1 if by_rows else 0
        )
        at_steps(move.events(), steps)

    if count > 1:
        weight_spec = ANY
    elif by_rows:
        weight_spec = pl.BlockSpec((TILE, inner), lambda tile: (tile, 0))
    else:
        weight_spec = pl.BlockSpec((inner, TILE), lambda tile: (0, tile))
    return pl.pallas_call(
        kernel,
        grid=(tiles,),
        out_shape=[
            jax.ShapeDtypeStruct(kind.shape(array), F32),
            jax.ShapeDtypeStruct((rows, columns), F32),
        ],
        in_specs=[kind.spec, ANY] + [weight_spec] * count,
        out_specs=[kind.spec, pl.BlockSpec((rows, TILE), lambda tile: (0, tile))],
        scratch_shapes=[
            pltpu.VMEM((rows, inner), BF16),
            pltpu.VMEM((rows, inner), BF16),
            pltpu.VMEM((2, 128, inner), F32),
            pltpu.SemaphoreType.DMA((2,)),
            pltpu.VMEM((2, inner, TILE) if count > 1 else (8, 128), F32),
            pltpu.SemaphoreType.DMA((2,)),
            *kind.scratch(array),
        ],
        compiler_params=pltpu.CompilerParams(
            collective_id=collective_id, has_side_effects=True, vmem_limit_bytes=VMEM_BYTES
        ),
        cost_estimate=pl.CostEstimate(
            flops=6 * rows * inner * columns, bytes_accessed=48 << 20, transcendentals=0
        ),
    )(array, left, *weights)


class Sum:
    spec = pl.BlockSpec(memory_space=pltpu.VMEM)

    def shape(part):
        return part.shape

    def scratch(part):
        rows, half = part.shape[0], part.shape[1] // 2
        return [
            pltpu.VMEM((4, rows, half), F32),
            pltpu.SemaphoreType.DMA((3,)),
            pltpu.SemaphoreType.DMA((3,)),
        ]

    def __init__(self, part_ref, out_ref, landing, send, recv):
        self.part, self.out, self.landing, self.sems_here = part_ref, out_ref, landing, (send, recv)
        self.z, self.x, self.y, self.core = where_am_i()
        self.half = part_ref.shape[1] // 2

    def columns(self, ref, core):
        return ref.at[:, pl.ds(pl.multiple_of(core * self.half, self.half), self.half)]

    def device(self, y, core):
        return (self.z * X + self.x, y * 2 + core)

    def first(self):
        return remote(
            self.columns(self.part, 1 - self.core),
            self.landing.at[0],
            self.sems_here,
            0,
            self.device(self.y, 1 - self.core),
        )

    def second(self):
        return remote(
            self.landing.at[1],
            self.landing.at[2],
            self.sems_here,
            1,
            self.device(1 - self.y, self.core),
        )

    def third(self):
        return remote(
            self.landing.at[1],
            self.landing.at[3],
            self.sems_here,
            2,
            self.device(self.y, 1 - self.core),
        )

    def begin(self):
        barrier = pltpu.get_barrier_semaphore()
        for device in (self.device(self.y, 1 - self.core), self.device(1 - self.y, self.core)):
            pl.semaphore_signal(barrier, inc=1, device_id=device, device_id_type=MESH)
        pl.semaphore_wait(barrier, 2)
        self.first().start()

    def to_y(self):
        self.first().wait()
        self.landing[1] = self.columns(self.part, self.core)[...] + self.landing[0]
        self.second().start()

    def back(self):
        self.second().wait()
        self.landing[1] = self.landing[1] + self.landing[2]
        self.third().start()

    def finish(self):
        self.third().wait()
        self.columns(self.out, self.core)[...] = self.landing[1]
        self.columns(self.out, 1 - self.core)[...] = self.landing[3]

    def events(self):
        return [self.to_y, self.back, self.finish]


def hidden_and_sum(part, normed_two, grad_hidden, w_gate, w_up, normed_cols, cot_cols, collective_id, steps):
    rows, inner = normed_two.shape
    columns = w_gate.shape[1]
    narrow = normed_cols.shape[1]
    tiles = pl.cdiv(columns, TILE)

    def kernel(
        part_ref, normed_ref, e_ref, gate_ref, up_ref, normed_cols_ref, cot_cols_ref,
        sum_ref, grad_gate_ref, grad_up_ref, grad_down_ref,
        high_ref, low_ref, stage_ref, stage_sem, *sum_scratch,
    ):
        total = Sum(part_ref, sum_ref, *sum_scratch)
        step = pl.program_id(0)
        pl.when(step == 0)(total.begin)
        pl.when(step == 0)(
            lambda: load_halves(normed_ref, high_ref, low_ref, stage_ref, stage_sem)
        )
        normed = high_ref[...], low_ref[...]
        a = three_pass(normed, halves(gate_ref[...]), 1, 0)
        b = three_pass(normed, halves(up_ref[...]), 1, 0)
        gate = jax.nn.sigmoid(a)
        silu_a = a * gate
        e = e_ref[...]
        cols = halves(normed_cols_ref[...])
        grad_gate_ref[...] = three_pass(
            cols, halves(e * b * (gate * (1.0 + a * (1.0 - gate)))), 0, 0
        )
        grad_up_ref[...] = three_pass(cols, halves(e * silu_a), 0, 0)
        grad_down_ref[...] = three_pass(halves(silu_a * b), halves(cot_cols_ref[...]), 0, 0)
        at_steps(total.events(), steps)

    whole = pl.BlockSpec(memory_space=pltpu.VMEM)
    by_column = pl.BlockSpec((inner, TILE), lambda tile: (0, tile))
    grad_spec = pl.BlockSpec((narrow, TILE), lambda tile: (0, tile))
    return pl.pallas_call(
        kernel,
        grid=(tiles,),
        out_shape=[
            jax.ShapeDtypeStruct(part.shape, F32),
            jax.ShapeDtypeStruct((narrow, columns), F32),
            jax.ShapeDtypeStruct((narrow, columns), F32),
            jax.ShapeDtypeStruct((columns, narrow), F32),
        ],
        in_specs=[
            Sum.spec, ANY, pl.BlockSpec((rows, TILE), lambda tile: (0, tile)), by_column, by_column, whole, whole,
        ],
        out_specs=[
            whole, grad_spec, grad_spec, pl.BlockSpec((TILE, narrow), lambda tile: (tile, 0)),
        ],
        scratch_shapes=[
            pltpu.VMEM((rows, inner), BF16),
            pltpu.VMEM((rows, inner), BF16),
            pltpu.VMEM((2, 128, inner), F32),
            pltpu.SemaphoreType.DMA((2,)),
        ]
        + Sum.scratch(part),
        compiler_params=pltpu.CompilerParams(
            collective_id=collective_id, has_side_effects=True, vmem_limit_bytes=VMEM_BYTES
        ),
        cost_estimate=pl.CostEstimate(
            flops=15 * rows * inner * columns, bytes_accessed=48 << 20, transcendentals=0
        ),
    )(part, normed_two, grad_hidden, w_gate, w_up, normed_cols, cot_cols)


def fast_shards(
    tokens_in,
    cotangent,
    lengths,
    lower_bound,
    query_weight,
    forget_weight,
    input_weight,
    gate_weight,
    out_weight,
    swiglu_gate,
    swiglu_up,
    swiglu_down,
    first_gain,
    group_gain,
    second_gain,
):
    place = lax.axis_index("seq")
    z, x = place // X, place % X
    core = core_place()
    rows, model = tokens_in.shape
    wide = model // Z
    narrow = model // (Z * X)
    width = query_weight.shape[1] // X
    share_rows = rows // 4

    def share(entries):
        return cut(entries, lax.axis_index("mp"), share_rows, 0)

    def own(entries, at):
        return cut(entries, at, rows, 0)

    token_count = rows * Z * X
    positions = jnp.arange(token_count, dtype=jnp.int32)
    offsets = jnp.cumsum(lengths) - lengths
    segment = jnp.sum((positions[:, None] >= offsets[None, :]).astype(jnp.int32), 1) - 1

    all_tokens = move_only(Gather, tokens_in, 1)
    normed_one = all_tokens * rms(all_tokens) * first_gain
    in_weights = (query_weight, forget_weight, input_weight, gate_weight)
    all_cotangent, projected = beside_product(
        Gather, cotangent, normed_one, in_weights, False, 2, (1, 2, 3, 3, 3)
    )
    mixer, mixer_back = jax.vjp(
        partial(mixer_all, lower_bound=cut(lower_bound, x, width, 0), segment=segment),
        *jnp.split(projected, 4, 1),
        cut(group_gain, x, width, 0),
    )
    mixer_other = x_swap(own(mixer, place + 1 - 2 * x))
    mixer_part = dot(own(mixer, place), cut(out_weight, x, width, 0), 1, 0) + dot(
        mixer_other, cut(out_weight, 1 - x, width, 0), 1, 0
    )
    mixer_sum, grad_hidden_all = beside_product(
        Sum, mixer_part, all_cotangent, (swiglu_down,), True, 3, (0, 4, 5)
    )
    residual = tokens_in + mixer_sum
    scale_two = rms(residual)
    normed_two = residual * scale_two * second_gain
    all_normed_two = move_only(Gather, normed_two, 4)

    a = dot(normed_two, swiglu_gate, 1, 0)
    b = dot(normed_two, swiglu_up, 1, 0)
    silu_a = jax.nn.silu(a)
    e = own(grad_hidden_all, place)
    normed_two_part = dot(e * b * silu_grad(a), swiglu_gate, 1, 1) + dot(
        e * silu_a, swiglu_up, 1, 1
    )
    ffn_part = dot(silu_a * b, swiglu_down, 1, 0)
    grad_normed_two, grad_sgate, grad_sup, grad_sdown = hidden_and_sum(
        normed_two_part,
        all_normed_two,
        grad_hidden_all,
        swiglu_gate,
        swiglu_up,
        cut(all_normed_two, place, narrow, 1),
        cut(all_cotangent, place, narrow, 1),
        5,
        (0, 2, 3),
    )
    pulled = grad_normed_two * second_gain
    grad_residual = (
        cotangent
        + scale_two * pulled
        - residual * scale_two**3 * jnp.mean(pulled * residual, -1, keepdims=True)
    )
    output = share(residual) + scatter_over_mp(ffn_part)

    grad_mixer_own = dot(grad_residual, out_weight, 1, 1)
    grad_mixer_here = jnp.stack(
        [cut(grad_mixer_own, x, width, 1), x_swap(cut(grad_mixer_own, 1 - x, width, 1))]
    )
    at_z = [grad_mixer_here] + [z_shift(grad_mixer_here, distance) for distance in range(1, Z)]
    grad_mixer = jnp.stack(in_place(at_z, z))
    grad_mixer = jnp.where(x == 0, grad_mixer, grad_mixer[:, ::-1]).reshape(token_count, width)

    half = wide // 2
    residual_parts = [
        cut(grad_residual, ((z + distance) % Z) * 2 + core, half, 1) for distance in range(Z)
    ]
    residual_parts = [residual_parts[0]] + [
        z_shift(residual_parts[distance], distance) for distance in range(1, Z)
    ]
    residual_mine = jnp.stack(in_place(residual_parts, z))
    residual_mine = in_order(
        x == 0, residual_mine[:, None], x_swap(residual_mine)[:, None], 1
    ).reshape(token_count, half)
    residual_cols = in_order(core == 0, residual_mine, core_swap(residual_mine), 1)

    *grad_rows, grad_group = mixer_back(grad_mixer)
    grad_group = jnp.where(
        x == 0,
        jnp.concatenate([grad_group, jnp.zeros_like(grad_group)]),
        jnp.concatenate([jnp.zeros_like(grad_group), grad_group]),
    )
    grad_group = cut(
        grad_group + x_swap(grad_group), place, group_gain.shape[0] // (Z * X), 0
    )
    others = x_swap(jnp.stack([own(part, place + 1 - 2 * x) for part in grad_rows]))
    normed_part = 0.0
    for index, weight in enumerate(in_weights):
        normed_part = normed_part + dot(
            in_order(x == 0, own(grad_rows[index], place), others[index], 1), weight, 1, 1
        )
    grad_normed_one = scatter_over_mp(normed_part)
    tokens_share = share(tokens_in)
    scale_one = rms(tokens_share)
    pulled_one = grad_normed_one * first_gain
    grad_tokens = (
        share(grad_residual)
        + scale_one * pulled_one
        - tokens_share * scale_one**3 * jnp.mean(pulled_one * tokens_share, -1, keepdims=True)
    )

    normed_one_cols = cut(normed_one, z, wide, 1)
    blocks = [dot(normed_one_cols, part, 0, 0) for part in grad_rows]
    block_mine = jnp.stack([cut(block, x, narrow, 0) for block in blocks])
    block_other = x_swap(jnp.stack([cut(block, 1 - x, narrow, 0) for block in blocks]))
    weight_grads = in_order(x == 0, block_mine, block_other, 2)
    out_block = dot(mixer, residual_cols, 0, 0)
    grad_outw = in_order(
        x == 0, cut(out_block, x, narrow, 1), x_swap(cut(out_block, 1 - x, narrow, 1)), 0
    )

    first_sum = 0.0
    for index, weight in enumerate(in_weights):
        first_sum = first_sum + jnp.sum(cut(weight, place, narrow, 0) * weight_grads[index], 1)
    second_sum = jnp.sum(
        cut(swiglu_gate, place, narrow, 0) * grad_sgate
        + cut(swiglu_up, place, narrow, 0) * grad_sup,
        1,
    )
    sums = jnp.stack([first_sum, second_sum])
    sums = sums + core_swap(sums)
    sums = sums + y_swap(sums)
    return (
        output,
        grad_tokens,
        weight_grads[0],
        weight_grads[1],
        weight_grads[2],
        weight_grads[3],
        grad_outw,
        grad_sgate,
        grad_sup,
        grad_sdown,
        sums[0] / cut(first_gain, place, narrow, 0),
        grad_group,
        sums[1] / cut(second_gain, place, narrow, 0),
    )


def solution(mesh):
    in_specs = (
        P("seq", None),
        P("seq", None),
        P(),
        P("mp"),
        P(None, "mp"),
        P(None, "mp"),
        P(None, "mp"),
        P(None, "mp"),
        P("mp", None),
        P(None, "mp"),
        P(None, "mp"),
        P("mp", None),
        P(),
        P("mp"),
        P(),
    )
    out_specs = (
        P(("seq", "mp"), None),
        P(("seq", "mp"), None),
        P("seq", "mp"),
        P("seq", "mp"),
        P("seq", "mp"),
        P("seq", "mp"),
        P("mp", "seq"),
        P("seq", "mp"),
        P("seq", "mp"),
        P("mp", "seq"),
        P("seq"),
        P(("mp", "seq")),
        P("seq"),
    )
    small = (mesh.shape["seq"], mesh.shape["mp"]) == (Z * X, 4)
    body = fast_shards if small else shards
    return jax.shard_map(body, mesh=mesh, in_specs=in_specs, out_specs=out_specs, check_vma=False)
```

```python
from functools import partial

import jax
import jax.numpy as jnp
from jax import lax
from jax.experimental import pallas as pl
from jax.experimental.pallas import tpu as pltpu
from jax.sharding import PartitionSpec as P

HDIM = 128
CHUNK = 128
HIGH = lax.Precision.HIGH
HIGHEST = lax.Precision.HIGHEST
norm_eps = 1e-06
group_eps = 1e-05


def dot(left, right, contract_left, contract_right, precision=HIGH):
    return lax.dot_general(
        left,
        right,
        (((contract_left,), (contract_right,)), ((), ())),
        precision=precision,
        preferred_element_type=jnp.float32,
    )


def rms(entries):
    return lax.rsqrt(jnp.mean(entries * entries, -1, keepdims=True) + norm_eps)


def silu_grad(entries):
    gate = jax.nn.sigmoid(entries)
    return gate * (1.0 + entries * (1.0 - gate))


def gather_tokens(block):
    return lax.all_gather(block, "seq", axis=0, tiled=True)


def recurrence(query_rows, key_vecs, value_rows, segment):
    token_count, width = query_rows.shape
    heads = width // HDIM
    chunks = token_count // CHUNK

    def split(entries):
        return entries.reshape(chunks, CHUNK, heads, HDIM)

    blocked = segment.reshape(chunks, CHUNK)
    last_seg = blocked[:, -1]
    first_segs = jnp.concatenate([jnp.full((1,), -1, segment.dtype), last_seg[:-1]])
    carry = (blocked == first_segs[:, None]).astype(jnp.float32)
    in_last = (blocked == last_seg[:, None]).astype(jnp.float32)
    places = jnp.arange(CHUNK)
    allowed = (places[None, :, None] >= places[None, None, :]) & (
        blocked[:, :, None] == blocked[:, None, :]
    )
    lower = (places[:, None] >= places[None, :]).astype(jnp.float32)
    queries, keys, values = split(query_rows), split(key_vecs), split(value_rows)
    log_decay = jnp.einsum("ts,cshk->cthk", lower, jnp.log1p(-keys), precision=HIGHEST)
    growth = jnp.exp(log_decay)
    grown = queries * growth
    last = log_decay[:, -1]
    scores = jnp.einsum("cthk,cshk->chts", grown, keys * jnp.exp(-log_decay), precision=HIGH)
    scores = jnp.where(allowed[:, None], scores, 0.0)
    inner = jnp.einsum("chts,cshv->cthv", scores, values, precision=HIGH)
    weighted = keys * jnp.exp(last[:, None] - log_decay) * in_last[:, :, None, None]
    updates = jnp.einsum("cshk,cshv->chkv", weighted, values, precision=HIGH)
    through = jnp.exp(last) * carry[:, -1][:, None, None]
    state = jnp.zeros_like(updates[0])
    states = []
    for chunk in range(chunks):
        states.append(state)
        state = state * through[chunk][:, :, None] + updates[chunk]
    outer = jnp.einsum(
        "cthk,chkv->cthv", grown * carry[:, :, None, None], jnp.stack(states), precision=HIGH
    )
    return (inner + outer).reshape(token_count, width)


def mixer_all(pre_query, pre_forget, value_rows, gate_in, group_gain, lower_bound, segment):
    key_vecs = (1.0 - lower_bound) * jax.nn.sigmoid(-pre_forget)
    raw = recurrence(jax.nn.silu(pre_query), key_vecs, value_rows, segment)
    heads = raw.reshape(raw.shape[0], -1, HDIM)
    scale = lax.rsqrt(jnp.mean(heads * heads, -1, keepdims=True) + group_eps)
    normed = (heads * scale).reshape(raw.shape)
    return normed * group_gain * jax.nn.silu(gate_in)


def shards(
    tokens_in,
    cotangent,
    lengths,
    lower_bound,
    query_weight,
    forget_weight,
    input_weight,
    gate_weight,
    out_weight,
    swiglu_gate,
    swiglu_up,
    swiglu_down,
    first_gain,
    group_gain,
    second_gain,
):
    seq_count = lax.axis_size("seq")
    seq_place = lax.axis_index("seq")
    own_rows, model = tokens_in.shape
    token_count = own_rows * seq_count
    share_rows = own_rows // lax.axis_size("mp")
    share_start = lax.axis_index("mp") * share_rows
    start_row = seq_place * own_rows
    own_cols = model // seq_count
    start_col = seq_place * own_cols

    def own(entries):
        return lax.dynamic_slice_in_dim(entries, start_row, own_rows, 0)

    def columns(entries):
        return lax.dynamic_slice_in_dim(entries, start_col, own_cols, 1)

    def share(entries):
        return lax.dynamic_slice_in_dim(entries, share_start, share_rows, 0)

    positions = jnp.arange(token_count, dtype=jnp.int32)
    offsets = jnp.cumsum(lengths) - lengths
    segment = jnp.sum((positions[:, None] >= offsets[None, :]).astype(jnp.int32), 1) - 1

    all_tokens = gather_tokens(tokens_in)
    all_cotangent = gather_tokens(cotangent)
    normed_one = all_tokens * rms(all_tokens) * first_gain
    pre_query = dot(normed_one, query_weight, 1, 0)
    pre_forget = dot(normed_one, forget_weight, 1, 0)
    value_rows = dot(normed_one, input_weight, 1, 0)
    gate_in = dot(normed_one, gate_weight, 1, 0)
    mixer, mixer_back = jax.vjp(
        partial(mixer_all, lower_bound=lower_bound, segment=segment),
        pre_query,
        pre_forget,
        value_rows,
        gate_in,
        group_gain,
    )
    residual = tokens_in + lax.psum(dot(own(mixer), out_weight, 1, 0), "mp")
    scale_two = rms(residual)
    normed_two = residual * scale_two * second_gain
    grad_hidden_all = dot(all_cotangent, swiglu_down, 1, 1)
    a = dot(normed_two, swiglu_gate, 1, 0)
    b = dot(normed_two, swiglu_up, 1, 0)
    silu_a = jax.nn.silu(a)
    ffn_part = dot(silu_a * b, swiglu_down, 1, 0)
    output = share(residual) + lax.psum_scatter(ffn_part, "mp", scatter_dimension=0, tiled=True)
    e = own(grad_hidden_all)
    grad_a = e * b * silu_grad(a)
    grad_b = e * silu_a
    grad_normed_two = lax.psum(
        dot(grad_a, swiglu_gate, 1, 1) + dot(grad_b, swiglu_up, 1, 1), "mp"
    )
    pulled = grad_normed_two * second_gain
    grad_residual = (
        cotangent
        + scale_two * pulled
        - residual * scale_two**3 * jnp.mean(pulled * residual, -1, keepdims=True)
    )
    all_normed_two = gather_tokens(normed_two)
    a_all = dot(all_normed_two, swiglu_gate, 1, 0)
    b_all = dot(all_normed_two, swiglu_up, 1, 0)
    silu_all = jax.nn.silu(a_all)
    hidden_all = silu_all * b_all
    grad_a_all = grad_hidden_all * b_all * silu_grad(a_all)
    grad_b_all = grad_hidden_all * silu_all
    normed_two_cols = columns(all_normed_two)
    grad_sgate = dot(normed_two_cols, grad_a_all, 0, 0)
    grad_sup = dot(normed_two_cols, grad_b_all, 0, 0)
    grad_sdown = dot(hidden_all, columns(all_cotangent), 0, 0)

    grad_mixer = gather_tokens(dot(grad_residual, out_weight, 1, 1))
    residual_cols = lax.all_to_all(grad_residual, "seq", 1, 0, tiled=True)
    grad_outw = dot(mixer, residual_cols, 0, 0)
    grad_query_rows, grad_forget_rows, grad_value_rows, grad_gate_rows, grad_group = mixer_back(
        grad_mixer
    )
    grad_group = lax.dynamic_slice_in_dim(
        grad_group, seq_place * (group_gain.shape[0] // seq_count), group_gain.shape[0] // seq_count
    )
    normed_one_cols = columns(normed_one)
    pairs = (
        (grad_query_rows, query_weight),
        (grad_forget_rows, forget_weight),
        (grad_value_rows, input_weight),
        (grad_gate_rows, gate_weight),
    )
    weight_grads = []
    normed_part = 0.0
    first_sum = 0.0
    for grad_rows, weight in pairs:
        weight_grad = dot(normed_one_cols, grad_rows, 0, 0)
        weight_grads.append(weight_grad)
        normed_part = normed_part + dot(own(grad_rows), weight, 1, 1)
        own_weight = lax.dynamic_slice_in_dim(weight, start_col, own_cols, 0)
        first_sum = first_sum + jnp.sum(own_weight * weight_grad, 1)
    second_sum = jnp.sum(
        lax.dynamic_slice_in_dim(swiglu_gate, start_col, own_cols, 0) * grad_sgate
        + lax.dynamic_slice_in_dim(swiglu_up, start_col, own_cols, 0) * grad_sup,
        1,
    )
    gains = jnp.stack(
        [
            lax.dynamic_slice_in_dim(first_gain, start_col, own_cols),
            lax.dynamic_slice_in_dim(second_gain, start_col, own_cols),
        ]
    )
    gain_grads = lax.psum(jnp.stack([first_sum, second_sum]), "mp") / gains
    grad_normed_one = lax.psum_scatter(normed_part, "mp", scatter_dimension=0, tiled=True)
    tokens_share = share(tokens_in)
    scale_one = rms(tokens_share)
    pulled_one = grad_normed_one * first_gain
    grad_tokens = (
        share(grad_residual)
        + scale_one * pulled_one
        - tokens_share * scale_one**3 * jnp.mean(pulled_one * tokens_share, -1, keepdims=True)
    )
    return (
        output,
        grad_tokens,
        weight_grads[0],
        weight_grads[1],
        weight_grads[2],
        weight_grads[3],
        grad_outw,
        grad_sgate,
        grad_sup,
        grad_sdown,
        gain_grads[0],
        grad_group,
        gain_grads[1],
    )


Z, X = 4, 2


def z_shift(array, distance):
    steps = [(z * X + x, (z + distance) % Z * X + x) for z in range(Z) for x in range(X)]
    return lax.ppermute(array, "seq", steps)


def x_swap(array):
    return lax.ppermute(array, "seq", [(s, s ^ 1) for s in range(Z * X)])


def core_swap(array):
    return lax.ppermute(array, "mp", [(m, m ^ 1) for m in range(4)])


def y_swap(array):
    return lax.ppermute(array, "mp", [(m, m ^ 2) for m in range(4)])


def cut(array, place, size, axis):
    return lax.dynamic_slice_in_dim(array, place * size, size, axis)


def in_order(first, mine, other, axis):
    return jnp.where(
        first, jnp.concatenate([mine, other], axis), jnp.concatenate([other, mine], axis)
    )


def in_place(shifted, z):
    return [lax.select_n((z - here) % Z, *shifted) for here in range(Z)]


def core_place():
    return lax.axis_index("mp") % 2


def scatter_over_mp(part):
    rows = part.shape[0] // 4
    core = core_place()
    place = lax.axis_index("mp") // 2
    pieces = part.reshape(2, 2, rows, part.shape[1])

    def of_core(index):
        return lax.dynamic_index_in_dim(pieces, index, 1, False)

    mine = of_core(core) + core_swap(of_core(1 - core))

    def of_y(index):
        return lax.dynamic_index_in_dim(mine, index, 0, False)

    return of_y(place) + y_swap(of_y(1 - place))


F32, BF16 = jnp.float32, jnp.bfloat16
MESH = pl.DeviceIdType.MESH
ANY = pl.BlockSpec(memory_space=pl.ANY)
TILE = 256
VMEM_BYTES = 60 << 20


def halves(entries):
    high = entries.astype(BF16)
    return high, (entries - high.astype(F32)).astype(BF16)


def product(left, right, contract_left, contract_right):
    return lax.dot_general(
        left,
        right,
        (((contract_left,), (contract_right,)), ((), ())),
        preferred_element_type=F32,
    )


def three_pass(left, right, contract_left, contract_right):
    (left_high, left_low), (right_high, right_low) = left, right
    return product(left_high, right_high, contract_left, contract_right) + (
        product(left_high, right_low, contract_left, contract_right)
        + product(left_low, right_high, contract_left, contract_right)
    )


def remote(src, dst, sems, index, device):
    return pltpu.make_async_remote_copy(
        src_ref=src,
        dst_ref=dst,
        send_sem=sems[0].at[index],
        recv_sem=sems[1].at[index],
        device_id=device,
        device_id_type=MESH,
    )


def where_am_i():
    place, part = lax.axis_index("seq"), lax.axis_index("mp")
    return place // X, place % X, part // 2, part % 2


class Gather:
    spec = pl.BlockSpec(memory_space=pl.ANY)

    def shape(block):
        return (Z * X * block.shape[0], block.shape[1])

    def scratch(block):
        return [
            pltpu.SemaphoreType.DMA((78,)),
            pltpu.SemaphoreType.DMA((78,)),
            pltpu.SemaphoreType.DMA((1,)),
        ]

    def __init__(self, block_ref, out_ref, send, recv, local):
        self.block, self.out, self.sems_here, self.local = block_ref, out_ref, (send, recv), local
        self.z, self.x, self.y, self.core = where_am_i()
        self.rows = block_ref.shape[0]
        self.tile = block_ref.shape[1] // 16

    def device(self, z, x, y, core):
        return (z * X + x, y * 2 + core)

    def columns(self, part, y, core):
        if part == 0:
            return pl.ds(pl.multiple_of((6 + 2 * core) * self.tile, self.tile), 2 * self.tile)
        return pl.ds(pl.multiple_of((10 * y + 3 * core) * self.tile, self.tile), 3 * self.tile)

    def region(self, z, x, part, y, core):
        return self.out.at[
            pl.ds(pl.multiple_of((z * X + x) * self.rows, self.rows), self.rows),
            self.columns(part, y, core),
        ]

    def own(self, part):
        return self.block.at[:, self.columns(part, self.y, self.core)]

    def here(self, z, x, part):
        return self.region(z, x, part, self.y, self.core)

    def along(self, way, step, part, arriving):
        source = self.z - way * (step if arriving else step - 1)
        dst = self.here(source, self.x, part)
        return remote(
            self.own(part) if step == 1 and not arriving else dst,
            dst,
            self.sems_here,
            26 * part + (0 if way > 0 else 3) + step - 1,
            self.device(self.z + way, self.x, self.y, self.core),
        )

    def across(self, way, step, part, arriving):
        x = 1 - self.x if arriving else self.x
        dst = self.here(self.z - way * step, x, part)
        return remote(
            self.own(part) if step == 0 and not arriving else dst,
            dst,
            self.sems_here,
            26 * part + 6 + self.slot(way, step),
            self.device(self.z, 1 - self.x, self.y, self.core),
        )

    def slot(self, way, step):
        return 0 if step == 0 else (0 if way > 0 else 3) + step

    def inside(self, way, step, other_x, part, arriving):
        x = 1 - self.x if other_x else self.x
        core = 1 - self.core if arriving else self.core
        region = self.region(self.z - way * step, x, part, self.y, core)
        return remote(
            region,
            region,
            self.sems_here,
            26 * part + 13 + self.slot(way, step) + (0 if other_x else 6),
            self.device(self.z, self.x, self.y, 1 - self.core),
        )

    def over_y(self, way, step, other_x, arriving):
        x = 1 - self.x if other_x else self.x
        y = 1 - self.y if arriving else self.y
        region = self.region(self.z - way * step, x, 1, y, self.core)
        return remote(
            region,
            region,
            self.sems_here,
            52 + self.slot(way, step) + (0 if other_x else 6),
            self.device(self.z, self.x, 1 - self.y, self.core),
        )

    def inside_y(self, way, step, other_x, arriving):
        x = 1 - self.x if other_x else self.x
        core = 1 - self.core if arriving else self.core
        region = self.region(self.z - way * step, x, 1, 1 - self.y, core)
        return remote(
            region,
            region,
            self.sems_here,
            65 + self.slot(way, step) + (0 if other_x else 6),
            self.device(self.z, self.x, self.y, 1 - self.core),
        )

    def holds(self, way, step):
        source = self.z - way * step
        return (source >= 0) & (source < Z)

    def goes_on(self, way, step):
        return self.holds(way, step - 1) & (self.z + way >= 0) & (self.z + way < Z)

    def each(self, step, action):
        if step == 0:
            action(1)
        else:
            for way in (1, -1):
                pl.when(self.holds(way, step))(lambda way=way: action(way))

    def begin(self):
        barrier = pltpu.get_barrier_semaphore()

        def signal(device):
            pl.semaphore_signal(barrier, inc=1, device_id=device, device_id_type=MESH)

        signal(self.device(self.z, 1 - self.x, self.y, self.core))
        signal(self.device(self.z, self.x, 1 - self.y, self.core))
        signal(self.device(self.z, self.x, self.y, 1 - self.core))
        for way in (1, -1):
            ahead = (self.z + way >= 0) & (self.z + way < Z)
            pl.when(ahead)(
                lambda way=way: signal(self.device(self.z + way, self.x, self.y, self.core))
            )
        neighbours = jnp.where(self.z > 0, 1, 0) + jnp.where(self.z < Z - 1, 1, 0)
        pl.semaphore_wait(barrier, 3 + neighbours)
        for part in (0, 1):
            self.across(1, 0, part, False).start()
            for way in (1, -1):
                pl.when(self.goes_on(way, 1))(
                    lambda way=way, part=part: self.along(way, 1, part, False).start()
                )
        self.own_copy().start()

    def own_copy(self):
        row = pl.multiple_of((self.z * X + self.x) * self.rows, self.rows)
        return pltpu.make_async_copy(
            self.block, self.out.at[pl.ds(row, self.rows), :], self.local.at[0]
        )

    def arrive_along(self, step):
        def action(way):
            for part in (1, 0):
                self.along(way, step, part, True).wait_recv()
                if step < Z - 1:
                    pl.when(self.goes_on(way, step + 1))(
                        lambda: self.along(way, step + 1, part, False).start()
                    )
                self.across(way, step, part, False).start()
                if part == 1:
                    self.over_y(way, step, False, False).start()
                self.inside(way, step, False, part, False).start()

        self.each(step, action)

    def arrive_across(self, step):
        def action(way):
            for part in (1, 0):
                self.across(way, step, part, True).wait_recv()
                if part == 1:
                    self.over_y(way, step, True, False).start()
                self.inside(way, step, True, part, False).start()

        self.each(step, action)

    def arrive_y(self, step, other_x):
        def action(way):
            self.over_y(way, step, other_x, True).wait_recv()
            self.inside_y(way, step, other_x, False).start()

        self.each(step, action)

    def finish(self):
        self.own_copy().wait()
        for way in (1, -1):
            for step in range(1, Z):
                for part in (0, 1):
                    pl.when(self.goes_on(way, step))(
                        lambda way=way, step=step, part=part: self.along(
                            way, step, part, False
                        ).wait_send()
                    )
        for step in range(Z):

            def action(way, step=step):
                for other_x in (False, True) if step else (True,):
                    for part in (0, 1):
                        self.inside(way, step, other_x, part, False).wait_send()
                        self.inside(way, step, other_x, part, True).wait_recv()
                    self.over_y(way, step, other_x, False).wait_send()
                    self.inside_y(way, step, other_x, False).wait_send()
                    self.inside_y(way, step, other_x, True).wait_recv()
                for part in (0, 1):
                    self.across(way, step, part, False).wait_send()

            self.each(step, action)

    def events(self):
        def round_of(step):
            def event():
                if step < Z:
                    self.arrive_along(step)
                if step <= Z:
                    self.arrive_across(step - 1)
                if 1 <= step - 1 < Z:
                    self.arrive_y(step - 1, False)
                if 0 <= step - 2 < Z:
                    self.arrive_y(step - 2, True)

            return event

        return [round_of(step) for step in range(1, Z + 2)] + [self.finish]


def move_only(kind, array, collective_id):
    def kernel(array_ref, out_ref, *scratch):
        move = kind(array_ref, out_ref, *scratch)
        move.begin()
        for event in move.events():
            event()

    return pl.pallas_call(
        kernel,
        out_shape=jax.ShapeDtypeStruct(kind.shape(array), F32),
        in_specs=[kind.spec],
        out_specs=kind.spec,
        scratch_shapes=kind.scratch(array),
        compiler_params=pltpu.CompilerParams(collective_id=collective_id, has_side_effects=True),
        cost_estimate=pl.CostEstimate(flops=0, bytes_accessed=16 << 20, transcendentals=0),
    )(array)


def load_halves(src_ref, high_ref, low_ref, stage_ref, sem, change=None):
    rows = stage_ref.shape[1]
    count = src_ref.shape[0] // rows

    def fetch(index):
        return pltpu.make_async_copy(
            src_ref.at[pl.ds(index * rows, rows), :], stage_ref.at[index % 2], sem.at[index % 2]
        )

    fetch(0).start()
    for index in range(count):
        if index + 1 < count:
            fetch(index + 1).start()
        fetch(index).wait()
        if change is not None:
            change(index)
        high, low = halves(stage_ref[index % 2])
        high_ref[index * rows : (index + 1) * rows, :] = high
        low_ref[index * rows : (index + 1) * rows, :] = low


def at_steps(events, steps):
    step = pl.program_id(0)
    for event, when in zip(events, steps, strict=True):
        pl.when(step == when)(event)


def kernel_params(collective_id):
    return pltpu.CompilerParams(
        collective_id=collective_id, has_side_effects=True, vmem_limit_bytes=VMEM_BYTES
    )


def halves_scratch(rows, inner):
    return [
        pltpu.VMEM((rows, inner), BF16),
        pltpu.VMEM((rows, inner), BF16),
        pltpu.VMEM((2, 128, inner), F32),
        pltpu.SemaphoreType.DMA((2,)),
    ]


def project_beside(kind, array, tokens, gain, weights, collective_id, steps):
    rows, inner = tokens.shape
    count = len(weights)
    wide = inner // Z

    def kernel(array_ref, tokens_ref, gain_ref, *refs):
        weight_refs, refs = refs[:count], refs[count:]
        out_ref, product_ref, cols_ref, high_ref, low_ref, stage_ref, stage_sem, *refs = refs
        weight_buf, weight_sem, *scratch = refs
        move = kind(array_ref, out_ref, *scratch)
        place = lax.axis_index("seq")
        start = pl.multiple_of((place % X) * TILE, TILE)
        first_col = pl.multiple_of((place // X) * wide, wide)
        step = pl.program_id(0)

        def fetch(index):
            return pltpu.make_async_copy(
                weight_refs[index].at[:, pl.ds(start, TILE)],
                weight_buf.at[index % 2],
                weight_sem.at[index % 2],
            )

        def normalize(index):
            entries = stage_ref[index % 2]
            stage_ref[index % 2] = entries * rms(entries) * gain_ref[...]
            cols_ref[index * 128 : (index + 1) * 128, :] = stage_ref[
                index % 2, :, pl.ds(first_col, wide)
            ]

        @pl.when(step == 0)
        def _():
            move.begin()
            fetch(0).start()
            load_halves(tokens_ref, high_ref, low_ref, stage_ref, stage_sem, normalize)

        for index in range(count - 1):
            pl.when(step == index)(fetch(index + 1).start)
        for index in range(count):
            pl.when(step == index)(fetch(index).wait)
        product_ref[...] = three_pass(
            (high_ref[...], low_ref[...]), halves(weight_buf[lax.rem(step, 2)]), 1, 0
        )
        at_steps(move.events(), steps)

    return pl.pallas_call(
        kernel,
        grid=(count,),
        out_shape=[
            jax.ShapeDtypeStruct(kind.shape(array), F32),
            jax.ShapeDtypeStruct((rows, count * TILE), F32),
            jax.ShapeDtypeStruct((rows, wide), F32),
        ],
        in_specs=[kind.spec, ANY, pl.BlockSpec(memory_space=pltpu.VMEM)] + [ANY] * count,
        out_specs=[
            kind.spec,
            pl.BlockSpec((rows, TILE), lambda tile: (0, tile)),
            pl.BlockSpec(memory_space=pltpu.VMEM),
        ],
        scratch_shapes=[
            *halves_scratch(rows, inner),
            pltpu.VMEM((2, inner, TILE), F32),
            pltpu.SemaphoreType.DMA((2,)),
            *kind.scratch(array),
        ],
        compiler_params=kernel_params(collective_id),
        cost_estimate=pl.CostEstimate(
            flops=6 * rows * inner * count * TILE, bytes_accessed=48 << 20, transcendentals=0
        ),
    )(array, tokens, gain[None], *weights)


def transposed_beside(kind, array, left, weight, collective_id, steps):
    rows, inner = left.shape
    columns = weight.shape[0]

    def kernel(array_ref, left_ref, weight_ref, out_ref, product_ref, *refs):
        high_ref, low_ref, stage_ref, stage_sem, *scratch = refs
        move = kind(array_ref, out_ref, *scratch)

        @pl.when(pl.program_id(0) == 0)
        def _():
            move.begin()
            load_halves(left_ref, high_ref, low_ref, stage_ref, stage_sem)

        product_ref[...] = three_pass(
            (high_ref[...], low_ref[...]), halves(weight_ref[...]), 1, 1
        )
        at_steps(move.events(), steps)

    return pl.pallas_call(
        kernel,
        grid=(pl.cdiv(columns, TILE),),
        out_shape=[
            jax.ShapeDtypeStruct(kind.shape(array), F32),
            jax.ShapeDtypeStruct((rows, columns), F32),
        ],
        in_specs=[kind.spec, ANY, pl.BlockSpec((TILE, inner), lambda tile: (tile, 0))],
        out_specs=[kind.spec, pl.BlockSpec((rows, TILE), lambda tile: (0, tile))],
        scratch_shapes=[*halves_scratch(rows, inner), *kind.scratch(array)],
        compiler_params=kernel_params(collective_id),
        cost_estimate=pl.CostEstimate(
            flops=6 * rows * inner * columns, bytes_accessed=48 << 20, transcendentals=0
        ),
    )(array, left, weight)


def few_rows(left, right, contract_right):
    (left_high, left_low), (right_high, right_low) = left, right
    rows = left_high.shape[0]
    both = product(jnp.concatenate([left_high, left_low]), right_high, 1, contract_right)
    return both[:rows] + (product(left_high, right_low, 1, contract_right) + both[rows:])


def feed_forward_beside(kind, array, normed_two, grad_hidden, w_gate, w_up, w_down, collective_id, steps):
    rows, inner = normed_two.shape
    columns = w_gate.shape[1]
    tiles = pl.cdiv(columns, TILE)

    def kernel(array_ref, normed_ref, e_ref, gate_ref, up_ref, down_ref, out_ref, ffn_ref, grad_ref, *scratch):
        move = kind(array_ref, out_ref, *scratch)
        step = pl.program_id(0)

        @pl.when(step == 0)
        def _():
            move.begin()
            ffn_ref[...] = jnp.zeros_like(ffn_ref)
            grad_ref[...] = jnp.zeros_like(grad_ref)

        def inside(shape, axis):
            return step * TILE + lax.broadcasted_iota(jnp.int32, shape, axis) < columns

        gate_weight = halves(jnp.where(inside((inner, TILE), 1), gate_ref[...], 0.0))
        up_weight = halves(jnp.where(inside((inner, TILE), 1), up_ref[...], 0.0))
        down_weight = halves(jnp.where(inside((TILE, inner), 0), down_ref[...], 0.0))
        normed = halves(normed_ref[...])
        a = few_rows(normed, gate_weight, 0)
        b = few_rows(normed, up_weight, 0)
        e = jnp.where(inside((rows, TILE), 1), e_ref[...], 0.0)
        gate = jax.nn.sigmoid(a)
        silu_a = a * gate
        ffn_ref[...] += few_rows(halves(silu_a * b), down_weight, 0)
        grad_ref[...] += few_rows(
            halves(e * b * (gate * (1.0 + a * (1.0 - gate)))), gate_weight, 1
        ) + few_rows(halves(e * silu_a), up_weight, 1)
        at_steps(move.events(), steps)

    whole = pl.BlockSpec(memory_space=pltpu.VMEM)
    by_column = pl.BlockSpec((inner, TILE), lambda tile: (0, tile))
    return pl.pallas_call(
        kernel,
        grid=(tiles,),
        out_shape=[
            jax.ShapeDtypeStruct(kind.shape(array), F32),
            jax.ShapeDtypeStruct((rows, inner), F32),
            jax.ShapeDtypeStruct((rows, inner), F32),
        ],
        in_specs=[
            kind.spec,
            whole,
            pl.BlockSpec((rows, TILE), lambda tile: (0, tile)),
            by_column,
            by_column,
            pl.BlockSpec((TILE, inner), lambda tile: (tile, 0)),
        ],
        out_specs=[kind.spec, whole, whole],
        scratch_shapes=kind.scratch(array),
        compiler_params=kernel_params(collective_id),
        cost_estimate=pl.CostEstimate(
            flops=30 * rows * inner * columns, bytes_accessed=40 << 20, transcendentals=0
        ),
    )(array, normed_two, grad_hidden, w_gate, w_up, w_down)


class Sum:
    spec = pl.BlockSpec(memory_space=pltpu.VMEM)

    def shape(part):
        return part.shape

    def scratch(part):
        rows, half = part.shape[0], part.shape[1] // 2
        return [
            pltpu.VMEM((4, rows, half), F32),
            pltpu.SemaphoreType.DMA((3,)),
            pltpu.SemaphoreType.DMA((3,)),
        ]

    def __init__(self, part_ref, out_ref, landing, send, recv):
        self.part, self.out, self.landing, self.sems_here = part_ref, out_ref, landing, (send, recv)
        self.z, self.x, self.y, self.core = where_am_i()
        self.half = part_ref.shape[1] // 2

    def columns(self, ref, core):
        return ref.at[:, pl.ds(pl.multiple_of(core * self.half, self.half), self.half)]

    def device(self, y, core):
        return (self.z * X + self.x, y * 2 + core)

    def first(self):
        return remote(
            self.columns(self.part, 1 - self.core),
            self.landing.at[0],
            self.sems_here,
            0,
            self.device(self.y, 1 - self.core),
        )

    def second(self):
        return remote(
            self.landing.at[1],
            self.landing.at[2],
            self.sems_here,
            1,
            self.device(1 - self.y, self.core),
        )

    def third(self):
        return remote(
            self.landing.at[1],
            self.landing.at[3],
            self.sems_here,
            2,
            self.device(self.y, 1 - self.core),
        )

    def begin(self):
        barrier = pltpu.get_barrier_semaphore()
        for device in (self.device(self.y, 1 - self.core), self.device(1 - self.y, self.core)):
            pl.semaphore_signal(barrier, inc=1, device_id=device, device_id_type=MESH)
        pl.semaphore_wait(barrier, 2)
        self.first().start()

    def to_y(self):
        self.first().wait()
        self.landing[1] = self.columns(self.part, self.core)[...] + self.landing[0]
        self.second().start()

    def back(self):
        self.second().wait()
        self.landing[1] = self.landing[1] + self.landing[2]
        self.third().start()

    def finish(self):
        self.third().wait()
        self.columns(self.out, self.core)[...] = self.landing[1]
        self.columns(self.out, 1 - self.core)[...] = self.landing[3]

    def events(self):
        return [self.to_y, self.back, self.finish]


def hidden_and_sum(part, normed_two, grad_hidden, w_gate, w_up, normed_cols, cot_cols, collective_id, steps):
    rows, inner = normed_two.shape
    columns = w_gate.shape[1]
    narrow = normed_cols.shape[1]
    tiles = pl.cdiv(columns, TILE)

    def kernel(
        part_ref, normed_ref, e_ref, gate_ref, up_ref, normed_cols_ref, cot_cols_ref,
        sum_ref, grad_gate_ref, grad_up_ref, grad_down_ref,
        high_ref, low_ref, stage_ref, stage_sem, *sum_scratch,
    ):
        total = Sum(part_ref, sum_ref, *sum_scratch)
        step = pl.program_id(0)
        pl.when(step == 0)(total.begin)
        pl.when(step == 0)(
            lambda: load_halves(normed_ref, high_ref, low_ref, stage_ref, stage_sem)
        )
        normed = high_ref[...], low_ref[...]
        a = three_pass(normed, halves(gate_ref[...]), 1, 0)
        b = three_pass(normed, halves(up_ref[...]), 1, 0)
        gate = jax.nn.sigmoid(a)
        silu_a = a * gate
        e = e_ref[...]
        cols = halves(normed_cols_ref[...])
        grad_gate_ref[...] = three_pass(
            cols, halves(e * b * (gate * (1.0 + a * (1.0 - gate)))), 0, 0
        )
        grad_up_ref[...] = three_pass(cols, halves(e * silu_a), 0, 0)
        grad_down_ref[...] = three_pass(halves(silu_a * b), halves(cot_cols_ref[...]), 0, 0)
        at_steps(total.events(), steps)

    whole = pl.BlockSpec(memory_space=pltpu.VMEM)
    by_column = pl.BlockSpec((inner, TILE), lambda tile: (0, tile))
    grad_spec = pl.BlockSpec((narrow, TILE), lambda tile: (0, tile))
    return pl.pallas_call(
        kernel,
        grid=(tiles,),
        out_shape=[
            jax.ShapeDtypeStruct(part.shape, F32),
            jax.ShapeDtypeStruct((narrow, columns), F32),
            jax.ShapeDtypeStruct((narrow, columns), F32),
            jax.ShapeDtypeStruct((columns, narrow), F32),
        ],
        in_specs=[
            Sum.spec, ANY, pl.BlockSpec((rows, TILE), lambda tile: (0, tile)), by_column, by_column, whole, whole,
        ],
        out_specs=[
            whole, grad_spec, grad_spec, pl.BlockSpec((TILE, narrow), lambda tile: (tile, 0)),
        ],
        scratch_shapes=[*halves_scratch(rows, inner), *Sum.scratch(part)],
        compiler_params=kernel_params(collective_id),
        cost_estimate=pl.CostEstimate(
            flops=15 * rows * inner * columns, bytes_accessed=48 << 20, transcendentals=0
        ),
    )(part, normed_two, grad_hidden, w_gate, w_up, normed_cols, cot_cols)


def fast_shards(
    tokens_in,
    cotangent,
    lengths,
    lower_bound,
    query_weight,
    forget_weight,
    input_weight,
    gate_weight,
    out_weight,
    swiglu_gate,
    swiglu_up,
    swiglu_down,
    first_gain,
    group_gain,
    second_gain,
):
    place = lax.axis_index("seq")
    z, x = place // X, place % X
    core = core_place()
    rows, model = tokens_in.shape
    wide = model // Z
    narrow = model // (Z * X)
    width = query_weight.shape[1] // X
    share_rows = rows // 4

    def share(entries):
        return cut(entries, lax.axis_index("mp"), share_rows, 0)

    def own(entries, at):
        return cut(entries, at, rows, 0)

    token_count = rows * Z * X
    positions = jnp.arange(token_count, dtype=jnp.int32)
    order = jnp.arange(lengths.shape[0])
    offsets = jnp.sum(jnp.where(order[:, None] < order[None, :], lengths[:, None], 0), 0)
    segment = jnp.sum((positions[:, None] >= offsets[None, :]).astype(jnp.int32), 1) - 1

    all_tokens = move_only(Gather, tokens_in, 1)
    in_weights = (query_weight, forget_weight, input_weight, gate_weight)
    all_cotangent, projected, normed_one_cols = project_beside(
        Gather, cotangent, all_tokens, first_gain, in_weights, 2, (1, 2, 3, 3, 3, 3)
    )
    mixer, mixer_back = jax.vjp(
        partial(mixer_all, lower_bound=cut(lower_bound, x, width, 0), segment=segment),
        *jnp.split(projected, 4, 1),
        cut(group_gain, x, width, 0),
    )
    mixer_other = x_swap(own(mixer, place + 1 - 2 * x))
    mixer_part = dot(own(mixer, place), cut(out_weight, x, width, 0), 1, 0) + dot(
        mixer_other, cut(out_weight, 1 - x, width, 0), 1, 0
    )
    mixer_sum, grad_hidden_all = transposed_beside(
        Sum, mixer_part, all_cotangent, swiglu_down, 3, (0, 3, 4)
    )
    residual = tokens_in + mixer_sum
    scale_two = rms(residual)
    normed_two = residual * scale_two * second_gain
    all_normed_two, ffn_part, normed_two_part = feed_forward_beside(
        Gather,
        normed_two,
        normed_two,
        own(grad_hidden_all, place),
        swiglu_gate,
        swiglu_up,
        swiglu_down,
        4,
        (1, 2, 3, 4, 5, 5),
    )
    grad_normed_two, grad_sgate, grad_sup, grad_sdown = hidden_and_sum(
        normed_two_part,
        all_normed_two,
        grad_hidden_all,
        swiglu_gate,
        swiglu_up,
        cut(all_normed_two, place, narrow, 1),
        cut(all_cotangent, place, narrow, 1),
        5,
        (0, 2, 3),
    )
    pulled = grad_normed_two * second_gain
    grad_residual = (
        cotangent
        + scale_two * pulled
        - residual * scale_two**3 * jnp.mean(pulled * residual, -1, keepdims=True)
    )
    output = share(residual) + scatter_over_mp(ffn_part)

    grad_mixer_own = dot(grad_residual, out_weight, 1, 1)
    grad_mixer_here = jnp.stack(
        [cut(grad_mixer_own, x, width, 1), x_swap(cut(grad_mixer_own, 1 - x, width, 1))]
    )
    at_z = [grad_mixer_here] + [z_shift(grad_mixer_here, distance) for distance in range(1, Z)]
    grad_mixer = jnp.stack(in_place(at_z, z))
    grad_mixer = jnp.where(x == 0, grad_mixer, grad_mixer[:, ::-1]).reshape(token_count, width)

    half = wide // 2
    residual_parts = [
        cut(grad_residual, ((z + distance) % Z) * 2 + core, half, 1) for distance in range(Z)
    ]
    residual_parts = [residual_parts[0]] + [
        z_shift(residual_parts[distance], distance) for distance in range(1, Z)
    ]
    residual_mine = jnp.stack(in_place(residual_parts, z))
    residual_mine = in_order(
        x == 0, residual_mine[:, None], x_swap(residual_mine)[:, None], 1
    ).reshape(token_count, half)
    residual_cols = in_order(core == 0, residual_mine, core_swap(residual_mine), 1)

    *grad_rows, grad_group = mixer_back(grad_mixer)
    grad_group = jnp.where(
        x == 0,
        jnp.concatenate([grad_group, jnp.zeros_like(grad_group)]),
        jnp.concatenate([jnp.zeros_like(grad_group), grad_group]),
    )
    grad_group = cut(
        grad_group + x_swap(grad_group), place, group_gain.shape[0] // (Z * X), 0
    )
    others = x_swap(jnp.stack([own(part, place + 1 - 2 * x) for part in grad_rows]))
    normed_part = 0.0
    for index, weight in enumerate(in_weights):
        normed_part = normed_part + dot(
            in_order(x == 0, own(grad_rows[index], place), others[index], 1), weight, 1, 1
        )
    grad_normed_one = scatter_over_mp(normed_part)
    tokens_share = share(tokens_in)
    scale_one = rms(tokens_share)
    pulled_one = grad_normed_one * first_gain
    grad_tokens = (
        share(grad_residual)
        + scale_one * pulled_one
        - tokens_share * scale_one**3 * jnp.mean(pulled_one * tokens_share, -1, keepdims=True)
    )

    blocks = [dot(normed_one_cols, part, 0, 0) for part in grad_rows]
    block_mine = jnp.stack([cut(block, x, narrow, 0) for block in blocks])
    block_other = x_swap(jnp.stack([cut(block, 1 - x, narrow, 0) for block in blocks]))
    weight_grads = in_order(x == 0, block_mine, block_other, 2)
    out_block = dot(mixer, residual_cols, 0, 0)
    grad_outw = in_order(
        x == 0, cut(out_block, x, narrow, 1), x_swap(cut(out_block, 1 - x, narrow, 1)), 0
    )

    first_sum = 0.0
    for index, weight in enumerate(in_weights):
        first_sum = first_sum + jnp.sum(cut(weight, place, narrow, 0) * weight_grads[index], 1)
    second_sum = jnp.sum(
        cut(swiglu_gate, place, narrow, 0) * grad_sgate
        + cut(swiglu_up, place, narrow, 0) * grad_sup,
        1,
    )
    sums = jnp.stack([first_sum, second_sum])
    sums = sums + core_swap(sums)
    sums = sums + y_swap(sums)
    return (
        output,
        grad_tokens,
        weight_grads[0],
        weight_grads[1],
        weight_grads[2],
        weight_grads[3],
        grad_outw,
        grad_sgate,
        grad_sup,
        grad_sdown,
        sums[0] / cut(first_gain, place, narrow, 0),
        grad_group,
        sums[1] / cut(second_gain, place, narrow, 0),
    )


def solution(mesh):
    in_specs = (
        P("seq", None),
        P("seq", None),
        P(),
        P("mp"),
        P(None, "mp"),
        P(None, "mp"),
        P(None, "mp"),
        P(None, "mp"),
        P("mp", None),
        P(None, "mp"),
        P(None, "mp"),
        P("mp", None),
        P(),
        P("mp"),
        P(),
    )
    out_specs = (
        P(("seq", "mp"), None),
        P(("seq", "mp"), None),
        P("seq", "mp"),
        P("seq", "mp"),
        P("seq", "mp"),
        P("seq", "mp"),
        P("mp", "seq"),
        P("seq", "mp"),
        P("seq", "mp"),
        P("mp", "seq"),
        P("seq"),
        P(("mp", "seq")),
        P("seq"),
    )
    small = (mesh.shape["seq"], mesh.shape["mp"]) == (Z * X, 4)
    body = fast_shards if small else shards
    return jax.shard_map(body, mesh=mesh, in_specs=in_specs, out_specs=out_specs, check_vma=False)
```

```python
from functools import partial

import jax
import jax.numpy as jnp
from jax import lax
from jax.experimental import pallas as pl
from jax.experimental.pallas import tpu as pltpu
from jax.sharding import PartitionSpec as P

HDIM = 128
CHUNK = 128
HIGH = lax.Precision.HIGH
HIGHEST = lax.Precision.HIGHEST
norm_eps = 1e-06
group_eps = 1e-05


def dot(left, right, contract_left, contract_right, precision=HIGH):
    return lax.dot_general(
        left,
        right,
        (((contract_left,), (contract_right,)), ((), ())),
        precision=precision,
        preferred_element_type=jnp.float32,
    )


def rms(entries):
    return lax.rsqrt(jnp.mean(entries * entries, -1, keepdims=True) + norm_eps)


def silu_grad(entries):
    gate = jax.nn.sigmoid(entries)
    return gate * (1.0 + entries * (1.0 - gate))


def gather_tokens(block):
    return lax.all_gather(block, "seq", axis=0, tiled=True)


def recurrence(query_rows, key_vecs, value_rows, segment):
    token_count, width = query_rows.shape
    heads = width // HDIM
    chunks = token_count // CHUNK

    def split(entries):
        return entries.reshape(chunks, CHUNK, heads, HDIM)

    blocked = segment.reshape(chunks, CHUNK)
    last_seg = blocked[:, -1]
    first_segs = jnp.concatenate([jnp.full((1,), -1, segment.dtype), last_seg[:-1]])
    carry = (blocked == first_segs[:, None]).astype(jnp.float32)
    in_last = (blocked == last_seg[:, None]).astype(jnp.float32)
    places = jnp.arange(CHUNK)
    allowed = (places[None, :, None] >= places[None, None, :]) & (
        blocked[:, :, None] == blocked[:, None, :]
    )
    lower = (places[:, None] >= places[None, :]).astype(jnp.float32)
    queries, keys, values = split(query_rows), split(key_vecs), split(value_rows)
    log_decay = jnp.einsum("ts,cshk->cthk", lower, jnp.log1p(-keys), precision=HIGHEST)
    growth = jnp.exp(log_decay)
    grown = queries * growth
    last = log_decay[:, -1]
    scores = jnp.einsum("cthk,cshk->chts", grown, keys * jnp.exp(-log_decay), precision=HIGH)
    scores = jnp.where(allowed[:, None], scores, 0.0)
    inner = jnp.einsum("chts,cshv->cthv", scores, values, precision=HIGH)
    weighted = keys * jnp.exp(last[:, None] - log_decay) * in_last[:, :, None, None]
    updates = jnp.einsum("cshk,cshv->chkv", weighted, values, precision=HIGH)
    through = jnp.exp(last) * carry[:, -1][:, None, None]
    state = jnp.zeros_like(updates[0])
    states = []
    for chunk in range(chunks):
        states.append(state)
        state = state * through[chunk][:, :, None] + updates[chunk]
    outer = jnp.einsum(
        "cthk,chkv->cthv", grown * carry[:, :, None, None], jnp.stack(states), precision=HIGH
    )
    return (inner + outer).reshape(token_count, width)


def mixer_all(pre_query, pre_forget, value_rows, gate_in, group_gain, lower_bound, segment):
    key_vecs = (1.0 - lower_bound) * jax.nn.sigmoid(-pre_forget)
    raw = recurrence(jax.nn.silu(pre_query), key_vecs, value_rows, segment)
    heads = raw.reshape(raw.shape[0], -1, HDIM)
    scale = lax.rsqrt(jnp.mean(heads * heads, -1, keepdims=True) + group_eps)
    normed = (heads * scale).reshape(raw.shape)
    return normed * group_gain * jax.nn.silu(gate_in)


def shards(
    tokens_in,
    cotangent,
    lengths,
    lower_bound,
    query_weight,
    forget_weight,
    input_weight,
    gate_weight,
    out_weight,
    swiglu_gate,
    swiglu_up,
    swiglu_down,
    first_gain,
    group_gain,
    second_gain,
):
    seq_count = lax.axis_size("seq")
    seq_place = lax.axis_index("seq")
    own_rows, model = tokens_in.shape
    token_count = own_rows * seq_count
    share_rows = own_rows // lax.axis_size("mp")
    share_start = lax.axis_index("mp") * share_rows
    start_row = seq_place * own_rows
    own_cols = model // seq_count
    start_col = seq_place * own_cols

    def own(entries):
        return lax.dynamic_slice_in_dim(entries, start_row, own_rows, 0)

    def columns(entries):
        return lax.dynamic_slice_in_dim(entries, start_col, own_cols, 1)

    def share(entries):
        return lax.dynamic_slice_in_dim(entries, share_start, share_rows, 0)

    positions = jnp.arange(token_count, dtype=jnp.int32)
    offsets = jnp.cumsum(lengths) - lengths
    segment = jnp.sum((positions[:, None] >= offsets[None, :]).astype(jnp.int32), 1) - 1

    all_tokens = gather_tokens(tokens_in)
    all_cotangent = gather_tokens(cotangent)
    normed_one = all_tokens * rms(all_tokens) * first_gain
    pre_query = dot(normed_one, query_weight, 1, 0)
    pre_forget = dot(normed_one, forget_weight, 1, 0)
    value_rows = dot(normed_one, input_weight, 1, 0)
    gate_in = dot(normed_one, gate_weight, 1, 0)
    mixer, mixer_back = jax.vjp(
        partial(mixer_all, lower_bound=lower_bound, segment=segment),
        pre_query,
        pre_forget,
        value_rows,
        gate_in,
        group_gain,
    )
    residual = tokens_in + lax.psum(dot(own(mixer), out_weight, 1, 0), "mp")
    scale_two = rms(residual)
    normed_two = residual * scale_two * second_gain
    grad_hidden_all = dot(all_cotangent, swiglu_down, 1, 1)
    a = dot(normed_two, swiglu_gate, 1, 0)
    b = dot(normed_two, swiglu_up, 1, 0)
    silu_a = jax.nn.silu(a)
    ffn_part = dot(silu_a * b, swiglu_down, 1, 0)
    output = share(residual) + lax.psum_scatter(ffn_part, "mp", scatter_dimension=0, tiled=True)
    e = own(grad_hidden_all)
    grad_a = e * b * silu_grad(a)
    grad_b = e * silu_a
    grad_normed_two = lax.psum(
        dot(grad_a, swiglu_gate, 1, 1) + dot(grad_b, swiglu_up, 1, 1), "mp"
    )
    pulled = grad_normed_two * second_gain
    grad_residual = (
        cotangent
        + scale_two * pulled
        - residual * scale_two**3 * jnp.mean(pulled * residual, -1, keepdims=True)
    )
    all_normed_two = gather_tokens(normed_two)
    a_all = dot(all_normed_two, swiglu_gate, 1, 0)
    b_all = dot(all_normed_two, swiglu_up, 1, 0)
    silu_all = jax.nn.silu(a_all)
    hidden_all = silu_all * b_all
    grad_a_all = grad_hidden_all * b_all * silu_grad(a_all)
    grad_b_all = grad_hidden_all * silu_all
    normed_two_cols = columns(all_normed_two)
    grad_sgate = dot(normed_two_cols, grad_a_all, 0, 0)
    grad_sup = dot(normed_two_cols, grad_b_all, 0, 0)
    grad_sdown = dot(hidden_all, columns(all_cotangent), 0, 0)

    grad_mixer = gather_tokens(dot(grad_residual, out_weight, 1, 1))
    residual_cols = lax.all_to_all(grad_residual, "seq", 1, 0, tiled=True)
    grad_outw = dot(mixer, residual_cols, 0, 0)
    grad_query_rows, grad_forget_rows, grad_value_rows, grad_gate_rows, grad_group = mixer_back(
        grad_mixer
    )
    grad_group = lax.dynamic_slice_in_dim(
        grad_group, seq_place * (group_gain.shape[0] // seq_count), group_gain.shape[0] // seq_count
    )
    normed_one_cols = columns(normed_one)
    pairs = (
        (grad_query_rows, query_weight),
        (grad_forget_rows, forget_weight),
        (grad_value_rows, input_weight),
        (grad_gate_rows, gate_weight),
    )
    weight_grads = []
    normed_part = 0.0
    first_sum = 0.0
    for grad_rows, weight in pairs:
        weight_grad = dot(normed_one_cols, grad_rows, 0, 0)
        weight_grads.append(weight_grad)
        normed_part = normed_part + dot(own(grad_rows), weight, 1, 1)
        own_weight = lax.dynamic_slice_in_dim(weight, start_col, own_cols, 0)
        first_sum = first_sum + jnp.sum(own_weight * weight_grad, 1)
    second_sum = jnp.sum(
        lax.dynamic_slice_in_dim(swiglu_gate, start_col, own_cols, 0) * grad_sgate
        + lax.dynamic_slice_in_dim(swiglu_up, start_col, own_cols, 0) * grad_sup,
        1,
    )
    gains = jnp.stack(
        [
            lax.dynamic_slice_in_dim(first_gain, start_col, own_cols),
            lax.dynamic_slice_in_dim(second_gain, start_col, own_cols),
        ]
    )
    gain_grads = lax.psum(jnp.stack([first_sum, second_sum]), "mp") / gains
    grad_normed_one = lax.psum_scatter(normed_part, "mp", scatter_dimension=0, tiled=True)
    tokens_share = share(tokens_in)
    scale_one = rms(tokens_share)
    pulled_one = grad_normed_one * first_gain
    grad_tokens = (
        share(grad_residual)
        + scale_one * pulled_one
        - tokens_share * scale_one**3 * jnp.mean(pulled_one * tokens_share, -1, keepdims=True)
    )
    return (
        output,
        grad_tokens,
        weight_grads[0],
        weight_grads[1],
        weight_grads[2],
        weight_grads[3],
        grad_outw,
        grad_sgate,
        grad_sup,
        grad_sdown,
        gain_grads[0],
        grad_group,
        gain_grads[1],
    )


Z, X = 4, 2


def z_shift(array, distance):
    steps = [(z * X + x, (z + distance) % Z * X + x) for z in range(Z) for x in range(X)]
    return lax.ppermute(array, "seq", steps)


def x_swap(array):
    return lax.ppermute(array, "seq", [(s, s ^ 1) for s in range(Z * X)])


def core_swap(array):
    return lax.ppermute(array, "mp", [(m, m ^ 1) for m in range(4)])


def y_swap(array):
    return lax.ppermute(array, "mp", [(m, m ^ 2) for m in range(4)])


def cut(array, place, size, axis):
    return lax.dynamic_slice_in_dim(array, place * size, size, axis)


def in_order(first, mine, other, axis):
    return jnp.where(
        first, jnp.concatenate([mine, other], axis), jnp.concatenate([other, mine], axis)
    )


def in_place(shifted, z):
    return [lax.select_n((z - here) % Z, *shifted) for here in range(Z)]


def core_place():
    return lax.axis_index("mp") % 2


def scatter_over_mp(part):
    rows = part.shape[0] // 4
    core = core_place()
    place = lax.axis_index("mp") // 2
    pieces = part.reshape(2, 2, rows, part.shape[1])

    def of_core(index):
        return lax.dynamic_index_in_dim(pieces, index, 1, False)

    mine = of_core(core) + core_swap(of_core(1 - core))

    def of_y(index):
        return lax.dynamic_index_in_dim(mine, index, 0, False)

    return of_y(place) + y_swap(of_y(1 - place))


F32, BF16 = jnp.float32, jnp.bfloat16
MESH = pl.DeviceIdType.MESH
ANY = pl.BlockSpec(memory_space=pl.ANY)
TILE = 256
VMEM_BYTES = 60 << 20


def halves(entries):
    high = entries.astype(BF16)
    return high, (entries - high.astype(F32)).astype(BF16)


def product(left, right, contract_left, contract_right):
    return lax.dot_general(
        left,
        right,
        (((contract_left,), (contract_right,)), ((), ())),
        preferred_element_type=F32,
    )


def three_pass(left, right, contract_left, contract_right):
    (left_high, left_low), (right_high, right_low) = left, right
    return product(left_high, right_high, contract_left, contract_right) + (
        product(left_high, right_low, contract_left, contract_right)
        + product(left_low, right_high, contract_left, contract_right)
    )


def remote(src, dst, sems, index, device):
    return pltpu.make_async_remote_copy(
        src_ref=src,
        dst_ref=dst,
        send_sem=sems[0].at[index],
        recv_sem=sems[1].at[index],
        device_id=device,
        device_id_type=MESH,
    )


def where_am_i():
    place, part = lax.axis_index("seq"), lax.axis_index("mp")
    return place // X, place % X, part // 2, part % 2


class Gather:
    spec = pl.BlockSpec(memory_space=pl.ANY)

    def shape(block):
        return (Z * X * block.shape[0], block.shape[1])

    def scratch(block):
        return [
            pltpu.SemaphoreType.DMA((78,)),
            pltpu.SemaphoreType.DMA((78,)),
            pltpu.SemaphoreType.DMA((1,)),
        ]

    def __init__(self, block_ref, out_ref, send, recv, local):
        self.block, self.out, self.sems_here, self.local = block_ref, out_ref, (send, recv), local
        self.z, self.x, self.y, self.core = where_am_i()
        self.rows = block_ref.shape[0]
        self.tile = block_ref.shape[1] // 16

    def device(self, z, x, y, core):
        return (z * X + x, y * 2 + core)

    def columns(self, part, y, core):
        if part == 0:
            return pl.ds(pl.multiple_of((6 + 2 * core) * self.tile, self.tile), 2 * self.tile)
        return pl.ds(pl.multiple_of((10 * y + 3 * core) * self.tile, self.tile), 3 * self.tile)

    def region(self, z, x, part, y, core):
        return self.out.at[
            pl.ds(pl.multiple_of((z * X + x) * self.rows, self.rows), self.rows),
            self.columns(part, y, core),
        ]

    def own(self, part):
        return self.block.at[:, self.columns(part, self.y, self.core)]

    def here(self, z, x, part):
        return self.region(z, x, part, self.y, self.core)

    def along(self, way, step, part, arriving):
        source = self.z - way * (step if arriving else step - 1)
        dst = self.here(source, self.x, part)
        return remote(
            self.own(part) if step == 1 and not arriving else dst,
            dst,
            self.sems_here,
            26 * part + (0 if way > 0 else 3) + step - 1,
            self.device(self.z + way, self.x, self.y, self.core),
        )

    def across(self, way, step, part, arriving):
        x = 1 - self.x if arriving else self.x
        dst = self.here(self.z - way * step, x, part)
        return remote(
            self.own(part) if step == 0 and not arriving else dst,
            dst,
            self.sems_here,
            26 * part + 6 + self.slot(way, step),
            self.device(self.z, 1 - self.x, self.y, self.core),
        )

    def slot(self, way, step):
        return 0 if step == 0 else (0 if way > 0 else 3) + step

    def inside(self, way, step, other_x, part, arriving):
        x = 1 - self.x if other_x else self.x
        core = 1 - self.core if arriving else self.core
        region = self.region(self.z - way * step, x, part, self.y, core)
        return remote(
            region,
            region,
            self.sems_here,
            26 * part + 13 + self.slot(way, step) + (0 if other_x else 6),
            self.device(self.z, self.x, self.y, 1 - self.core),
        )

    def over_y(self, way, step, other_x, arriving):
        x = 1 - self.x if other_x else self.x
        y = 1 - self.y if arriving else self.y
        region = self.region(self.z - way * step, x, 1, y, self.core)
        return remote(
            region,
            region,
            self.sems_here,
            52 + self.slot(way, step) + (0 if other_x else 6),
            self.device(self.z, self.x, 1 - self.y, self.core),
        )

    def inside_y(self, way, step, other_x, arriving):
        x = 1 - self.x if other_x else self.x
        core = 1 - self.core if arriving else self.core
        region = self.region(self.z - way * step, x, 1, 1 - self.y, core)
        return remote(
            region,
            region,
            self.sems_here,
            65 + self.slot(way, step) + (0 if other_x else 6),
            self.device(self.z, self.x, self.y, 1 - self.core),
        )

    def holds(self, way, step):
        source = self.z - way * step
        return (source >= 0) & (source < Z)

    def goes_on(self, way, step):
        return self.holds(way, step - 1) & (self.z + way >= 0) & (self.z + way < Z)

    def each(self, step, action):
        if step == 0:
            action(1)
        else:
            for way in (1, -1):
                pl.when(self.holds(way, step))(lambda way=way: action(way))

    def begin(self):
        barrier = pltpu.get_barrier_semaphore()

        def signal(device):
            pl.semaphore_signal(barrier, inc=1, device_id=device, device_id_type=MESH)

        signal(self.device(self.z, 1 - self.x, self.y, self.core))
        signal(self.device(self.z, self.x, 1 - self.y, self.core))
        signal(self.device(self.z, self.x, self.y, 1 - self.core))
        for way in (1, -1):
            ahead = (self.z + way >= 0) & (self.z + way < Z)
            pl.when(ahead)(
                lambda way=way: signal(self.device(self.z + way, self.x, self.y, self.core))
            )
        neighbours = jnp.where(self.z > 0, 1, 0) + jnp.where(self.z < Z - 1, 1, 0)
        pl.semaphore_wait(barrier, 3 + neighbours)
        for part in (0, 1):
            self.across(1, 0, part, False).start()
            for way in (1, -1):
                pl.when(self.goes_on(way, 1))(
                    lambda way=way, part=part: self.along(way, 1, part, False).start()
                )
        self.own_copy().start()

    def own_copy(self):
        row = pl.multiple_of((self.z * X + self.x) * self.rows, self.rows)
        return pltpu.make_async_copy(
            self.block, self.out.at[pl.ds(row, self.rows), :], self.local.at[0]
        )

    def arrive_along(self, step):
        def action(way):
            for part in (1, 0):
                self.along(way, step, part, True).wait_recv()
                if step < Z - 1:
                    pl.when(self.goes_on(way, step + 1))(
                        lambda: self.along(way, step + 1, part, False).start()
                    )
                self.across(way, step, part, False).start()
                if part == 1:
                    self.over_y(way, step, False, False).start()
                self.inside(way, step, False, part, False).start()

        self.each(step, action)

    def arrive_across(self, step):
        def action(way):
            for part in (1, 0):
                self.across(way, step, part, True).wait_recv()
                if part == 1:
                    self.over_y(way, step, True, False).start()
                self.inside(way, step, True, part, False).start()

        self.each(step, action)

    def arrive_y(self, step, other_x):
        def action(way):
            self.over_y(way, step, other_x, True).wait_recv()
            self.inside_y(way, step, other_x, False).start()

        self.each(step, action)

    def finish(self):
        self.own_copy().wait()
        for way in (1, -1):
            for step in range(1, Z):
                for part in (0, 1):
                    pl.when(self.goes_on(way, step))(
                        lambda way=way, step=step, part=part: self.along(
                            way, step, part, False
                        ).wait_send()
                    )
        for step in range(Z):

            def action(way, step=step):
                for other_x in (False, True) if step else (True,):
                    for part in (0, 1):
                        self.inside(way, step, other_x, part, False).wait_send()
                        self.inside(way, step, other_x, part, True).wait_recv()
                    self.over_y(way, step, other_x, False).wait_send()
                    self.inside_y(way, step, other_x, False).wait_send()
                    self.inside_y(way, step, other_x, True).wait_recv()
                for part in (0, 1):
                    self.across(way, step, part, False).wait_send()

            self.each(step, action)

    def events(self):
        def round_of(step):
            def event():
                if step < Z:
                    self.arrive_along(step)
                if step <= Z:
                    self.arrive_across(step - 1)
                if 1 <= step - 1 < Z:
                    self.arrive_y(step - 1, False)
                if 0 <= step - 2 < Z:
                    self.arrive_y(step - 2, True)

            return event

        return [round_of(step) for step in range(1, Z + 2)] + [self.finish]


def move_only(kind, array, collective_id):
    def kernel(array_ref, out_ref, *scratch):
        move = kind(array_ref, out_ref, *scratch)
        move.begin()
        for event in move.events():
            event()

    return pl.pallas_call(
        kernel,
        out_shape=jax.ShapeDtypeStruct(kind.shape(array), F32),
        in_specs=[kind.spec],
        out_specs=kind.spec,
        scratch_shapes=kind.scratch(array),
        compiler_params=pltpu.CompilerParams(collective_id=collective_id, has_side_effects=True),
        cost_estimate=pl.CostEstimate(flops=0, bytes_accessed=16 << 20, transcendentals=0),
    )(array)


def load_halves(src_ref, high_ref, low_ref, stage_ref, sem, change=None):
    rows = stage_ref.shape[1]
    count = src_ref.shape[0] // rows

    def fetch(index):
        return pltpu.make_async_copy(
            src_ref.at[pl.ds(index * rows, rows), :], stage_ref.at[index % 2], sem.at[index % 2]
        )

    fetch(0).start()
    for index in range(count):
        if index + 1 < count:
            fetch(index + 1).start()
        fetch(index).wait()
        if change is not None:
            change(index)
        high, low = halves(stage_ref[index % 2])
        high_ref[index * rows : (index + 1) * rows, :] = high
        low_ref[index * rows : (index + 1) * rows, :] = low


def at_steps(events, steps):
    step = pl.program_id(0)
    for event, when in zip(events, steps, strict=True):
        pl.when(step == when)(event)


def kernel_params(collective_id):
    return pltpu.CompilerParams(
        collective_id=collective_id, has_side_effects=True, vmem_limit_bytes=VMEM_BYTES
    )


def halves_scratch(rows, inner):
    return [
        pltpu.VMEM((rows, inner), BF16),
        pltpu.VMEM((rows, inner), BF16),
        pltpu.VMEM((2, 128, inner), F32),
        pltpu.SemaphoreType.DMA((2,)),
    ]


def project_beside(kind, array, tokens, gain, weights, collective_id, steps):
    rows, inner = tokens.shape
    count = len(weights)
    wide = inner // Z

    def kernel(array_ref, tokens_ref, gain_ref, *refs):
        weight_refs, refs = refs[:count], refs[count:]
        out_ref, product_ref, cols_ref, high_ref, low_ref, stage_ref, stage_sem, *refs = refs
        weight_buf, weight_sem, *scratch = refs
        move = kind(array_ref, out_ref, *scratch)
        place = lax.axis_index("seq")
        start = pl.multiple_of((place % X) * TILE, TILE)
        first_col = pl.multiple_of((place // X) * wide, wide)
        step = pl.program_id(0)

        def fetch(index):
            return pltpu.make_async_copy(
                weight_refs[index].at[:, pl.ds(start, TILE)],
                weight_buf.at[index % 2],
                weight_sem.at[index % 2],
            )

        def normalize(index):
            entries = stage_ref[index % 2]
            stage_ref[index % 2] = entries * rms(entries) * gain_ref[...]
            cols_ref[index * 128 : (index + 1) * 128, :] = stage_ref[
                index % 2, :, pl.ds(first_col, wide)
            ]

        @pl.when(step == 0)
        def _():
            move.begin()
            fetch(0).start()
            load_halves(tokens_ref, high_ref, low_ref, stage_ref, stage_sem, normalize)

        for index in range(count - 1):
            pl.when(step == index)(fetch(index + 1).start)
        for index in range(count):
            pl.when(step == index)(fetch(index).wait)
        product_ref[...] = three_pass(
            (high_ref[...], low_ref[...]), halves(weight_buf[lax.rem(step, 2)]), 1, 0
        )
        at_steps(move.events(), steps)

    return pl.pallas_call(
        kernel,
        grid=(count,),
        out_shape=[
            jax.ShapeDtypeStruct(kind.shape(array), F32),
            jax.ShapeDtypeStruct((rows, count * TILE), F32),
            jax.ShapeDtypeStruct((rows, wide), F32),
        ],
        in_specs=[kind.spec, ANY, pl.BlockSpec(memory_space=pltpu.VMEM)] + [ANY] * count,
        out_specs=[
            kind.spec,
            pl.BlockSpec((rows, TILE), lambda tile: (0, tile)),
            pl.BlockSpec(memory_space=pltpu.VMEM),
        ],
        scratch_shapes=[
            *halves_scratch(rows, inner),
            pltpu.VMEM((2, inner, TILE), F32),
            pltpu.SemaphoreType.DMA((2,)),
            *kind.scratch(array),
        ],
        compiler_params=kernel_params(collective_id),
        cost_estimate=pl.CostEstimate(
            flops=6 * rows * inner * count * TILE, bytes_accessed=48 << 20, transcendentals=0
        ),
    )(array, tokens, gain[None], *weights)


def transposed_beside(kind, array, left, weight, collective_id, steps):
    rows, inner = left.shape
    columns = weight.shape[0]

    def kernel(array_ref, left_ref, weight_ref, out_ref, product_ref, *refs):
        high_ref, low_ref, stage_ref, stage_sem, *scratch = refs
        move = kind(array_ref, out_ref, *scratch)

        @pl.when(pl.program_id(0) == 0)
        def _():
            move.begin()
            load_halves(left_ref, high_ref, low_ref, stage_ref, stage_sem)

        product_ref[...] = three_pass(
            (high_ref[...], low_ref[...]), halves(weight_ref[...]), 1, 1
        )
        at_steps(move.events(), steps)

    return pl.pallas_call(
        kernel,
        grid=(pl.cdiv(columns, TILE),),
        out_shape=[
            jax.ShapeDtypeStruct(kind.shape(array), F32),
            jax.ShapeDtypeStruct((rows, columns), F32),
        ],
        in_specs=[kind.spec, ANY, pl.BlockSpec((TILE, inner), lambda tile: (tile, 0))],
        out_specs=[kind.spec, pl.BlockSpec((rows, TILE), lambda tile: (0, tile))],
        scratch_shapes=[*halves_scratch(rows, inner), *kind.scratch(array)],
        compiler_params=kernel_params(collective_id),
        cost_estimate=pl.CostEstimate(
            flops=6 * rows * inner * columns, bytes_accessed=48 << 20, transcendentals=0
        ),
    )(array, left, weight)


def few_rows(left, right, contract_right):
    (left_high, left_low), (right_high, right_low) = left, right
    rows = left_high.shape[0]
    both = product(jnp.concatenate([left_high, left_low]), right_high, 1, contract_right)
    return both[:rows] + (product(left_high, right_low, 1, contract_right) + both[rows:])


def feed_forward_beside(kind, array, normed_two, grad_hidden, w_gate, w_up, w_down, collective_id, steps):
    rows, inner = normed_two.shape
    columns = w_gate.shape[1]
    tiles = pl.cdiv(columns, TILE)

    def kernel(array_ref, normed_ref, e_ref, gate_ref, up_ref, down_ref, out_ref, ffn_ref, grad_ref, *scratch):
        move = kind(array_ref, out_ref, *scratch)
        step = pl.program_id(0)

        @pl.when(step == 0)
        def _():
            move.begin()
            ffn_ref[...] = jnp.zeros_like(ffn_ref)
            grad_ref[...] = jnp.zeros_like(grad_ref)

        def inside(shape, axis):
            return step * TILE + lax.broadcasted_iota(jnp.int32, shape, axis) < columns

        gate_weight = halves(jnp.where(inside((inner, TILE), 1), gate_ref[...], 0.0))
        up_weight = halves(jnp.where(inside((inner, TILE), 1), up_ref[...], 0.0))
        down_weight = halves(jnp.where(inside((TILE, inner), 0), down_ref[...], 0.0))
        normed = halves(normed_ref[...])
        a = few_rows(normed, gate_weight, 0)
        b = few_rows(normed, up_weight, 0)
        e = jnp.where(inside((rows, TILE), 1), e_ref[...], 0.0)
        gate = jax.nn.sigmoid(a)
        silu_a = a * gate
        ffn_ref[...] += few_rows(halves(silu_a * b), down_weight, 0)
        grad_ref[...] += few_rows(
            halves(e * b * (gate * (1.0 + a * (1.0 - gate)))), gate_weight, 1
        ) + few_rows(halves(e * silu_a), up_weight, 1)
        at_steps(move.events(), steps)

    whole = pl.BlockSpec(memory_space=pltpu.VMEM)
    by_column = pl.BlockSpec((inner, TILE), lambda tile: (0, tile))
    return pl.pallas_call(
        kernel,
        grid=(tiles,),
        out_shape=[
            jax.ShapeDtypeStruct(kind.shape(array), F32),
            jax.ShapeDtypeStruct((rows, inner), F32),
            jax.ShapeDtypeStruct((rows, inner), F32),
        ],
        in_specs=[
            kind.spec,
            whole,
            pl.BlockSpec((rows, TILE), lambda tile: (0, tile)),
            by_column,
            by_column,
            pl.BlockSpec((TILE, inner), lambda tile: (tile, 0)),
        ],
        out_specs=[kind.spec, whole, whole],
        scratch_shapes=kind.scratch(array),
        compiler_params=kernel_params(collective_id),
        cost_estimate=pl.CostEstimate(
            flops=30 * rows * inner * columns, bytes_accessed=40 << 20, transcendentals=0
        ),
    )(array, normed_two, grad_hidden, w_gate, w_up, w_down)


class Sum:
    spec = pl.BlockSpec(memory_space=pltpu.VMEM)

    def shape(part):
        return part.shape

    def scratch(part):
        rows, half = part.shape[0], part.shape[1] // 2
        return [
            pltpu.VMEM((4, rows, half), F32),
            pltpu.SemaphoreType.DMA((3,)),
            pltpu.SemaphoreType.DMA((3,)),
        ]

    def __init__(self, part_ref, out_ref, landing, send, recv):
        self.part, self.out, self.landing, self.sems_here = part_ref, out_ref, landing, (send, recv)
        self.z, self.x, self.y, self.core = where_am_i()
        self.half = part_ref.shape[1] // 2

    def columns(self, ref, core):
        return ref.at[:, pl.ds(pl.multiple_of(core * self.half, self.half), self.half)]

    def device(self, y, core):
        return (self.z * X + self.x, y * 2 + core)

    def first(self):
        return remote(
            self.columns(self.part, 1 - self.core),
            self.landing.at[0],
            self.sems_here,
            0,
            self.device(self.y, 1 - self.core),
        )

    def second(self):
        return remote(
            self.landing.at[1],
            self.landing.at[2],
            self.sems_here,
            1,
            self.device(1 - self.y, self.core),
        )

    def third(self):
        return remote(
            self.landing.at[1],
            self.landing.at[3],
            self.sems_here,
            2,
            self.device(self.y, 1 - self.core),
        )

    def begin(self):
        barrier = pltpu.get_barrier_semaphore()
        for device in (self.device(self.y, 1 - self.core), self.device(1 - self.y, self.core)):
            pl.semaphore_signal(barrier, inc=1, device_id=device, device_id_type=MESH)
        pl.semaphore_wait(barrier, 2)
        self.first().start()

    def to_y(self):
        self.first().wait()
        self.landing[1] = self.columns(self.part, self.core)[...] + self.landing[0]
        self.second().start()

    def back(self):
        self.second().wait()
        self.landing[1] = self.landing[1] + self.landing[2]
        self.third().start()

    def finish(self):
        self.third().wait()
        self.columns(self.out, self.core)[...] = self.landing[1]
        self.columns(self.out, 1 - self.core)[...] = self.landing[3]

    def events(self):
        return [self.to_y, self.back, self.finish]


def hidden_and_sum(part, normed_two, grad_hidden, w_gate, w_up, normed_cols, cot_cols, collective_id, steps):
    rows, inner = normed_two.shape
    columns = w_gate.shape[1]
    narrow = normed_cols.shape[1]
    tiles = pl.cdiv(columns, TILE)

    def kernel(
        part_ref, normed_ref, e_ref, gate_ref, up_ref, normed_cols_ref, cot_cols_ref,
        sum_ref, grad_gate_ref, grad_up_ref, grad_down_ref,
        high_ref, low_ref, stage_ref, stage_sem, *sum_scratch,
    ):
        total = Sum(part_ref, sum_ref, *sum_scratch)
        step = pl.program_id(0)
        pl.when(step == 0)(total.begin)
        pl.when(step == 0)(
            lambda: load_halves(normed_ref, high_ref, low_ref, stage_ref, stage_sem)
        )
        normed = high_ref[...], low_ref[...]
        a = three_pass(normed, halves(gate_ref[...]), 1, 0)
        b = three_pass(normed, halves(up_ref[...]), 1, 0)
        gate = jax.nn.sigmoid(a)
        silu_a = a * gate
        e = e_ref[...]
        cols = halves(normed_cols_ref[...])
        grad_gate_ref[...] = three_pass(
            cols, halves(e * b * (gate * (1.0 + a * (1.0 - gate)))), 0, 0
        )
        grad_up_ref[...] = three_pass(cols, halves(e * silu_a), 0, 0)
        grad_down_ref[...] = three_pass(halves(silu_a * b), halves(cot_cols_ref[...]), 0, 0)
        at_steps(total.events(), steps)

    whole = pl.BlockSpec(memory_space=pltpu.VMEM)
    by_column = pl.BlockSpec((inner, TILE), lambda tile: (0, tile))
    grad_spec = pl.BlockSpec((narrow, TILE), lambda tile: (0, tile))
    return pl.pallas_call(
        kernel,
        grid=(tiles,),
        out_shape=[
            jax.ShapeDtypeStruct(part.shape, F32),
            jax.ShapeDtypeStruct((narrow, columns), F32),
            jax.ShapeDtypeStruct((narrow, columns), F32),
            jax.ShapeDtypeStruct((columns, narrow), F32),
        ],
        in_specs=[
            Sum.spec, ANY, pl.BlockSpec((rows, TILE), lambda tile: (0, tile)), by_column, by_column, whole, whole,
        ],
        out_specs=[
            whole, grad_spec, grad_spec, pl.BlockSpec((TILE, narrow), lambda tile: (tile, 0)),
        ],
        scratch_shapes=[*halves_scratch(rows, inner), *Sum.scratch(part)],
        compiler_params=kernel_params(collective_id),
        cost_estimate=pl.CostEstimate(
            flops=15 * rows * inner * columns, bytes_accessed=48 << 20, transcendentals=0
        ),
    )(part, normed_two, grad_hidden, w_gate, w_up, normed_cols, cot_cols)


def thin(left, right, contract_left, contract_right):
    (left_high, left_low), (right_high, right_low) = left, right
    return product(
        jnp.concatenate([left_high, left_low], contract_left),
        jnp.concatenate([right_high, right_high], contract_right),
        contract_left,
        contract_right,
    ) + product(left_high, right_low, contract_left, contract_right)


def join(first, second, axis):
    return tuple(jnp.concatenate(pair, axis) for pair in zip(first, second, strict=True))


def running_sum(triangle, entries):
    high, low = halves(entries)
    least = (entries - high.astype(F32) - low.astype(F32)).astype(BF16)
    return product(
        jnp.concatenate([triangle, triangle], 1), jnp.concatenate([high, low], 0), 1, 0
    ) + product(triangle, least, 1, 0)


def chunk_masks(offsets_ref, chunk):
    shape = (CHUNK, CHUNK)
    row = lax.broadcasted_iota(jnp.int32, shape, 0)
    column = lax.broadcasted_iota(jnp.int32, shape, 1)
    start = chunk * CHUNK

    def segment(position):
        return sum((position >= offsets_ref[j]).astype(jnp.int32) for j in range(offsets_ref.shape[0]))

    segment_row = segment(start + row)
    before, last = segment(start - 1), segment(start + CHUNK - 1)
    allowed = (row >= column) & (segment_row == segment(start + column))
    carry = (segment_row == before).astype(F32)
    in_last = (segment_row == last).astype(F32)
    lower = (row >= column).astype(F32).astype(BF16)
    return allowed, carry, in_last, (last == before).astype(F32), lower


def head_terms(pre_query, pre_forget, lower_bound, lower):
    query_gate = jax.nn.sigmoid(pre_query)
    forget_gate = jax.nn.sigmoid(-pre_forget)
    keys = (1.0 - lower_bound) * forget_gate
    log_decay = running_sum(lower, jnp.log1p(-keys))
    last = log_decay[CHUNK - 1 :, :]
    growth, shrink, trail = jnp.exp(log_decay), jnp.exp(-log_decay), jnp.exp(last - log_decay)
    return query_gate, forget_gate, keys, last, growth, shrink, trail


def tall(row):
    return jnp.transpose(jnp.broadcast_to(row, (HDIM, HDIM)))


def mixer_forward(projected, lower_bound, group_gain, offsets):
    rows, columns = projected.shape
    width = columns // 4
    heads = width // HDIM
    chunks = rows // CHUNK

    def kernel(offsets_ref, projected_ref, bound_ref, gain_ref, mixer_ref, raw_ref, states_ref, state_ref):
        chunk = pl.program_id(0)

        @pl.when(chunk == 0)
        def _():
            state_ref[...] = jnp.zeros_like(state_ref)

        allowed, carry, in_last, carry_last, lower = chunk_masks(offsets_ref, chunk)
        for head in range(heads):
            at = slice(head * HDIM, (head + 1) * HDIM)
            pre_query, pre_forget, values, gate_in = (
                projected_ref[:, part * width + head * HDIM : part * width + (head + 1) * HDIM]
                for part in range(4)
            )
            query_gate, _, keys, last, growth, shrink, trail = head_terms(
                pre_query, pre_forget, bound_ref[:, at], lower
            )
            grown = pre_query * query_gate * growth
            state = state_ref[head]
            states_ref[0, head] = state
            value_halves = halves(values)
            scores = thin(halves(grown), halves(keys * shrink), 1, 1)
            scores = jnp.where(allowed, scores, 0.0)
            raw = three_pass(
                join(halves(scores), halves(grown * carry), 1),
                join(value_halves, halves(state), 0),
                1,
                0,
            )
            state_ref[head] = state * (tall(jnp.exp(last)) * carry_last) + thin(
                halves(keys * trail * in_last), value_halves, 0, 0
            )
            raw_ref[:, at] = raw
            scale = lax.rsqrt(jnp.mean(raw * raw, -1, keepdims=True) + group_eps)
            mixer_ref[:, at] = raw * scale * gain_ref[:, at] * jax.nn.silu(gate_in)

    whole = pl.BlockSpec(memory_space=pltpu.VMEM)
    by_chunk = pl.BlockSpec((CHUNK, width), lambda chunk: (chunk, 0))
    return pl.pallas_call(
        kernel,
        grid=(chunks,),
        out_shape=[
            jax.ShapeDtypeStruct((rows, width), F32),
            jax.ShapeDtypeStruct((rows, width), F32),
            jax.ShapeDtypeStruct((chunks, heads, HDIM, HDIM), F32),
        ],
        in_specs=[
            pl.BlockSpec(memory_space=pltpu.SMEM),
            pl.BlockSpec((CHUNK, columns), lambda chunk: (chunk, 0)),
            whole,
            whole,
        ],
        out_specs=[
            by_chunk,
            by_chunk,
            pl.BlockSpec((1, heads, HDIM, HDIM), lambda chunk: (chunk, 0, 0, 0)),
        ],
        scratch_shapes=[pltpu.VMEM((heads, HDIM, HDIM), F32)],
        compiler_params=pltpu.CompilerParams(vmem_limit_bytes=32 << 20),
    )(offsets, projected, lower_bound[None], group_gain[None])


def mixer_backward(projected, raw_rows, states, grad_mixer, lower_bound, group_gain, offsets):
    rows, columns = projected.shape
    width = columns // 4
    heads = width // HDIM
    chunks = rows // CHUNK

    def kernel(
        offsets_ref, projected_ref, raw_ref, states_ref, grad_ref, bound_ref, gain_ref,
        grads_ref, group_ref, later_ref,
    ):
        step = pl.program_id(0)
        chunk = chunks - 1 - step

        @pl.when(step == 0)
        def _():
            later_ref[...] = jnp.zeros_like(later_ref)
            group_ref[...] = jnp.zeros_like(group_ref)

        allowed, carry, in_last, carry_last, lower = chunk_masks(offsets_ref, chunk)
        upper = jnp.transpose(lower.astype(F32)).astype(BF16)
        for head in range(heads):
            at = slice(head * HDIM, (head + 1) * HDIM)
            spots = [
                slice(part * width + head * HDIM, part * width + (head + 1) * HDIM)
                for part in range(4)
            ]
            pre_query, pre_forget, values, gate_in = (projected_ref[:, spot] for spot in spots)
            raw, grad, gain = raw_ref[:, at], grad_ref[:, at], gain_ref[:, at]
            state, later = states_ref[0, head], later_ref[head]

            scale = lax.rsqrt(jnp.mean(raw * raw, -1, keepdims=True) + group_eps)
            normed = raw * scale
            gate = jax.nn.sigmoid(gate_in)
            silu_gate = gate_in * gate
            weighted = grad * gain * silu_gate
            group_ref[:, at] += jnp.sum(grad * normed * silu_gate, 0, keepdims=True)
            grads_ref[:, spots[3]] = (
                grad * gain * normed * (gate * (1.0 + gate_in * (1.0 - gate)))
            )
            grad_raw = scale * weighted - raw * (
                scale * scale * scale * jnp.mean(weighted * raw, -1, keepdims=True)
            )

            query_gate, forget_gate, keys, last, growth, shrink, trail = head_terms(
                pre_query, pre_forget, bound_ref[:, at], lower
            )
            grown = pre_query * query_gate * growth
            shrunk = keys * shrink
            trailing = trail * in_last
            ends = keys * trailing
            grown_halves, shrunk_halves = halves(grown), halves(shrunk)
            raw_halves, value_halves, later_halves = halves(grad_raw), halves(values), halves(later)
            scores = jnp.where(allowed, thin(grown_halves, shrunk_halves, 1, 1), 0.0)
            grad_scores = jnp.where(allowed, thin(raw_halves, value_halves, 1, 1), 0.0)
            score_halves = halves(grad_scores)
            grads_ref[:, spots[2]] = three_pass(
                join(halves(jnp.transpose(scores)), halves(ends), 1),
                join(raw_halves, later_halves, 0),
                1,
                0,
            )
            grad_grown = three_pass(
                join(score_halves, halves(grad_raw * carry), 1),
                join(shrunk_halves, halves(jnp.transpose(state)), 0),
                1,
                0,
            )
            grad_shrunk = thin(score_halves, grown_halves, 0, 0)
            grad_ends = thin(value_halves, later_halves, 1, 1)
            through = tall(jnp.exp(last)) * carry_last
            later_ref[head] = later * through + thin(
                halves(grown * carry), raw_halves, 0, 0
            )
            grads_ref[:, spots[0]] = (
                grad_grown * growth * (query_gate * (1.0 + pre_query * (1.0 - query_gate)))
            )
            from_ends = grad_ends * ends
            grad_log = grad_grown * grown - grad_shrunk * shrunk - from_ends
            pulled = jnp.transpose(later * state * through)
            grad_last = jnp.sum(from_ends + pulled, 0, keepdims=True)
            grad_log_forget = running_sum(upper, grad_log) + grad_last
            grad_keys = (
                grad_shrunk * shrink + grad_ends * trailing - grad_log_forget / (1.0 - keys)
            )
            grads_ref[:, spots[1]] = -grad_keys * keys * (1.0 - forget_gate)

    whole = pl.BlockSpec(memory_space=pltpu.VMEM)

    def by_chunk(size):
        return pl.BlockSpec((CHUNK, size), lambda step: (chunks - 1 - step, 0))

    grads, grad_group = pl.pallas_call(
        kernel,
        grid=(chunks,),
        out_shape=[
            jax.ShapeDtypeStruct((rows, columns), F32),
            jax.ShapeDtypeStruct((1, width), F32),
        ],
        in_specs=[
            pl.BlockSpec(memory_space=pltpu.SMEM),
            by_chunk(columns),
            by_chunk(width),
            pl.BlockSpec((1, heads, HDIM, HDIM), lambda step: (chunks - 1 - step, 0, 0, 0)),
            by_chunk(width),
            whole,
            whole,
        ],
        out_specs=[by_chunk(columns), whole],
        scratch_shapes=[pltpu.VMEM((heads, HDIM, HDIM), F32)],
        compiler_params=pltpu.CompilerParams(vmem_limit_bytes=32 << 20),
    )(offsets, projected, raw_rows, states, grad_mixer, lower_bound[None], group_gain[None])
    return grads, grad_group[0]


def fast_shards(
    tokens_in,
    cotangent,
    lengths,
    lower_bound,
    query_weight,
    forget_weight,
    input_weight,
    gate_weight,
    out_weight,
    swiglu_gate,
    swiglu_up,
    swiglu_down,
    first_gain,
    group_gain,
    second_gain,
):
    place = lax.axis_index("seq")
    z, x = place // X, place % X
    core = core_place()
    rows, model = tokens_in.shape
    wide = model // Z
    narrow = model // (Z * X)
    width = query_weight.shape[1] // X
    share_rows = rows // 4

    def share(entries):
        return cut(entries, lax.axis_index("mp"), share_rows, 0)

    def own(entries, at):
        return cut(entries, at, rows, 0)

    token_count = rows * Z * X
    order = jnp.arange(lengths.shape[0])
    offsets = jnp.sum(jnp.where(order[:, None] < order[None, :], lengths[:, None], 0), 0)

    all_tokens = move_only(Gather, tokens_in, 1)
    in_weights = (query_weight, forget_weight, input_weight, gate_weight)
    all_cotangent, projected, normed_one_cols = project_beside(
        Gather, cotangent, all_tokens, first_gain, in_weights, 2, (1, 2, 3, 3, 3, 3)
    )
    bound_here, gain_here = cut(lower_bound, x, width, 0), cut(group_gain, x, width, 0)
    mixer, raw, states = mixer_forward(projected, bound_here, gain_here, offsets)
    mixer_other = x_swap(own(mixer, place + 1 - 2 * x))
    mixer_part = dot(own(mixer, place), cut(out_weight, x, width, 0), 1, 0) + dot(
        mixer_other, cut(out_weight, 1 - x, width, 0), 1, 0
    )
    mixer_sum, grad_hidden_all = transposed_beside(
        Sum, mixer_part, all_cotangent, swiglu_down, 3, (0, 3, 4)
    )
    residual = tokens_in + mixer_sum
    scale_two = rms(residual)
    normed_two = residual * scale_two * second_gain
    all_normed_two, ffn_part, normed_two_part = feed_forward_beside(
        Gather,
        normed_two,
        normed_two,
        own(grad_hidden_all, place),
        swiglu_gate,
        swiglu_up,
        swiglu_down,
        4,
        (1, 2, 3, 4, 5, 5),
    )
    grad_normed_two, grad_sgate, grad_sup, grad_sdown = hidden_and_sum(
        normed_two_part,
        all_normed_two,
        grad_hidden_all,
        swiglu_gate,
        swiglu_up,
        cut(all_normed_two, place, narrow, 1),
        cut(all_cotangent, place, narrow, 1),
        5,
        (0, 2, 3),
    )
    pulled = grad_normed_two * second_gain
    grad_residual = (
        cotangent
        + scale_two * pulled
        - residual * scale_two**3 * jnp.mean(pulled * residual, -1, keepdims=True)
    )
    output = share(residual) + scatter_over_mp(ffn_part)

    grad_mixer_own = dot(grad_residual, out_weight, 1, 1)
    grad_mixer_here = jnp.stack(
        [cut(grad_mixer_own, x, width, 1), x_swap(cut(grad_mixer_own, 1 - x, width, 1))]
    )
    at_z = [grad_mixer_here] + [z_shift(grad_mixer_here, distance) for distance in range(1, Z)]
    grad_mixer = jnp.stack(in_place(at_z, z))
    grad_mixer = jnp.where(x == 0, grad_mixer, grad_mixer[:, ::-1]).reshape(token_count, width)

    half = wide // 2
    residual_parts = [
        cut(grad_residual, ((z + distance) % Z) * 2 + core, half, 1) for distance in range(Z)
    ]
    residual_parts = [residual_parts[0]] + [
        z_shift(residual_parts[distance], distance) for distance in range(1, Z)
    ]
    residual_mine = jnp.stack(in_place(residual_parts, z))
    residual_mine = in_order(
        x == 0, residual_mine[:, None], x_swap(residual_mine)[:, None], 1
    ).reshape(token_count, half)
    residual_cols = in_order(core == 0, residual_mine, core_swap(residual_mine), 1)

    grads, grad_group = mixer_backward(
        projected, raw, states, grad_mixer, bound_here, gain_here, offsets
    )
    grad_rows = jnp.split(grads, 4, 1)
    grad_group = jnp.where(
        x == 0,
        jnp.concatenate([grad_group, jnp.zeros_like(grad_group)]),
        jnp.concatenate([jnp.zeros_like(grad_group), grad_group]),
    )
    grad_group = cut(
        grad_group + x_swap(grad_group), place, group_gain.shape[0] // (Z * X), 0
    )
    others = x_swap(jnp.stack([own(part, place + 1 - 2 * x) for part in grad_rows]))
    normed_part = 0.0
    for index, weight in enumerate(in_weights):
        normed_part = normed_part + dot(
            in_order(x == 0, own(grad_rows[index], place), others[index], 1), weight, 1, 1
        )
    grad_normed_one = scatter_over_mp(normed_part)
    tokens_share = share(tokens_in)
    scale_one = rms(tokens_share)
    pulled_one = grad_normed_one * first_gain
    grad_tokens = (
        share(grad_residual)
        + scale_one * pulled_one
        - tokens_share * scale_one**3 * jnp.mean(pulled_one * tokens_share, -1, keepdims=True)
    )

    blocks = [dot(normed_one_cols, part, 0, 0) for part in grad_rows]
    block_mine = jnp.stack([cut(block, x, narrow, 0) for block in blocks])
    block_other = x_swap(jnp.stack([cut(block, 1 - x, narrow, 0) for block in blocks]))
    weight_grads = in_order(x == 0, block_mine, block_other, 2)
    out_block = dot(mixer, residual_cols, 0, 0)
    grad_outw = in_order(
        x == 0, cut(out_block, x, narrow, 1), x_swap(cut(out_block, 1 - x, narrow, 1)), 0
    )

    first_sum = 0.0
    for index, weight in enumerate(in_weights):
        first_sum = first_sum + jnp.sum(cut(weight, place, narrow, 0) * weight_grads[index], 1)
    second_sum = jnp.sum(
        cut(swiglu_gate, place, narrow, 0) * grad_sgate
        + cut(swiglu_up, place, narrow, 0) * grad_sup,
        1,
    )
    sums = jnp.stack([first_sum, second_sum])
    sums = sums + core_swap(sums)
    sums = sums + y_swap(sums)
    return (
        output,
        grad_tokens,
        weight_grads[0],
        weight_grads[1],
        weight_grads[2],
        weight_grads[3],
        grad_outw,
        grad_sgate,
        grad_sup,
        grad_sdown,
        sums[0] / cut(first_gain, place, narrow, 0),
        grad_group,
        sums[1] / cut(second_gain, place, narrow, 0),
    )


def solution(mesh):
    in_specs = (
        P("seq", None),
        P("seq", None),
        P(),
        P("mp"),
        P(None, "mp"),
        P(None, "mp"),
        P(None, "mp"),
        P(None, "mp"),
        P("mp", None),
        P(None, "mp"),
        P(None, "mp"),
        P("mp", None),
        P(),
        P("mp"),
        P(),
    )
    out_specs = (
        P(("seq", "mp"), None),
        P(("seq", "mp"), None),
        P("seq", "mp"),
        P("seq", "mp"),
        P("seq", "mp"),
        P("seq", "mp"),
        P("mp", "seq"),
        P("seq", "mp"),
        P("seq", "mp"),
        P("mp", "seq"),
        P("seq"),
        P(("mp", "seq")),
        P("seq"),
    )
    small = (mesh.shape["seq"], mesh.shape["mp"]) == (Z * X, 4)
    body = fast_shards if small else shards
    return jax.shard_map(body, mesh=mesh, in_specs=in_specs, out_specs=out_specs, check_vma=False)
```

```python
from functools import partial

import jax
import jax.numpy as jnp
from jax import lax
from jax.experimental import pallas as pl
from jax.experimental.pallas import tpu as pltpu
from jax.sharding import PartitionSpec as P

HDIM = 128
CHUNK = 128
HIGH = lax.Precision.HIGH
HIGHEST = lax.Precision.HIGHEST
norm_eps = 1e-06
group_eps = 1e-05


def dot(left, right, contract_left, contract_right, precision=HIGH):
    return lax.dot_general(
        left,
        right,
        (((contract_left,), (contract_right,)), ((), ())),
        precision=precision,
        preferred_element_type=jnp.float32,
    )


def rms(entries):
    return lax.rsqrt(jnp.mean(entries * entries, -1, keepdims=True) + norm_eps)


def silu_grad(entries):
    gate = jax.nn.sigmoid(entries)
    return gate * (1.0 + entries * (1.0 - gate))


def gather_tokens(block):
    return lax.all_gather(block, "seq", axis=0, tiled=True)


def recurrence(query_rows, key_vecs, value_rows, segment):
    token_count, width = query_rows.shape
    heads = width // HDIM
    chunks = token_count // CHUNK

    def split(entries):
        return entries.reshape(chunks, CHUNK, heads, HDIM)

    blocked = segment.reshape(chunks, CHUNK)
    last_seg = blocked[:, -1]
    first_segs = jnp.concatenate([jnp.full((1,), -1, segment.dtype), last_seg[:-1]])
    carry = (blocked == first_segs[:, None]).astype(jnp.float32)
    in_last = (blocked == last_seg[:, None]).astype(jnp.float32)
    places = jnp.arange(CHUNK)
    allowed = (places[None, :, None] >= places[None, None, :]) & (
        blocked[:, :, None] == blocked[:, None, :]
    )
    lower = (places[:, None] >= places[None, :]).astype(jnp.float32)
    queries, keys, values = split(query_rows), split(key_vecs), split(value_rows)
    log_decay = jnp.einsum("ts,cshk->cthk", lower, jnp.log1p(-keys), precision=HIGHEST)
    growth = jnp.exp(log_decay)
    grown = queries * growth
    last = log_decay[:, -1]
    scores = jnp.einsum("cthk,cshk->chts", grown, keys * jnp.exp(-log_decay), precision=HIGH)
    scores = jnp.where(allowed[:, None], scores, 0.0)
    inner = jnp.einsum("chts,cshv->cthv", scores, values, precision=HIGH)
    weighted = keys * jnp.exp(last[:, None] - log_decay) * in_last[:, :, None, None]
    updates = jnp.einsum("cshk,cshv->chkv", weighted, values, precision=HIGH)
    through = jnp.exp(last) * carry[:, -1][:, None, None]
    state = jnp.zeros_like(updates[0])
    states = []
    for chunk in range(chunks):
        states.append(state)
        state = state * through[chunk][:, :, None] + updates[chunk]
    outer = jnp.einsum(
        "cthk,chkv->cthv", grown * carry[:, :, None, None], jnp.stack(states), precision=HIGH
    )
    return (inner + outer).reshape(token_count, width)


def mixer_all(pre_query, pre_forget, value_rows, gate_in, group_gain, lower_bound, segment):
    key_vecs = (1.0 - lower_bound) * jax.nn.sigmoid(-pre_forget)
    raw = recurrence(jax.nn.silu(pre_query), key_vecs, value_rows, segment)
    heads = raw.reshape(raw.shape[0], -1, HDIM)
    scale = lax.rsqrt(jnp.mean(heads * heads, -1, keepdims=True) + group_eps)
    normed = (heads * scale).reshape(raw.shape)
    return normed * group_gain * jax.nn.silu(gate_in)


def shards(
    tokens_in,
    cotangent,
    lengths,
    lower_bound,
    query_weight,
    forget_weight,
    input_weight,
    gate_weight,
    out_weight,
    swiglu_gate,
    swiglu_up,
    swiglu_down,
    first_gain,
    group_gain,
    second_gain,
):
    seq_count = lax.axis_size("seq")
    seq_place = lax.axis_index("seq")
    own_rows, model = tokens_in.shape
    token_count = own_rows * seq_count
    share_rows = own_rows // lax.axis_size("mp")
    share_start = lax.axis_index("mp") * share_rows
    start_row = seq_place * own_rows
    own_cols = model // seq_count
    start_col = seq_place * own_cols

    def own(entries):
        return lax.dynamic_slice_in_dim(entries, start_row, own_rows, 0)

    def columns(entries):
        return lax.dynamic_slice_in_dim(entries, start_col, own_cols, 1)

    def share(entries):
        return lax.dynamic_slice_in_dim(entries, share_start, share_rows, 0)

    positions = jnp.arange(token_count, dtype=jnp.int32)
    offsets = jnp.cumsum(lengths) - lengths
    segment = jnp.sum((positions[:, None] >= offsets[None, :]).astype(jnp.int32), 1) - 1

    all_tokens = gather_tokens(tokens_in)
    all_cotangent = gather_tokens(cotangent)
    normed_one = all_tokens * rms(all_tokens) * first_gain
    pre_query = dot(normed_one, query_weight, 1, 0)
    pre_forget = dot(normed_one, forget_weight, 1, 0)
    value_rows = dot(normed_one, input_weight, 1, 0)
    gate_in = dot(normed_one, gate_weight, 1, 0)
    mixer, mixer_back = jax.vjp(
        partial(mixer_all, lower_bound=lower_bound, segment=segment),
        pre_query,
        pre_forget,
        value_rows,
        gate_in,
        group_gain,
    )
    residual = tokens_in + lax.psum(dot(own(mixer), out_weight, 1, 0), "mp")
    scale_two = rms(residual)
    normed_two = residual * scale_two * second_gain
    grad_hidden_all = dot(all_cotangent, swiglu_down, 1, 1)
    a = dot(normed_two, swiglu_gate, 1, 0)
    b = dot(normed_two, swiglu_up, 1, 0)
    silu_a = jax.nn.silu(a)
    ffn_part = dot(silu_a * b, swiglu_down, 1, 0)
    output = share(residual) + lax.psum_scatter(ffn_part, "mp", scatter_dimension=0, tiled=True)
    e = own(grad_hidden_all)
    grad_a = e * b * silu_grad(a)
    grad_b = e * silu_a
    grad_normed_two = lax.psum(
        dot(grad_a, swiglu_gate, 1, 1) + dot(grad_b, swiglu_up, 1, 1), "mp"
    )
    pulled = grad_normed_two * second_gain
    grad_residual = (
        cotangent
        + scale_two * pulled
        - residual * scale_two**3 * jnp.mean(pulled * residual, -1, keepdims=True)
    )
    all_normed_two = gather_tokens(normed_two)
    a_all = dot(all_normed_two, swiglu_gate, 1, 0)
    b_all = dot(all_normed_two, swiglu_up, 1, 0)
    silu_all = jax.nn.silu(a_all)
    hidden_all = silu_all * b_all
    grad_a_all = grad_hidden_all * b_all * silu_grad(a_all)
    grad_b_all = grad_hidden_all * silu_all
    normed_two_cols = columns(all_normed_two)
    grad_sgate = dot(normed_two_cols, grad_a_all, 0, 0)
    grad_sup = dot(normed_two_cols, grad_b_all, 0, 0)
    grad_sdown = dot(hidden_all, columns(all_cotangent), 0, 0)

    grad_mixer = gather_tokens(dot(grad_residual, out_weight, 1, 1))
    residual_cols = lax.all_to_all(grad_residual, "seq", 1, 0, tiled=True)
    grad_outw = dot(mixer, residual_cols, 0, 0)
    grad_query_rows, grad_forget_rows, grad_value_rows, grad_gate_rows, grad_group = mixer_back(
        grad_mixer
    )
    grad_group = lax.dynamic_slice_in_dim(
        grad_group, seq_place * (group_gain.shape[0] // seq_count), group_gain.shape[0] // seq_count
    )
    normed_one_cols = columns(normed_one)
    pairs = (
        (grad_query_rows, query_weight),
        (grad_forget_rows, forget_weight),
        (grad_value_rows, input_weight),
        (grad_gate_rows, gate_weight),
    )
    weight_grads = []
    normed_part = 0.0
    first_sum = 0.0
    for grad_rows, weight in pairs:
        weight_grad = dot(normed_one_cols, grad_rows, 0, 0)
        weight_grads.append(weight_grad)
        normed_part = normed_part + dot(own(grad_rows), weight, 1, 1)
        own_weight = lax.dynamic_slice_in_dim(weight, start_col, own_cols, 0)
        first_sum = first_sum + jnp.sum(own_weight * weight_grad, 1)
    second_sum = jnp.sum(
        lax.dynamic_slice_in_dim(swiglu_gate, start_col, own_cols, 0) * grad_sgate
        + lax.dynamic_slice_in_dim(swiglu_up, start_col, own_cols, 0) * grad_sup,
        1,
    )
    gains = jnp.stack(
        [
            lax.dynamic_slice_in_dim(first_gain, start_col, own_cols),
            lax.dynamic_slice_in_dim(second_gain, start_col, own_cols),
        ]
    )
    gain_grads = lax.psum(jnp.stack([first_sum, second_sum]), "mp") / gains
    grad_normed_one = lax.psum_scatter(normed_part, "mp", scatter_dimension=0, tiled=True)
    tokens_share = share(tokens_in)
    scale_one = rms(tokens_share)
    pulled_one = grad_normed_one * first_gain
    grad_tokens = (
        share(grad_residual)
        + scale_one * pulled_one
        - tokens_share * scale_one**3 * jnp.mean(pulled_one * tokens_share, -1, keepdims=True)
    )
    return (
        output,
        grad_tokens,
        weight_grads[0],
        weight_grads[1],
        weight_grads[2],
        weight_grads[3],
        grad_outw,
        grad_sgate,
        grad_sup,
        grad_sdown,
        gain_grads[0],
        grad_group,
        gain_grads[1],
    )


Z, X = 4, 2


def x_swap(array):
    return lax.ppermute(array, "seq", [(s, s ^ 1) for s in range(Z * X)])


def cut(array, place, size, axis):
    return lax.dynamic_slice_in_dim(array, place * size, size, axis)


def in_order(first, mine, other, axis):
    return jnp.where(
        first, jnp.concatenate([mine, other], axis), jnp.concatenate([other, mine], axis)
    )


F32, BF16 = jnp.float32, jnp.bfloat16
MESH = pl.DeviceIdType.MESH
ANY = pl.BlockSpec(memory_space=pl.ANY)
WHOLE = pl.BlockSpec(memory_space=pltpu.VMEM)
TILE = 256
VMEM_BYTES = 60 << 20


def halves(entries):
    high = entries.astype(BF16)
    return high, (entries - high.astype(F32)).astype(BF16)


def product(left, right, contract_left, contract_right):
    return lax.dot_general(
        left,
        right,
        (((contract_left,), (contract_right,)), ((), ())),
        preferred_element_type=F32,
    )


def three_pass(left, right, contract_left, contract_right):
    (left_high, left_low), (right_high, right_low) = left, right
    return product(left_high, right_high, contract_left, contract_right) + (
        product(left_high, right_low, contract_left, contract_right)
        + product(left_low, right_high, contract_left, contract_right)
    )


def few_rows(left, right, contract_right):
    (left_high, left_low), (right_high, right_low) = left, right
    rows = left_high.shape[0]
    both = product(jnp.concatenate([left_high, left_low]), right_high, 1, contract_right)
    return both[:rows] + (product(left_high, right_low, 1, contract_right) + both[rows:])


def remote(src, dst, sems, index, device):
    return pltpu.make_async_remote_copy(
        src_ref=src,
        dst_ref=dst,
        send_sem=sems[0].at[index],
        recv_sem=sems[1].at[index],
        device_id=device,
        device_id_type=MESH,
    )


def dma_sems(count):
    return [pltpu.SemaphoreType.DMA((count,)), pltpu.SemaphoreType.DMA((count,))]


class Move:
    def __init__(self, ins, outs, scratch):
        self.ins, self.outs, self.scratch_refs = ins, outs, scratch
        place, part = lax.axis_index("seq"), lax.axis_index("mp")
        self.z, self.x, self.y, self.core = place // X, place % X, part // 2, part % 2
        self.setup()

    def setup(self):
        pass

    def device(self, z, x, y, core):
        return (z * X + x, y * 2 + core)

    def x_peer(self):
        return self.device(self.z, 1 - self.x, self.y, self.core)

    def y_peer(self):
        return self.device(self.z, self.x, 1 - self.y, self.core)

    def core_peer(self):
        return self.device(self.z, self.x, self.y, 1 - self.core)

    def holds(self, way, step):
        source = self.z - way * step
        return (source >= 0) & (source < Z)

    def goes_on(self, way, step):
        return self.holds(way, step - 1) & (self.z + way >= 0) & (self.z + way < Z)

    def each(self, step, action):
        if step == 0:
            action(1)
        else:
            for way in (1, -1):
                pl.when(self.holds(way, step))(lambda way=way: action(way))

    def greet(self, far):
        barrier = pltpu.get_barrier_semaphore()

        def signal(device):
            pl.semaphore_signal(barrier, inc=1, device_id=device, device_id_type=MESH)

        signal(self.x_peer())
        signal(self.y_peer())
        signal(self.core_peer())
        if far:
            for distance in range(1, Z):
                signal(self.device((self.z + distance) % Z, self.x, self.y, self.core))
            pl.semaphore_wait(barrier, 3 + Z - 1)
        else:
            for way in (1, -1):
                ahead = (self.z + way >= 0) & (self.z + way < Z)
                pl.when(ahead)(
                    lambda way=way: signal(self.device(self.z + way, self.x, self.y, self.core))
                )
            neighbours = jnp.where(self.z > 0, 1, 0) + jnp.where(self.z < Z - 1, 1, 0)
            pl.semaphore_wait(barrier, 3 + neighbours)


class Gather(Move):
    PIECES = 2

    def in_specs(arrays):
        return [ANY]

    def results(arrays):
        return [((Z * X * arrays[0].shape[0], arrays[0].shape[1]), ANY)]

    def scratch(arrays):
        return [*dma_sems(52 * Gather.PIECES), pltpu.SemaphoreType.DMA((1,))]

    def setup(self):
        (self.block,), (self.out,) = self.ins, self.outs
        self.sems, self.local = self.scratch_refs[:2], self.scratch_refs[2]
        self.rows = self.block.shape[0]
        self.size = self.rows // self.PIECES
        self.tile = self.block.shape[1] // 16

    def cols(self, first, count):
        return pl.ds(pl.multiple_of(first * self.tile, self.tile), count * self.tile)

    def columns(self, y, core):
        return self.cols(6 * y + 5 * core, 5)

    def y_columns(self, y, big):
        return self.cols(11 * y, 5) if big else self.cols(5 + 5 * y, 1)

    def region(self, z, x, piece, columns):
        row = (z * X + x) * self.rows + piece * self.size
        return self.out.at[pl.ds(pl.multiple_of(row, self.size), self.size), columns]

    def fetched(self, z, x, piece):
        return self.region(z, x, piece, self.columns(self.y, self.core))

    def own(self, piece):
        return self.block.at[
            pl.ds(piece * self.size, self.size), self.columns(self.y, self.core)
        ]

    def slot(self, way, step):
        return 0 if step == 0 else (0 if way > 0 else 3) + step

    def along(self, way, step, piece, arriving):
        dst = self.fetched(self.z - way * (step if arriving else step - 1), self.x, piece)
        return remote(
            self.own(piece) if step == 1 and not arriving else dst,
            dst,
            self.sems,
            52 * piece + (0 if way > 0 else 3) + step - 1,
            self.device(self.z + way, self.x, self.y, self.core),
        )

    def across(self, way, step, piece, arriving):
        dst = self.fetched(self.z - way * step, 1 - self.x if arriving else self.x, piece)
        return remote(
            self.own(piece) if step == 0 and not arriving else dst,
            dst,
            self.sems,
            52 * piece + 6 + self.slot(way, step),
            self.x_peer(),
        )

    def inside(self, way, step, other_x, piece, arriving):
        region = self.region(
            self.z - way * step,
            1 - self.x if other_x else self.x,
            piece,
            self.columns(self.y, 1 - self.core if arriving else self.core),
        )
        index = 52 * piece + 13 + self.slot(way, step) + (0 if other_x else 6)
        return remote(region, region, self.sems, index, self.core_peer())

    def over_y(self, way, step, other_x, piece, arriving, big):
        region = self.region(
            self.z - way * step,
            1 - self.x if other_x else self.x,
            piece,
            self.y_columns(1 - self.y if arriving else self.y, big),
        )
        index = 52 * piece + 26 + self.slot(way, step) + (0 if other_x else 6)
        return remote(region, region, self.sems, index, self.y_peer())

    def inside_y(self, way, step, other_x, piece, big):
        region = self.region(
            self.z - way * step,
            1 - self.x if other_x else self.x,
            piece,
            self.y_columns(1 - self.y, big),
        )
        index = 52 * piece + 39 + self.slot(way, step) + (0 if other_x else 6)
        return remote(region, region, self.sems, index, self.core_peer())

    def sized(self, big, action):
        pl.when(big)(lambda: action(True))
        pl.when(jnp.logical_not(big))(lambda: action(False))

    def pass_on(self, way, step, other_x, piece):
        self.sized(
            self.core == self.y,
            lambda big: self.over_y(way, step, other_x, piece, False, big).start(),
        )
        self.inside(way, step, other_x, piece, False).start()

    def begin(self):
        for piece in range(self.PIECES):
            self.across(1, 0, piece, False).start()
            for way in (1, -1):
                pl.when(self.goes_on(way, 1))(
                    lambda way=way, piece=piece: self.along(way, 1, piece, False).start()
                )
        self.own_copy().start()

    def own_copy(self):
        row = pl.multiple_of((self.z * X + self.x) * self.rows, self.rows)
        return pltpu.make_async_copy(
            self.block, self.out.at[pl.ds(row, self.rows), :], self.local.at[0]
        )

    def arrive_along(self, step, piece):
        def action(way):
            self.along(way, step, piece, True).wait_recv()
            if step < Z - 1:
                pl.when(self.goes_on(way, step + 1))(
                    lambda: self.along(way, step + 1, piece, False).start()
                )
            self.across(way, step, piece, False).start()
            self.pass_on(way, step, False, piece)

        self.each(step, action)

    def arrive_across(self, step, piece):
        def action(way):
            self.across(way, step, piece, True).wait_recv()
            self.pass_on(way, step, True, piece)

        self.each(step, action)

    def arrive_y(self, step, other_x, piece):
        def action(way):
            def sized(big):
                self.over_y(way, step, other_x, piece, True, big).wait_recv()
                self.inside_y(way, step, other_x, piece, big).start()

            self.sized(self.core != self.y, sized)

        self.each(step, action)

    def finish(self):
        self.own_copy().wait()
        for piece in range(self.PIECES):
            for way in (1, -1):
                for step in range(1, Z):
                    pl.when(self.goes_on(way, step))(
                        lambda way=way, step=step, piece=piece: self.along(
                            way, step, piece, False
                        ).wait_send()
                    )
            for step in range(Z):

                def action(way, step=step, piece=piece):
                    self.across(way, step, piece, False).wait_send()
                    for other_x in (False, True) if step else (True,):
                        self.inside(way, step, other_x, piece, False).wait_send()
                        self.inside(way, step, other_x, piece, True).wait_recv()

                        def sized(big, other_x=other_x):
                            self.over_y(way, step, other_x, piece, False, big).wait_send()
                            self.inside_y(way, step, other_x, piece, not big).wait_send()
                            self.inside_y(way, step, other_x, piece, big).wait_recv()

                        self.sized(self.core == self.y, sized)

                self.each(step, action)

    def events(self):
        def round_of(index):
            step, piece = index // 2 + 1, index % 2

            def event():
                if step < Z:
                    self.arrive_along(step, piece)
                if step <= Z:
                    self.arrive_across(step - 1, piece)
                if 1 <= step - 1 < Z:
                    self.arrive_y(step - 1, False, piece)
                if 0 <= step - 2 < Z:
                    self.arrive_y(step - 2, True, piece)

            return event

        return [round_of(index) for index in range(2 * (Z + 1))] + [self.finish]


class Sum(Move):
    def in_specs(arrays):
        return [WHOLE]

    def results(arrays):
        return [(arrays[0].shape, WHOLE)]

    def scratch(arrays):
        rows, columns = arrays[0].shape
        return [pltpu.VMEM((4, rows, columns // 2), F32), *dma_sems(3)]

    def setup(self):
        (self.part,), (self.out,) = self.ins, self.outs
        self.landing, self.sems = self.scratch_refs[0], self.scratch_refs[1:]
        self.half = self.part.shape[1] // 2

    def columns(self, ref, core):
        return ref.at[:, pl.ds(pl.multiple_of(core * self.half, self.half), self.half)]

    def first(self):
        return remote(
            self.columns(self.part, 1 - self.core),
            self.landing.at[0],
            self.sems,
            0,
            self.core_peer(),
        )

    def second(self):
        return remote(self.landing.at[1], self.landing.at[2], self.sems, 1, self.y_peer())

    def third(self):
        return remote(self.landing.at[1], self.landing.at[3], self.sems, 2, self.core_peer())

    def begin(self):
        self.first().start()

    def to_y(self):
        self.first().wait()
        self.landing[1] = self.columns(self.part, self.core)[...] + self.landing[0]
        self.second().start()

    def back(self):
        self.second().wait()
        self.landing[1] = self.landing[1] + self.landing[2]
        self.third().start()

    def finish(self):
        self.third().wait()
        self.columns(self.out, self.core)[...] = self.landing[1]
        self.columns(self.out, 1 - self.core)[...] = self.landing[3]

    def events(self):
        return [self.to_y, self.back, self.finish]


class Scatter(Move):
    def in_specs(arrays):
        return [WHOLE]

    def results(arrays):
        rows, columns = arrays[0].shape
        return [((rows // 4, columns), WHOLE)]

    def scratch(arrays):
        rows, columns = arrays[0].shape
        return [pltpu.VMEM((5, rows // 4, columns), F32), *dma_sems(3)]

    def setup(self):
        (self.part,), (self.out,) = self.ins, self.outs
        self.landing, self.sems = self.scratch_refs[0], self.scratch_refs[1:]
        self.rows = self.part.shape[0] // 4

    def block(self, y, core):
        row = pl.multiple_of((y * 2 + core) * self.rows, self.rows)
        return self.part.at[pl.ds(row, self.rows), :]

    def to_core(self, y):
        block = self.block(self.y if y == 0 else 1 - self.y, 1 - self.core)
        return remote(block, self.landing.at[y], self.sems, y, self.core_peer())

    def to_y(self):
        return remote(self.landing.at[2], self.landing.at[3], self.sems, 2, self.y_peer())

    def begin(self):
        self.to_core(1).start()
        self.to_core(0).start()

    def middle(self):
        self.to_core(1).wait()
        self.landing[2] = self.block(1 - self.y, self.core)[...] + self.landing[1]
        self.to_y().start()

    def finish(self):
        self.to_core(0).wait()
        self.to_y().wait()
        self.out[...] = (self.block(self.y, self.core)[...] + self.landing[0]) + self.landing[3]

    def events(self):
        return [self.middle, self.finish]


class Heads(Move):
    def in_specs(arrays):
        return [ANY]

    def results(arrays):
        rows, columns = arrays[0].shape
        return [((Z * X * rows, columns // X), ANY)]

    def scratch(arrays):
        return [*dma_sems(7), pltpu.SemaphoreType.DMA((1,))]

    def setup(self):
        (self.own,), (self.out,) = self.ins, self.outs
        self.sems, self.local = self.scratch_refs[:2], self.scratch_refs[2]
        self.rows, columns = self.own.shape
        self.width = columns // X

    def block(self, z, x):
        row = pl.multiple_of((z * X + x) * self.rows, self.rows)
        return self.out.at[pl.ds(row, self.rows), :]

    def plane(self, z):
        row = pl.multiple_of(z * X * self.rows, X * self.rows)
        return self.out.at[pl.ds(row, X * self.rows), :]

    def own_columns(self, x):
        return self.own.at[:, pl.ds(pl.multiple_of(x * self.width, self.width), self.width)]

    def swap(self):
        return remote(
            self.own_columns(1 - self.x), self.block(self.z, self.x), self.sems, 6, self.x_peer()
        )

    def keep(self):
        return pltpu.make_async_copy(
            self.own_columns(self.x), self.block(self.z, self.x), self.local.at[0]
        )

    def along(self, way, step, arriving):
        plane = self.plane(self.z - way * (step if arriving else step - 1))
        return remote(
            plane,
            plane,
            self.sems,
            (0 if way > 0 else 3) + step - 1,
            self.device(self.z + way, self.x, self.y, self.core),
        )

    def begin(self):
        self.swap().start()
        self.keep().start()

    def start_along(self, way, step):
        pl.when(self.goes_on(way, step))(lambda: self.along(way, step, False).start())

    def swapped(self):
        self.swap().wait()
        self.keep().wait()
        for way in (1, -1):
            self.start_along(way, 1)

    def arrive(self, step):
        def action(way):
            self.along(way, step, True).wait_recv()
            if step < Z - 1:
                self.start_along(way, step + 1)

        self.each(step, action)

    def finish(self):
        self.arrive(Z - 1)
        for way in (1, -1):
            for step in range(1, Z):
                pl.when(self.goes_on(way, step))(
                    lambda way=way, step=step: self.along(way, step, False).wait_send()
                )

    def events(self):
        return [self.swapped, lambda: self.arrive(1), lambda: self.arrive(2), self.finish]


class Columns(Move):
    def in_specs(arrays):
        return [ANY]

    def results(arrays):
        rows, columns = arrays[0].shape
        return [((Z, X, rows, columns // Z), ANY)]

    def scratch(arrays):
        return [*dma_sems(Z + Z + 1), pltpu.SemaphoreType.DMA((1,))]

    def setup(self):
        (self.own,), (self.out,) = self.ins, self.outs
        self.sems, self.local = self.scratch_refs[:2], self.scratch_refs[2]
        self.half = self.own.shape[1] // (2 * Z)

    def piece(self, z):
        start = pl.multiple_of((z * 2 + self.core) * self.half, self.half)
        return self.own.at[:, pl.ds(start, self.half)]

    def landing(self, z, x, core):
        start = pl.multiple_of(core * self.half, self.half)
        return self.out.at[z, x, :, pl.ds(start, self.half)]

    def along(self, distance):
        z = (self.z + distance) % Z
        return remote(
            self.piece(z),
            self.landing(self.z, self.x, self.core),
            self.sems,
            distance,
            self.device(z, self.x, self.y, self.core),
        )

    def keep(self):
        return pltpu.make_async_copy(
            self.piece(self.z), self.landing(self.z, self.x, self.core), self.local.at[0]
        )

    def across(self, distance):
        block = self.landing((self.z - distance) % Z, self.x, self.core)
        return remote(block, block, self.sems, Z + distance, self.x_peer())

    def inside(self):
        start = pl.multiple_of(self.core * self.half, self.half)
        part = self.out.at[:, :, :, pl.ds(start, self.half)]
        return remote(part, part, self.sems, 2 * Z, self.core_peer())

    def begin(self):
        self.keep().start()
        for distance in (1, 3, 2):
            self.along(distance).start()

    def arrived(self, distance):
        if distance == 0:
            self.keep().wait()
        else:
            self.along(distance).wait()
        self.across(distance).start()

    def all_here(self):
        for distance in range(Z):
            self.across(distance).wait()
        self.inside().start()

    def events(self):
        return [
            lambda: self.arrived(0),
            lambda: self.arrived(1),
            lambda: self.arrived(3),
            lambda: self.arrived(2),
            self.all_here,
            lambda: self.inside().wait(),
        ]


class SwapX(Move):
    def in_specs(arrays):
        return [ANY] * len(arrays)

    def results(arrays):
        return [(array.shape, ANY) for array in arrays]

    def scratch(arrays):
        return dma_sems(len(arrays))

    def setup(self):
        pass

    def copies(self):
        return [
            remote(src, dst, self.scratch_refs, index, self.x_peer())
            for index, (src, dst) in enumerate(zip(self.ins, self.outs, strict=True))
        ]

    def begin(self):
        for copy in self.copies():
            copy.start()

    def finish(self):
        for copy in self.copies():
            copy.wait()

    def events(self):
        return [self.finish]


class SwapBlocks(Move):
    def in_specs(arrays):
        return [ANY] * len(arrays)

    def results(arrays):
        return [((X, array.shape[0] // X, array.shape[1]), ANY) for array in arrays]

    def scratch(arrays):
        return [*dma_sems(len(arrays)), pltpu.SemaphoreType.DMA((len(arrays),))]

    def setup(self):
        self.sems, self.local = self.scratch_refs[:2], self.scratch_refs[2]

    def ends(self, index, x):
        src, dst = self.ins[index], self.outs[index]
        rows = src.shape[0] // X
        return src.at[pl.ds(pl.multiple_of(x * rows, rows), rows), :], dst.at[self.x]

    def send(self, index):
        return remote(*self.ends(index, 1 - self.x), self.sems, index, self.x_peer())

    def keep(self, index):
        return pltpu.make_async_copy(*self.ends(index, self.x), self.local.at[index])

    def begin(self):
        for index in range(len(self.ins)):
            self.send(index).start()
            self.keep(index).start()

    def finish(self):
        for index in range(len(self.ins)):
            self.send(index).wait()
            self.keep(index).wait()

    def events(self):
        return [self.finish]


class SumAll(Move):
    def in_specs(arrays):
        return [WHOLE]

    def results(arrays):
        rows, columns = arrays[0].shape
        return [((rows // X, columns), WHOLE)]

    def scratch(arrays):
        rows, columns = arrays[0].shape
        return [pltpu.VMEM((6, rows // X, columns), F32), *dma_sems(3)]

    def setup(self):
        (self.part,), (self.out,) = self.ins, self.outs
        self.landing, self.sems = self.scratch_refs[0], self.scratch_refs[1:]
        self.rows = self.part.shape[0] // X

    def half(self, x):
        return self.part.at[pl.ds(pl.multiple_of(x * self.rows, self.rows), self.rows), :]

    def first(self):
        return remote(self.half(1 - self.x), self.landing.at[0], self.sems, 0, self.x_peer())

    def second(self):
        return remote(self.landing.at[1], self.landing.at[2], self.sems, 1, self.core_peer())

    def third(self):
        return remote(self.landing.at[3], self.landing.at[4], self.sems, 2, self.y_peer())

    def begin(self):
        self.first().start()

    def to_core(self):
        self.first().wait()
        self.landing[1] = self.half(self.x)[...] + self.landing[0]
        self.second().start()

    def to_y(self):
        self.second().wait()
        self.landing[3] = self.landing[1] + self.landing[2]
        self.third().start()

    def finish(self):
        self.third().wait()
        self.out[...] = self.landing[3] + self.landing[4]

    def events(self):
        return [self.to_core, self.to_y, self.finish]


class Refs(dict):
    __getattr__ = dict.__getitem__


def fused(arrays, results, scratch, steps, body, collective_id, far=False, flops=0):
    names = [*arrays, *results, *scratch]

    def kernel(*refs):
        refs = list(refs)
        here = Refs(zip([*arrays, *results], refs, strict=False))
        del refs[: len(arrays) + len(results)]
        for name, needed in scratch.items():
            here[name] = refs[: len(needed)]
            del refs[: len(needed)]
        step = pl.program_id(0)
        if collective_id is not None:
            pl.when(step == 0)(lambda: Move([], [], []).greet(far))
        body(here, step)

    outputs = pl.pallas_call(
        kernel,
        grid=(steps,),
        out_shape=[jax.ShapeDtypeStruct(shape, F32) for shape, _ in results.values()],
        in_specs=[spec for _, spec in arrays.values()],
        out_specs=[spec for _, spec in results.values()],
        scratch_shapes=[one for needed in scratch.values() for one in needed],
        compiler_params=pltpu.CompilerParams(
            has_side_effects=True,
            vmem_limit_bytes=VMEM_BYTES,
            **({} if collective_id is None else dict(collective_id=collective_id)),
        ),
        cost_estimate=pl.CostEstimate(flops=flops, bytes_accessed=32 << 20, transcendentals=0),
    )(*(array for array, _ in arrays.values()))
    return Refs(zip(results, outputs, strict=True))


def at(now, when, *actions):
    for action in actions:
        pl.when(now == when)(action)


def schedule(now, when, events):
    for event, moment in zip(events, when, strict=True):
        pl.when(now == moment)(event)


def gather_tokens_fast(block, collective_id):
    def body(refs, step):
        move = Gather([refs.block], [refs.all], refs.move)
        move.begin()
        for event in move.events():
            event()

    return fused(
        dict(block=(block, ANY)),
        dict(all=Gather.results([block])[0]),
        dict(move=Gather.scratch([block])),
        1,
        body,
        collective_id,
    ).all


def halves_scratch(rows, inner):
    return [
        pltpu.VMEM((rows, inner), BF16),
        pltpu.VMEM((rows, inner), BF16),
        pltpu.VMEM((rows // 128, 128, inner), F32),
        pltpu.SemaphoreType.DMA((rows // 128,)),
    ]


def load_halves(src_ref, high_ref, low_ref, stage_ref, sem, change=None):
    count, rows, _ = stage_ref.shape

    def spot(index):
        return pl.ds(pl.multiple_of(index * rows, rows), rows)

    def fetch(index):
        return pltpu.make_async_copy(
            src_ref.at[spot(index), :], stage_ref.at[index], sem.at[index]
        )

    for index in range(count):
        fetch(index).start()

    def split(index, carried):
        fetch(index).wait()
        if change is not None:
            change(index)
        high, low = halves(stage_ref[index])
        high_ref[spot(index), :] = high
        low_ref[spot(index), :] = low
        return carried

    lax.fori_loop(0, count, split, 0)


STRIP = 256


def strips(rows, action):
    def one(index, carried):
        action(index, pl.ds(pl.multiple_of(index * STRIP, STRIP), STRIP))
        return carried

    lax.fori_loop(0, rows // STRIP, one, 0)


def block_fetch(src, buf, sem, index):
    return pltpu.make_async_copy(src, buf.at[index], sem.at[index])


def mixer_kernel(
    all_tokens, tokens_in, cotangent, lengths, lower_bound, in_weights, out_weight, w_down,
    first_gain, group_gain, second_gain, collective_id,
):
    rows, inner = all_tokens.shape
    own_rows = tokens_in.shape[0]
    count = len(in_weights)
    wide = inner // Z
    heads = TILE // HDIM
    chunks = rows // CHUNK
    columns = w_down.shape[0]
    tiles = pl.cdiv(columns, TILE)
    parts = rows // STRIP
    middle = count + chunks
    steps = middle + 1 + tiles

    def body(refs, step):
        place = lax.axis_index("seq")
        x = place % X
        here = pl.ds(pl.multiple_of(x * TILE, TILE), TILE)
        there = pl.ds(pl.multiple_of((1 - x) * TILE, TILE), TILE)
        first_col = pl.multiple_of((place // X) * wide, wide)
        gather = Gather([refs.cotangent], [refs.all_cotangent], refs.gather)
        part_ref, sum_ref, *sum_scratch = refs.sum
        total = Sum([part_ref], [sum_ref], sum_scratch)
        high_ref, low_ref, stage_ref, stage_sem = refs.halves
        weight_buf, weight_sem, out_buf, out_sem, down_buf, down_sem = refs.weights
        (state_ref,) = refs.state
        other_ref, send, recv = refs.swap
        weight_refs = [refs[f"weight_{index}"] for index in range(count)]
        now = step * parts

        def fetch(index):
            return block_fetch(weight_refs[index].at[:, here], weight_buf, weight_sem, index % 2)

        def fetch_out():
            return pltpu.make_async_copy(refs.out_weight, out_buf, out_sem.at[0])

        def fetch_down(tile, size=TILE):
            return pltpu.make_async_copy(
                refs.w_down.at[pl.ds(pl.multiple_of(tile * TILE, TILE), size), :],
                down_buf.at[lax.rem(tile, 2), pl.ds(0, size), :],
                down_sem.at[lax.rem(tile, 2)],
            )

        def sized(tile, action):
            last = columns - (tiles - 1) * TILE
            pl.when(tile < tiles - 1)(lambda: action(TILE))
            pl.when(tile == tiles - 1)(lambda: action(last))

        def swap():
            peer = pl.multiple_of((place + 1 - 2 * x) * own_rows, own_rows)
            return remote(
                refs.mixer.at[pl.ds(peer, own_rows), :], other_ref, (send, recv), 0, gather.x_peer()
            )

        def pause(part):
            schedule(now + part, (1, 3, 5, 7, 9, 11, 13, 15, 20, 24), gather.events()[:-1])
            schedule(now + part, (4 * middle + 4, 4 * middle + 15, 4 * middle + 19), total.events())

        def normalize(index):
            entries = stage_ref[index]
            stage_ref[index] = entries * rms(entries) * refs.first_gain[...]
            refs.normed_cols[pl.ds(pl.multiple_of(index * 128, 128), 128), :] = stage_ref[
                index, :, pl.ds(first_col, wide)
            ]

        @pl.when(step == 0)
        def _():
            gather.begin()
            fetch(0).start()
            fetch_out().start()
            load_halves(refs.tokens, high_ref, low_ref, stage_ref, stage_sem, normalize)
            state_ref[...] = jnp.zeros_like(state_ref)

        for index in range(count):

            @pl.when(step == index)
            def _(index=index):
                if index + 1 < count:
                    fetch(index + 1).start()
                fetch(index).wait()

        @pl.when(step < count)
        def _():
            weight = halves(weight_buf[lax.rem(step, 2)])
            target = pl.ds(pl.multiple_of(step * TILE, TILE), TILE)

            def strip(index, spot):
                refs.projected[spot, target] = three_pass(
                    (high_ref[spot, :], low_ref[spot, :]), weight, 1, 0
                )
                pause(index)

            strips(rows, strip)

        @pl.when((step >= count) & (step < middle))
        def _():
            chunk = step - count
            spot = pl.ds(pl.multiple_of(chunk * CHUNK, CHUNK), CHUNK)
            forward_chunk(
                chunk,
                refs.lengths,
                refs.projected.at[spot, :],
                refs.lower_bound.at[:, here],
                refs.group_gain.at[:, here],
                refs.mixer.at[spot, :],
                refs.raw.at[spot, :],
                refs.states.at[pl.ds(chunk, 1)],
                state_ref,
            )
            pause(0)

        @pl.when(step == middle)
        def _():
            swap().start()
            fetch_down(0).start()
            fetch_out().wait()
            own = refs.mixer[pl.ds(pl.multiple_of(place * own_rows, own_rows), own_rows), :]
            part_ref[...] = few_rows(halves(own), halves(out_buf[here, :]), 0)
            swap().wait()
            part_ref[...] += few_rows(halves(other_ref[...]), halves(out_buf[there, :]), 0)
            total.begin()
            gather.finish()
            load_halves(refs.all_cotangent, high_ref, low_ref, stage_ref, stage_sem)

        @pl.when(step > middle)
        def _():
            tile = step - middle - 1
            pl.when(tile < tiles - 1)(
                lambda: sized(tile + 1, lambda size: fetch_down(tile + 1, size).start())
            )
            sized(tile, lambda size: fetch_down(tile, size).wait())
            weight = halves(jnp.transpose(down_buf[lax.rem(tile, 2)]))

            def strip(index, spot):
                refs.grad_hidden[spot, :] = three_pass(
                    (high_ref[spot, :], low_ref[spot, :]), weight, 1, 0
                )
                pause(index)

            strips(rows, strip)

        @pl.when(step == steps - 1)
        def _():
            residual = refs.tokens_in[...] + sum_ref[...]
            refs.residual[...] = residual
            refs.normed_two[...] = residual * rms(residual) * refs.second_gain[...]

    own_shape = (own_rows, inner)
    return fused(
        dict(
            lengths=(lengths, pl.BlockSpec(memory_space=pltpu.SMEM)),
            tokens=(all_tokens, ANY),
            tokens_in=(tokens_in, WHOLE),
            cotangent=(cotangent, ANY),
            lower_bound=(lower_bound[None], WHOLE),
            first_gain=(first_gain[None], WHOLE),
            group_gain=(group_gain[None], WHOLE),
            second_gain=(second_gain[None], WHOLE),
            out_weight=(out_weight, ANY),
            w_down=(w_down, ANY),
            **{f"weight_{index}": (weight, ANY) for index, weight in enumerate(in_weights)},
        ),
        dict(
            all_cotangent=((rows, inner), ANY),
            projected=((rows, count * TILE), WHOLE),
            normed_cols=((rows, wide), WHOLE),
            mixer=((rows, TILE), WHOLE),
            raw=((rows, TILE), WHOLE),
            states=((chunks, heads, HDIM, HDIM), WHOLE),
            grad_hidden=(
                (rows, columns),
                pl.BlockSpec((rows, TILE), lambda step: (0, jnp.maximum(step - middle - 1, 0))),
            ),
            residual=(own_shape, WHOLE),
            normed_two=(own_shape, WHOLE),
        ),
        dict(
            halves=halves_scratch(rows, inner),
            weights=[
                pltpu.VMEM((2, inner, TILE), F32),
                pltpu.SemaphoreType.DMA((2,)),
                pltpu.VMEM(out_weight.shape, F32),
                pltpu.SemaphoreType.DMA((1,)),
                pltpu.VMEM((2, TILE, inner), F32),
                pltpu.SemaphoreType.DMA((2,)),
            ],
            state=[pltpu.VMEM((heads, HDIM, HDIM), F32)],
            swap=[pltpu.VMEM((own_rows, TILE), F32), *dma_sems(1)],
            gather=Gather.scratch([cotangent]),
            sum=[
                pltpu.VMEM(own_shape, F32),
                pltpu.VMEM(own_shape, F32),
                *Sum.scratch([tokens_in]),
            ],
        ),
        steps,
        body,
        collective_id,
        flops=6 * rows * inner * (count * TILE + columns),
    )


def feed_forward_kernel(
    normed_two, residual, cotangent, grad_hidden, w_gate, w_up, w_down, out_weight, second_gain, collective_id
):
    rows, inner = normed_two.shape
    columns = w_gate.shape[1]
    tiles = pl.cdiv(columns, TILE)

    def body(refs, step):
        gather = Gather([refs.normed_two], [refs.all_normed_two], refs.gather)
        part_ref, sum_ref, *sum_scratch = refs.sum
        total = Sum([part_ref], [sum_ref], sum_scratch)
        out_buf, out_sem = refs.out
        fetch_out = pltpu.make_async_copy(refs.out_weight, out_buf, out_sem.at[0])
        events = gather.events()

        def pause(part):
            schedule(step * 2 + part, (0, 1, 2, 3, 4, 5, 7, 9), events[:8])

        @pl.when(step == 0)
        def _():
            gather.begin()
            fetch_out.start()
            refs.ffn[...] = jnp.zeros_like(refs.ffn)
            part_ref[...] = jnp.zeros_like(part_ref)

        def inside(shape, axis):
            return step * TILE + lax.broadcasted_iota(jnp.int32, shape, axis) < columns

        gate_weight = halves(jnp.where(inside((inner, TILE), 1), refs.w_gate[...], 0.0))
        up_weight = halves(jnp.where(inside((inner, TILE), 1), refs.w_up[...], 0.0))
        normed = halves(refs.normed_two[...])
        a = few_rows(normed, gate_weight, 0)
        b = few_rows(normed, up_weight, 0)
        pause(0)
        e = jnp.where(inside((rows, TILE), 1), refs.grad_hidden[...], 0.0)
        gate = jax.nn.sigmoid(a)
        silu_a = a * gate
        down_weight = halves(jnp.where(inside((TILE, inner), 0), refs.w_down[...], 0.0))
        refs.ffn[...] += few_rows(halves(silu_a * b), down_weight, 0)
        part_ref[...] += few_rows(
            halves(e * b * (gate * (1.0 + a * (1.0 - gate)))), gate_weight, 1
        ) + few_rows(halves(e * silu_a), up_weight, 1)
        pause(1)

        @pl.when(step == tiles - 1)
        def _():
            total.begin()
            total.to_y()
            events[8]()
            events[9]()
            total.back()
            gather.finish()
            total.finish()
            residual_here = refs.residual[...]
            scale = rms(residual_here)
            summed = sum_ref[...]
            pulled = summed * refs.second_gain[...]
            grad_residual = (
                refs.cotangent[...]
                + scale * pulled
                - residual_here
                * (scale * scale * scale * jnp.mean(pulled * residual_here, -1, keepdims=True))
            )
            refs.grad_residual[...] = grad_residual
            refs.second[...] = jnp.broadcast_to(
                jnp.sum(summed * residual_here * scale, 0, keepdims=True), refs.second.shape
            )
            fetch_out.wait()
            refs.grad_mixer[...] = few_rows(halves(grad_residual), halves(out_buf[...]), 1)

    by_column = pl.BlockSpec((inner, TILE), lambda step: (0, step))
    return fused(
        dict(
            normed_two=(normed_two, WHOLE),
            residual=(residual, WHOLE),
            cotangent=(cotangent, WHOLE),
            grad_hidden=(
                grad_hidden,
                pl.BlockSpec((rows, TILE), lambda step: (lax.axis_index("seq"), step)),
            ),
            w_gate=(w_gate, by_column),
            w_up=(w_up, by_column),
            w_down=(w_down, pl.BlockSpec((TILE, inner), lambda step: (step, 0))),
            out_weight=(out_weight, ANY),
            second_gain=(second_gain[None], WHOLE),
        ),
        dict(
            all_normed_two=Gather.results([normed_two])[0],
            ffn=((rows, inner), WHOLE),
            grad_residual=((rows, inner), WHOLE),
            grad_mixer=((rows, out_weight.shape[0]), WHOLE),
            second=((8, inner), WHOLE),
        ),
        dict(
            gather=Gather.scratch([normed_two]),
            sum=[
                pltpu.VMEM((rows, inner), F32),
                pltpu.VMEM((rows, inner), F32),
                *Sum.scratch([normed_two]),
            ],
            out=[pltpu.VMEM(out_weight.shape, F32), pltpu.SemaphoreType.DMA((1,))],
        ),
        tiles,
        body,
        collective_id,
        flops=30 * rows * inner * columns,
    )


def tile_strips(refs, step, first_step, pause):
    high_ref, low_ref, stage_ref, stage_sem, cols_high_ref, cols_low_ref = refs.halves
    grads = refs.grad_gate, refs.grad_up, refs.grad_down

    @pl.when(step == first_step)
    def _():
        load_halves(refs.all_normed_two, high_ref, low_ref, stage_ref, stage_sem)
        cols_high_ref[...], cols_low_ref[...] = halves(jnp.transpose(refs.normed_cols[...]))

    gate_weight, up_weight = halves(refs.w_gate[...]), halves(refs.w_up[...])
    for grad_ref in grads:
        grad_ref[...] = jnp.zeros_like(grad_ref)

    def strip(index, spot):
        normed = high_ref[spot, :], low_ref[spot, :]
        a = three_pass(normed, gate_weight, 1, 0)
        b = three_pass(normed, up_weight, 1, 0)
        gate = jax.nn.sigmoid(a)
        silu_a = a * gate
        e = refs.grad_hidden[spot, :]
        cols = cols_high_ref[:, spot], cols_low_ref[:, spot]
        grads[0][...] += three_pass(cols, halves(e * b * (gate * (1.0 + a * (1.0 - gate)))), 1, 0)
        grads[1][...] += three_pass(cols, halves(e * silu_a), 1, 0)
        grads[2][...] += three_pass(
            halves(jnp.transpose(silu_a * b)), halves(refs.cot_cols[spot, :]), 1, 0
        )
        pause(index)

    strips(refs.all_normed_two.shape[0], strip)


def tile_parts(all_normed_two, all_cotangent, grad_hidden, w_gate, w_up, first, count, tile_of):
    rows, inner = all_normed_two.shape
    narrow = inner // (Z * X)
    columns = min(count * TILE, w_gate.shape[1] - first * TILE)
    own_columns = pl.BlockSpec((rows, narrow), lambda step: (0, lax.axis_index("seq")))
    by_column = pl.BlockSpec((inner, TILE), lambda step: (0, first + tile_of(step)))
    grad_spec = pl.BlockSpec((narrow, TILE), lambda step: (0, tile_of(step)))
    arrays = dict(
        all_normed_two=(all_normed_two, ANY),
        grad_hidden=(
            grad_hidden, pl.BlockSpec((rows, TILE), lambda step: (0, first + tile_of(step)))
        ),
        w_gate=(w_gate, by_column),
        w_up=(w_up, by_column),
        normed_cols=(all_normed_two, own_columns),
        cot_cols=(all_cotangent, own_columns),
    )
    results = dict(
        grad_gate=((narrow, columns), grad_spec),
        grad_up=((narrow, columns), grad_spec),
        grad_down=(
            (columns, narrow), pl.BlockSpec((TILE, narrow), lambda step: (tile_of(step), 0))
        ),
    )
    scratch = dict(
        halves=[
            *halves_scratch(rows, inner),
            pltpu.VMEM((narrow, rows), BF16),
            pltpu.VMEM((narrow, rows), BF16),
        ]
    )
    return arrays, results, scratch


def heads_kernel(grad_mixer, ffn, tiles, count, collective_id):
    arrays, results, scratch = tiles(lambda step: step)
    parts = arrays["all_normed_two"][0].shape[0] // STRIP

    def body(refs, step):
        heads = Heads([refs.grad_mixer], [refs.all_grad_mixer], refs.heads)
        scatter = Scatter([refs.ffn], [refs.ffn_share], refs.scatter)

        @pl.when(step == 0)
        def _():
            heads.begin()
            scatter.begin()

        def pause(part):
            now = step * parts + part
            schedule(now, (0, 2, 4, 6), heads.events())
            schedule(now, (1, 5), scatter.events())

        tile_strips(refs, step, 0, pause)

    return fused(
        dict(grad_mixer=(grad_mixer, ANY), ffn=(ffn, WHOLE), **arrays),
        dict(
            all_grad_mixer=Heads.results([grad_mixer])[0],
            ffn_share=Scatter.results([ffn])[0],
            **results,
        ),
        dict(heads=Heads.scratch([grad_mixer]), scatter=Scatter.scratch([ffn]), **scratch),
        count,
        body,
        collective_id,
    )


def last_kernel(grads, group, blocks, first_part, in_weights, tiles, count, collective_id):
    arrays, results, scratch = tiles(
        lambda step: jnp.where(step == 0, 0, jnp.maximum(step - len(in_weights), 0))
    )
    rows, columns = grads.shape
    own_rows = rows // (Z * X)
    inner = in_weights[0].shape[0]
    width = in_weights[0].shape[1]
    half = width // X
    matrices = len(in_weights)
    parts = rows // STRIP
    part_like = jax.ShapeDtypeStruct((own_rows, inner), F32)
    swapped = [jax.ShapeDtypeStruct((own_rows, columns), F32), group]

    def body(refs, step):
        place = lax.axis_index("seq")
        x = place % X
        peer = pl.multiple_of((place + 1 - 2 * x) * own_rows, own_rows)
        other_ref, *swap_scratch = refs.swap
        part_ref, *scatter_scratch = refs.scatter
        weight_buf, weight_sem = refs.weights
        swap = SwapX(
            [refs.grads.at[pl.ds(peer, own_rows), :], refs.group],
            [other_ref, refs.other_group],
            swap_scratch,
        )
        blocks_here = SwapBlocks(
            [refs[f"block_{index}"] for index in range(len(blocks))],
            [refs[f"swapped_{index}"] for index in range(len(blocks))],
            refs.blocks,
        )
        scatter = Scatter([part_ref], [refs.share], scatter_scratch)
        sums = SumAll([refs.first_part], [refs.first_sum], refs.sums)

        def fetch(index):
            return block_fetch(refs[f"weight_{index}"], weight_buf, weight_sem, index % 2)

        @pl.when(step == 0)
        def _():
            swap.begin()
            sums.begin()
            part_ref[...] = jnp.zeros_like(part_ref)

        def pause(part):
            now = step * parts + part
            schedule(now, (0, 1, 2), sums.events())
            schedule(now, (4 * matrices + 4, 4 * matrices + 7), scatter.events())

        @pl.when((step == 0) | (step > matrices))
        def _():
            tile_strips(refs, step, 0, pause)

        for index in range(matrices):

            @pl.when(step == index)
            def _(index=index):
                fetch(index).start()

            @pl.when(step == index + 1)
            def _(index=index):
                if index == 0:
                    swap.finish()
                    blocks_here.begin()
                fetch(index).wait()
                weight = halves(weight_buf[index % 2])
                own = refs.own_grads[:, index * half : (index + 1) * half]
                other = other_ref[:, index * half : (index + 1) * half]
                low_x, high_x = (jnp.where(x == place_x, own, other) for place_x in range(X))
                part_ref[...] += few_rows(halves(jnp.concatenate([low_x, high_x], 1)), weight, 1)
                if index == matrices - 1:
                    scatter.begin()

        pl.when(step == matrices + count - 1)(blocks_here.finish)

    return fused(
        dict(
            grads=(grads, ANY),
            own_grads=(
                grads, pl.BlockSpec((own_rows, columns), lambda step: (lax.axis_index("seq"), 0))
            ),
            group=(group, ANY),
            first_part=(first_part, WHOLE),
            **{f"block_{index}": (block, ANY) for index, block in enumerate(blocks)},
            **{f"weight_{index}": (weight, ANY) for index, weight in enumerate(in_weights)},
            **arrays,
        ),
        dict(
            other_group=(group.shape, ANY),
            share=Scatter.results([part_like])[0],
            first_sum=SumAll.results([first_part])[0],
            **{
                f"swapped_{index}": result for index, result in enumerate(SwapBlocks.results(blocks))
            },
            **results,
        ),
        dict(
            swap=[pltpu.VMEM((own_rows, columns), F32), *SwapX.scratch(swapped)],
            scatter=[pltpu.VMEM((own_rows, inner), F32), *Scatter.scratch([part_like])],
            blocks=SwapBlocks.scratch(blocks),
            sums=SumAll.scratch([first_part]),
            weights=[pltpu.VMEM((2, inner, width), F32), pltpu.SemaphoreType.DMA((2,))],
            **scratch,
        ),
        count + matrices,
        body,
        collective_id,
    )


def thin(left, right, contract_left, contract_right):
    (left_high, left_low), (right_high, right_low) = left, right
    return product(
        jnp.concatenate([left_high, left_low], contract_left),
        jnp.concatenate([right_high, right_high], contract_right),
        contract_left,
        contract_right,
    ) + product(left_high, right_low, contract_left, contract_right)


def join(first, second, axis):
    return tuple(jnp.concatenate(pair, axis) for pair in zip(first, second, strict=True))


def running_sum(triangle, entries):
    high, low = halves(entries)
    least = (entries - high.astype(F32) - low.astype(F32)).astype(BF16)
    return product(
        jnp.concatenate([triangle, triangle], 1), jnp.concatenate([high, low], 0), 1, 0
    ) + product(triangle, least, 1, 0)


def chunk_masks(lengths_ref, chunk):
    shape = (CHUNK, CHUNK)
    row = lax.broadcasted_iota(jnp.int32, shape, 0)
    column = lax.broadcasted_iota(jnp.int32, shape, 1)
    start = chunk * CHUNK

    offsets = [0]
    for index in range(lengths_ref.shape[0] - 1):
        offsets.append(offsets[-1] + lengths_ref[index])

    def segment(position):
        return sum(jnp.where(position >= offset, 1, 0) for offset in offsets)

    segment_row = segment(start + row)
    before, last = segment(start - 1), segment(start + CHUNK - 1)
    allowed = (row >= column) & (segment_row == segment(start + column))
    carry = (segment_row == before).astype(F32)
    in_last = (segment_row == last).astype(F32)
    lower = (row >= column).astype(F32).astype(BF16)
    return allowed, carry, in_last, (last == before).astype(F32), lower


def head_terms(pre_query, pre_forget, lower_bound, lower):
    query_gate = jax.nn.sigmoid(pre_query)
    forget_gate = jax.nn.sigmoid(-pre_forget)
    keys = (1.0 - lower_bound) * forget_gate
    log_decay = running_sum(lower, jnp.log1p(-keys))
    last = log_decay[CHUNK - 1 :, :]
    growth, shrink, trail = jnp.exp(log_decay), jnp.exp(-log_decay), jnp.exp(last - log_decay)
    return query_gate, forget_gate, keys, last, growth, shrink, trail


def tall(row):
    return jnp.transpose(jnp.broadcast_to(row, (HDIM, HDIM)))


def forward_chunk(
    chunk, lengths_ref, projected_ref, bound_ref, gain_ref, mixer_ref, raw_ref, states_ref, state_ref
):
    heads = state_ref.shape[0]
    width = heads * HDIM
    allowed, carry, in_last, carry_last, lower = chunk_masks(lengths_ref, chunk)
    for head in range(heads):
        at = slice(head * HDIM, (head + 1) * HDIM)
        pre_query, pre_forget, values, gate_in = (
            projected_ref[:, part * width + head * HDIM : part * width + (head + 1) * HDIM]
            for part in range(4)
        )
        query_gate, _, keys, last, growth, shrink, trail = head_terms(
            pre_query, pre_forget, bound_ref[:, at], lower
        )
        grown = pre_query * query_gate * growth
        state = state_ref[head]
        states_ref[0, head] = state
        value_halves = halves(values)
        scores = thin(halves(grown), halves(keys * shrink), 1, 1)
        scores = jnp.where(allowed, scores, 0.0)
        raw = three_pass(
            join(halves(scores), halves(grown * carry), 1),
            join(value_halves, halves(state), 0),
            1,
            0,
        )
        state_ref[head] = state * (tall(jnp.exp(last)) * carry_last) + thin(
            halves(keys * trail * in_last), value_halves, 0, 0
        )
        raw_ref[:, at] = raw
        scale = lax.rsqrt(jnp.mean(raw * raw, -1, keepdims=True) + group_eps)
        mixer_ref[:, at] = raw * scale * gain_ref[:, at] * jax.nn.silu(gate_in)


def backward_kernel(
    projected, raw_rows, states, grad_mixer, normed_cols, grad_residual, second, weights,
    lower_bound, group_gain, lengths, collective_id,
):
    rows, columns = projected.shape
    count = len(weights)
    width = columns // count
    heads = width // HDIM
    chunks = rows // CHUNK
    wide = normed_cols.shape[1]

    def body(refs, step):
        lengths_ref, projected_ref, raw_ref, states_ref = refs.lengths, refs.projected, refs.raw, refs.states
        grad_ref, grads_ref, group_ref = refs.grad_mixer, refs.grads, refs.group
        later_ref, weight_buf, weight_sem = refs.work
        chunk = chunks - 1 - step
        place = lax.axis_index("seq")
        here = pl.ds(pl.multiple_of((place % X) * width, width), width)
        bound_ref, gain_ref = refs.lower_bound.at[:, here], refs.group_gain.at[:, here]
        block_refs = [refs[f"block_{index}"] for index in range(count)]
        move = Columns([refs.grad_residual], [refs.residual_cols], refs.columns)
        small = Columns([refs.second], [refs.second_cols], refs.small)

        def fetch(index):
            return block_fetch(
                refs[f"weight_{index}"].at[
                    pl.ds(pl.multiple_of((place // X) * wide, wide), wide), here
                ],
                weight_buf,
                weight_sem,
                index,
            )

        @pl.when(step == 0)
        def _():
            move.begin()
            small.begin()
            later_ref[...] = jnp.zeros_like(later_ref)
            group_ref[...] = jnp.zeros_like(group_ref)
            for index in range(count):
                fetch(index).start()
                block_refs[index][...] = jnp.zeros_like(block_refs[index])

        allowed, carry, in_last, carry_last, lower = chunk_masks(lengths_ref, chunk)
        upper = jnp.transpose(lower.astype(F32)).astype(BF16)
        for head in range(heads):
            at = slice(head * HDIM, (head + 1) * HDIM)
            spots = [
                slice(part * width + head * HDIM, part * width + (head + 1) * HDIM)
                for part in range(4)
            ]
            pre_query, pre_forget, values, gate_in = (projected_ref[:, spot] for spot in spots)
            raw, grad, gain = raw_ref[:, at], grad_ref[:, at], gain_ref[:, at]
            state, later = states_ref[0, head], later_ref[head]

            scale = lax.rsqrt(jnp.mean(raw * raw, -1, keepdims=True) + group_eps)
            normed = raw * scale
            gate = jax.nn.sigmoid(gate_in)
            silu_gate = gate_in * gate
            weighted = grad * gain * silu_gate
            group_ref[:, at] += jnp.sum(grad * normed * silu_gate, 0, keepdims=True)
            grads_ref[:, spots[3]] = (
                grad * gain * normed * (gate * (1.0 + gate_in * (1.0 - gate)))
            )
            grad_raw = scale * weighted - raw * (
                scale * scale * scale * jnp.mean(weighted * raw, -1, keepdims=True)
            )

            query_gate, forget_gate, keys, last, growth, shrink, trail = head_terms(
                pre_query, pre_forget, bound_ref[:, at], lower
            )
            grown = pre_query * query_gate * growth
            shrunk = keys * shrink
            trailing = trail * in_last
            ends = keys * trailing
            grown_halves, shrunk_halves = halves(grown), halves(shrunk)
            raw_halves, value_halves, later_halves = halves(grad_raw), halves(values), halves(later)
            scores = jnp.where(allowed, thin(grown_halves, shrunk_halves, 1, 1), 0.0)
            grad_scores = jnp.where(allowed, thin(raw_halves, value_halves, 1, 1), 0.0)
            score_halves = halves(grad_scores)
            grads_ref[:, spots[2]] = three_pass(
                join(halves(jnp.transpose(scores)), halves(ends), 1),
                join(raw_halves, later_halves, 0),
                1,
                0,
            )
            grad_grown = three_pass(
                join(score_halves, halves(grad_raw * carry), 1),
                join(shrunk_halves, halves(jnp.transpose(state)), 0),
                1,
                0,
            )
            grad_shrunk = thin(score_halves, grown_halves, 0, 0)
            grad_ends = thin(value_halves, later_halves, 1, 1)
            through = tall(jnp.exp(last)) * carry_last
            later_ref[head] = later * through + thin(
                halves(grown * carry), raw_halves, 0, 0
            )
            grads_ref[:, spots[0]] = (
                grad_grown * growth * (query_gate * (1.0 + pre_query * (1.0 - query_gate)))
            )
            from_ends = grad_ends * ends
            grad_log = grad_grown * grown - grad_shrunk * shrunk - from_ends
            pulled = jnp.transpose(later * state * through)
            grad_last = jnp.sum(from_ends + pulled, 0, keepdims=True)
            grad_log_forget = running_sum(upper, grad_log) + grad_last
            grad_keys = (
                grad_shrunk * shrink + grad_ends * trailing - grad_log_forget / (1.0 - keys)
            )
            grads_ref[:, spots[1]] = -grad_keys * keys * (1.0 - forget_gate)

        cols = halves(jnp.transpose(refs.normed_cols[...]))
        for index in range(count):
            part = grads_ref[:, index * width : (index + 1) * width]
            block_refs[index][...] += thin(cols, halves(part), 1, 0)

        @pl.when(step == chunks - 1)
        def _():
            total = 0.0
            for index in range(count):
                fetch(index).wait()
                total = total + weight_buf[index] * block_refs[index][...]
            ones = jnp.ones((8, width), BF16)
            high, low = halves(total)
            refs.sums[...] = product(ones, high, 1, 1) + product(ones, low, 1, 1)

        schedule(step, (0, 2, 4, 6, 7, 7), move.events())
        schedule(step, (0, 2, 4, 6, 7, 7), small.events())

    def by_chunk(size):
        return pl.BlockSpec((CHUNK, size), lambda step: (chunks - 1 - step, 0))

    return fused(
        dict(
            lengths=(lengths, pl.BlockSpec(memory_space=pltpu.SMEM)),
            projected=(projected, by_chunk(columns)),
            raw=(raw_rows, by_chunk(width)),
            states=(
                states,
                pl.BlockSpec((1, heads, HDIM, HDIM), lambda step: (chunks - 1 - step, 0, 0, 0)),
            ),
            grad_mixer=(grad_mixer, by_chunk(width)),
            normed_cols=(normed_cols, by_chunk(wide)),
            lower_bound=(lower_bound[None], WHOLE),
            group_gain=(group_gain[None], WHOLE),
            grad_residual=(grad_residual, ANY),
            second=(second, ANY),
            **{f"weight_{index}": (weight, ANY) for index, weight in enumerate(weights)},
        ),
        dict(
            grads=((rows, columns), by_chunk(columns)),
            group=((1, width), WHOLE),
            sums=((8, wide), WHOLE),
            residual_cols=Columns.results([grad_residual])[0],
            second_cols=Columns.results([second])[0],
            **{f"block_{index}": ((wide, width), WHOLE) for index in range(count)},
        ),
        dict(
            work=[
                pltpu.VMEM((heads, HDIM, HDIM), F32),
                pltpu.VMEM((count, wide, width), F32),
                pltpu.SemaphoreType.DMA((count,)),
            ],
            columns=Columns.scratch([grad_residual]),
            small=Columns.scratch([second]),
        ),
        chunks,
        body,
        collective_id,
        far=True,
        flops=60 * rows * HDIM * width + 6 * rows * wide * columns,
    )


def fast_shards(
    tokens_in,
    cotangent,
    lengths,
    lower_bound,
    query_weight,
    forget_weight,
    input_weight,
    gate_weight,
    out_weight,
    swiglu_gate,
    swiglu_up,
    swiglu_down,
    first_gain,
    group_gain,
    second_gain,
):
    place = lax.axis_index("seq")
    z, x = place // X, place % X
    rows, model = tokens_in.shape
    wide = model // Z
    narrow = model // (Z * X)
    width = query_weight.shape[1] // X
    share_rows = rows // 4
    token_count = rows * Z * X

    def share(entries):
        return cut(entries, lax.axis_index("mp"), share_rows, 0)

    in_weights = (query_weight, forget_weight, input_weight, gate_weight)
    all_tokens = gather_tokens_fast(tokens_in, 1)
    mixed = mixer_kernel(
        all_tokens,
        tokens_in,
        cotangent,
        lengths,
        lower_bound,
        in_weights,
        out_weight,
        swiglu_down,
        first_gain,
        group_gain,
        second_gain,
        2,
    )
    fed = feed_forward_kernel(
        mixed.normed_two,
        mixed.residual,
        cotangent,
        mixed.grad_hidden,
        swiglu_gate,
        swiglu_up,
        swiglu_down,
        out_weight,
        second_gain,
        3,
    )
    grad_residual = fed.grad_residual

    def tiles(first, count):
        return partial(
            tile_parts,
            fed.all_normed_two,
            mixed.all_cotangent,
            mixed.grad_hidden,
            swiglu_gate,
            swiglu_up,
            first,
            count,
        )

    split = 3
    left = pl.cdiv(swiglu_gate.shape[1], TILE) - split
    sent = heads_kernel(fed.grad_mixer, fed.ffn, tiles(0, split), split, 4)
    output = share(mixed.residual) + sent.ffn_share
    back = backward_kernel(
        mixed.projected,
        mixed.raw,
        mixed.states,
        sent.all_grad_mixer,
        mixed.normed_cols,
        grad_residual,
        fed.second,
        in_weights,
        lower_bound,
        group_gain,
        lengths,
        5,
    )
    second_cols = jnp.sum(back.second_cols[:, :, 0], (0, 1))
    out_block = dot(back.residual_cols.reshape(token_count, wide), mixed.mixer, 0, 0)
    last = last_kernel(
        back.grads,
        jnp.broadcast_to(back.group, (8, width)),
        [*(back[f"block_{index}"] for index in range(4)), out_block],
        jnp.concatenate([back.sums[:, :narrow], back.sums[:, narrow:]]),
        in_weights,
        tiles(split, left),
        left,
        6,
    )
    grad_group = in_order(x == 0, back.group[0], last.other_group[0], 0)
    *weight_grads, grad_outw = (
        jnp.concatenate([last[f"swapped_{index}"][0], last[f"swapped_{index}"][1]], 1)
        for index in range(5)
    )
    grad_normed_one, first_sum = last.share, last.first_sum
    grad_sgate, grad_sup, grad_sdown = (
        jnp.concatenate([sent[name], last[name]], axis)
        for name, axis in (("grad_gate", 1), ("grad_up", 1), ("grad_down", 0))
    )
    tokens_share = share(tokens_in)
    scale_one = rms(tokens_share)
    pulled_one = grad_normed_one * first_gain
    grad_tokens = (
        share(grad_residual)
        + scale_one * pulled_one
        - tokens_share * scale_one**3 * jnp.mean(pulled_one * tokens_share, -1, keepdims=True)
    )
    return (
        output,
        grad_tokens,
        *weight_grads,
        jnp.transpose(grad_outw),
        grad_sgate,
        grad_sup,
        grad_sdown,
        first_sum[0] / cut(first_gain, place, narrow, 0),
        cut(grad_group, place, group_gain.shape[0] // (Z * X), 0),
        cut(second_cols, x, narrow, 0),
    )


def solution(mesh):
    in_specs = (
        P("seq", None),
        P("seq", None),
        P(),
        P("mp"),
        P(None, "mp"),
        P(None, "mp"),
        P(None, "mp"),
        P(None, "mp"),
        P("mp", None),
        P(None, "mp"),
        P(None, "mp"),
        P("mp", None),
        P(),
        P("mp"),
        P(),
    )
    out_specs = (
        P(("seq", "mp"), None),
        P(("seq", "mp"), None),
        P("seq", "mp"),
        P("seq", "mp"),
        P("seq", "mp"),
        P("seq", "mp"),
        P("mp", "seq"),
        P("seq", "mp"),
        P("seq", "mp"),
        P("mp", "seq"),
        P("seq"),
        P(("mp", "seq")),
        P("seq"),
    )
    small = (mesh.shape["seq"], mesh.shape["mp"]) == (Z * X, 4)
    body = fast_shards if small else shards
    return jax.shard_map(body, mesh=mesh, in_specs=in_specs, out_specs=out_specs, check_vma=False)
```

```python
from functools import partial

import jax
import jax.numpy as jnp
from jax import lax
from jax.experimental import pallas as pl
from jax.experimental.pallas import tpu as pltpu
from jax.sharding import PartitionSpec as P

HDIM = 128
CHUNK = 128
HIGH = lax.Precision.HIGH
HIGHEST = lax.Precision.HIGHEST
norm_eps = 1e-06
group_eps = 1e-05


def dot(left, right, contract_left, contract_right, precision=HIGH):
    return lax.dot_general(
        left,
        right,
        (((contract_left,), (contract_right,)), ((), ())),
        precision=precision,
        preferred_element_type=jnp.float32,
    )


def rms(entries):
    return lax.rsqrt(jnp.mean(entries * entries, -1, keepdims=True) + norm_eps)


def silu_grad(entries):
    gate = jax.nn.sigmoid(entries)
    return gate * (1.0 + entries * (1.0 - gate))


def gather_tokens(block):
    return lax.all_gather(block, "seq", axis=0, tiled=True)


def recurrence(query_rows, key_vecs, value_rows, segment):
    token_count, width = query_rows.shape
    heads = width // HDIM
    chunks = token_count // CHUNK

    def split(entries):
        return entries.reshape(chunks, CHUNK, heads, HDIM)

    blocked = segment.reshape(chunks, CHUNK)
    last_seg = blocked[:, -1]
    first_segs = jnp.concatenate([jnp.full((1,), -1, segment.dtype), last_seg[:-1]])
    carry = (blocked == first_segs[:, None]).astype(jnp.float32)
    in_last = (blocked == last_seg[:, None]).astype(jnp.float32)
    places = jnp.arange(CHUNK)
    allowed = (places[None, :, None] >= places[None, None, :]) & (
        blocked[:, :, None] == blocked[:, None, :]
    )
    lower = (places[:, None] >= places[None, :]).astype(jnp.float32)
    queries, keys, values = split(query_rows), split(key_vecs), split(value_rows)
    log_decay = jnp.einsum("ts,cshk->cthk", lower, jnp.log1p(-keys), precision=HIGHEST)
    growth = jnp.exp(log_decay)
    grown = queries * growth
    last = log_decay[:, -1]
    scores = jnp.einsum("cthk,cshk->chts", grown, keys * jnp.exp(-log_decay), precision=HIGH)
    scores = jnp.where(allowed[:, None], scores, 0.0)
    inner = jnp.einsum("chts,cshv->cthv", scores, values, precision=HIGH)
    weighted = keys * jnp.exp(last[:, None] - log_decay) * in_last[:, :, None, None]
    updates = jnp.einsum("cshk,cshv->chkv", weighted, values, precision=HIGH)
    through = jnp.exp(last) * carry[:, -1][:, None, None]
    state = jnp.zeros_like(updates[0])
    states = []
    for chunk in range(chunks):
        states.append(state)
        state = state * through[chunk][:, :, None] + updates[chunk]
    outer = jnp.einsum(
        "cthk,chkv->cthv", grown * carry[:, :, None, None], jnp.stack(states), precision=HIGH
    )
    return (inner + outer).reshape(token_count, width)


def mixer_all(pre_query, pre_forget, value_rows, gate_in, group_gain, lower_bound, segment):
    key_vecs = (1.0 - lower_bound) * jax.nn.sigmoid(-pre_forget)
    raw = recurrence(jax.nn.silu(pre_query), key_vecs, value_rows, segment)
    heads = raw.reshape(raw.shape[0], -1, HDIM)
    scale = lax.rsqrt(jnp.mean(heads * heads, -1, keepdims=True) + group_eps)
    normed = (heads * scale).reshape(raw.shape)
    return normed * group_gain * jax.nn.silu(gate_in)


def shards(
    tokens_in,
    cotangent,
    lengths,
    lower_bound,
    query_weight,
    forget_weight,
    input_weight,
    gate_weight,
    out_weight,
    swiglu_gate,
    swiglu_up,
    swiglu_down,
    first_gain,
    group_gain,
    second_gain,
):
    seq_count = lax.axis_size("seq")
    seq_place = lax.axis_index("seq")
    own_rows, model = tokens_in.shape
    token_count = own_rows * seq_count
    share_rows = own_rows // lax.axis_size("mp")
    share_start = lax.axis_index("mp") * share_rows
    start_row = seq_place * own_rows
    own_cols = model // seq_count
    start_col = seq_place * own_cols

    def own(entries):
        return lax.dynamic_slice_in_dim(entries, start_row, own_rows, 0)

    def columns(entries):
        return lax.dynamic_slice_in_dim(entries, start_col, own_cols, 1)

    def share(entries):
        return lax.dynamic_slice_in_dim(entries, share_start, share_rows, 0)

    positions = jnp.arange(token_count, dtype=jnp.int32)
    offsets = jnp.cumsum(lengths) - lengths
    segment = jnp.sum((positions[:, None] >= offsets[None, :]).astype(jnp.int32), 1) - 1

    all_tokens = gather_tokens(tokens_in)
    all_cotangent = gather_tokens(cotangent)
    normed_one = all_tokens * rms(all_tokens) * first_gain
    pre_query = dot(normed_one, query_weight, 1, 0)
    pre_forget = dot(normed_one, forget_weight, 1, 0)
    value_rows = dot(normed_one, input_weight, 1, 0)
    gate_in = dot(normed_one, gate_weight, 1, 0)
    mixer, mixer_back = jax.vjp(
        partial(mixer_all, lower_bound=lower_bound, segment=segment),
        pre_query,
        pre_forget,
        value_rows,
        gate_in,
        group_gain,
    )
    residual = tokens_in + lax.psum(dot(own(mixer), out_weight, 1, 0), "mp")
    scale_two = rms(residual)
    normed_two = residual * scale_two * second_gain
    grad_hidden_all = dot(all_cotangent, swiglu_down, 1, 1)
    a = dot(normed_two, swiglu_gate, 1, 0)
    b = dot(normed_two, swiglu_up, 1, 0)
    silu_a = jax.nn.silu(a)
    ffn_part = dot(silu_a * b, swiglu_down, 1, 0)
    output = share(residual) + lax.psum_scatter(ffn_part, "mp", scatter_dimension=0, tiled=True)
    e = own(grad_hidden_all)
    grad_a = e * b * silu_grad(a)
    grad_b = e * silu_a
    grad_normed_two = lax.psum(
        dot(grad_a, swiglu_gate, 1, 1) + dot(grad_b, swiglu_up, 1, 1), "mp"
    )
    pulled = grad_normed_two * second_gain
    grad_residual = (
        cotangent
        + scale_two * pulled
        - residual * scale_two**3 * jnp.mean(pulled * residual, -1, keepdims=True)
    )
    all_normed_two = gather_tokens(normed_two)
    a_all = dot(all_normed_two, swiglu_gate, 1, 0)
    b_all = dot(all_normed_two, swiglu_up, 1, 0)
    silu_all = jax.nn.silu(a_all)
    hidden_all = silu_all * b_all
    grad_a_all = grad_hidden_all * b_all * silu_grad(a_all)
    grad_b_all = grad_hidden_all * silu_all
    normed_two_cols = columns(all_normed_two)
    grad_sgate = dot(normed_two_cols, grad_a_all, 0, 0)
    grad_sup = dot(normed_two_cols, grad_b_all, 0, 0)
    grad_sdown = dot(hidden_all, columns(all_cotangent), 0, 0)

    grad_mixer = gather_tokens(dot(grad_residual, out_weight, 1, 1))
    residual_cols = lax.all_to_all(grad_residual, "seq", 1, 0, tiled=True)
    grad_outw = dot(mixer, residual_cols, 0, 0)
    grad_query_rows, grad_forget_rows, grad_value_rows, grad_gate_rows, grad_group = mixer_back(
        grad_mixer
    )
    grad_group = lax.dynamic_slice_in_dim(
        grad_group, seq_place * (group_gain.shape[0] // seq_count), group_gain.shape[0] // seq_count
    )
    normed_one_cols = columns(normed_one)
    pairs = (
        (grad_query_rows, query_weight),
        (grad_forget_rows, forget_weight),
        (grad_value_rows, input_weight),
        (grad_gate_rows, gate_weight),
    )
    weight_grads = []
    normed_part = 0.0
    first_sum = 0.0
    for grad_rows, weight in pairs:
        weight_grad = dot(normed_one_cols, grad_rows, 0, 0)
        weight_grads.append(weight_grad)
        normed_part = normed_part + dot(own(grad_rows), weight, 1, 1)
        own_weight = lax.dynamic_slice_in_dim(weight, start_col, own_cols, 0)
        first_sum = first_sum + jnp.sum(own_weight * weight_grad, 1)
    second_sum = jnp.sum(
        lax.dynamic_slice_in_dim(swiglu_gate, start_col, own_cols, 0) * grad_sgate
        + lax.dynamic_slice_in_dim(swiglu_up, start_col, own_cols, 0) * grad_sup,
        1,
    )
    gains = jnp.stack(
        [
            lax.dynamic_slice_in_dim(first_gain, start_col, own_cols),
            lax.dynamic_slice_in_dim(second_gain, start_col, own_cols),
        ]
    )
    gain_grads = lax.psum(jnp.stack([first_sum, second_sum]), "mp") / gains
    grad_normed_one = lax.psum_scatter(normed_part, "mp", scatter_dimension=0, tiled=True)
    tokens_share = share(tokens_in)
    scale_one = rms(tokens_share)
    pulled_one = grad_normed_one * first_gain
    grad_tokens = (
        share(grad_residual)
        + scale_one * pulled_one
        - tokens_share * scale_one**3 * jnp.mean(pulled_one * tokens_share, -1, keepdims=True)
    )
    return (
        output,
        grad_tokens,
        weight_grads[0],
        weight_grads[1],
        weight_grads[2],
        weight_grads[3],
        grad_outw,
        grad_sgate,
        grad_sup,
        grad_sdown,
        gain_grads[0],
        grad_group,
        gain_grads[1],
    )


Z, X = 4, 2


def x_swap(array):
    return lax.ppermute(array, "seq", [(s, s ^ 1) for s in range(Z * X)])


def cut(array, place, size, axis):
    return lax.dynamic_slice_in_dim(array, place * size, size, axis)


def in_order(first, mine, other, axis):
    return jnp.where(
        first, jnp.concatenate([mine, other], axis), jnp.concatenate([other, mine], axis)
    )


F32, BF16 = jnp.float32, jnp.bfloat16
MESH = pl.DeviceIdType.MESH
ANY = pl.BlockSpec(memory_space=pl.ANY)
WHOLE = pl.BlockSpec(memory_space=pltpu.VMEM)
TILE = 256
VMEM_BYTES = 60 << 20


def halves(entries):
    high = entries.astype(BF16)
    return high, (entries - high.astype(F32)).astype(BF16)


def product(left, right, contract_left, contract_right):
    return lax.dot_general(
        left,
        right,
        (((contract_left,), (contract_right,)), ((), ())),
        preferred_element_type=F32,
    )


def three_pass(left, right, contract_left, contract_right):
    (left_high, left_low), (right_high, right_low) = left, right
    return product(left_high, right_high, contract_left, contract_right) + (
        product(left_high, right_low, contract_left, contract_right)
        + product(left_low, right_high, contract_left, contract_right)
    )


def few_rows(left, right, contract_right):
    (left_high, left_low), (right_high, right_low) = left, right
    rows = left_high.shape[0]
    both = product(jnp.concatenate([left_high, left_low]), right_high, 1, contract_right)
    return both[:rows] + (product(left_high, right_low, 1, contract_right) + both[rows:])


def remote(src, dst, sems, index, device):
    return pltpu.make_async_remote_copy(
        src_ref=src,
        dst_ref=dst,
        send_sem=sems[0].at[index],
        recv_sem=sems[1].at[index],
        device_id=device,
        device_id_type=MESH,
    )


def dma_sems(count):
    return [pltpu.SemaphoreType.DMA((count,)), pltpu.SemaphoreType.DMA((count,))]


class Move:
    def __init__(self, ins, outs, scratch):
        self.ins, self.outs, self.scratch_refs = ins, outs, scratch
        place, part = lax.axis_index("seq"), lax.axis_index("mp")
        self.z, self.x, self.y, self.core = place // X, place % X, part // 2, part % 2
        self.setup()

    def setup(self):
        pass

    def device(self, z, x, y, core):
        return (z * X + x, y * 2 + core)

    def x_peer(self):
        return self.device(self.z, 1 - self.x, self.y, self.core)

    def y_peer(self):
        return self.device(self.z, self.x, 1 - self.y, self.core)

    def core_peer(self):
        return self.device(self.z, self.x, self.y, 1 - self.core)

    def holds(self, way, step):
        source = self.z - way * step
        return (source >= 0) & (source < Z)

    def goes_on(self, way, step):
        return self.holds(way, step - 1) & (self.z + way >= 0) & (self.z + way < Z)

    def each(self, step, action):
        if step == 0:
            action(1)
        else:
            for way in (1, -1):
                pl.when(self.holds(way, step))(lambda way=way: action(way))

    def greet(self, far):
        barrier = pltpu.get_barrier_semaphore()

        def signal(device):
            pl.semaphore_signal(barrier, inc=1, device_id=device, device_id_type=MESH)

        signal(self.x_peer())
        signal(self.y_peer())
        signal(self.core_peer())
        if far:
            for distance in range(1, Z):
                signal(self.device((self.z + distance) % Z, self.x, self.y, self.core))
            pl.semaphore_wait(barrier, 3 + Z - 1)
        else:
            for way in (1, -1):
                ahead = (self.z + way >= 0) & (self.z + way < Z)
                pl.when(ahead)(
                    lambda way=way: signal(self.device(self.z + way, self.x, self.y, self.core))
                )
            neighbours = jnp.where(self.z > 0, 1, 0) + jnp.where(self.z < Z - 1, 1, 0)
            pl.semaphore_wait(barrier, 3 + neighbours)


class Gather(Move):
    PIECES = 2
    OWN = 5

    def in_specs(arrays):
        return [ANY]

    def results(arrays):
        return [((Z * X * arrays[0].shape[0], arrays[0].shape[1]), ANY)]

    def scratch(arrays):
        return [*dma_sems(52 * Gather.PIECES), pltpu.SemaphoreType.DMA((1,))]

    def setup(self):
        (self.block,), (self.out,) = self.ins, self.outs
        self.sems, self.local = self.scratch_refs[:2], self.scratch_refs[2]
        self.rows = self.block.shape[0]
        self.size = self.rows // self.PIECES
        self.tile = self.block.shape[1] // 16

    def cols(self, first, count):
        return pl.ds(pl.multiple_of(first * self.tile, self.tile), count * self.tile)

    def columns(self, y, core):
        return self.cols((16 - 2 * self.OWN) * y + self.OWN * core, self.OWN)

    def y_count(self, big):
        most = min(16 - 2 * self.OWN, self.OWN)
        return most if big else 16 - 2 * self.OWN - most

    def y_columns(self, y, big):
        count = self.y_count(big)
        first = (16 - count) * y if big else self.OWN * (1 - y) + 2 * self.OWN * y
        return self.cols(first, count)

    def region(self, z, x, piece, columns):
        row = (z * X + x) * self.rows + piece * self.size
        return self.out.at[pl.ds(pl.multiple_of(row, self.size), self.size), columns]

    def fetched(self, z, x, piece):
        return self.region(z, x, piece, self.columns(self.y, self.core))

    def own(self, piece):
        return self.block.at[
            pl.ds(piece * self.size, self.size), self.columns(self.y, self.core)
        ]

    def slot(self, way, step):
        return 0 if step == 0 else (0 if way > 0 else 3) + step

    def along(self, way, step, piece, arriving):
        dst = self.fetched(self.z - way * (step if arriving else step - 1), self.x, piece)
        return remote(
            self.own(piece) if step == 1 and not arriving else dst,
            dst,
            self.sems,
            52 * piece + (0 if way > 0 else 3) + step - 1,
            self.device(self.z + way, self.x, self.y, self.core),
        )

    def across(self, way, step, piece, arriving):
        dst = self.fetched(self.z - way * step, 1 - self.x if arriving else self.x, piece)
        return remote(
            self.own(piece) if step == 0 and not arriving else dst,
            dst,
            self.sems,
            52 * piece + 6 + self.slot(way, step),
            self.x_peer(),
        )

    def inside(self, way, step, other_x, piece, arriving):
        region = self.region(
            self.z - way * step,
            1 - self.x if other_x else self.x,
            piece,
            self.columns(self.y, 1 - self.core if arriving else self.core),
        )
        index = 52 * piece + 13 + self.slot(way, step) + (0 if other_x else 6)
        return remote(region, region, self.sems, index, self.core_peer())

    def over_y(self, way, step, other_x, piece, arriving, big):
        region = self.region(
            self.z - way * step,
            1 - self.x if other_x else self.x,
            piece,
            self.y_columns(1 - self.y if arriving else self.y, big),
        )
        index = 52 * piece + 26 + self.slot(way, step) + (0 if other_x else 6)
        return remote(region, region, self.sems, index, self.y_peer())

    def inside_y(self, way, step, other_x, piece, big):
        region = self.region(
            self.z - way * step,
            1 - self.x if other_x else self.x,
            piece,
            self.y_columns(1 - self.y, big),
        )
        index = 52 * piece + 39 + self.slot(way, step) + (0 if other_x else 6)
        return remote(region, region, self.sems, index, self.core_peer())

    def sized(self, big, action):
        if self.y_count(True):
            pl.when(big)(lambda: action(True))
        if self.y_count(False):
            pl.when(jnp.logical_not(big))(lambda: action(False))

    def pass_on(self, way, step, other_x, piece):
        self.sized(
            self.core == self.y,
            lambda big: self.over_y(way, step, other_x, piece, False, big).start(),
        )
        self.inside(way, step, other_x, piece, False).start()

    def begin(self):
        for piece in range(self.PIECES):
            self.across(1, 0, piece, False).start()
            for way in (1, -1):
                pl.when(self.goes_on(way, 1))(
                    lambda way=way, piece=piece: self.along(way, 1, piece, False).start()
                )
        self.own_copy().start()

    def own_copy(self):
        row = pl.multiple_of((self.z * X + self.x) * self.rows, self.rows)
        return pltpu.make_async_copy(
            self.block, self.out.at[pl.ds(row, self.rows), :], self.local.at[0]
        )

    def arrive_along(self, step, piece):
        def action(way):
            self.along(way, step, piece, True).wait_recv()
            if step < Z - 1:
                pl.when(self.goes_on(way, step + 1))(
                    lambda: self.along(way, step + 1, piece, False).start()
                )
            self.across(way, step, piece, False).start()
            self.pass_on(way, step, False, piece)

        self.each(step, action)

    def arrive_across(self, step, piece):
        def action(way):
            self.across(way, step, piece, True).wait_recv()
            self.pass_on(way, step, True, piece)

        self.each(step, action)

    def arrive_y(self, step, other_x, piece):
        def action(way):
            def sized(big):
                self.over_y(way, step, other_x, piece, True, big).wait_recv()
                self.inside_y(way, step, other_x, piece, big).start()

            self.sized(self.core != self.y, sized)

        self.each(step, action)

    def finish(self):
        self.own_copy().wait()
        for piece in range(self.PIECES):
            for way in (1, -1):
                for step in range(1, Z):
                    pl.when(self.goes_on(way, step))(
                        lambda way=way, step=step, piece=piece: self.along(
                            way, step, piece, False
                        ).wait_send()
                    )
            for step in range(Z):

                def action(way, step=step, piece=piece):
                    self.across(way, step, piece, False).wait_send()
                    for other_x in (False, True) if step else (True,):
                        self.inside(way, step, other_x, piece, False).wait_send()
                        self.inside(way, step, other_x, piece, True).wait_recv()

                        def sent(big, other_x=other_x):
                            self.over_y(way, step, other_x, piece, False, big).wait_send()
                            self.inside_y(way, step, other_x, piece, big).wait_recv()

                        def handed(big, other_x=other_x):
                            self.inside_y(way, step, other_x, piece, big).wait_send()

                        self.sized(self.core == self.y, sent)
                        self.sized(self.core != self.y, handed)

                self.each(step, action)

    def events(self):
        def round_of(index):
            step, piece = index // 2 + 1, index % 2

            def event():
                if step < Z:
                    self.arrive_along(step, piece)
                if step <= Z:
                    self.arrive_across(step - 1, piece)
                if 1 <= step - 1 < Z:
                    self.arrive_y(step - 1, False, piece)
                if 0 <= step - 2 < Z:
                    self.arrive_y(step - 2, True, piece)

            return event

        return [round_of(index) for index in range(2 * (Z + 1))] + [self.finish]


class Gather12(Gather):
    OWN = 6


class Sum(Move):
    def in_specs(arrays):
        return [WHOLE]

    def results(arrays):
        return [(arrays[0].shape, WHOLE)]

    def scratch(arrays):
        rows, columns = arrays[0].shape
        return [pltpu.VMEM((4, rows, columns // 2), F32), *dma_sems(3)]

    def setup(self):
        (self.part,), (self.out,) = self.ins, self.outs
        self.landing, self.sems = self.scratch_refs[0], self.scratch_refs[1:]
        self.half = self.part.shape[1] // 2

    def columns(self, ref, core):
        return ref.at[:, pl.ds(pl.multiple_of(core * self.half, self.half), self.half)]

    def first(self):
        return remote(
            self.columns(self.part, 1 - self.core),
            self.landing.at[0],
            self.sems,
            0,
            self.core_peer(),
        )

    def second(self):
        return remote(self.landing.at[1], self.landing.at[2], self.sems, 1, self.y_peer())

    def third(self):
        return remote(self.landing.at[1], self.landing.at[3], self.sems, 2, self.core_peer())

    def begin(self):
        self.first().start()

    def to_y(self):
        self.first().wait()
        self.landing[1] = self.columns(self.part, self.core)[...] + self.landing[0]
        self.second().start()

    def back(self):
        self.second().wait()
        self.landing[1] = self.landing[1] + self.landing[2]
        self.third().start()

    def finish(self):
        self.third().wait()
        self.columns(self.out, self.core)[...] = self.landing[1]
        self.columns(self.out, 1 - self.core)[...] = self.landing[3]

    def events(self):
        return [self.to_y, self.back, self.finish]


class Scatter(Move):
    def in_specs(arrays):
        return [WHOLE]

    def results(arrays):
        rows, columns = arrays[0].shape
        return [((rows // 4, columns), WHOLE)]

    def scratch(arrays):
        rows, columns = arrays[0].shape
        return [pltpu.VMEM((5, rows // 4, columns), F32), *dma_sems(3)]

    def setup(self):
        (self.part,), (self.out,) = self.ins, self.outs
        self.landing, self.sems = self.scratch_refs[0], self.scratch_refs[1:]
        self.rows = self.part.shape[0] // 4

    def block(self, y, core):
        row = pl.multiple_of((y * 2 + core) * self.rows, self.rows)
        return self.part.at[pl.ds(row, self.rows), :]

    def to_core(self, y):
        block = self.block(self.y if y == 0 else 1 - self.y, 1 - self.core)
        return remote(block, self.landing.at[y], self.sems, y, self.core_peer())

    def to_y(self):
        return remote(self.landing.at[2], self.landing.at[3], self.sems, 2, self.y_peer())

    def begin(self):
        self.to_core(1).start()
        self.to_core(0).start()

    def middle(self):
        self.to_core(1).wait()
        self.landing[2] = self.block(1 - self.y, self.core)[...] + self.landing[1]
        self.to_y().start()

    def finish(self):
        self.to_core(0).wait()
        self.to_y().wait()
        self.out[...] = (self.block(self.y, self.core)[...] + self.landing[0]) + self.landing[3]

    def events(self):
        return [self.middle, self.finish]


class Heads(Move):
    def in_specs(arrays):
        return [ANY]

    def results(arrays):
        rows, columns = arrays[0].shape
        return [((Z * X * rows, columns // X), ANY)]

    def scratch(arrays):
        return [*dma_sems(7), pltpu.SemaphoreType.DMA((1,))]

    def setup(self):
        (self.own,), (self.out,) = self.ins, self.outs
        self.sems, self.local = self.scratch_refs[:2], self.scratch_refs[2]
        self.rows, columns = self.own.shape
        self.width = columns // X

    def block(self, z, x):
        row = pl.multiple_of((z * X + x) * self.rows, self.rows)
        return self.out.at[pl.ds(row, self.rows), :]

    def plane(self, z):
        row = pl.multiple_of(z * X * self.rows, X * self.rows)
        return self.out.at[pl.ds(row, X * self.rows), :]

    def own_columns(self, x):
        return self.own.at[:, pl.ds(pl.multiple_of(x * self.width, self.width), self.width)]

    def swap(self):
        return remote(
            self.own_columns(1 - self.x), self.block(self.z, self.x), self.sems, 6, self.x_peer()
        )

    def keep(self):
        return pltpu.make_async_copy(
            self.own_columns(self.x), self.block(self.z, self.x), self.local.at[0]
        )

    def along(self, way, step, arriving):
        plane = self.plane(self.z - way * (step if arriving else step - 1))
        return remote(
            plane,
            plane,
            self.sems,
            (0 if way > 0 else 3) + step - 1,
            self.device(self.z + way, self.x, self.y, self.core),
        )

    def begin(self):
        self.swap().start()
        self.keep().start()

    def start_along(self, way, step):
        pl.when(self.goes_on(way, step))(lambda: self.along(way, step, False).start())

    def swapped(self):
        self.swap().wait()
        self.keep().wait()
        for way in (1, -1):
            self.start_along(way, 1)

    def arrive(self, step):
        def action(way):
            self.along(way, step, True).wait_recv()
            if step < Z - 1:
                self.start_along(way, step + 1)

        self.each(step, action)

    def finish(self):
        self.arrive(Z - 1)
        for way in (1, -1):
            for step in range(1, Z):
                pl.when(self.goes_on(way, step))(
                    lambda way=way, step=step: self.along(way, step, False).wait_send()
                )

    def events(self):
        return [self.swapped, lambda: self.arrive(1), lambda: self.arrive(2), self.finish]


class Columns(Move):
    def in_specs(arrays):
        return [ANY]

    def results(arrays):
        rows, columns = arrays[0].shape
        return [((Z, X, rows, columns // Z), ANY)]

    def scratch(arrays):
        return [*dma_sems(Z + Z + 1), pltpu.SemaphoreType.DMA((1,))]

    def setup(self):
        (self.own,), (self.out,) = self.ins, self.outs
        self.sems, self.local = self.scratch_refs[:2], self.scratch_refs[2]
        self.half = self.own.shape[1] // (2 * Z)

    def piece(self, z):
        start = pl.multiple_of((z * 2 + self.core) * self.half, self.half)
        return self.own.at[:, pl.ds(start, self.half)]

    def landing(self, z, x, core):
        start = pl.multiple_of(core * self.half, self.half)
        return self.out.at[z, x, :, pl.ds(start, self.half)]

    def along(self, distance):
        z = (self.z + distance) % Z
        return remote(
            self.piece(z),
            self.landing(self.z, self.x, self.core),
            self.sems,
            distance,
            self.device(z, self.x, self.y, self.core),
        )

    def keep(self):
        return pltpu.make_async_copy(
            self.piece(self.z), self.landing(self.z, self.x, self.core), self.local.at[0]
        )

    def across(self, distance):
        block = self.landing((self.z - distance) % Z, self.x, self.core)
        return remote(block, block, self.sems, Z + distance, self.x_peer())

    def inside(self):
        start = pl.multiple_of(self.core * self.half, self.half)
        part = self.out.at[:, :, :, pl.ds(start, self.half)]
        return remote(part, part, self.sems, 2 * Z, self.core_peer())

    def begin(self):
        self.keep().start()
        for distance in (1, 3, 2):
            self.along(distance).start()

    def arrived(self, distance):
        if distance == 0:
            self.keep().wait()
        else:
            self.along(distance).wait()
        self.across(distance).start()

    def all_here(self):
        for distance in range(Z):
            self.across(distance).wait()
        self.inside().start()

    def events(self):
        return [
            lambda: self.arrived(0),
            lambda: self.arrived(1),
            lambda: self.arrived(3),
            lambda: self.arrived(2),
            self.all_here,
            lambda: self.inside().wait(),
        ]


class SwapX(Move):
    def in_specs(arrays):
        return [ANY] * len(arrays)

    def results(arrays):
        return [(array.shape, ANY) for array in arrays]

    def scratch(arrays):
        return dma_sems(len(arrays))

    def setup(self):
        pass

    def copies(self):
        return [
            remote(src, dst, self.scratch_refs, index, self.x_peer())
            for index, (src, dst) in enumerate(zip(self.ins, self.outs, strict=True))
        ]

    def begin(self):
        for copy in self.copies():
            copy.start()

    def finish(self):
        for copy in self.copies():
            copy.wait()

    def events(self):
        return [self.finish]


class SwapBlocks(Move):
    def in_specs(arrays):
        return [ANY] * len(arrays)

    def results(arrays):
        return [((X, array.shape[0] // X, array.shape[1]), ANY) for array in arrays]

    def scratch(arrays):
        return [*dma_sems(len(arrays)), pltpu.SemaphoreType.DMA((len(arrays),))]

    def setup(self):
        self.sems, self.local = self.scratch_refs[:2], self.scratch_refs[2]

    def ends(self, index, x):
        src, dst = self.ins[index], self.outs[index]
        rows = src.shape[0] // X
        return src.at[pl.ds(pl.multiple_of(x * rows, rows), rows), :], dst.at[self.x]

    def send(self, index):
        return remote(*self.ends(index, 1 - self.x), self.sems, index, self.x_peer())

    def keep(self, index):
        return pltpu.make_async_copy(*self.ends(index, self.x), self.local.at[index])

    def begin(self):
        for index in range(len(self.ins)):
            self.send(index).start()
            self.keep(index).start()

    def finish(self):
        for index in range(len(self.ins)):
            self.send(index).wait()
            self.keep(index).wait()

    def events(self):
        return [self.finish]


class SumAll(Move):
    def in_specs(arrays):
        return [WHOLE]

    def results(arrays):
        rows, columns = arrays[0].shape
        return [((rows // X, columns), WHOLE)]

    def scratch(arrays):
        rows, columns = arrays[0].shape
        return [pltpu.VMEM((6, rows // X, columns), F32), *dma_sems(3)]

    def setup(self):
        (self.part,), (self.out,) = self.ins, self.outs
        self.landing, self.sems = self.scratch_refs[0], self.scratch_refs[1:]
        self.rows = self.part.shape[0] // X

    def half(self, x):
        return self.part.at[pl.ds(pl.multiple_of(x * self.rows, self.rows), self.rows), :]

    def first(self):
        return remote(self.half(1 - self.x), self.landing.at[0], self.sems, 0, self.x_peer())

    def second(self):
        return remote(self.landing.at[1], self.landing.at[2], self.sems, 1, self.core_peer())

    def third(self):
        return remote(self.landing.at[3], self.landing.at[4], self.sems, 2, self.y_peer())

    def begin(self):
        self.first().start()

    def to_core(self):
        self.first().wait()
        self.landing[1] = self.half(self.x)[...] + self.landing[0]
        self.second().start()

    def to_y(self):
        self.second().wait()
        self.landing[3] = self.landing[1] + self.landing[2]
        self.third().start()

    def finish(self):
        self.third().wait()
        self.out[...] = self.landing[3] + self.landing[4]

    def events(self):
        return [self.to_core, self.to_y, self.finish]


class Refs(dict):
    __getattr__ = dict.__getitem__


def fused(arrays, results, scratch, steps, body, collective_id, far=False, flops=0):
    names = [*arrays, *results, *scratch]

    def kernel(*refs):
        refs = list(refs)
        here = Refs(zip([*arrays, *results], refs, strict=False))
        del refs[: len(arrays) + len(results)]
        for name, needed in scratch.items():
            here[name] = refs[: len(needed)]
            del refs[: len(needed)]
        step = pl.program_id(0)
        if collective_id is not None:
            pl.when(step == 0)(lambda: Move([], [], []).greet(far))
        body(here, step)

    outputs = pl.pallas_call(
        kernel,
        grid=(steps,),
        out_shape=[
            jax.ShapeDtypeStruct(result[0], result[2] if len(result) > 2 else F32)
            for result in results.values()
        ],
        in_specs=[spec for _, spec in arrays.values()],
        out_specs=[result[1] for result in results.values()],
        scratch_shapes=[one for needed in scratch.values() for one in needed],
        compiler_params=pltpu.CompilerParams(
            has_side_effects=True,
            vmem_limit_bytes=VMEM_BYTES,
            **({} if collective_id is None else dict(collective_id=collective_id)),
        ),
        cost_estimate=pl.CostEstimate(flops=flops, bytes_accessed=32 << 20, transcendentals=0),
    )(*(array for array, _ in arrays.values()))
    return Refs(zip(results, outputs, strict=True))


def at(now, when, *actions):
    for action in actions:
        pl.when(now == when)(action)


def schedule(now, when, events):
    for event, moment in zip(events, when, strict=True):
        pl.when(now == moment)(event)


SPLIT_ROWS = 128


def first_kernel(block, out_weight, w_gate, w_up, w_down, collective_id):
    inner, columns = w_gate.shape
    padded = pl.cdiv(columns, TILE) * TILE
    steps = inner // SPLIT_ROWS
    down_steps = padded // SPLIT_ROWS
    out_rows = out_weight.shape[0] // steps

    def body(refs, step):
        gather = Gather12([refs.block], [refs.all], refs.gather)
        pl.when(step == 0)(gather.begin)

        def store(name, entries, spot):
            refs[f"{name}_high"][:, spot], refs[f"{name}_low"][:, spot] = halves(entries)

        whole = slice(None)
        store("out", refs.out[...], whole)
        for name in ("gate", "up"):
            store(name, refs[name][...], slice(0, columns))
            for half in ("high", "low"):
                refs[f"{name}_{half}"][:, columns:] = jnp.zeros(
                    (SPLIT_ROWS, padded - columns), BF16
                )
        row = jnp.minimum(step, down_steps - 1) * SPLIT_ROWS + lax.broadcasted_iota(
            jnp.int32, (SPLIT_ROWS, inner), 0
        )
        down = jnp.where(row < columns, refs.down[...], 0.0)
        store("down", down, whole)
        store("turned", jnp.transpose(down), whole)
        schedule(step, (2, 3, 5, 6, 8, 10, 11, 13, 14, 15, 15), gather.events())

    def by_rows(rows, columns, last=steps - 1):
        return pl.BlockSpec((rows, columns), lambda step: (jnp.minimum(step, last), 0))

    results = dict(all=Gather.results([block])[0])
    for half in ("high", "low"):
        for name in ("gate", "up"):
            results[f"{name}_{half}"] = ((inner, padded), by_rows(SPLIT_ROWS, padded), BF16)
        results[f"out_{half}"] = (out_weight.shape, by_rows(out_rows, inner), BF16)
        results[f"down_{half}"] = (
            (padded, inner), by_rows(SPLIT_ROWS, inner, down_steps - 1), BF16
        )
        results[f"turned_{half}"] = (
            (inner, padded),
            pl.BlockSpec(
                (inner, SPLIT_ROWS), lambda step: (0, jnp.minimum(step, down_steps - 1))
            ),
            BF16,
        )
    return fused(
        dict(
            block=(block, ANY),
            gate=(w_gate, by_rows(SPLIT_ROWS, columns)),
            up=(w_up, by_rows(SPLIT_ROWS, columns)),
            down=(w_down, by_rows(SPLIT_ROWS, inner, pl.cdiv(columns, SPLIT_ROWS) - 1)),
            out=(out_weight, by_rows(out_rows, inner)),
        ),
        results,
        dict(gather=Gather.scratch([block])),
        steps,
        body,
        collective_id,
    )


def halves_scratch(rows, inner):
    return [
        pltpu.VMEM((rows, inner), BF16),
        pltpu.VMEM((rows, inner), BF16),
        pltpu.VMEM((rows // 128, 128, inner), F32),
        pltpu.SemaphoreType.DMA((rows // 128,)),
    ]


def load_halves(src_ref, high_ref, low_ref, stage_ref, sem, change=None, start=True, split=True):
    count, rows, _ = stage_ref.shape

    def spot(index):
        return pl.ds(pl.multiple_of(index * rows, rows), rows)

    def fetch(index):
        return pltpu.make_async_copy(
            src_ref.at[spot(index), :], stage_ref.at[index], sem.at[index]
        )

    def one(index, carried):
        fetch(index).wait()
        if change is not None:
            change(index)
        high, low = halves(stage_ref[index])
        high_ref[spot(index), :] = high
        low_ref[spot(index), :] = low
        return carried

    if start:
        for index in range(count):
            fetch(index).start()
    if split:
        lax.fori_loop(0, count, one, 0)


STRIP = 512


def strips(rows, action):
    def one(index, carried):
        action(index, pl.ds(pl.multiple_of(index * STRIP, STRIP), STRIP))
        return carried

    lax.fori_loop(0, rows // STRIP, one, 0)


def block_fetch(src, buf, sem, index):
    return pltpu.make_async_copy(src, buf.at[index], sem.at[index])


EARLY = 3


def mixer_kernel(
    all_tokens, tokens_in, cotangent, lengths, lower_bound, in_weights, split, first_gain, group_gain,
    second_gain, collective_id,
):
    rows, inner = all_tokens.shape
    own_rows = tokens_in.shape[0]
    count = 4
    wide = inner // Z
    heads = TILE // HDIM
    chunks = rows // CHUNK
    tiles = EARLY
    columns = tiles * TILE
    parts = rows // STRIP
    middle = count + chunks
    steps = middle + 1 + tiles

    def body(refs, step):
        place = lax.axis_index("seq")
        x = place % X
        here = pl.ds(pl.multiple_of(x * TILE, TILE), TILE)
        there = pl.ds(pl.multiple_of((1 - x) * TILE, TILE), TILE)
        first_col = pl.multiple_of((place // X) * wide, wide)
        gather = Gather([refs.cotangent], [refs.all_cotangent], refs.gather)
        part_ref, sum_ref, *sum_scratch = refs.sum
        total = Sum([part_ref], [sum_ref], sum_scratch)
        high_ref, low_ref, stage_ref, stage_sem = refs.halves
        weight_buf, weight_sem, down_buf, down_sem, out_buf, out_sem, ready_ref = refs.weights
        (state_ref,) = refs.state
        other_ref, send, recv = refs.swap
        now = step * parts

        def fetch(index):
            return [
                pltpu.make_async_copy(
                    refs[f"weight_{index}"].at[:, here],
                    weight_buf.at[index % 2],
                    weight_sem.at[index % 2],
                )
            ]

        def fetch_down(tile):
            slot = lax.rem(tile, 2)
            spot = pl.ds(pl.multiple_of(tile * TILE, TILE), TILE)
            return [
                pltpu.make_async_copy(
                    refs[f"turned_{half}"].at[:, spot], down_buf.at[slot, at], down_sem.at[slot, at]
                )
                for at, half in enumerate(("high", "low"))
            ]

        def start(copies):
            for copy in copies:
                copy.start()

        def wait(copies):
            for copy in copies:
                copy.wait()

        def fetch_out():
            return [
                pltpu.make_async_copy(refs[f"out_{half}"], out_buf.at[at], out_sem.at[at])
                for at, half in enumerate(("high", "low"))
            ]

        def swap():
            peer = pl.multiple_of((place + 1 - 2 * x) * own_rows, own_rows)
            return remote(
                refs.mixer.at[pl.ds(peer, own_rows), :], other_ref, (send, recv), 0, gather.x_peer()
            )

        def pause(part):
            mixing = count * parts
            schedule(
                now + part,
                (0, 1, 2, 3, 5, mixing, mixing + 2 * parts, mixing + 4 * parts, mixing + 7 * parts),
                gather.events()[:9],
            )

        def normalize(index):
            entries = stage_ref[index]
            stage_ref[index] = entries * rms(entries) * refs.first_gain[...]
            refs.normed_cols[pl.ds(pl.multiple_of(index * 128, 128), 128), :] = stage_ref[
                index, :, pl.ds(first_col, wide)
            ]

        @pl.when(step == 0)
        def _():
            gather.begin()
            start(fetch(0))
            start(fetch_out())
            load_halves(refs.tokens, high_ref, low_ref, stage_ref, stage_sem, normalize)
            state_ref[...] = jnp.zeros_like(state_ref)

        for index in range(count):

            @pl.when(step == index)
            def _(index=index):
                if index + 1 < count:
                    start(fetch(index + 1))
                wait(fetch(index))

        @pl.when(step < count)
        def _():
            ready_ref[0], ready_ref[1] = halves(weight_buf[lax.rem(step, 2)])
            target = pl.ds(pl.multiple_of(step * TILE, TILE), TILE)

            def strip(index, spot):
                refs.projected[spot, target] = three_pass(
                    (high_ref[spot, :], low_ref[spot, :]),
                    (ready_ref[0], ready_ref[1]),
                    1,
                    0,
                )
                pause(index)

            strips(rows, strip)

        @pl.when((step >= count) & (step < middle))
        def _():
            chunk = step - count
            spot = pl.ds(pl.multiple_of(chunk * CHUNK, CHUNK), CHUNK)
            forward_chunk(
                chunk,
                refs.lengths,
                refs.projected.at[spot, :],
                refs.lower_bound.at[:, here],
                refs.group_gain.at[:, here],
                refs.mixer.at[spot, :],
                refs.raw.at[spot, :],
                refs.states.at[pl.ds(chunk, 1)],
                state_ref,
            )
            pause(0)

        @pl.when(step == middle)
        def _():
            swap().start()
            start(fetch_down(0))
            wait(fetch_out())

            def out_rows(spot):
                return out_buf[0, spot, :], out_buf[1, spot, :]

            own = refs.mixer[pl.ds(pl.multiple_of(place * own_rows, own_rows), own_rows), :]
            part_ref[...] = few_rows(halves(own), out_rows(here), 0)
            swap().wait()
            part_ref[...] += few_rows(halves(other_ref[...]), out_rows(there), 0)
            total.begin()
            total.to_y()
            gather.events()[9]()
            gather.finish()
            load_halves(refs.all_cotangent, high_ref, low_ref, stage_ref, stage_sem)

        @pl.when(step > middle)
        def _():
            tile = step - middle - 1
            pl.when(tile < tiles - 1)(lambda: start(fetch_down(tile + 1)))
            wait(fetch_down(tile))
            slot = lax.rem(tile, 2)
            refs.grad_hidden[...] = three_pass(
                (high_ref[...], low_ref[...]), (down_buf[slot, 0], down_buf[slot, 1]), 1, 0
            )

        @pl.when(step == steps - 1)
        def _():
            total.back()
            total.finish()
            residual = refs.tokens_in[...] + sum_ref[...]
            refs.residual[...] = residual
            refs.normed_two[...] = residual * rms(residual) * refs.second_gain[...]

    own_shape = (own_rows, inner)
    return fused(
        dict(
            lengths=(lengths, pl.BlockSpec(memory_space=pltpu.SMEM)),
            tokens=(all_tokens, ANY),
            tokens_in=(tokens_in, WHOLE),
            cotangent=(cotangent, ANY),
            lower_bound=(lower_bound[None], WHOLE),
            first_gain=(first_gain[None], WHOLE),
            group_gain=(group_gain[None], WHOLE),
            second_gain=(second_gain[None], WHOLE),
            **{f"weight_{index}": (weight, ANY) for index, weight in enumerate(in_weights)},
            **{
                f"{name}_{half}": (split[f"{name}_{half}"], ANY)
                for name in ("out", "turned")
                for half in ("high", "low")
            },
        ),
        dict(
            all_cotangent=((rows, inner), ANY),
            projected=((rows, count * TILE), WHOLE),
            normed_cols=((rows, wide), WHOLE),
            mixer=((rows, TILE), WHOLE),
            raw=((rows, TILE), WHOLE),
            states=((chunks, heads, HDIM, HDIM), WHOLE),
            grad_hidden=(
                (rows, columns),
                pl.BlockSpec((rows, TILE), lambda step: (0, jnp.maximum(step - middle - 1, 0))),
            ),
            residual=(own_shape, WHOLE),
            normed_two=(own_shape, WHOLE),
        ),
        dict(
            halves=halves_scratch(rows, inner),
            weights=[
                pltpu.VMEM((2, inner, TILE), F32),
                pltpu.SemaphoreType.DMA((2,)),
                pltpu.VMEM((2, 2, inner, TILE), BF16),
                pltpu.SemaphoreType.DMA((2, 2)),
                pltpu.VMEM((2, *split.out_high.shape), BF16),
                pltpu.SemaphoreType.DMA((2,)),
                pltpu.VMEM((2, inner, TILE), BF16),
            ],
            state=[pltpu.VMEM((heads, HDIM, HDIM), F32)],
            swap=[pltpu.VMEM((own_rows, TILE), F32), *dma_sems(1)],
            gather=Gather.scratch([cotangent]),
            sum=[
                pltpu.VMEM(own_shape, F32),
                pltpu.VMEM(own_shape, F32),
                *Sum.scratch([tokens_in]),
            ],
        ),
        steps,
        body,
        collective_id,
        flops=6 * rows * inner * (count * TILE + columns),
    )


def feed_forward_kernel(normed_two, all_cotangent, grad_hidden, split, collective_id):
    rows, inner = normed_two.shape
    token_count = all_cotangent.shape[0]
    columns = split.gate_high.shape[1]
    tiles = columns // TILE

    def body(refs, step):
        gather = Gather([refs.normed_two], [refs.all_normed_two], refs.gather)
        high_ref, low_ref, stage_ref, stage_sem = refs.halves
        (e_ref,) = refs.e
        load = partial(load_halves, refs.all_cotangent, high_ref, low_ref, stage_ref, stage_sem)

        @pl.when(step == 0)
        def _():
            gather.begin()
            load(split=False)
            refs.ffn[...] = jnp.zeros_like(refs.ffn)
            refs.grad[...] = jnp.zeros_like(refs.grad)

        pl.when(step == EARLY - 1)(lambda: load(start=False))

        def both(name):
            return refs[f"{name}_high"][...], refs[f"{name}_low"][...]

        @pl.when(step < EARLY)
        def _():
            e_ref[...] = refs.early[...]

        @pl.when(step >= EARLY)
        def _():
            refs.late[...] = three_pass((high_ref[...], low_ref[...]), both("turned"), 1, 0)
            row = pl.multiple_of(lax.axis_index("seq") * rows, rows)
            e_ref[...] = refs.late[pl.ds(row, rows), :]

        moments = (1, 3, 4, 5, 6, 7, 7, 8, 9, 10, 11)
        schedule(2 * step, moments, gather.events())
        normed = halves(refs.normed_two[...])
        a = few_rows(normed, both("gate"), 0)
        b = few_rows(normed, both("up"), 0)
        e = e_ref[...]
        gate = jax.nn.sigmoid(a)
        silu_a = a * gate
        refs.ffn[...] += few_rows(halves(silu_a * b), both("down"), 0)
        refs.grad[...] += few_rows(
            halves(e * b * (gate * (1.0 + a * (1.0 - gate)))), both("gate"), 1
        ) + few_rows(halves(e * silu_a), both("up"), 1)
        schedule(2 * step + 1, moments, gather.events())

    by_column = pl.BlockSpec((inner, TILE), lambda step: (0, step))
    return fused(
        dict(
            normed_two=(normed_two, WHOLE),
            all_cotangent=(all_cotangent, ANY),
            early=(
                grad_hidden,
                pl.BlockSpec(
                    (rows, TILE), lambda step: (lax.axis_index("seq"), jnp.minimum(step, EARLY - 1))
                ),
            ),
            **{
                f"{name}_{half}": (split[f"{name}_{half}"], spec)
                for name, spec in (
                    ("gate", by_column),
                    ("up", by_column),
                    ("down", pl.BlockSpec((TILE, inner), lambda step: (step, 0))),
                    (
                        "turned",
                        pl.BlockSpec((inner, TILE), lambda step: (0, jnp.maximum(step, EARLY))),
                    ),
                )
                for half in ("high", "low")
            },
        ),
        dict(
            all_normed_two=Gather.results([normed_two])[0],
            ffn=((rows, inner), WHOLE),
            grad=((rows, inner), WHOLE),
            late=(
                (token_count, columns - EARLY * TILE),
                pl.BlockSpec((token_count, TILE), lambda step: (0, jnp.maximum(step - EARLY, 0))),
            ),
        ),
        dict(
            gather=Gather.scratch([normed_two]),
            halves=halves_scratch(token_count, inner),
            e=[pltpu.VMEM((rows, TILE), F32)],
        ),
        tiles,
        body,
        collective_id,
        flops=30 * rows * inner * columns,
    )


SHARES = 2


def tile_share(refs, share, tile):
    high_ref, low_ref, cols_high_ref, cols_low_ref, cot_high_ref, cot_low_ref = refs.halves
    size = high_ref.shape[0] // SHARES
    spot = pl.ds(pl.multiple_of(share * size, size), size)
    normed = high_ref[spot, :], low_ref[spot, :]
    a = three_pass(normed, (refs.gate_high[...], refs.gate_low[...]), 1, 0)
    b = three_pass(normed, (refs.up_high[...], refs.up_low[...]), 1, 0)
    gate = jax.nn.sigmoid(a)
    silu_a = a * gate
    e = jnp.where(tile < EARLY, refs.early[spot, :], refs.late[spot, :])
    cols = cols_high_ref[:, spot], cols_low_ref[:, spot]
    cot = cot_high_ref[spot, :], cot_low_ref[spot, :]
    grads = (
        three_pass(cols, halves(e * b * (gate * (1.0 + a * (1.0 - gate)))), 1, 0),
        three_pass(cols, halves(e * silu_a), 1, 0),
        three_pass(halves(jnp.transpose(silu_a * b)), cot, 1, 0),
    )
    for ref, grad in zip((refs.grad_gate, refs.grad_up, refs.grad_down), grads, strict=True):
        ref[...] = jnp.where(share == 0, 0.0, ref[...]) + grad


def tile_columns(refs):
    cols_high_ref, cols_low_ref, cot_high_ref, cot_low_ref = refs.halves[2:]
    cols_high_ref[...], cols_low_ref[...] = halves(jnp.transpose(refs.normed_cols[...]))
    cot_high_ref[...], cot_low_ref[...] = halves(refs.cot_cols[...])


def tile_parts(all_normed_two, all_cotangent, early, late, split, first, count, tile_of):
    rows, inner = all_normed_two.shape
    narrow = inner // (Z * X)
    columns = count * TILE
    own_columns = pl.BlockSpec((rows, narrow), lambda step: (0, lax.axis_index("seq")))
    by_column = pl.BlockSpec((inner, TILE), lambda step: (0, first + tile_of(step)))
    grad_spec = pl.BlockSpec((narrow, TILE), lambda step: (0, tile_of(step)))
    arrays = dict(
        early=(
            early,
            pl.BlockSpec((rows, TILE), lambda step: (0, jnp.minimum(first + tile_of(step), EARLY - 1))),
        ),
        late=(
            late,
            pl.BlockSpec(
                (rows, TILE), lambda step: (0, jnp.maximum(first + tile_of(step) - EARLY, 0))
            ),
        ),
        **{
            f"{name}_{half}": (split[f"{name}_{half}"], by_column)
            for name in ("gate", "up")
            for half in ("high", "low")
        },
        normed_cols=(all_normed_two, own_columns),
        cot_cols=(all_cotangent, own_columns),
    )
    results = dict(
        grad_gate=((narrow, columns), grad_spec),
        grad_up=((narrow, columns), grad_spec),
        grad_down=(
            (columns, narrow), pl.BlockSpec((TILE, narrow), lambda step: (tile_of(step), 0))
        ),
    )
    scratch = dict(
        halves=[
            pltpu.VMEM((rows, inner), BF16),
            pltpu.VMEM((rows, inner), BF16),
            pltpu.VMEM((narrow, rows), BF16),
            pltpu.VMEM((narrow, rows), BF16),
            pltpu.VMEM((rows, narrow), BF16),
            pltpu.VMEM((rows, narrow), BF16),
        ]
    )
    return arrays, results, scratch


def residual_kernel(
    part, ffn, residual, cotangent, second_gain, split, all_normed_two, tiles, count, collective_id
):
    arrays, results, scratch = tiles(lambda step: step // SHARES)
    rows, inner = all_normed_two.shape
    own_rows = part.shape[0]
    out_shape = split.out_high.shape
    grad_like = jax.ShapeDtypeStruct((own_rows, out_shape[0]), F32)

    def body(refs, step):
        sum_ref, *sum_scratch = refs.sum
        grad_mixer_ref, *heads_scratch = refs.heads
        total = Sum([refs.part], [sum_ref], sum_scratch)
        heads = Heads([grad_mixer_ref], [refs.all_grad_mixer], heads_scratch)
        scatter = Scatter([refs.ffn], [refs.ffn_share], refs.scatter)
        high_ref, low_ref = refs.halves[:2]
        stage_ref, stage_sem, out_sem = refs.stage
        out_buf, out_buf_sem = refs.out
        keep = [
            pltpu.make_async_copy(high_ref, refs.normed_high, out_sem.at[0]),
            pltpu.make_async_copy(low_ref, refs.normed_low, out_sem.at[1]),
        ]
        fetch_out = [
            pltpu.make_async_copy(refs[f"out_{half}"], out_buf.at[at], out_buf_sem.at[at])
            for at, half in enumerate(("high", "low"))
        ]

        def to_heads():
            total.finish()
            residual_here = refs.residual[...]
            scale = rms(residual_here)
            summed = sum_ref[...]
            pulled = summed * refs.second_gain[...]
            grad_residual = (
                refs.cotangent[...]
                + scale * pulled
                - residual_here
                * (scale * scale * scale * jnp.mean(pulled * residual_here, -1, keepdims=True))
            )
            refs.grad_residual[...] = grad_residual
            refs.second[...] = jnp.broadcast_to(
                jnp.sum(summed * residual_here * scale, 0, keepdims=True), refs.second.shape
            )
            for copy in fetch_out:
                copy.wait()
            grad_mixer_ref[...] = few_rows(halves(grad_residual), (out_buf[0], out_buf[1]), 1)
            heads.begin()

        @pl.when(step == 0)
        def _():
            total.begin()
            for copy in fetch_out:
                copy.start()
            load_halves(refs.all_normed_two, high_ref, low_ref, stage_ref, stage_sem)
            total.to_y()
            for copy in keep:
                copy.start()
            tile_columns(refs)

        tile_share(refs, lax.rem(step, SHARES), step // SHARES)
        schedule(step, (1, 2, 3, 5, 6, 8), [total.back, to_heads, *heads.events()])
        schedule(step, (3, 4, 6), [scatter.begin, *scatter.events()])

        @pl.when(step == count * SHARES - 1)
        def _():
            for copy in keep:
                copy.wait()

    return fused(
        dict(
            part=(part, WHOLE),
            ffn=(ffn, WHOLE),
            residual=(residual, WHOLE),
            cotangent=(cotangent, WHOLE),
            second_gain=(second_gain[None], WHOLE),
            out_high=(split.out_high, ANY),
            out_low=(split.out_low, ANY),
            all_normed_two=(all_normed_two, ANY),
            **arrays,
        ),
        dict(
            all_grad_mixer=Heads.results([grad_like])[0],
            ffn_share=Scatter.results([ffn])[0],
            grad_residual=((own_rows, inner), WHOLE),
            second=((8, inner), WHOLE),
            normed_high=((rows, inner), ANY, BF16),
            normed_low=((rows, inner), ANY, BF16),
            **results,
        ),
        dict(
            sum=[pltpu.VMEM((own_rows, inner), F32), *Sum.scratch([part])],
            heads=[pltpu.VMEM(grad_like.shape, F32), *Heads.scratch([grad_like])],
            scatter=Scatter.scratch([ffn]),
            stage=[*halves_scratch(rows, inner)[2:], pltpu.SemaphoreType.DMA((2,))],
            out=[pltpu.VMEM((2, *out_shape), BF16), pltpu.SemaphoreType.DMA((2,))],
            **scratch,
        ),
        count * SHARES,
        body,
        collective_id,
    )


def last_kernel(
    grads, group, blocks, first_part, in_weights, normed_high, normed_low, tiles, count, collective_id
):
    arrays, results, scratch = tiles(
        lambda step: jnp.where(step < SHARES, 0, jnp.maximum(step - 4, 0) // SHARES)
    )
    rows, columns = grads.shape
    own_rows = rows // (Z * X)
    inner, width = in_weights[0].shape
    half = width // X
    matrices = 4
    part_like = jax.ShapeDtypeStruct((own_rows, inner), F32)
    swapped = [jax.ShapeDtypeStruct((own_rows, columns), F32), group]

    def body(refs, step):
        place = lax.axis_index("seq")
        x = place % X
        peer = pl.multiple_of((place + 1 - 2 * x) * own_rows, own_rows)
        other_ref, *swap_scratch = refs.swap
        part_ref, *scatter_scratch = refs.scatter
        weight_buf, weight_sem, load_sem = refs.weights
        swap = SwapX(
            [refs.grads.at[pl.ds(peer, own_rows), :], refs.group],
            [other_ref, refs.other_group],
            swap_scratch,
        )
        blocks_here = SwapBlocks(
            [refs[f"block_{index}"] for index in range(len(blocks))],
            [refs[f"swapped_{index}"] for index in range(len(blocks))],
            refs.blocks,
        )
        scatter = Scatter([part_ref], [refs.share], scatter_scratch)
        sums = SumAll([refs.first_part], [refs.first_sum], refs.sums)

        def fetch(index):
            return block_fetch(refs[f"weight_{index}"], weight_buf, weight_sem, index % 2)

        load = [
            pltpu.make_async_copy(refs[f"normed_{name}"], refs.halves[at], load_sem.at[at])
            for at, name in enumerate(("high", "low"))
        ]

        @pl.when(step == 0)
        def _():
            for copy in load:
                copy.start()
            swap.begin()
            sums.begin()
            part_ref[...] = jnp.zeros_like(part_ref)
            for copy in load:
                copy.wait()
            for index in range(2):
                fetch(index).start()

        @pl.when(step == 1)
        def _():
            swap.finish()
            blocks_here.begin()

        pl.when(step == 0)(lambda: tile_columns(refs))

        @pl.when((step < SHARES) | (step >= matrices + SHARES))
        def _():
            tile_share(refs, lax.rem(step, SHARES), EARLY)

        schedule(step, (0, 1, 2), sums.events())
        for index in range(matrices):

            @pl.when(step == index + SHARES)
            def _(index=index):
                fetch(index).wait()
                weight = halves(weight_buf[index % 2])
                if index + 2 < matrices:
                    fetch(index + 2).start()
                own = refs.own_grads[:, index * half : (index + 1) * half]
                other = other_ref[:, index * half : (index + 1) * half]
                low_x, high_x = (jnp.where(x == place_x, own, other) for place_x in range(X))
                part_ref[...] += few_rows(halves(jnp.concatenate([low_x, high_x], 1)), weight, 1)

        @pl.when(step == matrices + count * SHARES - 1)
        def _():
            scatter.begin()
            scatter.middle()
            scatter.finish()
            blocks_here.finish()


    return fused(
        dict(
            grads=(grads, ANY),
            own_grads=(
                grads, pl.BlockSpec((own_rows, columns), lambda step: (lax.axis_index("seq"), 0))
            ),
            group=(group, ANY),
            first_part=(first_part, WHOLE),
            **{f"block_{index}": (block, ANY) for index, block in enumerate(blocks)},
            **{f"weight_{index}": (weight, ANY) for index, weight in enumerate(in_weights)},
            normed_high=(normed_high, ANY),
            normed_low=(normed_low, ANY),
            **arrays,
        ),
        dict(
            other_group=(group.shape, ANY),
            share=Scatter.results([part_like])[0],
            first_sum=SumAll.results([first_part])[0],
            **{
                f"swapped_{index}": result for index, result in enumerate(SwapBlocks.results(blocks))
            },
            **results,
        ),
        dict(
            swap=[pltpu.VMEM((own_rows, columns), F32), *SwapX.scratch(swapped)],
            scatter=[pltpu.VMEM((own_rows, inner), F32), *Scatter.scratch([part_like])],
            blocks=SwapBlocks.scratch(blocks),
            sums=SumAll.scratch([first_part]),
            weights=[
                pltpu.VMEM((2, inner, width), F32),
                pltpu.SemaphoreType.DMA((2,)),
                pltpu.SemaphoreType.DMA((2,)),
            ],
            **scratch,
        ),
        count * SHARES + matrices,
        body,
        collective_id,
    )


def thin(left, right, contract_left, contract_right):
    (left_high, left_low), (right_high, right_low) = left, right
    return product(
        jnp.concatenate([left_high, left_low], contract_left),
        jnp.concatenate([right_high, right_high], contract_right),
        contract_left,
        contract_right,
    ) + product(left_high, right_low, contract_left, contract_right)


def join(first, second, axis):
    return tuple(jnp.concatenate(pair, axis) for pair in zip(first, second, strict=True))


def running_sum(triangle, entries):
    high, low = halves(entries)
    least = (entries - high.astype(F32) - low.astype(F32)).astype(BF16)
    return product(
        jnp.concatenate([triangle, triangle], 1), jnp.concatenate([high, low], 0), 1, 0
    ) + product(triangle, least, 1, 0)


def chunk_masks(lengths_ref, chunk):
    shape = (CHUNK, CHUNK)
    row = lax.broadcasted_iota(jnp.int32, shape, 0)
    column = lax.broadcasted_iota(jnp.int32, shape, 1)
    start = chunk * CHUNK

    offsets = [0]
    for index in range(lengths_ref.shape[0] - 1):
        offsets.append(offsets[-1] + lengths_ref[index])

    def segment(position):
        return sum(jnp.where(position >= offset, 1, 0) for offset in offsets)

    segment_row = segment(start + row)
    before, last = segment(start - 1), segment(start + CHUNK - 1)
    allowed = (row >= column) & (segment_row == segment(start + column))
    carry = (segment_row == before).astype(F32)
    in_last = (segment_row == last).astype(F32)
    lower = (row >= column).astype(F32).astype(BF16)
    return allowed, carry, in_last, (last == before).astype(F32), lower


def head_terms(pre_query, pre_forget, lower_bound, lower):
    query_gate = jax.nn.sigmoid(pre_query)
    forget_gate = jax.nn.sigmoid(-pre_forget)
    keys = (1.0 - lower_bound) * forget_gate
    log_decay = running_sum(lower, jnp.log1p(-keys))
    last = log_decay[CHUNK - 1 :, :]
    growth, shrink, trail = jnp.exp(log_decay), jnp.exp(-log_decay), jnp.exp(last - log_decay)
    return query_gate, forget_gate, keys, last, growth, shrink, trail


def tall(row):
    return jnp.transpose(jnp.broadcast_to(row, (HDIM, HDIM)))


def forward_chunk(
    chunk, lengths_ref, projected_ref, bound_ref, gain_ref, mixer_ref, raw_ref, states_ref, state_ref
):
    heads = state_ref.shape[0]
    width = heads * HDIM
    allowed, carry, in_last, carry_last, lower = chunk_masks(lengths_ref, chunk)
    for head in range(heads):
        at = slice(head * HDIM, (head + 1) * HDIM)
        pre_query, pre_forget, values, gate_in = (
            projected_ref[:, part * width + head * HDIM : part * width + (head + 1) * HDIM]
            for part in range(4)
        )
        query_gate, _, keys, last, growth, shrink, trail = head_terms(
            pre_query, pre_forget, bound_ref[:, at], lower
        )
        grown = pre_query * query_gate * growth
        state = state_ref[head]
        states_ref[0, head] = state
        value_halves = halves(values)
        scores = thin(halves(grown), halves(keys * shrink), 1, 1)
        scores = jnp.where(allowed, scores, 0.0)
        raw = three_pass(
            join(halves(scores), halves(grown * carry), 1),
            join(value_halves, halves(state), 0),
            1,
            0,
        )
        state_ref[head] = state * (tall(jnp.exp(last)) * carry_last) + thin(
            halves(keys * trail * in_last), value_halves, 0, 0
        )
        raw_ref[:, at] = raw
        scale = lax.rsqrt(jnp.mean(raw * raw, -1, keepdims=True) + group_eps)
        mixer_ref[:, at] = raw * scale * gain_ref[:, at] * jax.nn.silu(gate_in)


def backward_kernel(
    projected, raw_rows, states, grad_mixer, normed_cols, grad_residual, second, weights,
    lower_bound, group_gain, lengths, collective_id,
):
    rows, columns = projected.shape
    count = len(weights)
    width = columns // count
    heads = width // HDIM
    chunks = rows // CHUNK
    wide = normed_cols.shape[1]

    def body(refs, step):
        lengths_ref, projected_ref, raw_ref, states_ref = refs.lengths, refs.projected, refs.raw, refs.states
        grad_ref, grads_ref, group_ref = refs.grad_mixer, refs.grads, refs.group
        later_ref, weight_buf, weight_sem = refs.work
        chunk = chunks - 1 - step
        place = lax.axis_index("seq")
        here = pl.ds(pl.multiple_of((place % X) * width, width), width)
        bound_ref, gain_ref = refs.lower_bound.at[:, here], refs.group_gain.at[:, here]
        block_refs = [refs[f"block_{index}"] for index in range(count)]
        move = Columns([refs.grad_residual], [refs.residual_cols], refs.columns)
        small = Columns([refs.second], [refs.second_cols], refs.small)

        def fetch(index):
            return block_fetch(
                refs[f"weight_{index}"].at[
                    pl.ds(pl.multiple_of((place // X) * wide, wide), wide), here
                ],
                weight_buf,
                weight_sem,
                index,
            )

        @pl.when(step == 0)
        def _():
            move.begin()
            small.begin()
            later_ref[...] = jnp.zeros_like(later_ref)
            group_ref[...] = jnp.zeros_like(group_ref)
            for index in range(count):
                fetch(index).start()
                block_refs[index][...] = jnp.zeros_like(block_refs[index])

        allowed, carry, in_last, carry_last, lower = chunk_masks(lengths_ref, chunk)
        upper = jnp.transpose(lower.astype(F32)).astype(BF16)
        for head in range(heads):
            at = slice(head * HDIM, (head + 1) * HDIM)
            spots = [
                slice(part * width + head * HDIM, part * width + (head + 1) * HDIM)
                for part in range(4)
            ]
            pre_query, pre_forget, values, gate_in = (projected_ref[:, spot] for spot in spots)
            raw, grad, gain = raw_ref[:, at], grad_ref[:, at], gain_ref[:, at]
            state, later = states_ref[0, head], later_ref[head]

            scale = lax.rsqrt(jnp.mean(raw * raw, -1, keepdims=True) + group_eps)
            normed = raw * scale
            gate = jax.nn.sigmoid(gate_in)
            silu_gate = gate_in * gate
            weighted = grad * gain * silu_gate
            group_ref[:, at] += jnp.sum(grad * normed * silu_gate, 0, keepdims=True)
            grads_ref[:, spots[3]] = (
                grad * gain * normed * (gate * (1.0 + gate_in * (1.0 - gate)))
            )
            grad_raw = scale * weighted - raw * (
                scale * scale * scale * jnp.mean(weighted * raw, -1, keepdims=True)
            )

            query_gate, forget_gate, keys, last, growth, shrink, trail = head_terms(
                pre_query, pre_forget, bound_ref[:, at], lower
            )
            grown = pre_query * query_gate * growth
            shrunk = keys * shrink
            trailing = trail * in_last
            ends = keys * trailing
            grown_halves, shrunk_halves = halves(grown), halves(shrunk)
            raw_halves, value_halves, later_halves = halves(grad_raw), halves(values), halves(later)
            scores = jnp.where(allowed, thin(grown_halves, shrunk_halves, 1, 1), 0.0)
            grad_scores = jnp.where(allowed, thin(raw_halves, value_halves, 1, 1), 0.0)
            score_halves = halves(grad_scores)
            grads_ref[:, spots[2]] = three_pass(
                join(halves(jnp.transpose(scores)), halves(ends), 1),
                join(raw_halves, later_halves, 0),
                1,
                0,
            )
            grad_grown = three_pass(
                join(score_halves, halves(grad_raw * carry), 1),
                join(shrunk_halves, halves(jnp.transpose(state)), 0),
                1,
                0,
            )
            grad_shrunk = thin(score_halves, grown_halves, 0, 0)
            grad_ends = thin(value_halves, later_halves, 1, 1)
            through = tall(jnp.exp(last)) * carry_last
            later_ref[head] = later * through + thin(
                halves(grown * carry), raw_halves, 0, 0
            )
            grads_ref[:, spots[0]] = (
                grad_grown * growth * (query_gate * (1.0 + pre_query * (1.0 - query_gate)))
            )
            from_ends = grad_ends * ends
            grad_log = grad_grown * grown - grad_shrunk * shrunk - from_ends
            pulled = jnp.transpose(later * state * through)
            grad_last = jnp.sum(from_ends + pulled, 0, keepdims=True)
            grad_log_forget = running_sum(upper, grad_log) + grad_last
            grad_keys = (
                grad_shrunk * shrink + grad_ends * trailing - grad_log_forget / (1.0 - keys)
            )
            grads_ref[:, spots[1]] = -grad_keys * keys * (1.0 - forget_gate)

        cols = halves(jnp.transpose(refs.normed_cols[...]))
        for index in range(count):
            part = grads_ref[:, index * width : (index + 1) * width]
            block_refs[index][...] += thin(cols, halves(part), 1, 0)

        @pl.when(step == chunks - 1)
        def _():
            total = 0.0
            for index in range(count):
                fetch(index).wait()
                total = total + weight_buf[index] * block_refs[index][...]
            ones = jnp.ones((8, width), BF16)
            high, low = halves(total)
            refs.sums[...] = product(ones, high, 1, 1) + product(ones, low, 1, 1)

        schedule(step, (0, 1, 2, 4, 6, 7), small.events())
        schedule(step, (0, 2, 3, 5, 7, 7), move.events())

    def by_chunk(size):
        return pl.BlockSpec((CHUNK, size), lambda step: (chunks - 1 - step, 0))

    return fused(
        dict(
            lengths=(lengths, pl.BlockSpec(memory_space=pltpu.SMEM)),
            projected=(projected, by_chunk(columns)),
            raw=(raw_rows, by_chunk(width)),
            states=(
                states,
                pl.BlockSpec((1, heads, HDIM, HDIM), lambda step: (chunks - 1 - step, 0, 0, 0)),
            ),
            grad_mixer=(grad_mixer, by_chunk(width)),
            normed_cols=(normed_cols, by_chunk(wide)),
            lower_bound=(lower_bound[None], WHOLE),
            group_gain=(group_gain[None], WHOLE),
            grad_residual=(grad_residual, ANY),
            second=(second, ANY),
            **{f"weight_{index}": (weight, ANY) for index, weight in enumerate(weights)},
        ),
        dict(
            grads=((rows, columns), by_chunk(columns)),
            group=((1, width), WHOLE),
            sums=((8, wide), WHOLE),
            residual_cols=Columns.results([grad_residual])[0],
            second_cols=Columns.results([second])[0],
            **{f"block_{index}": ((wide, width), WHOLE) for index in range(count)},
        ),
        dict(
            work=[
                pltpu.VMEM((heads, HDIM, HDIM), F32),
                pltpu.VMEM((count, wide, width), F32),
                pltpu.SemaphoreType.DMA((count,)),
            ],
            columns=Columns.scratch([grad_residual]),
            small=Columns.scratch([second]),
        ),
        chunks,
        body,
        collective_id,
        far=True,
        flops=60 * rows * HDIM * width + 6 * rows * wide * columns,
    )


def fast_shards(
    tokens_in,
    cotangent,
    lengths,
    lower_bound,
    query_weight,
    forget_weight,
    input_weight,
    gate_weight,
    out_weight,
    swiglu_gate,
    swiglu_up,
    swiglu_down,
    first_gain,
    group_gain,
    second_gain,
):
    place = lax.axis_index("seq")
    z, x = place // X, place % X
    rows, model = tokens_in.shape
    wide = model // Z
    narrow = model // (Z * X)
    width = query_weight.shape[1] // X
    share_rows = rows // 4
    token_count = rows * Z * X

    def share(entries):
        return cut(entries, lax.axis_index("mp"), share_rows, 0)

    in_weights = (query_weight, forget_weight, input_weight, gate_weight)
    split = first_kernel(tokens_in, out_weight, swiglu_gate, swiglu_up, swiglu_down, 1)
    mixed = mixer_kernel(
        split.all,
        tokens_in,
        cotangent,
        lengths,
        lower_bound,
        in_weights,
        split,
        first_gain,
        group_gain,
        second_gain,
        2,
    )
    fed = feed_forward_kernel(
        mixed.normed_two, mixed.all_cotangent, mixed.grad_hidden, split, 3
    )

    def tiles(first, count):
        return partial(
            tile_parts,
            fed.all_normed_two,
            mixed.all_cotangent,
            mixed.grad_hidden,
            fed.late,
            split,
            first,
            count,
        )

    early = 5
    late = pl.cdiv(swiglu_gate.shape[1], TILE) - early
    sent = residual_kernel(
        fed.grad,
        fed.ffn,
        mixed.residual,
        cotangent,
        second_gain,
        split,
        fed.all_normed_two,
        tiles(0, early),
        early,
        4,
    )
    grad_residual = sent.grad_residual
    output = share(mixed.residual) + sent.ffn_share
    back = backward_kernel(
        mixed.projected,
        mixed.raw,
        mixed.states,
        sent.all_grad_mixer,
        mixed.normed_cols,
        grad_residual,
        sent.second,
        in_weights,
        lower_bound,
        group_gain,
        lengths,
        5,
    )
    second_cols = jnp.sum(back.second_cols[:, :, 0], (0, 1))
    out_block = dot(back.residual_cols.reshape(token_count, wide), mixed.mixer, 0, 0)
    last = last_kernel(
        back.grads,
        jnp.broadcast_to(back.group, (8, width)),
        [*(back[f"block_{index}"] for index in range(4)), out_block],
        jnp.concatenate([back.sums[:, :narrow], back.sums[:, narrow:]]),
        in_weights,
        sent.normed_high,
        sent.normed_low,
        tiles(early, late),
        late,
        6,
    )
    grad_group = in_order(x == 0, back.group[0], last.other_group[0], 0)
    *weight_grads, grad_outw = (
        jnp.concatenate([last[f"swapped_{index}"][0], last[f"swapped_{index}"][1]], 1)
        for index in range(5)
    )
    grad_normed_one, first_sum = last.share, last.first_sum
    rest = swiglu_gate.shape[1] - early * TILE
    grad_sgate, grad_sup, grad_sdown = (
        jnp.concatenate([sent[name], lax.slice_in_dim(last[name], 0, rest, axis=axis)], axis)
        for name, axis in (("grad_gate", 1), ("grad_up", 1), ("grad_down", 0))
    )
    tokens_share = share(tokens_in)
    scale_one = rms(tokens_share)
    pulled_one = grad_normed_one * first_gain
    grad_tokens = (
        share(grad_residual)
        + scale_one * pulled_one
        - tokens_share * scale_one**3 * jnp.mean(pulled_one * tokens_share, -1, keepdims=True)
    )
    return (
        output,
        grad_tokens,
        *weight_grads,
        jnp.transpose(grad_outw),
        grad_sgate,
        grad_sup,
        grad_sdown,
        first_sum[0] / cut(first_gain, place, narrow, 0),
        cut(grad_group, place, group_gain.shape[0] // (Z * X), 0),
        cut(second_cols, x, narrow, 0),
    )


def solution(mesh):
    in_specs = (
        P("seq", None),
        P("seq", None),
        P(),
        P("mp"),
        P(None, "mp"),
        P(None, "mp"),
        P(None, "mp"),
        P(None, "mp"),
        P("mp", None),
        P(None, "mp"),
        P(None, "mp"),
        P("mp", None),
        P(),
        P("mp"),
        P(),
    )
    out_specs = (
        P(("seq", "mp"), None),
        P(("seq", "mp"), None),
        P("seq", "mp"),
        P("seq", "mp"),
        P("seq", "mp"),
        P("seq", "mp"),
        P("mp", "seq"),
        P("seq", "mp"),
        P("seq", "mp"),
        P("mp", "seq"),
        P("seq"),
        P(("mp", "seq")),
        P("seq"),
    )
    small = (mesh.shape["seq"], mesh.shape["mp"]) == (Z * X, 4)
    body = fast_shards if small else shards
    return jax.shard_map(body, mesh=mesh, in_specs=in_specs, out_specs=out_specs, check_vma=False)
```

```python
from functools import partial

import jax
import jax.numpy as jnp
from jax import lax
from jax.experimental import pallas as pl
from jax.experimental.pallas import tpu as pltpu
from jax.sharding import PartitionSpec as P

HDIM = 128
CHUNK = 128
HIGH = lax.Precision.HIGH
HIGHEST = lax.Precision.HIGHEST
norm_eps = 1e-06
group_eps = 1e-05


def dot(left, right, contract_left, contract_right, precision=HIGH):
    return lax.dot_general(
        left,
        right,
        (((contract_left,), (contract_right,)), ((), ())),
        precision=precision,
        preferred_element_type=jnp.float32,
    )


def rms(entries):
    return lax.rsqrt(jnp.mean(entries * entries, -1, keepdims=True) + norm_eps)


def silu_grad(entries):
    gate = jax.nn.sigmoid(entries)
    return gate * (1.0 + entries * (1.0 - gate))


def gather_tokens(block):
    return lax.all_gather(block, "seq", axis=0, tiled=True)


def recurrence(query_rows, key_vecs, value_rows, segment):
    token_count, width = query_rows.shape
    heads = width // HDIM
    chunks = token_count // CHUNK

    def split(entries):
        return entries.reshape(chunks, CHUNK, heads, HDIM)

    blocked = segment.reshape(chunks, CHUNK)
    last_seg = blocked[:, -1]
    first_segs = jnp.concatenate([jnp.full((1,), -1, segment.dtype), last_seg[:-1]])
    carry = (blocked == first_segs[:, None]).astype(jnp.float32)
    in_last = (blocked == last_seg[:, None]).astype(jnp.float32)
    places = jnp.arange(CHUNK)
    allowed = (places[None, :, None] >= places[None, None, :]) & (
        blocked[:, :, None] == blocked[:, None, :]
    )
    lower = (places[:, None] >= places[None, :]).astype(jnp.float32)
    queries, keys, values = split(query_rows), split(key_vecs), split(value_rows)
    log_decay = jnp.einsum("ts,cshk->cthk", lower, jnp.log1p(-keys), precision=HIGHEST)
    growth = jnp.exp(log_decay)
    grown = queries * growth
    last = log_decay[:, -1]
    scores = jnp.einsum("cthk,cshk->chts", grown, keys * jnp.exp(-log_decay), precision=HIGH)
    scores = jnp.where(allowed[:, None], scores, 0.0)
    inner = jnp.einsum("chts,cshv->cthv", scores, values, precision=HIGH)
    weighted = keys * jnp.exp(last[:, None] - log_decay) * in_last[:, :, None, None]
    updates = jnp.einsum("cshk,cshv->chkv", weighted, values, precision=HIGH)
    through = jnp.exp(last) * carry[:, -1][:, None, None]
    state = jnp.zeros_like(updates[0])
    states = []
    for chunk in range(chunks):
        states.append(state)
        state = state * through[chunk][:, :, None] + updates[chunk]
    outer = jnp.einsum(
        "cthk,chkv->cthv", grown * carry[:, :, None, None], jnp.stack(states), precision=HIGH
    )
    return (inner + outer).reshape(token_count, width)


def mixer_all(pre_query, pre_forget, value_rows, gate_in, group_gain, lower_bound, segment):
    key_vecs = (1.0 - lower_bound) * jax.nn.sigmoid(-pre_forget)
    raw = recurrence(jax.nn.silu(pre_query), key_vecs, value_rows, segment)
    heads = raw.reshape(raw.shape[0], -1, HDIM)
    scale = lax.rsqrt(jnp.mean(heads * heads, -1, keepdims=True) + group_eps)
    normed = (heads * scale).reshape(raw.shape)
    return normed * group_gain * jax.nn.silu(gate_in)


def shards(
    tokens_in,
    cotangent,
    lengths,
    lower_bound,
    query_weight,
    forget_weight,
    input_weight,
    gate_weight,
    out_weight,
    swiglu_gate,
    swiglu_up,
    swiglu_down,
    first_gain,
    group_gain,
    second_gain,
):
    seq_count = lax.axis_size("seq")
    seq_place = lax.axis_index("seq")
    own_rows, model = tokens_in.shape
    token_count = own_rows * seq_count
    share_rows = own_rows // lax.axis_size("mp")
    share_start = lax.axis_index("mp") * share_rows
    start_row = seq_place * own_rows
    own_cols = model // seq_count
    start_col = seq_place * own_cols

    def own(entries):
        return lax.dynamic_slice_in_dim(entries, start_row, own_rows, 0)

    def columns(entries):
        return lax.dynamic_slice_in_dim(entries, start_col, own_cols, 1)

    def share(entries):
        return lax.dynamic_slice_in_dim(entries, share_start, share_rows, 0)

    positions = jnp.arange(token_count, dtype=jnp.int32)
    offsets = jnp.cumsum(lengths) - lengths
    segment = jnp.sum((positions[:, None] >= offsets[None, :]).astype(jnp.int32), 1) - 1

    all_tokens = gather_tokens(tokens_in)
    all_cotangent = gather_tokens(cotangent)
    normed_one = all_tokens * rms(all_tokens) * first_gain
    pre_query = dot(normed_one, query_weight, 1, 0)
    pre_forget = dot(normed_one, forget_weight, 1, 0)
    value_rows = dot(normed_one, input_weight, 1, 0)
    gate_in = dot(normed_one, gate_weight, 1, 0)
    mixer, mixer_back = jax.vjp(
        partial(mixer_all, lower_bound=lower_bound, segment=segment),
        pre_query,
        pre_forget,
        value_rows,
        gate_in,
        group_gain,
    )
    residual = tokens_in + lax.psum(dot(own(mixer), out_weight, 1, 0), "mp")
    scale_two = rms(residual)
    normed_two = residual * scale_two * second_gain
    grad_hidden_all = dot(all_cotangent, swiglu_down, 1, 1)
    a = dot(normed_two, swiglu_gate, 1, 0)
    b = dot(normed_two, swiglu_up, 1, 0)
    silu_a = jax.nn.silu(a)
    ffn_part = dot(silu_a * b, swiglu_down, 1, 0)
    output = share(residual) + lax.psum_scatter(ffn_part, "mp", scatter_dimension=0, tiled=True)
    e = own(grad_hidden_all)
    grad_a = e * b * silu_grad(a)
    grad_b = e * silu_a
    grad_normed_two = lax.psum(
        dot(grad_a, swiglu_gate, 1, 1) + dot(grad_b, swiglu_up, 1, 1), "mp"
    )
    pulled = grad_normed_two * second_gain
    grad_residual = (
        cotangent
        + scale_two * pulled
        - residual * scale_two**3 * jnp.mean(pulled * residual, -1, keepdims=True)
    )
    all_normed_two = gather_tokens(normed_two)
    a_all = dot(all_normed_two, swiglu_gate, 1, 0)
    b_all = dot(all_normed_two, swiglu_up, 1, 0)
    silu_all = jax.nn.silu(a_all)
    hidden_all = silu_all * b_all
    grad_a_all = grad_hidden_all * b_all * silu_grad(a_all)
    grad_b_all = grad_hidden_all * silu_all
    normed_two_cols = columns(all_normed_two)
    grad_sgate = dot(normed_two_cols, grad_a_all, 0, 0)
    grad_sup = dot(normed_two_cols, grad_b_all, 0, 0)
    grad_sdown = dot(hidden_all, columns(all_cotangent), 0, 0)

    grad_mixer = gather_tokens(dot(grad_residual, out_weight, 1, 1))
    residual_cols = lax.all_to_all(grad_residual, "seq", 1, 0, tiled=True)
    grad_outw = dot(mixer, residual_cols, 0, 0)
    grad_query_rows, grad_forget_rows, grad_value_rows, grad_gate_rows, grad_group = mixer_back(
        grad_mixer
    )
    grad_group = lax.dynamic_slice_in_dim(
        grad_group, seq_place * (group_gain.shape[0] // seq_count), group_gain.shape[0] // seq_count
    )
    normed_one_cols = columns(normed_one)
    pairs = (
        (grad_query_rows, query_weight),
        (grad_forget_rows, forget_weight),
        (grad_value_rows, input_weight),
        (grad_gate_rows, gate_weight),
    )
    weight_grads = []
    normed_part = 0.0
    first_sum = 0.0
    for grad_rows, weight in pairs:
        weight_grad = dot(normed_one_cols, grad_rows, 0, 0)
        weight_grads.append(weight_grad)
        normed_part = normed_part + dot(own(grad_rows), weight, 1, 1)
        own_weight = lax.dynamic_slice_in_dim(weight, start_col, own_cols, 0)
        first_sum = first_sum + jnp.sum(own_weight * weight_grad, 1)
    second_sum = jnp.sum(
        lax.dynamic_slice_in_dim(swiglu_gate, start_col, own_cols, 0) * grad_sgate
        + lax.dynamic_slice_in_dim(swiglu_up, start_col, own_cols, 0) * grad_sup,
        1,
    )
    gains = jnp.stack(
        [
            lax.dynamic_slice_in_dim(first_gain, start_col, own_cols),
            lax.dynamic_slice_in_dim(second_gain, start_col, own_cols),
        ]
    )
    gain_grads = lax.psum(jnp.stack([first_sum, second_sum]), "mp") / gains
    grad_normed_one = lax.psum_scatter(normed_part, "mp", scatter_dimension=0, tiled=True)
    tokens_share = share(tokens_in)
    scale_one = rms(tokens_share)
    pulled_one = grad_normed_one * first_gain
    grad_tokens = (
        share(grad_residual)
        + scale_one * pulled_one
        - tokens_share * scale_one**3 * jnp.mean(pulled_one * tokens_share, -1, keepdims=True)
    )
    return (
        output,
        grad_tokens,
        weight_grads[0],
        weight_grads[1],
        weight_grads[2],
        weight_grads[3],
        grad_outw,
        grad_sgate,
        grad_sup,
        grad_sdown,
        gain_grads[0],
        grad_group,
        gain_grads[1],
    )


Z, X = 4, 2


def x_swap(array):
    return lax.ppermute(array, "seq", [(s, s ^ 1) for s in range(Z * X)])


def cut(array, place, size, axis):
    return lax.dynamic_slice_in_dim(array, place * size, size, axis)


def in_order(first, mine, other, axis):
    return jnp.where(
        first, jnp.concatenate([mine, other], axis), jnp.concatenate([other, mine], axis)
    )


F32, BF16 = jnp.float32, jnp.bfloat16
MESH = pl.DeviceIdType.MESH
ANY = pl.BlockSpec(memory_space=pl.ANY)
WHOLE = pl.BlockSpec(memory_space=pltpu.VMEM)
TILE = 256
VMEM_BYTES = 60 << 20


def halves(entries):
    high = entries.astype(BF16)
    return high, (entries - high.astype(F32)).astype(BF16)


def product(left, right, contract_left, contract_right):
    return lax.dot_general(
        left,
        right,
        (((contract_left,), (contract_right,)), ((), ())),
        preferred_element_type=F32,
    )


def three_pass(left, right, contract_left, contract_right):
    (left_high, left_low), (right_high, right_low) = left, right
    return product(left_high, right_high, contract_left, contract_right) + (
        product(left_high, right_low, contract_left, contract_right)
        + product(left_low, right_high, contract_left, contract_right)
    )


def few_rows(left, right, contract_right):
    (left_high, left_low), (right_high, right_low) = left, right
    rows = left_high.shape[0]
    both = product(jnp.concatenate([left_high, left_low]), right_high, 1, contract_right)
    return both[:rows] + (product(left_high, right_low, 1, contract_right) + both[rows:])


def remote(src, dst, sems, index, device):
    return pltpu.make_async_remote_copy(
        src_ref=src,
        dst_ref=dst,
        send_sem=sems[0].at[index],
        recv_sem=sems[1].at[index],
        device_id=device,
        device_id_type=MESH,
    )


def dma_sems(count):
    return [pltpu.SemaphoreType.DMA((count,)), pltpu.SemaphoreType.DMA((count,))]


class Move:
    def __init__(self, ins, outs, scratch):
        self.ins, self.outs, self.scratch_refs = ins, outs, scratch
        place, part = lax.axis_index("seq"), lax.axis_index("mp")
        self.z, self.x, self.y, self.core = place // X, place % X, part // 2, part % 2
        self.setup()

    def setup(self):
        pass

    def device(self, z, x, y, core):
        return (z * X + x, y * 2 + core)

    def x_peer(self):
        return self.device(self.z, 1 - self.x, self.y, self.core)

    def y_peer(self):
        return self.device(self.z, self.x, 1 - self.y, self.core)

    def core_peer(self):
        return self.device(self.z, self.x, self.y, 1 - self.core)

    def holds(self, way, step):
        source = self.z - way * step
        return (source >= 0) & (source < Z)

    def goes_on(self, way, step):
        return self.holds(way, step - 1) & (self.z + way >= 0) & (self.z + way < Z)

    def each(self, step, action):
        if step == 0:
            action(1)
        else:
            for way in (1, -1):
                pl.when(self.holds(way, step))(lambda way=way: action(way))

    def greet(self, far):
        barrier = pltpu.get_barrier_semaphore()

        def signal(device):
            pl.semaphore_signal(barrier, inc=1, device_id=device, device_id_type=MESH)

        signal(self.x_peer())
        signal(self.y_peer())
        signal(self.core_peer())
        if far:
            for distance in range(1, Z):
                signal(self.device((self.z + distance) % Z, self.x, self.y, self.core))
            pl.semaphore_wait(barrier, 3 + Z - 1)
        else:
            for way in (1, -1):
                ahead = (self.z + way >= 0) & (self.z + way < Z)
                pl.when(ahead)(
                    lambda way=way: signal(self.device(self.z + way, self.x, self.y, self.core))
                )
            neighbours = jnp.where(self.z > 0, 1, 0) + jnp.where(self.z < Z - 1, 1, 0)
            pl.semaphore_wait(barrier, 3 + neighbours)


class Gather(Move):
    PIECES = 2
    OWN = 5

    def in_specs(arrays):
        return [ANY]

    def results(arrays):
        return [((Z * X * arrays[0].shape[0], arrays[0].shape[1]), ANY)]

    def scratch(arrays):
        return [*dma_sems(52 * Gather.PIECES), pltpu.SemaphoreType.DMA((1,))]

    def setup(self):
        (self.block,), (self.out,) = self.ins, self.outs
        self.sems, self.local = self.scratch_refs[:2], self.scratch_refs[2]
        self.rows = self.block.shape[0]
        self.size = self.rows // self.PIECES
        self.tile = self.block.shape[1] // 16

    def cols(self, first, count):
        return pl.ds(pl.multiple_of(first * self.tile, self.tile), count * self.tile)

    def columns(self, y, core):
        return self.cols((16 - 2 * self.OWN) * y + self.OWN * core, self.OWN)

    def y_count(self, big):
        most = min(16 - 2 * self.OWN, self.OWN)
        return most if big else 16 - 2 * self.OWN - most

    def y_columns(self, y, big):
        count = self.y_count(big)
        first = (16 - count) * y if big else self.OWN * (1 - y) + 2 * self.OWN * y
        return self.cols(first, count)

    def region(self, z, x, piece, columns):
        row = (z * X + x) * self.rows + piece * self.size
        return self.out.at[pl.ds(pl.multiple_of(row, self.size), self.size), columns]

    def fetched(self, z, x, piece):
        return self.region(z, x, piece, self.columns(self.y, self.core))

    def own(self, piece):
        return self.block.at[
            pl.ds(piece * self.size, self.size), self.columns(self.y, self.core)
        ]

    def slot(self, way, step):
        return 0 if step == 0 else (0 if way > 0 else 3) + step

    def along(self, way, step, piece, arriving):
        dst = self.fetched(self.z - way * (step if arriving else step - 1), self.x, piece)
        return remote(
            self.own(piece) if step == 1 and not arriving else dst,
            dst,
            self.sems,
            52 * piece + (0 if way > 0 else 3) + step - 1,
            self.device(self.z + way, self.x, self.y, self.core),
        )

    def across(self, way, step, piece, arriving):
        dst = self.fetched(self.z - way * step, 1 - self.x if arriving else self.x, piece)
        return remote(
            self.own(piece) if step == 0 and not arriving else dst,
            dst,
            self.sems,
            52 * piece + 6 + self.slot(way, step),
            self.x_peer(),
        )

    def inside(self, way, step, other_x, piece, arriving):
        region = self.region(
            self.z - way * step,
            1 - self.x if other_x else self.x,
            piece,
            self.columns(self.y, 1 - self.core if arriving else self.core),
        )
        index = 52 * piece + 13 + self.slot(way, step) + (0 if other_x else 6)
        return remote(region, region, self.sems, index, self.core_peer())

    def over_y(self, way, step, other_x, piece, arriving, big):
        region = self.region(
            self.z - way * step,
            1 - self.x if other_x else self.x,
            piece,
            self.y_columns(1 - self.y if arriving else self.y, big),
        )
        index = 52 * piece + 26 + self.slot(way, step) + (0 if other_x else 6)
        return remote(region, region, self.sems, index, self.y_peer())

    def inside_y(self, way, step, other_x, piece, big):
        region = self.region(
            self.z - way * step,
            1 - self.x if other_x else self.x,
            piece,
            self.y_columns(1 - self.y, big),
        )
        index = 52 * piece + 39 + self.slot(way, step) + (0 if other_x else 6)
        return remote(region, region, self.sems, index, self.core_peer())

    def sized(self, big, action):
        if self.y_count(True):
            pl.when(big)(lambda: action(True))
        if self.y_count(False):
            pl.when(jnp.logical_not(big))(lambda: action(False))

    def pass_on(self, way, step, other_x, piece):
        self.sized(
            self.core == self.y,
            lambda big: self.over_y(way, step, other_x, piece, False, big).start(),
        )
        self.inside(way, step, other_x, piece, False).start()

    def begin(self):
        for piece in range(self.PIECES):
            self.across(1, 0, piece, False).start()
            for way in (1, -1):
                pl.when(self.goes_on(way, 1))(
                    lambda way=way, piece=piece: self.along(way, 1, piece, False).start()
                )
        self.own_copy().start()

    def own_copy(self):
        row = pl.multiple_of((self.z * X + self.x) * self.rows, self.rows)
        return pltpu.make_async_copy(
            self.block, self.out.at[pl.ds(row, self.rows), :], self.local.at[0]
        )

    def arrive_along(self, step, piece):
        def action(way):
            self.along(way, step, piece, True).wait_recv()
            if step < Z - 1:
                pl.when(self.goes_on(way, step + 1))(
                    lambda: self.along(way, step + 1, piece, False).start()
                )
            self.across(way, step, piece, False).start()
            self.pass_on(way, step, False, piece)

        self.each(step, action)

    def arrive_across(self, step, piece):
        def action(way):
            self.across(way, step, piece, True).wait_recv()
            self.pass_on(way, step, True, piece)

        self.each(step, action)

    def arrive_y(self, step, other_x, piece):
        def action(way):
            def sized(big):
                self.over_y(way, step, other_x, piece, True, big).wait_recv()
                self.inside_y(way, step, other_x, piece, big).start()

            self.sized(self.core != self.y, sized)

        self.each(step, action)

    def finish(self):
        self.own_copy().wait()
        for piece in range(self.PIECES):
            for way in (1, -1):
                for step in range(1, Z):
                    pl.when(self.goes_on(way, step))(
                        lambda way=way, step=step, piece=piece: self.along(
                            way, step, piece, False
                        ).wait_send()
                    )
            for step in range(Z):

                def action(way, step=step, piece=piece):
                    self.across(way, step, piece, False).wait_send()
                    for other_x in (False, True) if step else (True,):
                        self.inside(way, step, other_x, piece, False).wait_send()
                        self.inside(way, step, other_x, piece, True).wait_recv()

                        def sent(big, other_x=other_x):
                            self.over_y(way, step, other_x, piece, False, big).wait_send()
                            self.inside_y(way, step, other_x, piece, big).wait_recv()

                        def handed(big, other_x=other_x):
                            self.inside_y(way, step, other_x, piece, big).wait_send()

                        self.sized(self.core == self.y, sent)
                        self.sized(self.core != self.y, handed)

                self.each(step, action)

    def events(self):
        def round_of(index):
            step, piece = index // 2 + 1, index % 2

            def event():
                if step < Z:
                    self.arrive_along(step, piece)
                if step <= Z:
                    self.arrive_across(step - 1, piece)
                if 1 <= step - 1 < Z:
                    self.arrive_y(step - 1, False, piece)
                if 0 <= step - 2 < Z:
                    self.arrive_y(step - 2, True, piece)

            return event

        return [round_of(index) for index in range(2 * (Z + 1))] + [self.finish]


class Gather12(Gather):
    OWN = 6


class Sum(Move):
    def in_specs(arrays):
        return [WHOLE]

    def results(arrays):
        return [(arrays[0].shape, WHOLE)]

    def scratch(arrays):
        rows, columns = arrays[0].shape
        return [pltpu.VMEM((4, rows, columns // 2), F32), *dma_sems(3)]

    def setup(self):
        (self.part,), (self.out,) = self.ins, self.outs
        self.landing, self.sems = self.scratch_refs[0], self.scratch_refs[1:]
        self.half = self.part.shape[1] // 2

    def columns(self, ref, core):
        return ref.at[:, pl.ds(pl.multiple_of(core * self.half, self.half), self.half)]

    def first(self):
        return remote(
            self.columns(self.part, 1 - self.core),
            self.landing.at[0],
            self.sems,
            0,
            self.core_peer(),
        )

    def second(self):
        return remote(self.landing.at[1], self.landing.at[2], self.sems, 1, self.y_peer())

    def third(self):
        return remote(self.landing.at[1], self.landing.at[3], self.sems, 2, self.core_peer())

    def begin(self):
        self.first().start()

    def to_y(self):
        self.first().wait()
        self.landing[1] = self.columns(self.part, self.core)[...] + self.landing[0]
        self.second().start()

    def back(self):
        self.second().wait()
        self.landing[1] = self.landing[1] + self.landing[2]
        self.third().start()

    def finish(self):
        self.third().wait()
        self.columns(self.out, self.core)[...] = self.landing[1]
        self.columns(self.out, 1 - self.core)[...] = self.landing[3]

    def events(self):
        return [self.to_y, self.back, self.finish]


class Scatter(Move):
    def in_specs(arrays):
        return [WHOLE]

    def results(arrays):
        rows, columns = arrays[0].shape
        return [((rows // 4, columns), WHOLE)]

    def scratch(arrays):
        rows, columns = arrays[0].shape
        return [pltpu.VMEM((5, rows // 4, columns), F32), *dma_sems(3)]

    def setup(self):
        (self.part,), (self.out,) = self.ins, self.outs
        self.landing, self.sems = self.scratch_refs[0], self.scratch_refs[1:]
        self.rows = self.part.shape[0] // 4

    def block(self, y, core):
        row = pl.multiple_of((y * 2 + core) * self.rows, self.rows)
        return self.part.at[pl.ds(row, self.rows), :]

    def to_core(self, y):
        block = self.block(self.y if y == 0 else 1 - self.y, 1 - self.core)
        return remote(block, self.landing.at[y], self.sems, y, self.core_peer())

    def to_y(self):
        return remote(self.landing.at[2], self.landing.at[3], self.sems, 2, self.y_peer())

    def begin(self):
        self.to_core(1).start()
        self.to_core(0).start()

    def middle(self):
        self.to_core(1).wait()
        self.landing[2] = self.block(1 - self.y, self.core)[...] + self.landing[1]
        self.to_y().start()

    def finish(self):
        self.to_core(0).wait()
        self.to_y().wait()
        self.out[...] = (self.block(self.y, self.core)[...] + self.landing[0]) + self.landing[3]

    def events(self):
        return [self.middle, self.finish]


class Heads(Move):
    def in_specs(arrays):
        return [ANY]

    def results(arrays):
        rows, columns = arrays[0].shape
        return [((Z * X * rows, columns // X), ANY)]

    def scratch(arrays):
        return [*dma_sems(7), pltpu.SemaphoreType.DMA((1,))]

    def setup(self):
        (self.own,), (self.out,) = self.ins, self.outs
        self.sems, self.local = self.scratch_refs[:2], self.scratch_refs[2]
        self.rows, columns = self.own.shape
        self.width = columns // X

    def block(self, z, x):
        row = pl.multiple_of((z * X + x) * self.rows, self.rows)
        return self.out.at[pl.ds(row, self.rows), :]

    def plane(self, z):
        row = pl.multiple_of(z * X * self.rows, X * self.rows)
        return self.out.at[pl.ds(row, X * self.rows), :]

    def own_columns(self, x):
        return self.own.at[:, pl.ds(pl.multiple_of(x * self.width, self.width), self.width)]

    def swap(self):
        return remote(
            self.own_columns(1 - self.x), self.block(self.z, self.x), self.sems, 6, self.x_peer()
        )

    def keep(self):
        return pltpu.make_async_copy(
            self.own_columns(self.x), self.block(self.z, self.x), self.local.at[0]
        )

    def along(self, way, step, arriving):
        plane = self.plane(self.z - way * (step if arriving else step - 1))
        return remote(
            plane,
            plane,
            self.sems,
            (0 if way > 0 else 3) + step - 1,
            self.device(self.z + way, self.x, self.y, self.core),
        )

    def begin(self):
        self.swap().start()
        self.keep().start()

    def start_along(self, way, step):
        pl.when(self.goes_on(way, step))(lambda: self.along(way, step, False).start())

    def swapped(self):
        self.swap().wait()
        self.keep().wait()
        for way in (1, -1):
            self.start_along(way, 1)

    def arrive(self, step):
        def action(way):
            self.along(way, step, True).wait_recv()
            if step < Z - 1:
                self.start_along(way, step + 1)

        self.each(step, action)

    def finish(self):
        self.arrive(Z - 1)
        for way in (1, -1):
            for step in range(1, Z):
                pl.when(self.goes_on(way, step))(
                    lambda way=way, step=step: self.along(way, step, False).wait_send()
                )

    def events(self):
        return [self.swapped, lambda: self.arrive(1), lambda: self.arrive(2), self.finish]


class Columns(Move):
    def in_specs(arrays):
        return [ANY]

    def results(arrays):
        rows, columns = arrays[0].shape
        return [((Z, X, rows, columns // Z), ANY)]

    def scratch(arrays):
        return [*dma_sems(Z + Z + 1), pltpu.SemaphoreType.DMA((1,))]

    def setup(self):
        (self.own,), (self.out,) = self.ins, self.outs
        self.sems, self.local = self.scratch_refs[:2], self.scratch_refs[2]
        self.half = self.own.shape[1] // (2 * Z)

    def piece(self, z):
        start = pl.multiple_of((z * 2 + self.core) * self.half, self.half)
        return self.own.at[:, pl.ds(start, self.half)]

    def landing(self, z, x, core):
        start = pl.multiple_of(core * self.half, self.half)
        return self.out.at[z, x, :, pl.ds(start, self.half)]

    def along(self, distance):
        z = (self.z + distance) % Z
        return remote(
            self.piece(z),
            self.landing(self.z, self.x, self.core),
            self.sems,
            distance,
            self.device(z, self.x, self.y, self.core),
        )

    def keep(self):
        return pltpu.make_async_copy(
            self.piece(self.z), self.landing(self.z, self.x, self.core), self.local.at[0]
        )

    def across(self, distance):
        block = self.landing((self.z - distance) % Z, self.x, self.core)
        return remote(block, block, self.sems, Z + distance, self.x_peer())

    def inside(self):
        start = pl.multiple_of(self.core * self.half, self.half)
        part = self.out.at[:, :, :, pl.ds(start, self.half)]
        return remote(part, part, self.sems, 2 * Z, self.core_peer())

    def begin(self):
        self.keep().start()
        for distance in (1, 3, 2):
            self.along(distance).start()

    def arrived(self, distance):
        if distance == 0:
            self.keep().wait()
        else:
            self.along(distance).wait()
        self.across(distance).start()

    def all_here(self):
        for distance in range(Z):
            self.across(distance).wait()
        self.inside().start()

    def events(self):
        return [
            lambda: self.arrived(0),
            lambda: self.arrived(1),
            lambda: self.arrived(3),
            lambda: self.arrived(2),
            self.all_here,
            lambda: self.inside().wait(),
        ]


class SwapX(Move):
    def in_specs(arrays):
        return [ANY] * len(arrays)

    def results(arrays):
        return [(array.shape, ANY) for array in arrays]

    def scratch(arrays):
        return dma_sems(len(arrays))

    def setup(self):
        pass

    def copies(self):
        return [
            remote(src, dst, self.scratch_refs, index, self.x_peer())
            for index, (src, dst) in enumerate(zip(self.ins, self.outs, strict=True))
        ]

    def begin(self):
        for copy in self.copies():
            copy.start()

    def finish(self):
        for copy in self.copies():
            copy.wait()

    def events(self):
        return [self.finish]


class SwapBlocks(Move):
    def in_specs(arrays):
        return [ANY] * len(arrays)

    def results(arrays):
        return [((array.shape[0] // X, array.shape[1]), ANY) for array in arrays]

    def scratch(arrays):
        return dma_sems(len(arrays))

    def send(self, index):
        src = self.ins[index]
        rows = src.shape[0] // X
        return remote(
            src.at[pl.ds(pl.multiple_of((1 - self.x) * rows, rows), rows), :],
            self.outs[index],
            self.scratch_refs,
            index,
            self.x_peer(),
        )

    def begin(self):
        for index in range(len(self.ins)):
            self.send(index).start()

    def finish(self):
        for index in range(len(self.ins)):
            self.send(index).wait()

    def events(self):
        return [self.finish]


class SumAll(Move):
    def in_specs(arrays):
        return [WHOLE]

    def results(arrays):
        rows, columns = arrays[0].shape
        return [((rows // X, columns), WHOLE)]

    def scratch(arrays):
        rows, columns = arrays[0].shape
        return [pltpu.VMEM((6, rows // X, columns), F32), *dma_sems(3)]

    def setup(self):
        (self.part,), (self.out,) = self.ins, self.outs
        self.landing, self.sems = self.scratch_refs[0], self.scratch_refs[1:]
        self.rows = self.part.shape[0] // X

    def half(self, x):
        return self.part.at[pl.ds(pl.multiple_of(x * self.rows, self.rows), self.rows), :]

    def first(self):
        return remote(self.half(1 - self.x), self.landing.at[0], self.sems, 0, self.x_peer())

    def second(self):
        return remote(self.landing.at[1], self.landing.at[2], self.sems, 1, self.core_peer())

    def third(self):
        return remote(self.landing.at[3], self.landing.at[4], self.sems, 2, self.y_peer())

    def begin(self):
        self.first().start()

    def to_core(self):
        self.first().wait()
        self.landing[1] = self.half(self.x)[...] + self.landing[0]
        self.second().start()

    def to_y(self):
        self.second().wait()
        self.landing[3] = self.landing[1] + self.landing[2]
        self.third().start()

    def finish(self):
        self.third().wait()
        self.out[...] = self.landing[3] + self.landing[4]

    def events(self):
        return [self.to_core, self.to_y, self.finish]


class Refs(dict):
    __getattr__ = dict.__getitem__


def fused(arrays, results, scratch, steps, body, collective_id, far=False, flops=0):
    names = [*arrays, *results, *scratch]

    def kernel(*refs):
        refs = list(refs)
        here = Refs(zip([*arrays, *results], refs, strict=False))
        del refs[: len(arrays) + len(results)]
        for name, needed in scratch.items():
            here[name] = refs[: len(needed)]
            del refs[: len(needed)]
        step = pl.program_id(0)
        if collective_id is not None:
            pl.when(step == 0)(lambda: Move([], [], []).greet(far))
        body(here, step)

    outputs = pl.pallas_call(
        kernel,
        grid=(steps,),
        out_shape=[
            jax.ShapeDtypeStruct(result[0], result[2] if len(result) > 2 else F32)
            for result in results.values()
        ],
        in_specs=[spec for _, spec in arrays.values()],
        out_specs=[result[1] for result in results.values()],
        scratch_shapes=[one for needed in scratch.values() for one in needed],
        compiler_params=pltpu.CompilerParams(
            has_side_effects=True,
            vmem_limit_bytes=VMEM_BYTES,
            **({} if collective_id is None else dict(collective_id=collective_id)),
        ),
        cost_estimate=pl.CostEstimate(flops=flops, bytes_accessed=32 << 20, transcendentals=0),
    )(*(array for array, _ in arrays.values()))
    return Refs(zip(results, outputs, strict=True))


def at(now, when, *actions):
    for action in actions:
        pl.when(now == when)(action)


def schedule(now, when, events):
    for event, moment in zip(events, when, strict=True):
        pl.when(now == moment)(event)


SPLIT_ROWS = 128


def first_kernel(block, out_weight, w_gate, w_up, w_down, collective_id):
    inner, columns = w_gate.shape
    padded = pl.cdiv(columns, TILE) * TILE
    steps = inner // SPLIT_ROWS
    down_steps = padded // SPLIT_ROWS
    out_rows = out_weight.shape[0] // steps

    def body(refs, step):
        gather = Gather12([refs.block], [refs.all], refs.gather)
        pl.when(step == 0)(gather.begin)

        def store(name, entries, spot):
            refs[f"{name}_high"][:, spot], refs[f"{name}_low"][:, spot] = halves(entries)

        whole = slice(None)
        store("out", refs.out[...], whole)
        for name in ("gate", "up"):
            store(name, refs[name][...], slice(0, columns))
            for half in ("high", "low"):
                refs[f"{name}_{half}"][:, columns:] = jnp.zeros(
                    (SPLIT_ROWS, padded - columns), BF16
                )
        row = jnp.minimum(step, down_steps - 1) * SPLIT_ROWS + lax.broadcasted_iota(
            jnp.int32, (SPLIT_ROWS, inner), 0
        )
        down = jnp.where(row < columns, refs.down[...], 0.0)
        store("down", down, whole)
        store("turned", jnp.transpose(down), whole)
        schedule(step, (2, 3, 5, 6, 8, 10, 11, 13, 14, 15, 15), gather.events())

    def by_rows(rows, columns, last=steps - 1):
        return pl.BlockSpec((rows, columns), lambda step: (jnp.minimum(step, last), 0))

    results = dict(all=Gather.results([block])[0])
    for half in ("high", "low"):
        for name in ("gate", "up"):
            results[f"{name}_{half}"] = ((inner, padded), by_rows(SPLIT_ROWS, padded), BF16)
        results[f"out_{half}"] = (out_weight.shape, by_rows(out_rows, inner), BF16)
        results[f"down_{half}"] = (
            (padded, inner), by_rows(SPLIT_ROWS, inner, down_steps - 1), BF16
        )
        results[f"turned_{half}"] = (
            (inner, padded),
            pl.BlockSpec(
                (inner, SPLIT_ROWS), lambda step: (0, jnp.minimum(step, down_steps - 1))
            ),
            BF16,
        )
    return fused(
        dict(
            block=(block, WHOLE),
            gate=(w_gate, by_rows(SPLIT_ROWS, columns)),
            up=(w_up, by_rows(SPLIT_ROWS, columns)),
            down=(w_down, by_rows(SPLIT_ROWS, inner, pl.cdiv(columns, SPLIT_ROWS) - 1)),
            out=(out_weight, by_rows(out_rows, inner)),
        ),
        results,
        dict(gather=Gather.scratch([block])),
        steps,
        body,
        collective_id,
    )


def halves_scratch(rows, inner):
    return [
        pltpu.VMEM((rows, inner), BF16),
        pltpu.VMEM((rows, inner), BF16),
        pltpu.VMEM((rows // 128, 128, inner), F32),
        pltpu.SemaphoreType.DMA((rows // 128,)),
    ]


def load_halves(src_ref, high_ref, low_ref, stage_ref, sem, change=None, start=True, split=True):
    count, rows, _ = stage_ref.shape

    def spot(index):
        return pl.ds(pl.multiple_of(index * rows, rows), rows)

    def fetch(index):
        return pltpu.make_async_copy(
            src_ref.at[spot(index), :], stage_ref.at[index], sem.at[index]
        )

    def one(index, carried):
        fetch(index).wait()
        if change is not None:
            change(index)
        high, low = halves(stage_ref[index])
        high_ref[spot(index), :] = high
        low_ref[spot(index), :] = low
        return carried

    if start:
        for index in range(count):
            fetch(index).start()
    if split:
        lax.fori_loop(0, count, one, 0)


STRIP = 512


def strips(rows, action):
    def one(index, carried):
        action(index, pl.ds(pl.multiple_of(index * STRIP, STRIP), STRIP))
        return carried

    lax.fori_loop(0, rows // STRIP, one, 0)


def block_fetch(src, buf, sem, index):
    return pltpu.make_async_copy(src, buf.at[index], sem.at[index])


EARLY = 3


def mixer_kernel(
    all_tokens, tokens_in, cotangent, lengths, lower_bound, in_weights, split, first_gain, group_gain,
    second_gain, collective_id,
):
    rows, inner = all_tokens.shape
    own_rows = tokens_in.shape[0]
    count = 4
    wide = inner // Z
    heads = TILE // HDIM
    chunks = rows // CHUNK
    tiles = EARLY
    columns = tiles * TILE
    parts = rows // STRIP
    middle = count + chunks
    steps = middle + 1 + tiles

    def body(refs, step):
        place = lax.axis_index("seq")
        x = place % X
        here = pl.ds(pl.multiple_of(x * TILE, TILE), TILE)
        there = pl.ds(pl.multiple_of((1 - x) * TILE, TILE), TILE)
        first_col = pl.multiple_of((place // X) * wide, wide)
        gather = Gather([refs.cotangent], [refs.all_cotangent], refs.gather)
        part_ref, sum_ref, *sum_scratch = refs.sum
        total = Sum([part_ref], [sum_ref], sum_scratch)
        high_ref, low_ref, stage_ref, stage_sem = refs.halves
        weight_buf, weight_sem, down_buf, down_sem, out_buf, out_sem, ready_ref = refs.weights
        (state_ref,) = refs.state
        other_ref, send, recv = refs.swap
        now = step * parts

        def fetch(index):
            return [
                pltpu.make_async_copy(
                    refs[f"weight_{index}"].at[:, here],
                    weight_buf.at[index % 2],
                    weight_sem.at[index % 2],
                )
            ]

        def fetch_down(tile):
            slot = lax.rem(tile, 2)
            spot = pl.ds(pl.multiple_of(tile * TILE, TILE), TILE)
            return [
                pltpu.make_async_copy(
                    refs[f"turned_{half}"].at[:, spot], down_buf.at[slot, at], down_sem.at[slot, at]
                )
                for at, half in enumerate(("high", "low"))
            ]

        def start(copies):
            for copy in copies:
                copy.start()

        def wait(copies):
            for copy in copies:
                copy.wait()

        def fetch_out():
            return [
                pltpu.make_async_copy(refs[f"out_{half}"], out_buf.at[at], out_sem.at[at])
                for at, half in enumerate(("high", "low"))
            ]

        def swap():
            peer = pl.multiple_of((place + 1 - 2 * x) * own_rows, own_rows)
            return remote(
                refs.mixer.at[pl.ds(peer, own_rows), :], other_ref, (send, recv), 0, gather.x_peer()
            )

        def pause(part):
            mixing = count * parts
            schedule(
                now + part,
                (0, 1, 2, 3, 5, mixing, mixing + 2 * parts, mixing + 4 * parts, mixing + 7 * parts),
                gather.events()[:9],
            )

        def normalize(index):
            entries = stage_ref[index]
            stage_ref[index] = entries * rms(entries) * refs.first_gain[...]
            refs.normed_cols[pl.ds(pl.multiple_of(index * 128, 128), 128), :] = stage_ref[
                index, :, pl.ds(first_col, wide)
            ]

        @pl.when(step == 0)
        def _():
            gather.begin()
            start(fetch(0))
            start(fetch_out())
            load_halves(refs.tokens, high_ref, low_ref, stage_ref, stage_sem, normalize)
            state_ref[...] = jnp.zeros_like(state_ref)

        for index in range(count):

            @pl.when(step == index)
            def _(index=index):
                if index + 1 < count:
                    start(fetch(index + 1))
                wait(fetch(index))

        @pl.when(step < count)
        def _():
            ready_ref[0], ready_ref[1] = halves(weight_buf[lax.rem(step, 2)])
            target = pl.ds(pl.multiple_of(step * TILE, TILE), TILE)

            def strip(index, spot):
                refs.projected[spot, target] = three_pass(
                    (high_ref[spot, :], low_ref[spot, :]),
                    (ready_ref[0], ready_ref[1]),
                    1,
                    0,
                )
                pause(index)

            strips(rows, strip)

        @pl.when((step >= count) & (step < middle))
        def _():
            chunk = step - count
            spot = pl.ds(pl.multiple_of(chunk * CHUNK, CHUNK), CHUNK)
            forward_chunk(
                chunk,
                refs.lengths,
                refs.projected.at[spot, :],
                refs.lower_bound.at[:, here],
                refs.group_gain.at[:, here],
                refs.mixer.at[spot, :],
                refs.raw.at[spot, :],
                refs.states.at[pl.ds(chunk, 1)],
                state_ref,
            )
            pause(0)

        @pl.when(step == middle)
        def _():
            swap().start()
            start(fetch_down(0))
            wait(fetch_out())

            def out_rows(spot):
                return out_buf[0, spot, :], out_buf[1, spot, :]

            own = refs.mixer[pl.ds(pl.multiple_of(place * own_rows, own_rows), own_rows), :]
            part_ref[...] = few_rows(halves(own), out_rows(here), 0)
            swap().wait()
            part_ref[...] += few_rows(halves(other_ref[...]), out_rows(there), 0)
            total.begin()
            total.to_y()
            gather.events()[9]()
            gather.finish()
            load_halves(refs.all_cotangent, high_ref, low_ref, stage_ref, stage_sem)

        @pl.when(step > middle)
        def _():
            tile = step - middle - 1
            pl.when(tile < tiles - 1)(lambda: start(fetch_down(tile + 1)))
            wait(fetch_down(tile))
            slot = lax.rem(tile, 2)
            refs.grad_hidden[...] = three_pass(
                (high_ref[...], low_ref[...]), (down_buf[slot, 0], down_buf[slot, 1]), 1, 0
            )

        @pl.when(step == steps - 1)
        def _():
            total.back()
            total.finish()
            residual = refs.tokens_in[...] + sum_ref[...]
            refs.residual[...] = residual
            refs.normed_two[...] = residual * rms(residual) * refs.second_gain[...]

    own_shape = (own_rows, inner)
    return fused(
        dict(
            lengths=(lengths, pl.BlockSpec(memory_space=pltpu.SMEM)),
            tokens=(all_tokens, ANY),
            tokens_in=(tokens_in, WHOLE),
            cotangent=(cotangent, WHOLE),
            lower_bound=(lower_bound[None], WHOLE),
            first_gain=(first_gain[None], WHOLE),
            group_gain=(group_gain[None], WHOLE),
            second_gain=(second_gain[None], WHOLE),
            **{f"weight_{index}": (weight, ANY) for index, weight in enumerate(in_weights)},
            **{
                f"{name}_{half}": (split[f"{name}_{half}"], ANY)
                for name in ("out", "turned")
                for half in ("high", "low")
            },
        ),
        dict(
            all_cotangent=((rows, inner), ANY),
            projected=((rows, count * TILE), WHOLE),
            normed_cols=((rows, wide), WHOLE),
            mixer=((rows, TILE), WHOLE),
            raw=((rows, TILE), WHOLE),
            states=((chunks, heads, HDIM, HDIM), WHOLE),
            grad_hidden=(
                (rows, columns),
                pl.BlockSpec((rows, TILE), lambda step: (0, jnp.maximum(step - middle - 1, 0))),
            ),
            residual=(own_shape, WHOLE),
            normed_two=(own_shape, WHOLE),
        ),
        dict(
            halves=halves_scratch(rows, inner),
            weights=[
                pltpu.VMEM((2, inner, TILE), F32),
                pltpu.SemaphoreType.DMA((2,)),
                pltpu.VMEM((2, 2, inner, TILE), BF16),
                pltpu.SemaphoreType.DMA((2, 2)),
                pltpu.VMEM((2, *split.out_high.shape), BF16),
                pltpu.SemaphoreType.DMA((2,)),
                pltpu.VMEM((2, inner, TILE), BF16),
            ],
            state=[pltpu.VMEM((heads, HDIM, HDIM), F32)],
            swap=[pltpu.VMEM((own_rows, TILE), F32), *dma_sems(1)],
            gather=Gather.scratch([cotangent]),
            sum=[
                pltpu.VMEM(own_shape, F32),
                pltpu.VMEM(own_shape, F32),
                *Sum.scratch([tokens_in]),
            ],
        ),
        steps,
        body,
        collective_id,
        flops=6 * rows * inner * (count * TILE + columns),
    )


def feed_forward_kernel(normed_two, all_cotangent, grad_hidden, split, collective_id):
    rows, inner = normed_two.shape
    token_count = all_cotangent.shape[0]
    columns = split.gate_high.shape[1]
    tiles = columns // TILE

    def body(refs, step):
        gather = Gather([refs.normed_two], [refs.all_normed_two], refs.gather)
        high_ref, low_ref, stage_ref, stage_sem = refs.halves
        (e_ref,) = refs.e
        load = partial(load_halves, refs.all_cotangent, high_ref, low_ref, stage_ref, stage_sem)

        @pl.when(step == 0)
        def _():
            gather.begin()
            load(split=False)
            refs.ffn[...] = jnp.zeros_like(refs.ffn)
            refs.grad[...] = jnp.zeros_like(refs.grad)

        pl.when(step == EARLY - 1)(lambda: load(start=False))

        def both(name):
            return refs[f"{name}_high"][...], refs[f"{name}_low"][...]

        @pl.when(step < EARLY)
        def _():
            e_ref[...] = refs.early[...]

        @pl.when(step >= EARLY)
        def _():
            refs.late[...] = three_pass((high_ref[...], low_ref[...]), both("turned"), 1, 0)
            row = pl.multiple_of(lax.axis_index("seq") * rows, rows)
            e_ref[...] = refs.late[pl.ds(row, rows), :]

        moments = (1, 3, 4, 5, 6, 7, 7, 8, 9, 10, 11)
        schedule(2 * step, moments, gather.events())
        normed = halves(refs.normed_two[...])
        a = few_rows(normed, both("gate"), 0)
        b = few_rows(normed, both("up"), 0)
        e = e_ref[...]
        gate = jax.nn.sigmoid(a)
        silu_a = a * gate
        refs.ffn[...] += few_rows(halves(silu_a * b), both("down"), 0)
        refs.grad[...] += few_rows(
            halves(e * b * (gate * (1.0 + a * (1.0 - gate)))), both("gate"), 1
        ) + few_rows(halves(e * silu_a), both("up"), 1)
        schedule(2 * step + 1, moments, gather.events())

    by_column = pl.BlockSpec((inner, TILE), lambda step: (0, step))
    return fused(
        dict(
            normed_two=(normed_two, WHOLE),
            all_cotangent=(all_cotangent, ANY),
            early=(
                grad_hidden,
                pl.BlockSpec(
                    (rows, TILE), lambda step: (lax.axis_index("seq"), jnp.minimum(step, EARLY - 1))
                ),
            ),
            **{
                f"{name}_{half}": (split[f"{name}_{half}"], spec)
                for name, spec in (
                    ("gate", by_column),
                    ("up", by_column),
                    ("down", pl.BlockSpec((TILE, inner), lambda step: (step, 0))),
                    (
                        "turned",
                        pl.BlockSpec((inner, TILE), lambda step: (0, jnp.maximum(step, EARLY))),
                    ),
                )
                for half in ("high", "low")
            },
        ),
        dict(
            all_normed_two=Gather.results([normed_two])[0],
            ffn=((rows, inner), WHOLE),
            grad=((rows, inner), WHOLE),
            late=(
                (token_count, columns - EARLY * TILE),
                pl.BlockSpec((token_count, TILE), lambda step: (0, jnp.maximum(step - EARLY, 0))),
            ),
        ),
        dict(
            gather=Gather.scratch([normed_two]),
            halves=halves_scratch(token_count, inner),
            e=[pltpu.VMEM((rows, TILE), F32)],
        ),
        tiles,
        body,
        collective_id,
        flops=30 * rows * inner * columns,
    )


SHARES = 2


def tile_share(refs, share, tile):
    high_ref, low_ref, cols_high_ref, cols_low_ref, cot_high_ref, cot_low_ref = refs.halves
    size = high_ref.shape[0] // SHARES
    spot = pl.ds(pl.multiple_of(share * size, size), size)
    normed = high_ref[spot, :], low_ref[spot, :]
    a = three_pass(normed, (refs.gate_high[...], refs.gate_low[...]), 1, 0)
    b = three_pass(normed, (refs.up_high[...], refs.up_low[...]), 1, 0)
    gate = jax.nn.sigmoid(a)
    silu_a = a * gate
    e = jnp.where(tile < EARLY, refs.early[spot, :], refs.late[spot, :])
    cols = cols_high_ref[:, spot], cols_low_ref[:, spot]
    cot = cot_high_ref[spot, :], cot_low_ref[spot, :]
    grads = (
        three_pass(cols, halves(e * b * (gate * (1.0 + a * (1.0 - gate)))), 1, 0),
        three_pass(cols, halves(e * silu_a), 1, 0),
        three_pass(halves(jnp.transpose(silu_a * b)), cot, 1, 0),
    )
    for ref, grad in zip((refs.grad_gate, refs.grad_up, refs.grad_down), grads, strict=True):
        ref[...] = jnp.where(share == 0, 0.0, ref[...]) + grad


def tile_columns(refs):
    cols_high_ref, cols_low_ref, cot_high_ref, cot_low_ref = refs.halves[2:]
    cols_high_ref[...], cols_low_ref[...] = halves(jnp.transpose(refs.normed_cols[...]))
    cot_high_ref[...], cot_low_ref[...] = halves(refs.cot_cols[...])


def tile_parts(all_normed_two, all_cotangent, early, late, split, first, count, tile_of):
    rows, inner = all_normed_two.shape
    narrow = inner // (Z * X)
    columns = count * TILE
    own_columns = pl.BlockSpec((rows, narrow), lambda step: (0, lax.axis_index("seq")))
    by_column = pl.BlockSpec((inner, TILE), lambda step: (0, first + tile_of(step)))
    grad_spec = pl.BlockSpec((narrow, TILE), lambda step: (0, tile_of(step)))
    arrays = dict(
        early=(
            early,
            pl.BlockSpec((rows, TILE), lambda step: (0, jnp.minimum(first + tile_of(step), EARLY - 1))),
        ),
        late=(
            late,
            pl.BlockSpec(
                (rows, TILE), lambda step: (0, jnp.maximum(first + tile_of(step) - EARLY, 0))
            ),
        ),
        **{
            f"{name}_{half}": (split[f"{name}_{half}"], by_column)
            for name in ("gate", "up")
            for half in ("high", "low")
        },
        normed_cols=(all_normed_two, own_columns),
        cot_cols=(all_cotangent, own_columns),
    )
    results = dict(
        grad_gate=((narrow, columns), grad_spec),
        grad_up=((narrow, columns), grad_spec),
        grad_down=(
            (columns, narrow), pl.BlockSpec((TILE, narrow), lambda step: (tile_of(step), 0))
        ),
    )
    scratch = dict(
        halves=[
            pltpu.VMEM((rows, inner), BF16),
            pltpu.VMEM((rows, inner), BF16),
            pltpu.VMEM((narrow, rows), BF16),
            pltpu.VMEM((narrow, rows), BF16),
            pltpu.VMEM((rows, narrow), BF16),
            pltpu.VMEM((rows, narrow), BF16),
        ]
    )
    return arrays, results, scratch


def residual_kernel(
    part, ffn, residual, cotangent, second_gain, split, all_normed_two, tiles, count, collective_id
):
    arrays, results, scratch = tiles(lambda step: step // SHARES)
    rows, inner = all_normed_two.shape
    own_rows = part.shape[0]
    out_shape = split.out_high.shape
    grad_like = jax.ShapeDtypeStruct((own_rows, out_shape[0]), F32)

    def body(refs, step):
        sum_ref, *sum_scratch = refs.sum
        grad_mixer_ref, *heads_scratch = refs.heads
        total = Sum([refs.part], [sum_ref], sum_scratch)
        heads = Heads([grad_mixer_ref], [refs.all_grad_mixer], heads_scratch)
        scatter = Scatter([refs.ffn], [refs.ffn_share], refs.scatter)
        high_ref, low_ref = refs.halves[:2]
        stage_ref, stage_sem, out_sem = refs.stage
        out_buf, out_buf_sem = refs.out
        keep = [
            pltpu.make_async_copy(high_ref, refs.normed_high, out_sem.at[0]),
            pltpu.make_async_copy(low_ref, refs.normed_low, out_sem.at[1]),
        ]
        fetch_out = [
            pltpu.make_async_copy(refs[f"out_{half}"], out_buf.at[at], out_buf_sem.at[at])
            for at, half in enumerate(("high", "low"))
        ]

        def to_heads():
            total.finish()
            residual_here = refs.residual[...]
            scale = rms(residual_here)
            summed = sum_ref[...]
            pulled = summed * refs.second_gain[...]
            grad_residual = (
                refs.cotangent[...]
                + scale * pulled
                - residual_here
                * (scale * scale * scale * jnp.mean(pulled * residual_here, -1, keepdims=True))
            )
            refs.grad_residual[...] = grad_residual
            refs.second[...] = jnp.broadcast_to(
                jnp.sum(summed * residual_here * scale, 0, keepdims=True), refs.second.shape
            )
            for copy in fetch_out:
                copy.wait()
            grad_mixer_ref[...] = few_rows(halves(grad_residual), (out_buf[0], out_buf[1]), 1)
            heads.begin()

        @pl.when(step == 0)
        def _():
            total.begin()
            for copy in fetch_out:
                copy.start()
            load_halves(refs.all_normed_two, high_ref, low_ref, stage_ref, stage_sem)
            total.to_y()
            for copy in keep:
                copy.start()
            tile_columns(refs)

        tile_share(refs, lax.rem(step, SHARES), step // SHARES)
        schedule(step, (1, 2, 3, 5, 6, 7), [total.back, to_heads, *heads.events()])
        schedule(step, (3, 4, 6), [scatter.begin, *scatter.events()])

        @pl.when(step == count * SHARES - 1)
        def _():
            for copy in keep:
                copy.wait()

    return fused(
        dict(
            part=(part, WHOLE),
            ffn=(ffn, WHOLE),
            residual=(residual, WHOLE),
            cotangent=(cotangent, WHOLE),
            second_gain=(second_gain[None], WHOLE),
            out_high=(split.out_high, ANY),
            out_low=(split.out_low, ANY),
            all_normed_two=(all_normed_two, ANY),
            **arrays,
        ),
        dict(
            all_grad_mixer=Heads.results([grad_like])[0],
            ffn_share=Scatter.results([ffn])[0],
            grad_residual=((own_rows, inner), WHOLE),
            second=((8, inner), WHOLE),
            normed_high=((rows, inner), ANY, BF16),
            normed_low=((rows, inner), ANY, BF16),
            **results,
        ),
        dict(
            sum=[pltpu.VMEM((own_rows, inner), F32), *Sum.scratch([part])],
            heads=[pltpu.VMEM(grad_like.shape, F32), *Heads.scratch([grad_like])],
            scatter=Scatter.scratch([ffn]),
            stage=[*halves_scratch(rows, inner)[2:], pltpu.SemaphoreType.DMA((2,))],
            out=[pltpu.VMEM((2, *out_shape), BF16), pltpu.SemaphoreType.DMA((2,))],
            **scratch,
        ),
        count * SHARES,
        body,
        collective_id,
    )


def last_kernel(
    grads, group, blocks, first_part, in_weights, normed_high, normed_low, tiles, count, collective_id
):
    arrays, results, scratch = tiles(
        lambda step: jnp.where(step < SHARES, 0, jnp.maximum(step - 4, 0) // SHARES)
    )
    rows, columns = grads.shape
    own_rows = rows // (Z * X)
    inner, width = in_weights[0].shape
    half = width // X
    matrices = 4
    part_like = jax.ShapeDtypeStruct((own_rows, inner), F32)
    swapped = [jax.ShapeDtypeStruct((own_rows, columns), F32), group]

    def body(refs, step):
        place = lax.axis_index("seq")
        x = place % X
        peer = pl.multiple_of((place + 1 - 2 * x) * own_rows, own_rows)
        other_ref, *swap_scratch = refs.swap
        part_ref, *scatter_scratch = refs.scatter
        weight_buf, weight_sem, load_sem = refs.weights
        swap = SwapX(
            [refs.grads.at[pl.ds(peer, own_rows), :], refs.group],
            [other_ref, refs.other_group],
            swap_scratch,
        )
        blocks_here = SwapBlocks(
            [refs[f"block_{index}"] for index in range(len(blocks))],
            [refs[f"swapped_{index}"] for index in range(len(blocks))],
            refs.blocks,
        )
        scatter = Scatter([part_ref], [refs.share], scatter_scratch)
        sums = SumAll([refs.first_part], [refs.first_sum], refs.sums)

        def fetch(index):
            return block_fetch(refs[f"weight_{index}"], weight_buf, weight_sem, index % 2)

        load = [
            pltpu.make_async_copy(refs[f"normed_{name}"], refs.halves[at], load_sem.at[at])
            for at, name in enumerate(("high", "low"))
        ]

        @pl.when(step == 0)
        def _():
            for copy in load:
                copy.start()
            swap.begin()
            sums.begin()
            part_ref[...] = jnp.zeros_like(part_ref)
            for copy in load:
                copy.wait()
            for index in range(2):
                fetch(index).start()

        @pl.when(step == 1)
        def _():
            swap.finish()
            blocks_here.begin()

        pl.when(step == 0)(lambda: tile_columns(refs))

        @pl.when((step < SHARES) | (step >= matrices + SHARES))
        def _():
            tile_share(refs, lax.rem(step, SHARES), EARLY)

        schedule(step, (0, 1, 2), sums.events())
        pl.when(step == matrices + SHARES)(scatter.middle)
        for index in range(matrices):

            @pl.when(step == index + SHARES)
            def _(index=index):
                fetch(index).wait()
                weight = halves(weight_buf[index % 2])
                if index + 2 < matrices:
                    fetch(index + 2).start()
                own = refs.own_grads[:, index * half : (index + 1) * half]
                other = other_ref[:, index * half : (index + 1) * half]
                low_x, high_x = (jnp.where(x == place_x, own, other) for place_x in range(X))
                part_ref[...] += few_rows(halves(jnp.concatenate([low_x, high_x], 1)), weight, 1)
                if index == matrices - 1:
                    scatter.begin()

        @pl.when(step == matrices + count * SHARES - 1)
        def _():
            scatter.finish()
            blocks_here.finish()


    return fused(
        dict(
            grads=(grads, ANY),
            own_grads=(
                grads, pl.BlockSpec((own_rows, columns), lambda step: (lax.axis_index("seq"), 0))
            ),
            group=(group, ANY),
            first_part=(first_part, WHOLE),
            **{f"block_{index}": (block, ANY) for index, block in enumerate(blocks)},
            **{f"weight_{index}": (weight, ANY) for index, weight in enumerate(in_weights)},
            normed_high=(normed_high, ANY),
            normed_low=(normed_low, ANY),
            **arrays,
        ),
        dict(
            other_group=(group.shape, ANY),
            share=Scatter.results([part_like])[0],
            first_sum=SumAll.results([first_part])[0],
            **{
                f"swapped_{index}": result for index, result in enumerate(SwapBlocks.results(blocks))
            },
            **results,
        ),
        dict(
            swap=[pltpu.VMEM((own_rows, columns), F32), *SwapX.scratch(swapped)],
            scatter=[pltpu.VMEM((own_rows, inner), F32), *Scatter.scratch([part_like])],
            blocks=SwapBlocks.scratch(blocks),
            sums=SumAll.scratch([first_part]),
            weights=[
                pltpu.VMEM((2, inner, width), F32),
                pltpu.SemaphoreType.DMA((2,)),
                pltpu.SemaphoreType.DMA((2,)),
            ],
            **scratch,
        ),
        count * SHARES + matrices,
        body,
        collective_id,
    )


def thin(left, right, contract_left, contract_right):
    (left_high, left_low), (right_high, right_low) = left, right
    return product(
        jnp.concatenate([left_high, left_low], contract_left),
        jnp.concatenate([right_high, right_high], contract_right),
        contract_left,
        contract_right,
    ) + product(left_high, right_low, contract_left, contract_right)


def join(first, second, axis):
    return tuple(jnp.concatenate(pair, axis) for pair in zip(first, second, strict=True))


def running_sum(triangle, entries):
    high, low = halves(entries)
    least = (entries - high.astype(F32) - low.astype(F32)).astype(BF16)
    return product(
        jnp.concatenate([triangle, triangle], 1), jnp.concatenate([high, low], 0), 1, 0
    ) + product(triangle, least, 1, 0)


def chunk_masks(lengths_ref, chunk):
    shape = (CHUNK, CHUNK)
    row = lax.broadcasted_iota(jnp.int32, shape, 0)
    column = lax.broadcasted_iota(jnp.int32, shape, 1)
    start = chunk * CHUNK

    offsets = [0]
    for index in range(lengths_ref.shape[0] - 1):
        offsets.append(offsets[-1] + lengths_ref[index])

    def segment(position):
        return sum(jnp.where(position >= offset, 1, 0) for offset in offsets)

    segment_row = segment(start + row)
    before, last = segment(start - 1), segment(start + CHUNK - 1)
    allowed = (row >= column) & (segment_row == segment(start + column))
    carry = (segment_row == before).astype(F32)
    in_last = (segment_row == last).astype(F32)
    lower = (row >= column).astype(F32).astype(BF16)
    return allowed, carry, in_last, (last == before).astype(F32), lower


def head_terms(pre_query, pre_forget, lower_bound, lower):
    query_gate = jax.nn.sigmoid(pre_query)
    forget_gate = jax.nn.sigmoid(-pre_forget)
    keys = (1.0 - lower_bound) * forget_gate
    log_decay = running_sum(lower, jnp.log1p(-keys))
    last = log_decay[CHUNK - 1 :, :]
    growth, shrink, trail = jnp.exp(log_decay), jnp.exp(-log_decay), jnp.exp(last - log_decay)
    return query_gate, forget_gate, keys, last, growth, shrink, trail


def tall(row):
    return jnp.transpose(jnp.broadcast_to(row, (HDIM, HDIM)))


def forward_chunk(
    chunk, lengths_ref, projected_ref, bound_ref, gain_ref, mixer_ref, raw_ref, states_ref, state_ref
):
    heads = state_ref.shape[0]
    width = heads * HDIM
    allowed, carry, in_last, carry_last, lower = chunk_masks(lengths_ref, chunk)
    for head in range(heads):
        at = slice(head * HDIM, (head + 1) * HDIM)
        pre_query, pre_forget, values, gate_in = (
            projected_ref[:, part * width + head * HDIM : part * width + (head + 1) * HDIM]
            for part in range(4)
        )
        query_gate, _, keys, last, growth, shrink, trail = head_terms(
            pre_query, pre_forget, bound_ref[:, at], lower
        )
        grown = pre_query * query_gate * growth
        state = state_ref[head]
        states_ref[0, head] = state
        value_halves = halves(values)
        scores = thin(halves(grown), halves(keys * shrink), 1, 1)
        scores = jnp.where(allowed, scores, 0.0)
        raw = three_pass(
            join(halves(scores), halves(grown * carry), 1),
            join(value_halves, halves(state), 0),
            1,
            0,
        )
        state_ref[head] = state * (tall(jnp.exp(last)) * carry_last) + thin(
            halves(keys * trail * in_last), value_halves, 0, 0
        )
        raw_ref[:, at] = raw
        scale = lax.rsqrt(jnp.mean(raw * raw, -1, keepdims=True) + group_eps)
        mixer_ref[:, at] = raw * scale * gain_ref[:, at] * jax.nn.silu(gate_in)


def backward_kernel(
    projected, raw_rows, states, grad_mixer, normed_cols, grad_residual, second, weights,
    lower_bound, group_gain, lengths, collective_id,
):
    rows, columns = projected.shape
    count = len(weights)
    width = columns // count
    heads = width // HDIM
    chunks = rows // CHUNK
    wide = normed_cols.shape[1]

    def body(refs, step):
        lengths_ref, projected_ref, raw_ref, states_ref = refs.lengths, refs.projected, refs.raw, refs.states
        grad_ref, grads_ref, group_ref = refs.grad_mixer, refs.grads, refs.group
        later_ref, weight_buf, weight_sem = refs.work
        chunk = chunks - 1 - step
        place = lax.axis_index("seq")
        here = pl.ds(pl.multiple_of((place % X) * width, width), width)
        bound_ref, gain_ref = refs.lower_bound.at[:, here], refs.group_gain.at[:, here]
        block_refs = [refs[f"block_{index}"] for index in range(count)]
        move = Columns([refs.grad_residual], [refs.residual_cols], refs.columns)
        small = Columns([refs.second], [refs.second_cols], refs.small)

        def fetch(index):
            return block_fetch(
                refs[f"weight_{index}"].at[
                    pl.ds(pl.multiple_of((place // X) * wide, wide), wide), here
                ],
                weight_buf,
                weight_sem,
                index,
            )

        @pl.when(step == 0)
        def _():
            move.begin()
            small.begin()
            later_ref[...] = jnp.zeros_like(later_ref)
            group_ref[...] = jnp.zeros_like(group_ref)
            for index in range(count):
                fetch(index).start()
                block_refs[index][...] = jnp.zeros_like(block_refs[index])

        allowed, carry, in_last, carry_last, lower = chunk_masks(lengths_ref, chunk)
        upper = jnp.transpose(lower.astype(F32)).astype(BF16)
        for head in range(heads):
            at = slice(head * HDIM, (head + 1) * HDIM)
            spots = [
                slice(part * width + head * HDIM, part * width + (head + 1) * HDIM)
                for part in range(4)
            ]
            pre_query, pre_forget, values, gate_in = (projected_ref[:, spot] for spot in spots)
            raw, grad, gain = raw_ref[:, at], grad_ref[:, at], gain_ref[:, at]
            state, later = states_ref[0, head], later_ref[head]

            scale = lax.rsqrt(jnp.mean(raw * raw, -1, keepdims=True) + group_eps)
            normed = raw * scale
            gate = jax.nn.sigmoid(gate_in)
            silu_gate = gate_in * gate
            weighted = grad * gain * silu_gate
            group_ref[:, at] += jnp.sum(grad * normed * silu_gate, 0, keepdims=True)
            grads_ref[:, spots[3]] = (
                grad * gain * normed * (gate * (1.0 + gate_in * (1.0 - gate)))
            )
            grad_raw = scale * weighted - raw * (
                scale * scale * scale * jnp.mean(weighted * raw, -1, keepdims=True)
            )

            query_gate, forget_gate, keys, last, growth, shrink, trail = head_terms(
                pre_query, pre_forget, bound_ref[:, at], lower
            )
            grown = pre_query * query_gate * growth
            shrunk = keys * shrink
            trailing = trail * in_last
            ends = keys * trailing
            grown_halves, shrunk_halves = halves(grown), halves(shrunk)
            raw_halves, value_halves, later_halves = halves(grad_raw), halves(values), halves(later)
            scores = jnp.where(allowed, thin(grown_halves, shrunk_halves, 1, 1), 0.0)
            grad_scores = jnp.where(allowed, thin(raw_halves, value_halves, 1, 1), 0.0)
            score_halves = halves(grad_scores)
            grads_ref[:, spots[2]] = three_pass(
                join(halves(jnp.transpose(scores)), halves(ends), 1),
                join(raw_halves, later_halves, 0),
                1,
                0,
            )
            grad_grown = three_pass(
                join(score_halves, halves(grad_raw * carry), 1),
                join(shrunk_halves, halves(jnp.transpose(state)), 0),
                1,
                0,
            )
            grad_shrunk = thin(score_halves, grown_halves, 0, 0)
            grad_ends = thin(value_halves, later_halves, 1, 1)
            through = tall(jnp.exp(last)) * carry_last
            later_ref[head] = later * through + thin(
                halves(grown * carry), raw_halves, 0, 0
            )
            grads_ref[:, spots[0]] = (
                grad_grown * growth * (query_gate * (1.0 + pre_query * (1.0 - query_gate)))
            )
            from_ends = grad_ends * ends
            grad_log = grad_grown * grown - grad_shrunk * shrunk - from_ends
            pulled = jnp.transpose(later * state * through)
            grad_last = jnp.sum(from_ends + pulled, 0, keepdims=True)
            grad_log_forget = running_sum(upper, grad_log) + grad_last
            grad_keys = (
                grad_shrunk * shrink + grad_ends * trailing - grad_log_forget / (1.0 - keys)
            )
            grads_ref[:, spots[1]] = -grad_keys * keys * (1.0 - forget_gate)

        cols = halves(jnp.transpose(refs.normed_cols[...]))
        for index in range(count):
            part = grads_ref[:, index * width : (index + 1) * width]
            block_refs[index][...] += thin(cols, halves(part), 1, 0)

        @pl.when(step == chunks - 1)
        def _():
            total = 0.0
            for index in range(count):
                fetch(index).wait()
                total = total + weight_buf[index] * block_refs[index][...]
            ones = jnp.ones((8, width), BF16)
            high, low = halves(total)
            refs.sums[...] = product(ones, high, 1, 1) + product(ones, low, 1, 1)

        schedule(step, (0, 1, 2, 4, 6, 7), small.events())
        schedule(step, (0, 2, 3, 5, 7, 7), move.events())

    def by_chunk(size):
        return pl.BlockSpec((CHUNK, size), lambda step: (chunks - 1 - step, 0))

    return fused(
        dict(
            lengths=(lengths, pl.BlockSpec(memory_space=pltpu.SMEM)),
            projected=(projected, by_chunk(columns)),
            raw=(raw_rows, by_chunk(width)),
            states=(
                states,
                pl.BlockSpec((1, heads, HDIM, HDIM), lambda step: (chunks - 1 - step, 0, 0, 0)),
            ),
            grad_mixer=(grad_mixer, by_chunk(width)),
            normed_cols=(normed_cols, by_chunk(wide)),
            lower_bound=(lower_bound[None], WHOLE),
            group_gain=(group_gain[None], WHOLE),
            grad_residual=(grad_residual, WHOLE),
            second=(second, WHOLE),
            **{f"weight_{index}": (weight, ANY) for index, weight in enumerate(weights)},
        ),
        dict(
            grads=((rows, columns), by_chunk(columns)),
            group=((1, width), WHOLE),
            sums=((8, wide), WHOLE),
            residual_cols=Columns.results([grad_residual])[0],
            second_cols=Columns.results([second])[0],
            **{f"block_{index}": ((wide, width), WHOLE) for index in range(count)},
        ),
        dict(
            work=[
                pltpu.VMEM((heads, HDIM, HDIM), F32),
                pltpu.VMEM((count, wide, width), F32),
                pltpu.SemaphoreType.DMA((count,)),
            ],
            columns=Columns.scratch([grad_residual]),
            small=Columns.scratch([second]),
        ),
        chunks,
        body,
        collective_id,
        far=True,
        flops=60 * rows * HDIM * width + 6 * rows * wide * columns,
    )


def fast_shards(
    tokens_in,
    cotangent,
    lengths,
    lower_bound,
    query_weight,
    forget_weight,
    input_weight,
    gate_weight,
    out_weight,
    swiglu_gate,
    swiglu_up,
    swiglu_down,
    first_gain,
    group_gain,
    second_gain,
):
    place = lax.axis_index("seq")
    z, x = place // X, place % X
    rows, model = tokens_in.shape
    wide = model // Z
    narrow = model // (Z * X)
    width = query_weight.shape[1] // X
    share_rows = rows // 4
    token_count = rows * Z * X

    def share(entries):
        return cut(entries, lax.axis_index("mp"), share_rows, 0)

    in_weights = (query_weight, forget_weight, input_weight, gate_weight)
    split = first_kernel(tokens_in, out_weight, swiglu_gate, swiglu_up, swiglu_down, 1)
    mixed = mixer_kernel(
        split.all,
        tokens_in,
        cotangent,
        lengths,
        lower_bound,
        in_weights,
        split,
        first_gain,
        group_gain,
        second_gain,
        2,
    )
    fed = feed_forward_kernel(
        mixed.normed_two, mixed.all_cotangent, mixed.grad_hidden, split, 3
    )

    def tiles(first, count):
        return partial(
            tile_parts,
            fed.all_normed_two,
            mixed.all_cotangent,
            mixed.grad_hidden,
            fed.late,
            split,
            first,
            count,
        )

    early = 4
    late = pl.cdiv(swiglu_gate.shape[1], TILE) - early
    sent = residual_kernel(
        fed.grad,
        fed.ffn,
        mixed.residual,
        cotangent,
        second_gain,
        split,
        fed.all_normed_two,
        tiles(0, early),
        early,
        4,
    )
    grad_residual = sent.grad_residual
    output = share(mixed.residual) + sent.ffn_share
    back = backward_kernel(
        mixed.projected,
        mixed.raw,
        mixed.states,
        sent.all_grad_mixer,
        mixed.normed_cols,
        grad_residual,
        sent.second,
        in_weights,
        lower_bound,
        group_gain,
        lengths,
        5,
    )
    second_cols = jnp.sum(back.second_cols[:, :, 0], (0, 1))
    out_block = dot(back.residual_cols.reshape(token_count, wide), mixed.mixer, 0, 0)
    blocks = [*(back[f"block_{index}"] for index in range(4)), out_block]
    last = last_kernel(
        back.grads,
        jnp.broadcast_to(back.group, (8, width)),
        blocks,
        jnp.concatenate([back.sums[:, :narrow], back.sums[:, narrow:]]),
        in_weights,
        sent.normed_high,
        sent.normed_low,
        tiles(early, late),
        late,
        6,
    )
    grad_group = in_order(x == 0, back.group[0], last.other_group[0], 0)
    *weight_grads, grad_outw = (
        in_order(x == 0, cut(block, x, narrow, 0), last[f"swapped_{index}"], 1)
        for index, block in enumerate(blocks)
    )
    grad_normed_one, first_sum = last.share, last.first_sum
    rest = swiglu_gate.shape[1] - early * TILE
    grad_sgate, grad_sup, grad_sdown = (
        jnp.concatenate([sent[name], lax.slice_in_dim(last[name], 0, rest, axis=axis)], axis)
        for name, axis in (("grad_gate", 1), ("grad_up", 1), ("grad_down", 0))
    )
    tokens_share = share(tokens_in)
    scale_one = rms(tokens_share)
    pulled_one = grad_normed_one * first_gain
    grad_tokens = (
        share(grad_residual)
        + scale_one * pulled_one
        - tokens_share * scale_one**3 * jnp.mean(pulled_one * tokens_share, -1, keepdims=True)
    )
    return (
        output,
        grad_tokens,
        *weight_grads,
        jnp.transpose(grad_outw),
        grad_sgate,
        grad_sup,
        grad_sdown,
        first_sum[0] / cut(first_gain, place, narrow, 0),
        cut(grad_group, place, group_gain.shape[0] // (Z * X), 0),
        cut(second_cols, x, narrow, 0),
    )


def solution(mesh):
    in_specs = (
        P("seq", None),
        P("seq", None),
        P(),
        P("mp"),
        P(None, "mp"),
        P(None, "mp"),
        P(None, "mp"),
        P(None, "mp"),
        P("mp", None),
        P(None, "mp"),
        P(None, "mp"),
        P("mp", None),
        P(),
        P("mp"),
        P(),
    )
    out_specs = (
        P(("seq", "mp"), None),
        P(("seq", "mp"), None),
        P("seq", "mp"),
        P("seq", "mp"),
        P("seq", "mp"),
        P("seq", "mp"),
        P("mp", "seq"),
        P("seq", "mp"),
        P("seq", "mp"),
        P("mp", "seq"),
        P("seq"),
        P(("mp", "seq")),
        P("seq"),
    )
    small = (mesh.shape["seq"], mesh.shape["mp"]) == (Z * X, 4)
    body = fast_shards if small else shards
    return jax.shard_map(body, mesh=mesh, in_specs=in_specs, out_specs=out_specs, check_vma=False)
```

```python
from functools import partial

import jax
import jax.numpy as jnp
from jax import lax
from jax.experimental import pallas as pl
from jax.experimental.pallas import tpu as pltpu
from jax.sharding import PartitionSpec as P

HDIM = 128
CHUNK = 128
HIGH = lax.Precision.HIGH
HIGHEST = lax.Precision.HIGHEST
norm_eps = 1e-06
group_eps = 1e-05


def dot(left, right, contract_left, contract_right, precision=HIGH):
    return lax.dot_general(
        left,
        right,
        (((contract_left,), (contract_right,)), ((), ())),
        precision=precision,
        preferred_element_type=jnp.float32,
    )


def rms(entries):
    return lax.rsqrt(jnp.mean(entries * entries, -1, keepdims=True) + norm_eps)


def silu_grad(entries):
    gate = jax.nn.sigmoid(entries)
    return gate * (1.0 + entries * (1.0 - gate))


def gather_tokens(block):
    return lax.all_gather(block, "seq", axis=0, tiled=True)


def recurrence(query_rows, key_vecs, value_rows, segment):
    token_count, width = query_rows.shape
    heads = width // HDIM
    chunks = token_count // CHUNK

    def split(entries):
        return entries.reshape(chunks, CHUNK, heads, HDIM)

    blocked = segment.reshape(chunks, CHUNK)
    last_seg = blocked[:, -1]
    first_segs = jnp.concatenate([jnp.full((1,), -1, segment.dtype), last_seg[:-1]])
    carry = (blocked == first_segs[:, None]).astype(jnp.float32)
    in_last = (blocked == last_seg[:, None]).astype(jnp.float32)
    places = jnp.arange(CHUNK)
    allowed = (places[None, :, None] >= places[None, None, :]) & (
        blocked[:, :, None] == blocked[:, None, :]
    )
    lower = (places[:, None] >= places[None, :]).astype(jnp.float32)
    queries, keys, values = split(query_rows), split(key_vecs), split(value_rows)
    log_decay = jnp.einsum("ts,cshk->cthk", lower, jnp.log1p(-keys), precision=HIGHEST)
    growth = jnp.exp(log_decay)
    grown = queries * growth
    last = log_decay[:, -1]
    scores = jnp.einsum("cthk,cshk->chts", grown, keys * jnp.exp(-log_decay), precision=HIGH)
    scores = jnp.where(allowed[:, None], scores, 0.0)
    inner = jnp.einsum("chts,cshv->cthv", scores, values, precision=HIGH)
    weighted = keys * jnp.exp(last[:, None] - log_decay) * in_last[:, :, None, None]
    updates = jnp.einsum("cshk,cshv->chkv", weighted, values, precision=HIGH)
    through = jnp.exp(last) * carry[:, -1][:, None, None]
    state = jnp.zeros_like(updates[0])
    states = []
    for chunk in range(chunks):
        states.append(state)
        state = state * through[chunk][:, :, None] + updates[chunk]
    outer = jnp.einsum(
        "cthk,chkv->cthv", grown * carry[:, :, None, None], jnp.stack(states), precision=HIGH
    )
    return (inner + outer).reshape(token_count, width)


def mixer_all(pre_query, pre_forget, value_rows, gate_in, group_gain, lower_bound, segment):
    key_vecs = (1.0 - lower_bound) * jax.nn.sigmoid(-pre_forget)
    raw = recurrence(jax.nn.silu(pre_query), key_vecs, value_rows, segment)
    heads = raw.reshape(raw.shape[0], -1, HDIM)
    scale = lax.rsqrt(jnp.mean(heads * heads, -1, keepdims=True) + group_eps)
    normed = (heads * scale).reshape(raw.shape)
    return normed * group_gain * jax.nn.silu(gate_in)


def shards(
    tokens_in,
    cotangent,
    lengths,
    lower_bound,
    query_weight,
    forget_weight,
    input_weight,
    gate_weight,
    out_weight,
    swiglu_gate,
    swiglu_up,
    swiglu_down,
    first_gain,
    group_gain,
    second_gain,
):
    seq_count = lax.axis_size("seq")
    seq_place = lax.axis_index("seq")
    own_rows, model = tokens_in.shape
    token_count = own_rows * seq_count
    share_rows = own_rows // lax.axis_size("mp")
    share_start = lax.axis_index("mp") * share_rows
    start_row = seq_place * own_rows
    own_cols = model // seq_count
    start_col = seq_place * own_cols

    def own(entries):
        return lax.dynamic_slice_in_dim(entries, start_row, own_rows, 0)

    def columns(entries):
        return lax.dynamic_slice_in_dim(entries, start_col, own_cols, 1)

    def share(entries):
        return lax.dynamic_slice_in_dim(entries, share_start, share_rows, 0)

    positions = jnp.arange(token_count, dtype=jnp.int32)
    offsets = jnp.cumsum(lengths) - lengths
    segment = jnp.sum((positions[:, None] >= offsets[None, :]).astype(jnp.int32), 1) - 1

    all_tokens = gather_tokens(tokens_in)
    all_cotangent = gather_tokens(cotangent)
    normed_one = all_tokens * rms(all_tokens) * first_gain
    pre_query = dot(normed_one, query_weight, 1, 0)
    pre_forget = dot(normed_one, forget_weight, 1, 0)
    value_rows = dot(normed_one, input_weight, 1, 0)
    gate_in = dot(normed_one, gate_weight, 1, 0)
    mixer, mixer_back = jax.vjp(
        partial(mixer_all, lower_bound=lower_bound, segment=segment),
        pre_query,
        pre_forget,
        value_rows,
        gate_in,
        group_gain,
    )
    residual = tokens_in + lax.psum(dot(own(mixer), out_weight, 1, 0), "mp")
    scale_two = rms(residual)
    normed_two = residual * scale_two * second_gain
    grad_hidden_all = dot(all_cotangent, swiglu_down, 1, 1)
    a = dot(normed_two, swiglu_gate, 1, 0)
    b = dot(normed_two, swiglu_up, 1, 0)
    silu_a = jax.nn.silu(a)
    ffn_part = dot(silu_a * b, swiglu_down, 1, 0)
    output = share(residual) + lax.psum_scatter(ffn_part, "mp", scatter_dimension=0, tiled=True)
    e = own(grad_hidden_all)
    grad_a = e * b * silu_grad(a)
    grad_b = e * silu_a
    grad_normed_two = lax.psum(
        dot(grad_a, swiglu_gate, 1, 1) + dot(grad_b, swiglu_up, 1, 1), "mp"
    )
    pulled = grad_normed_two * second_gain
    grad_residual = (
        cotangent
        + scale_two * pulled
        - residual * scale_two**3 * jnp.mean(pulled * residual, -1, keepdims=True)
    )
    all_normed_two = gather_tokens(normed_two)
    a_all = dot(all_normed_two, swiglu_gate, 1, 0)
    b_all = dot(all_normed_two, swiglu_up, 1, 0)
    silu_all = jax.nn.silu(a_all)
    hidden_all = silu_all * b_all
    grad_a_all = grad_hidden_all * b_all * silu_grad(a_all)
    grad_b_all = grad_hidden_all * silu_all
    normed_two_cols = columns(all_normed_two)
    grad_sgate = dot(normed_two_cols, grad_a_all, 0, 0)
    grad_sup = dot(normed_two_cols, grad_b_all, 0, 0)
    grad_sdown = dot(hidden_all, columns(all_cotangent), 0, 0)

    grad_mixer = gather_tokens(dot(grad_residual, out_weight, 1, 1))
    residual_cols = lax.all_to_all(grad_residual, "seq", 1, 0, tiled=True)
    grad_outw = dot(mixer, residual_cols, 0, 0)
    grad_query_rows, grad_forget_rows, grad_value_rows, grad_gate_rows, grad_group = mixer_back(
        grad_mixer
    )
    grad_group = lax.dynamic_slice_in_dim(
        grad_group, seq_place * (group_gain.shape[0] // seq_count), group_gain.shape[0] // seq_count
    )
    normed_one_cols = columns(normed_one)
    pairs = (
        (grad_query_rows, query_weight),
        (grad_forget_rows, forget_weight),
        (grad_value_rows, input_weight),
        (grad_gate_rows, gate_weight),
    )
    weight_grads = []
    normed_part = 0.0
    first_sum = 0.0
    for grad_rows, weight in pairs:
        weight_grad = dot(normed_one_cols, grad_rows, 0, 0)
        weight_grads.append(weight_grad)
        normed_part = normed_part + dot(own(grad_rows), weight, 1, 1)
        own_weight = lax.dynamic_slice_in_dim(weight, start_col, own_cols, 0)
        first_sum = first_sum + jnp.sum(own_weight * weight_grad, 1)
    second_sum = jnp.sum(
        lax.dynamic_slice_in_dim(swiglu_gate, start_col, own_cols, 0) * grad_sgate
        + lax.dynamic_slice_in_dim(swiglu_up, start_col, own_cols, 0) * grad_sup,
        1,
    )
    gains = jnp.stack(
        [
            lax.dynamic_slice_in_dim(first_gain, start_col, own_cols),
            lax.dynamic_slice_in_dim(second_gain, start_col, own_cols),
        ]
    )
    gain_grads = lax.psum(jnp.stack([first_sum, second_sum]), "mp") / gains
    grad_normed_one = lax.psum_scatter(normed_part, "mp", scatter_dimension=0, tiled=True)
    tokens_share = share(tokens_in)
    scale_one = rms(tokens_share)
    pulled_one = grad_normed_one * first_gain
    grad_tokens = (
        share(grad_residual)
        + scale_one * pulled_one
        - tokens_share * scale_one**3 * jnp.mean(pulled_one * tokens_share, -1, keepdims=True)
    )
    return (
        output,
        grad_tokens,
        weight_grads[0],
        weight_grads[1],
        weight_grads[2],
        weight_grads[3],
        grad_outw,
        grad_sgate,
        grad_sup,
        grad_sdown,
        gain_grads[0],
        grad_group,
        gain_grads[1],
    )


Z, X = 4, 2


def x_swap(array):
    return lax.ppermute(array, "seq", [(s, s ^ 1) for s in range(Z * X)])


def cut(array, place, size, axis):
    return lax.dynamic_slice_in_dim(array, place * size, size, axis)


def in_order(first, mine, other, axis):
    return jnp.where(
        first, jnp.concatenate([mine, other], axis), jnp.concatenate([other, mine], axis)
    )


F32, BF16 = jnp.float32, jnp.bfloat16
MESH = pl.DeviceIdType.MESH
ANY = pl.BlockSpec(memory_space=pl.ANY)
WHOLE = pl.BlockSpec(memory_space=pltpu.VMEM)
TILE = 256
VMEM_BYTES = 60 << 20


def halves(entries):
    high = entries.astype(BF16)
    return high, (entries - high.astype(F32)).astype(BF16)


def product(left, right, contract_left, contract_right):
    return lax.dot_general(
        left,
        right,
        (((contract_left,), (contract_right,)), ((), ())),
        preferred_element_type=F32,
    )


def three_pass(left, right, contract_left, contract_right):
    (left_high, left_low), (right_high, right_low) = left, right
    return product(left_high, right_high, contract_left, contract_right) + (
        product(left_high, right_low, contract_left, contract_right)
        + product(left_low, right_high, contract_left, contract_right)
    )


def few_rows(left, right, contract_right):
    (left_high, left_low), (right_high, right_low) = left, right
    rows = left_high.shape[0]
    both = product(jnp.concatenate([left_high, left_low]), right_high, 1, contract_right)
    return both[:rows] + (product(left_high, right_low, 1, contract_right) + both[rows:])


def remote(src, dst, sems, index, device):
    return pltpu.make_async_remote_copy(
        src_ref=src,
        dst_ref=dst,
        send_sem=sems[0].at[index],
        recv_sem=sems[1].at[index],
        device_id=device,
        device_id_type=MESH,
    )


def dma_sems(count):
    return [pltpu.SemaphoreType.DMA((count,)), pltpu.SemaphoreType.DMA((count,))]


class Move:
    def __init__(self, ins, outs, scratch):
        self.ins, self.outs, self.scratch_refs = ins, outs, scratch
        place, part = lax.axis_index("seq"), lax.axis_index("mp")
        self.z, self.x, self.y, self.core = place // X, place % X, part // 2, part % 2
        self.setup()

    def setup(self):
        pass

    def device(self, z, x, y, core):
        return (z * X + x, y * 2 + core)

    def x_peer(self):
        return self.device(self.z, 1 - self.x, self.y, self.core)

    def y_peer(self):
        return self.device(self.z, self.x, 1 - self.y, self.core)

    def core_peer(self):
        return self.device(self.z, self.x, self.y, 1 - self.core)

    def holds(self, way, step):
        source = self.z - way * step
        return (source >= 0) & (source < Z)

    def goes_on(self, way, step):
        return self.holds(way, step - 1) & (self.z + way >= 0) & (self.z + way < Z)

    def each(self, step, action):
        if step == 0:
            action(1)
        else:
            for way in (1, -1):
                pl.when(self.holds(way, step))(lambda way=way: action(way))

    def greet(self, far):
        barrier = pltpu.get_barrier_semaphore()

        def signal(device):
            pl.semaphore_signal(barrier, inc=1, device_id=device, device_id_type=MESH)

        signal(self.x_peer())
        signal(self.y_peer())
        signal(self.core_peer())
        if far:
            for distance in range(1, Z):
                signal(self.device((self.z + distance) % Z, self.x, self.y, self.core))
            pl.semaphore_wait(barrier, 3 + Z - 1)
        else:
            for way in (1, -1):
                ahead = (self.z + way >= 0) & (self.z + way < Z)
                pl.when(ahead)(
                    lambda way=way: signal(self.device(self.z + way, self.x, self.y, self.core))
                )
            neighbours = jnp.where(self.z > 0, 1, 0) + jnp.where(self.z < Z - 1, 1, 0)
            pl.semaphore_wait(barrier, 3 + neighbours)


class Gather(Move):
    PIECES = 2
    OWN = 5

    def in_specs(arrays):
        return [ANY]

    def results(arrays):
        return [((Z * X * arrays[0].shape[0], arrays[0].shape[1]), ANY)]

    def scratch(arrays):
        return [*dma_sems(52 * Gather.PIECES), pltpu.SemaphoreType.DMA((1,))]

    def setup(self):
        (self.block,), (self.out,) = self.ins, self.outs
        self.sems, self.local = self.scratch_refs[:2], self.scratch_refs[2]
        self.rows = self.block.shape[0]
        self.size = self.rows // self.PIECES
        self.tile = self.block.shape[1] // 16

    def cols(self, first, count):
        return pl.ds(pl.multiple_of(first * self.tile, self.tile), count * self.tile)

    def columns(self, y, core):
        return self.cols((16 - 2 * self.OWN) * y + self.OWN * core, self.OWN)

    def y_count(self, big):
        most = min(16 - 2 * self.OWN, self.OWN)
        return most if big else 16 - 2 * self.OWN - most

    def y_columns(self, y, big):
        count = self.y_count(big)
        first = (16 - count) * y if big else self.OWN * (1 - y) + 2 * self.OWN * y
        return self.cols(first, count)

    def region(self, z, x, piece, columns):
        row = (z * X + x) * self.rows + piece * self.size
        return self.out.at[pl.ds(pl.multiple_of(row, self.size), self.size), columns]

    def fetched(self, z, x, piece):
        return self.region(z, x, piece, self.columns(self.y, self.core))

    def own(self, piece):
        return self.block.at[
            pl.ds(piece * self.size, self.size), self.columns(self.y, self.core)
        ]

    def slot(self, way, step):
        return 0 if step == 0 else (0 if way > 0 else 3) + step

    def along(self, way, step, piece, arriving):
        dst = self.fetched(self.z - way * (step if arriving else step - 1), self.x, piece)
        return remote(
            self.own(piece) if step == 1 and not arriving else dst,
            dst,
            self.sems,
            52 * piece + (0 if way > 0 else 3) + step - 1,
            self.device(self.z + way, self.x, self.y, self.core),
        )

    def across(self, way, step, piece, arriving):
        dst = self.fetched(self.z - way * step, 1 - self.x if arriving else self.x, piece)
        return remote(
            self.own(piece) if step == 0 and not arriving else dst,
            dst,
            self.sems,
            52 * piece + 6 + self.slot(way, step),
            self.x_peer(),
        )

    def inside(self, way, step, other_x, piece, arriving):
        region = self.region(
            self.z - way * step,
            1 - self.x if other_x else self.x,
            piece,
            self.columns(self.y, 1 - self.core if arriving else self.core),
        )
        index = 52 * piece + 13 + self.slot(way, step) + (0 if other_x else 6)
        return remote(region, region, self.sems, index, self.core_peer())

    def over_y(self, way, step, other_x, piece, arriving, big):
        region = self.region(
            self.z - way * step,
            1 - self.x if other_x else self.x,
            piece,
            self.y_columns(1 - self.y if arriving else self.y, big),
        )
        index = 52 * piece + 26 + self.slot(way, step) + (0 if other_x else 6)
        return remote(region, region, self.sems, index, self.y_peer())

    def inside_y(self, way, step, other_x, piece, big):
        region = self.region(
            self.z - way * step,
            1 - self.x if other_x else self.x,
            piece,
            self.y_columns(1 - self.y, big),
        )
        index = 52 * piece + 39 + self.slot(way, step) + (0 if other_x else 6)
        return remote(region, region, self.sems, index, self.core_peer())

    def sized(self, big, action):
        if self.y_count(True):
            pl.when(big)(lambda: action(True))
        if self.y_count(False):
            pl.when(jnp.logical_not(big))(lambda: action(False))

    def pass_on(self, way, step, other_x, piece):
        self.sized(
            self.core == self.y,
            lambda big: self.over_y(way, step, other_x, piece, False, big).start(),
        )
        self.inside(way, step, other_x, piece, False).start()

    def begin(self):
        for piece in range(self.PIECES):
            self.across(1, 0, piece, False).start()
            for way in (1, -1):
                pl.when(self.goes_on(way, 1))(
                    lambda way=way, piece=piece: self.along(way, 1, piece, False).start()
                )
        self.own_copy().start()

    def own_copy(self):
        row = pl.multiple_of((self.z * X + self.x) * self.rows, self.rows)
        return pltpu.make_async_copy(
            self.block, self.out.at[pl.ds(row, self.rows), :], self.local.at[0]
        )

    def arrive_along(self, step, piece):
        def action(way):
            self.along(way, step, piece, True).wait_recv()
            if step < Z - 1:
                pl.when(self.goes_on(way, step + 1))(
                    lambda: self.along(way, step + 1, piece, False).start()
                )
            self.across(way, step, piece, False).start()
            self.pass_on(way, step, False, piece)

        self.each(step, action)

    def arrive_across(self, step, piece):
        def action(way):
            self.across(way, step, piece, True).wait_recv()
            self.pass_on(way, step, True, piece)

        self.each(step, action)

    def arrive_y(self, step, other_x, piece):
        def action(way):
            def sized(big):
                self.over_y(way, step, other_x, piece, True, big).wait_recv()
                self.inside_y(way, step, other_x, piece, big).start()

            self.sized(self.core != self.y, sized)

        self.each(step, action)

    def finish(self):
        self.own_copy().wait()
        for piece in range(self.PIECES):
            for way in (1, -1):
                for step in range(1, Z):
                    pl.when(self.goes_on(way, step))(
                        lambda way=way, step=step, piece=piece: self.along(
                            way, step, piece, False
                        ).wait_send()
                    )
            for step in range(Z):

                def action(way, step=step, piece=piece):
                    self.across(way, step, piece, False).wait_send()
                    for other_x in (False, True) if step else (True,):
                        self.inside(way, step, other_x, piece, False).wait_send()
                        self.inside(way, step, other_x, piece, True).wait_recv()

                        def sent(big, other_x=other_x):
                            self.over_y(way, step, other_x, piece, False, big).wait_send()
                            self.inside_y(way, step, other_x, piece, big).wait_recv()

                        def handed(big, other_x=other_x):
                            self.inside_y(way, step, other_x, piece, big).wait_send()

                        self.sized(self.core == self.y, sent)
                        self.sized(self.core != self.y, handed)

                self.each(step, action)

    def events(self):
        def round_of(index):
            step, piece = index // 2 + 1, index % 2

            def event():
                if step < Z:
                    self.arrive_along(step, piece)
                if step <= Z:
                    self.arrive_across(step - 1, piece)
                if 1 <= step - 1 < Z:
                    self.arrive_y(step - 1, False, piece)
                if 0 <= step - 2 < Z:
                    self.arrive_y(step - 2, True, piece)

            return event

        return [round_of(index) for index in range(2 * (Z + 1))] + [self.finish]


class Gather12(Gather):
    OWN = 6


class Sum(Move):
    def in_specs(arrays):
        return [WHOLE]

    def results(arrays):
        return [(arrays[0].shape, WHOLE)]

    def scratch(arrays):
        rows, columns = arrays[0].shape
        return [pltpu.VMEM((4, rows, columns // 2), F32), *dma_sems(3)]

    def setup(self):
        (self.part,), (self.out,) = self.ins, self.outs
        self.landing, self.sems = self.scratch_refs[0], self.scratch_refs[1:]
        self.half = self.part.shape[1] // 2

    def columns(self, ref, core):
        return ref.at[:, pl.ds(pl.multiple_of(core * self.half, self.half), self.half)]

    def first(self):
        return remote(
            self.columns(self.part, 1 - self.core),
            self.landing.at[0],
            self.sems,
            0,
            self.core_peer(),
        )

    def second(self):
        return remote(self.landing.at[1], self.landing.at[2], self.sems, 1, self.y_peer())

    def third(self):
        return remote(self.landing.at[1], self.landing.at[3], self.sems, 2, self.core_peer())

    def begin(self):
        self.first().start()

    def to_y(self):
        self.first().wait()
        self.landing[1] = self.columns(self.part, self.core)[...] + self.landing[0]
        self.second().start()

    def back(self):
        self.second().wait()
        self.landing[1] = self.landing[1] + self.landing[2]
        self.third().start()

    def finish(self):
        self.third().wait()
        self.columns(self.out, self.core)[...] = self.landing[1]
        self.columns(self.out, 1 - self.core)[...] = self.landing[3]

    def events(self):
        return [self.to_y, self.back, self.finish]


class Scatter(Move):
    def in_specs(arrays):
        return [WHOLE]

    def results(arrays):
        rows, columns = arrays[0].shape
        return [((rows // 4, columns), WHOLE)]

    def scratch(arrays):
        rows, columns = arrays[0].shape
        return [pltpu.VMEM((5, rows // 4, columns), F32), *dma_sems(3)]

    def setup(self):
        (self.part,), (self.out,) = self.ins, self.outs
        self.landing, self.sems = self.scratch_refs[0], self.scratch_refs[1:]
        self.rows = self.part.shape[0] // 4

    def block(self, y, core):
        row = pl.multiple_of((y * 2 + core) * self.rows, self.rows)
        return self.part.at[pl.ds(row, self.rows), :]

    def to_core(self, y):
        block = self.block(self.y if y == 0 else 1 - self.y, 1 - self.core)
        return remote(block, self.landing.at[y], self.sems, y, self.core_peer())

    def to_y(self):
        return remote(self.landing.at[2], self.landing.at[3], self.sems, 2, self.y_peer())

    def begin(self):
        self.to_core(1).start()
        self.to_core(0).start()

    def middle(self):
        self.to_core(1).wait()
        self.landing[2] = self.block(1 - self.y, self.core)[...] + self.landing[1]
        self.to_y().start()

    def finish(self):
        self.to_core(0).wait()
        self.to_y().wait()
        self.out[...] = (self.block(self.y, self.core)[...] + self.landing[0]) + self.landing[3]

    def events(self):
        return [self.middle, self.finish]


class Heads(Move):
    def in_specs(arrays):
        return [ANY]

    def results(arrays):
        rows, columns = arrays[0].shape
        return [((Z * X * rows, columns // X), ANY)]

    def scratch(arrays):
        return [*dma_sems(7), pltpu.SemaphoreType.DMA((1,))]

    def setup(self):
        (self.own,), (self.out,) = self.ins, self.outs
        self.sems, self.local = self.scratch_refs[:2], self.scratch_refs[2]
        self.rows, columns = self.own.shape
        self.width = columns // X

    def block(self, z, x):
        row = pl.multiple_of((z * X + x) * self.rows, self.rows)
        return self.out.at[pl.ds(row, self.rows), :]

    def plane(self, z):
        row = pl.multiple_of(z * X * self.rows, X * self.rows)
        return self.out.at[pl.ds(row, X * self.rows), :]

    def own_columns(self, x):
        return self.own.at[:, pl.ds(pl.multiple_of(x * self.width, self.width), self.width)]

    def swap(self):
        return remote(
            self.own_columns(1 - self.x), self.block(self.z, self.x), self.sems, 6, self.x_peer()
        )

    def keep(self):
        return pltpu.make_async_copy(
            self.own_columns(self.x), self.block(self.z, self.x), self.local.at[0]
        )

    def along(self, way, step, arriving):
        plane = self.plane(self.z - way * (step if arriving else step - 1))
        return remote(
            plane,
            plane,
            self.sems,
            (0 if way > 0 else 3) + step - 1,
            self.device(self.z + way, self.x, self.y, self.core),
        )

    def begin(self):
        self.swap().start()
        self.keep().start()

    def start_along(self, way, step):
        pl.when(self.goes_on(way, step))(lambda: self.along(way, step, False).start())

    def swapped(self):
        self.swap().wait()
        self.keep().wait()
        for way in (1, -1):
            self.start_along(way, 1)

    def arrive(self, step):
        def action(way):
            self.along(way, step, True).wait_recv()
            if step < Z - 1:
                self.start_along(way, step + 1)

        self.each(step, action)

    def finish(self):
        self.arrive(Z - 1)
        for way in (1, -1):
            for step in range(1, Z):
                pl.when(self.goes_on(way, step))(
                    lambda way=way, step=step: self.along(way, step, False).wait_send()
                )

    def events(self):
        return [self.swapped, lambda: self.arrive(1), lambda: self.arrive(2), self.finish]


class Columns(Move):
    def in_specs(arrays):
        return [ANY]

    def results(arrays):
        rows, columns = arrays[0].shape
        return [((Z, X, rows, columns // Z), ANY)]

    def scratch(arrays):
        return [*dma_sems(Z + Z + 1), pltpu.SemaphoreType.DMA((1,))]

    def setup(self):
        (self.own,), (self.out,) = self.ins, self.outs
        self.sems, self.local = self.scratch_refs[:2], self.scratch_refs[2]
        self.half = self.own.shape[1] // (2 * Z)

    def piece(self, z):
        start = pl.multiple_of((z * 2 + self.core) * self.half, self.half)
        return self.own.at[:, pl.ds(start, self.half)]

    def landing(self, z, x, core):
        start = pl.multiple_of(core * self.half, self.half)
        return self.out.at[z, x, :, pl.ds(start, self.half)]

    def along(self, distance):
        z = (self.z + distance) % Z
        return remote(
            self.piece(z),
            self.landing(self.z, self.x, self.core),
            self.sems,
            distance,
            self.device(z, self.x, self.y, self.core),
        )

    def keep(self):
        return pltpu.make_async_copy(
            self.piece(self.z), self.landing(self.z, self.x, self.core), self.local.at[0]
        )

    def across(self, distance):
        block = self.landing((self.z - distance) % Z, self.x, self.core)
        return remote(block, block, self.sems, Z + distance, self.x_peer())

    def inside(self):
        start = pl.multiple_of(self.core * self.half, self.half)
        part = self.out.at[:, :, :, pl.ds(start, self.half)]
        return remote(part, part, self.sems, 2 * Z, self.core_peer())

    def begin(self):
        self.keep().start()
        for distance in (1, 3, 2):
            self.along(distance).start()

    def arrived(self, distance):
        if distance == 0:
            self.keep().wait()
        else:
            self.along(distance).wait()
        self.across(distance).start()

    def all_here(self):
        for distance in range(Z):
            self.across(distance).wait()
        self.inside().start()

    def events(self):
        return [
            lambda: self.arrived(0),
            lambda: self.arrived(1),
            lambda: self.arrived(3),
            lambda: self.arrived(2),
            self.all_here,
            lambda: self.inside().wait(),
        ]


class SwapX(Move):
    def in_specs(arrays):
        return [ANY] * len(arrays)

    def results(arrays):
        return [(array.shape, ANY) for array in arrays]

    def scratch(arrays):
        return dma_sems(len(arrays))

    def setup(self):
        pass

    def copies(self):
        return [
            remote(src, dst, self.scratch_refs, index, self.x_peer())
            for index, (src, dst) in enumerate(zip(self.ins, self.outs, strict=True))
        ]

    def begin(self):
        for copy in self.copies():
            copy.start()

    def finish(self):
        for copy in self.copies():
            copy.wait()

    def events(self):
        return [self.finish]


class SwapBlocks(Move):
    def in_specs(arrays):
        return [ANY] * len(arrays)

    def results(arrays):
        return [((array.shape[0] // X, array.shape[1]), ANY) for array in arrays]

    def scratch(arrays):
        return dma_sems(len(arrays))

    def send(self, index):
        src = self.ins[index]
        rows = src.shape[0] // X
        return remote(
            src.at[pl.ds(pl.multiple_of((1 - self.x) * rows, rows), rows), :],
            self.outs[index],
            self.scratch_refs,
            index,
            self.x_peer(),
        )

    def begin(self):
        for index in range(len(self.ins)):
            self.send(index).start()

    def finish(self):
        for index in range(len(self.ins)):
            self.send(index).wait()

    def events(self):
        return [self.finish]


class SumAll(Move):
    def in_specs(arrays):
        return [WHOLE]

    def results(arrays):
        rows, columns = arrays[0].shape
        return [((rows // X, columns), WHOLE)]

    def scratch(arrays):
        rows, columns = arrays[0].shape
        return [pltpu.VMEM((6, rows // X, columns), F32), *dma_sems(3)]

    def setup(self):
        (self.part,), (self.out,) = self.ins, self.outs
        self.landing, self.sems = self.scratch_refs[0], self.scratch_refs[1:]
        self.rows = self.part.shape[0] // X

    def half(self, x):
        return self.part.at[pl.ds(pl.multiple_of(x * self.rows, self.rows), self.rows), :]

    def first(self):
        return remote(self.half(1 - self.x), self.landing.at[0], self.sems, 0, self.x_peer())

    def second(self):
        return remote(self.landing.at[1], self.landing.at[2], self.sems, 1, self.core_peer())

    def third(self):
        return remote(self.landing.at[3], self.landing.at[4], self.sems, 2, self.y_peer())

    def begin(self):
        self.first().start()

    def to_core(self):
        self.first().wait()
        self.landing[1] = self.half(self.x)[...] + self.landing[0]
        self.second().start()

    def to_y(self):
        self.second().wait()
        self.landing[3] = self.landing[1] + self.landing[2]
        self.third().start()

    def finish(self):
        self.third().wait()
        self.out[...] = self.landing[3] + self.landing[4]

    def events(self):
        return [self.to_core, self.to_y, self.finish]


class Refs(dict):
    __getattr__ = dict.__getitem__


def fused(arrays, results, scratch, steps, body, collective_id, far=False, flops=0):
    names = [*arrays, *results, *scratch]

    def kernel(*refs):
        refs = list(refs)
        here = Refs(zip([*arrays, *results], refs, strict=False))
        del refs[: len(arrays) + len(results)]
        for name, needed in scratch.items():
            here[name] = refs[: len(needed)]
            del refs[: len(needed)]
        step = pl.program_id(0)
        if collective_id is not None:
            pl.when(step == 0)(lambda: Move([], [], []).greet(far))
        body(here, step)

    outputs = pl.pallas_call(
        kernel,
        grid=(steps,),
        out_shape=[
            jax.ShapeDtypeStruct(result[0], result[2] if len(result) > 2 else F32)
            for result in results.values()
        ],
        in_specs=[spec for _, spec in arrays.values()],
        out_specs=[result[1] for result in results.values()],
        scratch_shapes=[one for needed in scratch.values() for one in needed],
        compiler_params=pltpu.CompilerParams(
            has_side_effects=True,
            vmem_limit_bytes=VMEM_BYTES,
            **({} if collective_id is None else dict(collective_id=collective_id)),
        ),
        cost_estimate=pl.CostEstimate(flops=flops, bytes_accessed=32 << 20, transcendentals=0),
    )(*(array for array, _ in arrays.values()))
    return Refs(zip(results, outputs, strict=True))


def at(now, when, *actions):
    for action in actions:
        pl.when(now == when)(action)


def schedule(now, when, events):
    for event, moment in zip(events, when, strict=True):
        pl.when(now == moment)(event)


SPLIT_ROWS = 128


def first_kernel(block, out_weight, w_gate, w_up, w_down, collective_id):
    inner, columns = w_gate.shape
    padded = pl.cdiv(columns, TILE) * TILE
    steps = inner // SPLIT_ROWS
    down_steps = padded // SPLIT_ROWS
    out_rows = out_weight.shape[0] // steps

    def body(refs, step):
        gather = Gather12([refs.block], [refs.all], refs.gather)
        pl.when(step == 0)(gather.begin)

        def store(name, entries, spot):
            refs[f"{name}_high"][:, spot], refs[f"{name}_low"][:, spot] = halves(entries)

        whole = slice(None)
        store("out", refs.out[...], whole)
        for name in ("gate", "up"):
            store(name, refs[name][...], slice(0, columns))
            for half in ("high", "low"):
                refs[f"{name}_{half}"][:, columns:] = jnp.zeros(
                    (SPLIT_ROWS, padded - columns), BF16
                )
        row = jnp.minimum(step, down_steps - 1) * SPLIT_ROWS + lax.broadcasted_iota(
            jnp.int32, (SPLIT_ROWS, inner), 0
        )
        down = jnp.where(row < columns, refs.down[...], 0.0)
        store("down", down, whole)
        store("turned", jnp.transpose(down), whole)
        schedule(step, (2, 3, 5, 6, 8, 10, 11, 13, 14, 15, 15), gather.events())

    def by_rows(rows, columns, last=steps - 1):
        return pl.BlockSpec((rows, columns), lambda step: (jnp.minimum(step, last), 0))

    results = dict(all=Gather.results([block])[0])
    for half in ("high", "low"):
        for name in ("gate", "up"):
            results[f"{name}_{half}"] = ((inner, padded), by_rows(SPLIT_ROWS, padded), BF16)
        results[f"out_{half}"] = (out_weight.shape, by_rows(out_rows, inner), BF16)
        results[f"down_{half}"] = (
            (padded, inner), by_rows(SPLIT_ROWS, inner, down_steps - 1), BF16
        )
        results[f"turned_{half}"] = (
            (inner, padded),
            pl.BlockSpec(
                (inner, SPLIT_ROWS), lambda step: (0, jnp.minimum(step, down_steps - 1))
            ),
            BF16,
        )
    return fused(
        dict(
            block=(block, WHOLE),
            gate=(w_gate, by_rows(SPLIT_ROWS, columns)),
            up=(w_up, by_rows(SPLIT_ROWS, columns)),
            down=(w_down, by_rows(SPLIT_ROWS, inner, pl.cdiv(columns, SPLIT_ROWS) - 1)),
            out=(out_weight, by_rows(out_rows, inner)),
        ),
        results,
        dict(gather=Gather.scratch([block])),
        steps,
        body,
        collective_id,
    )


def halves_scratch(rows, inner):
    return [
        pltpu.VMEM((rows, inner), BF16),
        pltpu.VMEM((rows, inner), BF16),
        pltpu.VMEM((rows // 128, 128, inner), F32),
        pltpu.SemaphoreType.DMA((rows // 128,)),
    ]


def load_halves(src_ref, high_ref, low_ref, stage_ref, sem, change=None, start=True, split=True):
    count, rows, _ = stage_ref.shape

    def spot(index):
        return pl.ds(pl.multiple_of(index * rows, rows), rows)

    def fetch(index):
        return pltpu.make_async_copy(
            src_ref.at[spot(index), :], stage_ref.at[index], sem.at[index]
        )

    def one(index, carried):
        fetch(index).wait()
        if change is not None:
            change(index)
        high, low = halves(stage_ref[index])
        high_ref[spot(index), :] = high
        low_ref[spot(index), :] = low
        return carried

    if start:
        for index in range(count):
            fetch(index).start()
    if split:
        lax.fori_loop(0, count, one, 0)


STRIP = 512


def strips(rows, action):
    def one(index, carried):
        action(index, pl.ds(pl.multiple_of(index * STRIP, STRIP), STRIP))
        return carried

    lax.fori_loop(0, rows // STRIP, one, 0)


def block_fetch(src, buf, sem, index):
    return pltpu.make_async_copy(src, buf.at[index], sem.at[index])


EARLY = 3


def mixer_kernel(
    all_tokens, tokens_in, cotangent, lengths, lower_bound, in_weights, split, first_gain, group_gain,
    second_gain, collective_id,
):
    rows, inner = all_tokens.shape
    own_rows = tokens_in.shape[0]
    count = 4
    wide = inner // Z
    heads = TILE // HDIM
    chunks = rows // CHUNK
    tiles = EARLY
    columns = tiles * TILE
    parts = rows // STRIP
    middle = count + chunks
    steps = middle + 1 + tiles

    def body(refs, step):
        place = lax.axis_index("seq")
        x = place % X
        here = pl.ds(pl.multiple_of(x * TILE, TILE), TILE)
        there = pl.ds(pl.multiple_of((1 - x) * TILE, TILE), TILE)
        first_col = pl.multiple_of((place // X) * wide, wide)
        gather = Gather([refs.cotangent], [refs.all_cotangent], refs.gather)
        part_ref, sum_ref, *sum_scratch = refs.sum
        total = Sum([part_ref], [sum_ref], sum_scratch)
        high_ref, low_ref, stage_ref, stage_sem = refs.halves
        weight_buf, weight_sem, down_buf, down_sem, out_buf, out_sem, ready_ref = refs.weights
        (state_ref,) = refs.state
        other_ref, send, recv = refs.swap
        now = step * parts

        def fetch(index):
            return [
                pltpu.make_async_copy(
                    refs[f"weight_{index}"].at[:, here],
                    weight_buf.at[index % 2],
                    weight_sem.at[index % 2],
                )
            ]

        def fetch_down(tile):
            slot = lax.rem(tile, 2)
            spot = pl.ds(pl.multiple_of(tile * TILE, TILE), TILE)
            return [
                pltpu.make_async_copy(
                    refs[f"turned_{half}"].at[:, spot], down_buf.at[slot, at], down_sem.at[slot, at]
                )
                for at, half in enumerate(("high", "low"))
            ]

        def start(copies):
            for copy in copies:
                copy.start()

        def wait(copies):
            for copy in copies:
                copy.wait()

        def fetch_out():
            return [
                pltpu.make_async_copy(refs[f"out_{half}"], out_buf.at[at], out_sem.at[at])
                for at, half in enumerate(("high", "low"))
            ]

        def swap():
            peer = pl.multiple_of((place + 1 - 2 * x) * own_rows, own_rows)
            return remote(
                refs.mixer.at[pl.ds(peer, own_rows), :], other_ref, (send, recv), 0, gather.x_peer()
            )

        def pause(part):
            mixing = count * parts
            schedule(
                now + part,
                (0, 1, 2, 3, 5, mixing, mixing + 2 * parts, mixing + 4 * parts, mixing + 7 * parts),
                gather.events()[:9],
            )

        def normalize(index):
            entries = stage_ref[index]
            stage_ref[index] = entries * rms(entries) * refs.first_gain[...]
            refs.normed_cols[pl.ds(pl.multiple_of(index * 128, 128), 128), :] = stage_ref[
                index, :, pl.ds(first_col, wide)
            ]

        @pl.when(step == 0)
        def _():
            gather.begin()
            start(fetch(0))
            start(fetch_out())
            load_halves(refs.tokens, high_ref, low_ref, stage_ref, stage_sem, normalize)
            state_ref[...] = jnp.zeros_like(state_ref)

        for index in range(count):

            @pl.when(step == index)
            def _(index=index):
                if index + 1 < count:
                    start(fetch(index + 1))
                wait(fetch(index))

        @pl.when(step < count)
        def _():
            ready_ref[0], ready_ref[1] = halves(weight_buf[lax.rem(step, 2)])
            target = pl.ds(pl.multiple_of(step * TILE, TILE), TILE)

            def strip(index, spot):
                refs.projected[spot, target] = three_pass(
                    (high_ref[spot, :], low_ref[spot, :]),
                    (ready_ref[0], ready_ref[1]),
                    1,
                    0,
                )
                pause(index)

            strips(rows, strip)

        @pl.when((step >= count) & (step < middle))
        def _():
            chunk = step - count
            spot = pl.ds(pl.multiple_of(chunk * CHUNK, CHUNK), CHUNK)
            forward_chunk(
                chunk,
                refs.lengths,
                refs.projected.at[spot, :],
                refs.lower_bound.at[:, here],
                refs.group_gain.at[:, here],
                refs.mixer.at[spot, :],
                refs.raw.at[spot, :],
                refs.states.at[pl.ds(chunk, 1)],
                state_ref,
            )
            pause(0)

        @pl.when(step == middle)
        def _():
            swap().start()
            start(fetch_down(0))
            wait(fetch_out())

            def out_rows(spot):
                return out_buf[0, spot, :], out_buf[1, spot, :]

            own = refs.mixer[pl.ds(pl.multiple_of(place * own_rows, own_rows), own_rows), :]
            part_ref[...] = few_rows(halves(own), out_rows(here), 0)
            swap().wait()
            part_ref[...] += few_rows(halves(other_ref[...]), out_rows(there), 0)
            total.begin()
            total.to_y()
            gather.events()[9]()
            gather.finish()
            load_halves(refs.all_cotangent, high_ref, low_ref, stage_ref, stage_sem)

        @pl.when(step > middle)
        def _():
            tile = step - middle - 1
            pl.when(tile < tiles - 1)(lambda: start(fetch_down(tile + 1)))
            wait(fetch_down(tile))
            slot = lax.rem(tile, 2)
            refs.grad_hidden[...] = three_pass(
                (high_ref[...], low_ref[...]), (down_buf[slot, 0], down_buf[slot, 1]), 1, 0
            )

        @pl.when(step == steps - 1)
        def _():
            total.back()
            total.finish()
            residual = refs.tokens_in[...] + sum_ref[...]
            refs.residual[...] = residual
            refs.normed_two[...] = residual * rms(residual) * refs.second_gain[...]

    own_shape = (own_rows, inner)
    return fused(
        dict(
            lengths=(lengths, pl.BlockSpec(memory_space=pltpu.SMEM)),
            tokens=(all_tokens, ANY),
            tokens_in=(tokens_in, WHOLE),
            cotangent=(cotangent, WHOLE),
            lower_bound=(lower_bound[None], WHOLE),
            first_gain=(first_gain[None], WHOLE),
            group_gain=(group_gain[None], WHOLE),
            second_gain=(second_gain[None], WHOLE),
            **{f"weight_{index}": (weight, ANY) for index, weight in enumerate(in_weights)},
            **{
                f"{name}_{half}": (split[f"{name}_{half}"], ANY)
                for name in ("out", "turned")
                for half in ("high", "low")
            },
        ),
        dict(
            all_cotangent=((rows, inner), ANY),
            projected=((rows, count * TILE), WHOLE),
            normed_cols=((rows, wide), WHOLE),
            mixer=((rows, TILE), WHOLE),
            raw=((rows, TILE), WHOLE),
            states=((chunks, heads, HDIM, HDIM), WHOLE),
            grad_hidden=(
                (rows, columns),
                pl.BlockSpec((rows, TILE), lambda step: (0, jnp.maximum(step - middle - 1, 0))),
            ),
            residual=(own_shape, WHOLE),
            normed_two=(own_shape, WHOLE),
        ),
        dict(
            halves=halves_scratch(rows, inner),
            weights=[
                pltpu.VMEM((2, inner, TILE), F32),
                pltpu.SemaphoreType.DMA((2,)),
                pltpu.VMEM((2, 2, inner, TILE), BF16),
                pltpu.SemaphoreType.DMA((2, 2)),
                pltpu.VMEM((2, *split.out_high.shape), BF16),
                pltpu.SemaphoreType.DMA((2,)),
                pltpu.VMEM((2, inner, TILE), BF16),
            ],
            state=[pltpu.VMEM((heads, HDIM, HDIM), F32)],
            swap=[pltpu.VMEM((own_rows, TILE), F32), *dma_sems(1)],
            gather=Gather.scratch([cotangent]),
            sum=[
                pltpu.VMEM(own_shape, F32),
                pltpu.VMEM(own_shape, F32),
                *Sum.scratch([tokens_in]),
            ],
        ),
        steps,
        body,
        collective_id,
        flops=6 * rows * inner * (count * TILE + columns),
    )


def feed_forward_kernel(normed_two, all_cotangent, grad_hidden, split, collective_id):
    rows, inner = normed_two.shape
    token_count = all_cotangent.shape[0]
    columns = split.gate_high.shape[1]
    tiles = columns // TILE

    def body(refs, step):
        gather = Gather([refs.normed_two], [refs.all_normed_two], refs.gather)
        high_ref, low_ref, stage_ref, stage_sem = refs.halves
        (e_ref,) = refs.e
        load = partial(load_halves, refs.all_cotangent, high_ref, low_ref, stage_ref, stage_sem)

        @pl.when(step == 0)
        def _():
            gather.begin()
            load(split=False)
            refs.ffn[...] = jnp.zeros_like(refs.ffn)
            refs.grad[...] = jnp.zeros_like(refs.grad)

        pl.when(step == EARLY - 1)(lambda: load(start=False))

        def both(name):
            return refs[f"{name}_high"][...], refs[f"{name}_low"][...]

        @pl.when(step < EARLY)
        def _():
            e_ref[...] = refs.early[...]

        @pl.when(step >= EARLY)
        def _():
            refs.late[...] = three_pass((high_ref[...], low_ref[...]), both("turned"), 1, 0)
            row = pl.multiple_of(lax.axis_index("seq") * rows, rows)
            e_ref[...] = refs.late[pl.ds(row, rows), :]

        moments = (1, 3, 4, 5, 6, 7, 7, 8, 9, 10, 11)
        schedule(2 * step, moments, gather.events())
        normed = halves(refs.normed_two[...])
        a = few_rows(normed, both("gate"), 0)
        b = few_rows(normed, both("up"), 0)
        e = e_ref[...]
        gate = jax.nn.sigmoid(a)
        silu_a = a * gate
        refs.ffn[...] += few_rows(halves(silu_a * b), both("down"), 0)
        refs.grad[...] += few_rows(
            halves(e * b * (gate * (1.0 + a * (1.0 - gate)))), both("gate"), 1
        ) + few_rows(halves(e * silu_a), both("up"), 1)
        schedule(2 * step + 1, moments, gather.events())

    by_column = pl.BlockSpec((inner, TILE), lambda step: (0, step))
    return fused(
        dict(
            normed_two=(normed_two, WHOLE),
            all_cotangent=(all_cotangent, ANY),
            early=(
                grad_hidden,
                pl.BlockSpec(
                    (rows, TILE), lambda step: (lax.axis_index("seq"), jnp.minimum(step, EARLY - 1))
                ),
            ),
            **{
                f"{name}_{half}": (split[f"{name}_{half}"], spec)
                for name, spec in (
                    ("gate", by_column),
                    ("up", by_column),
                    ("down", pl.BlockSpec((TILE, inner), lambda step: (step, 0))),
                    (
                        "turned",
                        pl.BlockSpec((inner, TILE), lambda step: (0, jnp.maximum(step, EARLY))),
                    ),
                )
                for half in ("high", "low")
            },
        ),
        dict(
            all_normed_two=Gather.results([normed_two])[0],
            ffn=((rows, inner), WHOLE),
            grad=((rows, inner), WHOLE),
            late=(
                (token_count, columns - EARLY * TILE),
                pl.BlockSpec((token_count, TILE), lambda step: (0, jnp.maximum(step - EARLY, 0))),
            ),
        ),
        dict(
            gather=Gather.scratch([normed_two]),
            halves=halves_scratch(token_count, inner),
            e=[pltpu.VMEM((rows, TILE), F32)],
        ),
        tiles,
        body,
        collective_id,
        flops=30 * rows * inner * columns,
    )


SHARES = 2


def tile_share(refs, share, tile):
    high_ref, low_ref, cols_high_ref, cols_low_ref, cot_high_ref, cot_low_ref = refs.halves
    size = high_ref.shape[0] // SHARES
    spot = pl.ds(pl.multiple_of(share * size, size), size)
    normed = high_ref[spot, :], low_ref[spot, :]
    a = three_pass(normed, (refs.gate_high[...], refs.gate_low[...]), 1, 0)
    b = three_pass(normed, (refs.up_high[...], refs.up_low[...]), 1, 0)
    gate = jax.nn.sigmoid(a)
    silu_a = a * gate
    e = jnp.where(tile < EARLY, refs.early[spot, :], refs.late[spot, :])
    cols = cols_high_ref[:, spot], cols_low_ref[:, spot]
    cot = cot_high_ref[spot, :], cot_low_ref[spot, :]
    grads = (
        three_pass(cols, halves(e * b * (gate * (1.0 + a * (1.0 - gate)))), 1, 0),
        three_pass(cols, halves(e * silu_a), 1, 0),
        three_pass(halves(jnp.transpose(silu_a * b)), cot, 1, 0),
    )
    for ref, grad in zip((refs.grad_gate, refs.grad_up, refs.grad_down), grads, strict=True):
        ref[...] = jnp.where(share == 0, 0.0, ref[...]) + grad


def tile_columns(refs):
    cols_high_ref, cols_low_ref, cot_high_ref, cot_low_ref = refs.halves[2:]
    cols_high_ref[...], cols_low_ref[...] = halves(jnp.transpose(refs.normed_cols[...]))
    cot_high_ref[...], cot_low_ref[...] = halves(refs.cot_cols[...])


def tile_parts(all_normed_two, all_cotangent, early, late, split, columns, first, count, tile_of):
    rows, inner = all_normed_two.shape
    narrow = inner // (Z * X)
    columns = min(count * TILE, columns - first * TILE)
    own_columns = pl.BlockSpec((rows, narrow), lambda step: (0, lax.axis_index("seq")))
    by_column = pl.BlockSpec((inner, TILE), lambda step: (0, first + tile_of(step)))
    grad_spec = pl.BlockSpec((narrow, TILE), lambda step: (0, tile_of(step)))
    arrays = dict(
        early=(
            early,
            pl.BlockSpec((rows, TILE), lambda step: (0, jnp.minimum(first + tile_of(step), EARLY - 1))),
        ),
        late=(
            late,
            pl.BlockSpec(
                (rows, TILE), lambda step: (0, jnp.maximum(first + tile_of(step) - EARLY, 0))
            ),
        ),
        **{
            f"{name}_{half}": (split[f"{name}_{half}"], by_column)
            for name in ("gate", "up")
            for half in ("high", "low")
        },
        normed_cols=(all_normed_two, own_columns),
        cot_cols=(all_cotangent, own_columns),
    )
    results = dict(
        grad_gate=((narrow, columns), grad_spec),
        grad_up=((narrow, columns), grad_spec),
        grad_down=(
            (columns, narrow), pl.BlockSpec((TILE, narrow), lambda step: (tile_of(step), 0))
        ),
    )
    scratch = dict(
        halves=[
            pltpu.VMEM((rows, inner), BF16),
            pltpu.VMEM((rows, inner), BF16),
            pltpu.VMEM((narrow, rows), BF16),
            pltpu.VMEM((narrow, rows), BF16),
            pltpu.VMEM((rows, narrow), BF16),
            pltpu.VMEM((rows, narrow), BF16),
        ]
    )
    return arrays, results, scratch


def residual_kernel(
    part, ffn, residual, cotangent, second_gain, split, all_normed_two, tiles, count, collective_id
):
    arrays, results, scratch = tiles(lambda step: step // SHARES)
    rows, inner = all_normed_two.shape
    own_rows = part.shape[0]
    out_shape = split.out_high.shape
    grad_like = jax.ShapeDtypeStruct((own_rows, out_shape[0]), F32)

    def body(refs, step):
        sum_ref, *sum_scratch = refs.sum
        grad_mixer_ref, *heads_scratch = refs.heads
        total = Sum([refs.part], [sum_ref], sum_scratch)
        heads = Heads([grad_mixer_ref], [refs.all_grad_mixer], heads_scratch)
        scatter = Scatter([refs.ffn], [refs.ffn_share], refs.scatter)
        high_ref, low_ref = refs.halves[:2]
        stage_ref, stage_sem, out_sem = refs.stage
        out_buf, out_buf_sem = refs.out
        keep = [
            pltpu.make_async_copy(high_ref, refs.normed_high, out_sem.at[0]),
            pltpu.make_async_copy(low_ref, refs.normed_low, out_sem.at[1]),
        ]
        fetch_out = [
            pltpu.make_async_copy(refs[f"out_{half}"], out_buf.at[at], out_buf_sem.at[at])
            for at, half in enumerate(("high", "low"))
        ]

        def to_heads():
            total.finish()
            residual_here = refs.residual[...]
            scale = rms(residual_here)
            summed = sum_ref[...]
            pulled = summed * refs.second_gain[...]
            grad_residual = (
                refs.cotangent[...]
                + scale * pulled
                - residual_here
                * (scale * scale * scale * jnp.mean(pulled * residual_here, -1, keepdims=True))
            )
            refs.grad_residual[...] = grad_residual
            refs.second[...] = jnp.broadcast_to(
                jnp.sum(summed * residual_here * scale, 0, keepdims=True), refs.second.shape
            )
            for copy in fetch_out:
                copy.wait()
            grad_mixer_ref[...] = few_rows(halves(grad_residual), (out_buf[0], out_buf[1]), 1)
            heads.begin()

        @pl.when(step == 0)
        def _():
            total.begin()
            for copy in fetch_out:
                copy.start()
            load_halves(refs.all_normed_two, high_ref, low_ref, stage_ref, stage_sem)
            total.to_y()
            for copy in keep:
                copy.start()
            tile_columns(refs)

        tile_share(refs, lax.rem(step, SHARES), step // SHARES)
        schedule(step, (1, 2, 3, 5, 6, 7), [total.back, to_heads, *heads.events()])
        schedule(step, (3, 4, 6), [scatter.begin, *scatter.events()])

        @pl.when(step == count * SHARES - 1)
        def _():
            for copy in keep:
                copy.wait()

    return fused(
        dict(
            part=(part, WHOLE),
            ffn=(ffn, WHOLE),
            residual=(residual, WHOLE),
            cotangent=(cotangent, WHOLE),
            second_gain=(second_gain[None], WHOLE),
            out_high=(split.out_high, ANY),
            out_low=(split.out_low, ANY),
            all_normed_two=(all_normed_two, ANY),
            **arrays,
        ),
        dict(
            all_grad_mixer=Heads.results([grad_like])[0],
            ffn_share=Scatter.results([ffn])[0],
            grad_residual=((own_rows, inner), WHOLE),
            second=((8, inner), WHOLE),
            normed_high=((rows, inner), ANY, BF16),
            normed_low=((rows, inner), ANY, BF16),
            **results,
        ),
        dict(
            sum=[pltpu.VMEM((own_rows, inner), F32), *Sum.scratch([part])],
            heads=[pltpu.VMEM(grad_like.shape, F32), *Heads.scratch([grad_like])],
            scatter=Scatter.scratch([ffn]),
            stage=[*halves_scratch(rows, inner)[2:], pltpu.SemaphoreType.DMA((2,))],
            out=[pltpu.VMEM((2, *out_shape), BF16), pltpu.SemaphoreType.DMA((2,))],
            **scratch,
        ),
        count * SHARES,
        body,
        collective_id,
    )


def last_kernel(
    grads, group, blocks, first_part, in_weights, normed_high, normed_low, tiles, count, collective_id
):
    arrays, results, scratch = tiles(
        lambda step: jnp.where(step < SHARES, 0, jnp.maximum(step - 4, 0) // SHARES)
    )
    rows, columns = grads.shape
    own_rows = rows // (Z * X)
    inner, width = in_weights[0].shape
    half = width // X
    matrices = 4
    part_like = jax.ShapeDtypeStruct((own_rows, inner), F32)
    swapped = [jax.ShapeDtypeStruct((own_rows, columns), F32), group]

    def body(refs, step):
        place = lax.axis_index("seq")
        x = place % X
        peer = pl.multiple_of((place + 1 - 2 * x) * own_rows, own_rows)
        other_ref, *swap_scratch = refs.swap
        part_ref, *scatter_scratch = refs.scatter
        weight_buf, weight_sem, load_sem = refs.weights
        swap = SwapX(
            [refs.grads.at[pl.ds(peer, own_rows), :], refs.group],
            [other_ref, refs.other_group],
            swap_scratch,
        )
        blocks_here = SwapBlocks(
            [refs[f"block_{index}"] for index in range(len(blocks))],
            [refs[f"swapped_{index}"] for index in range(len(blocks))],
            refs.blocks,
        )
        scatter = Scatter([part_ref], [refs.share], scatter_scratch)
        sums = SumAll([refs.first_part], [refs.first_sum], refs.sums)

        def fetch(index):
            return block_fetch(refs[f"weight_{index}"], weight_buf, weight_sem, index % 2)

        load = [
            pltpu.make_async_copy(refs[f"normed_{name}"], refs.halves[at], load_sem.at[at])
            for at, name in enumerate(("high", "low"))
        ]

        @pl.when(step == 0)
        def _():
            for copy in load:
                copy.start()
            swap.begin()
            sums.begin()
            part_ref[...] = jnp.zeros_like(part_ref)
            for copy in load:
                copy.wait()
            for index in range(2):
                fetch(index).start()

        @pl.when(step == 1)
        def _():
            swap.finish()
            blocks_here.begin()

        pl.when(step == 0)(lambda: tile_columns(refs))

        @pl.when((step < SHARES) | (step >= matrices + SHARES))
        def _():
            tile_share(refs, lax.rem(step, SHARES), EARLY)

        schedule(step, (0, 1, 2), sums.events())
        pl.when(step == matrices + SHARES)(scatter.middle)
        for index in range(matrices):

            @pl.when(step == index + SHARES)
            def _(index=index):
                fetch(index).wait()
                weight = halves(weight_buf[index % 2])
                if index + 2 < matrices:
                    fetch(index + 2).start()
                own = refs.own_grads[:, index * half : (index + 1) * half]
                other = other_ref[:, index * half : (index + 1) * half]
                low_x, high_x = (jnp.where(x == place_x, own, other) for place_x in range(X))
                part_ref[...] += few_rows(halves(jnp.concatenate([low_x, high_x], 1)), weight, 1)
                if index == matrices - 1:
                    scatter.begin()

        @pl.when(step == matrices + count * SHARES - 1)
        def _():
            scatter.finish()
            blocks_here.finish()


    return fused(
        dict(
            grads=(grads, ANY),
            own_grads=(
                grads, pl.BlockSpec((own_rows, columns), lambda step: (lax.axis_index("seq"), 0))
            ),
            group=(group, ANY),
            first_part=(first_part, WHOLE),
            **{f"block_{index}": (block, ANY) for index, block in enumerate(blocks)},
            **{f"weight_{index}": (weight, ANY) for index, weight in enumerate(in_weights)},
            normed_high=(normed_high, ANY),
            normed_low=(normed_low, ANY),
            **arrays,
        ),
        dict(
            other_group=(group.shape, ANY),
            share=Scatter.results([part_like])[0],
            first_sum=SumAll.results([first_part])[0],
            **{
                f"swapped_{index}": result for index, result in enumerate(SwapBlocks.results(blocks))
            },
            **results,
        ),
        dict(
            swap=[pltpu.VMEM((own_rows, columns), F32), *SwapX.scratch(swapped)],
            scatter=[pltpu.VMEM((own_rows, inner), F32), *Scatter.scratch([part_like])],
            blocks=SwapBlocks.scratch(blocks),
            sums=SumAll.scratch([first_part]),
            weights=[
                pltpu.VMEM((2, inner, width), F32),
                pltpu.SemaphoreType.DMA((2,)),
                pltpu.SemaphoreType.DMA((2,)),
            ],
            **scratch,
        ),
        count * SHARES + matrices,
        body,
        collective_id,
    )


def thin(left, right, contract_left, contract_right):
    (left_high, left_low), (right_high, right_low) = left, right
    return product(
        jnp.concatenate([left_high, left_low], contract_left),
        jnp.concatenate([right_high, right_high], contract_right),
        contract_left,
        contract_right,
    ) + product(left_high, right_low, contract_left, contract_right)


def join(first, second, axis):
    return tuple(jnp.concatenate(pair, axis) for pair in zip(first, second, strict=True))


def running_sum(triangle, entries):
    high, low = halves(entries)
    least = (entries - high.astype(F32) - low.astype(F32)).astype(BF16)
    return product(
        jnp.concatenate([triangle, triangle], 1), jnp.concatenate([high, low], 0), 1, 0
    ) + product(triangle, least, 1, 0)


def chunk_masks(lengths_ref, chunk):
    shape = (CHUNK, CHUNK)
    row = lax.broadcasted_iota(jnp.int32, shape, 0)
    column = lax.broadcasted_iota(jnp.int32, shape, 1)
    start = chunk * CHUNK

    offsets = [0]
    for index in range(lengths_ref.shape[0] - 1):
        offsets.append(offsets[-1] + lengths_ref[index])

    def segment(position):
        return sum(jnp.where(position >= offset, 1, 0) for offset in offsets)

    segment_row = segment(start + row)
    before, last = segment(start - 1), segment(start + CHUNK - 1)
    allowed = (row >= column) & (segment_row == segment(start + column))
    carry = (segment_row == before).astype(F32)
    in_last = (segment_row == last).astype(F32)
    lower = (row >= column).astype(F32).astype(BF16)
    return allowed, carry, in_last, (last == before).astype(F32), lower


def head_terms(pre_query, pre_forget, lower_bound, lower):
    query_gate = jax.nn.sigmoid(pre_query)
    forget_gate = jax.nn.sigmoid(-pre_forget)
    keys = (1.0 - lower_bound) * forget_gate
    log_decay = running_sum(lower, jnp.log1p(-keys))
    last = log_decay[CHUNK - 1 :, :]
    growth, shrink, trail = jnp.exp(log_decay), jnp.exp(-log_decay), jnp.exp(last - log_decay)
    return query_gate, forget_gate, keys, last, growth, shrink, trail


def tall(row):
    return jnp.transpose(jnp.broadcast_to(row, (HDIM, HDIM)))


def forward_chunk(
    chunk, lengths_ref, projected_ref, bound_ref, gain_ref, mixer_ref, raw_ref, states_ref, state_ref
):
    heads = state_ref.shape[0]
    width = heads * HDIM
    allowed, carry, in_last, carry_last, lower = chunk_masks(lengths_ref, chunk)
    for head in range(heads):
        at = slice(head * HDIM, (head + 1) * HDIM)
        pre_query, pre_forget, values, gate_in = (
            projected_ref[:, part * width + head * HDIM : part * width + (head + 1) * HDIM]
            for part in range(4)
        )
        query_gate, _, keys, last, growth, shrink, trail = head_terms(
            pre_query, pre_forget, bound_ref[:, at], lower
        )
        grown = pre_query * query_gate * growth
        state = state_ref[head]
        states_ref[0, head] = state
        value_halves = halves(values)
        scores = thin(halves(grown), halves(keys * shrink), 1, 1)
        scores = jnp.where(allowed, scores, 0.0)
        raw = three_pass(
            join(halves(scores), halves(grown * carry), 1),
            join(value_halves, halves(state), 0),
            1,
            0,
        )
        state_ref[head] = state * (tall(jnp.exp(last)) * carry_last) + thin(
            halves(keys * trail * in_last), value_halves, 0, 0
        )
        raw_ref[:, at] = raw
        scale = lax.rsqrt(jnp.mean(raw * raw, -1, keepdims=True) + group_eps)
        mixer_ref[:, at] = raw * scale * gain_ref[:, at] * jax.nn.silu(gate_in)


def backward_kernel(
    projected, raw_rows, states, grad_mixer, normed_cols, grad_residual, second, weights,
    lower_bound, group_gain, lengths, collective_id,
):
    rows, columns = projected.shape
    count = len(weights)
    width = columns // count
    heads = width // HDIM
    chunks = rows // CHUNK
    wide = normed_cols.shape[1]

    def body(refs, step):
        lengths_ref, projected_ref, raw_ref, states_ref = refs.lengths, refs.projected, refs.raw, refs.states
        grad_ref, grads_ref, group_ref = refs.grad_mixer, refs.grads, refs.group
        later_ref, weight_buf, weight_sem = refs.work
        chunk = chunks - 1 - step
        place = lax.axis_index("seq")
        here = pl.ds(pl.multiple_of((place % X) * width, width), width)
        bound_ref, gain_ref = refs.lower_bound.at[:, here], refs.group_gain.at[:, here]
        block_refs = [refs[f"block_{index}"] for index in range(count)]
        move = Columns([refs.grad_residual], [refs.residual_cols], refs.columns)
        small = Columns([refs.second], [refs.second_cols], refs.small)

        def fetch(index):
            return block_fetch(
                refs[f"weight_{index}"].at[
                    pl.ds(pl.multiple_of((place // X) * wide, wide), wide), here
                ],
                weight_buf,
                weight_sem,
                index,
            )

        @pl.when(step == 0)
        def _():
            move.begin()
            small.begin()
            later_ref[...] = jnp.zeros_like(later_ref)
            group_ref[...] = jnp.zeros_like(group_ref)
            for index in range(count):
                fetch(index).start()
                block_refs[index][...] = jnp.zeros_like(block_refs[index])

        allowed, carry, in_last, carry_last, lower = chunk_masks(lengths_ref, chunk)
        upper = jnp.transpose(lower.astype(F32)).astype(BF16)
        for head in range(heads):
            at = slice(head * HDIM, (head + 1) * HDIM)
            spots = [
                slice(part * width + head * HDIM, part * width + (head + 1) * HDIM)
                for part in range(4)
            ]
            pre_query, pre_forget, values, gate_in = (projected_ref[:, spot] for spot in spots)
            raw, grad, gain = raw_ref[:, at], grad_ref[:, at], gain_ref[:, at]
            state, later = states_ref[0, head], later_ref[head]

            scale = lax.rsqrt(jnp.mean(raw * raw, -1, keepdims=True) + group_eps)
            normed = raw * scale
            gate = jax.nn.sigmoid(gate_in)
            silu_gate = gate_in * gate
            weighted = grad * gain * silu_gate
            group_ref[:, at] += jnp.sum(grad * normed * silu_gate, 0, keepdims=True)
            grads_ref[:, spots[3]] = (
                grad * gain * normed * (gate * (1.0 + gate_in * (1.0 - gate)))
            )
            grad_raw = scale * weighted - raw * (
                scale * scale * scale * jnp.mean(weighted * raw, -1, keepdims=True)
            )

            query_gate, forget_gate, keys, last, growth, shrink, trail = head_terms(
                pre_query, pre_forget, bound_ref[:, at], lower
            )
            grown = pre_query * query_gate * growth
            shrunk = keys * shrink
            trailing = trail * in_last
            ends = keys * trailing
            grown_halves, shrunk_halves = halves(grown), halves(shrunk)
            raw_halves, value_halves, later_halves = halves(grad_raw), halves(values), halves(later)
            scores = jnp.where(allowed, thin(grown_halves, shrunk_halves, 1, 1), 0.0)
            grad_scores = jnp.where(allowed, thin(raw_halves, value_halves, 1, 1), 0.0)
            score_halves = halves(grad_scores)
            grads_ref[:, spots[2]] = three_pass(
                join(halves(jnp.transpose(scores)), halves(ends), 1),
                join(raw_halves, later_halves, 0),
                1,
                0,
            )
            grad_grown = three_pass(
                join(score_halves, halves(grad_raw * carry), 1),
                join(shrunk_halves, halves(jnp.transpose(state)), 0),
                1,
                0,
            )
            grad_shrunk = thin(score_halves, grown_halves, 0, 0)
            grad_ends = thin(value_halves, later_halves, 1, 1)
            through = tall(jnp.exp(last)) * carry_last
            later_ref[head] = later * through + thin(
                halves(grown * carry), raw_halves, 0, 0
            )
            grads_ref[:, spots[0]] = (
                grad_grown * growth * (query_gate * (1.0 + pre_query * (1.0 - query_gate)))
            )
            from_ends = grad_ends * ends
            grad_log = grad_grown * grown - grad_shrunk * shrunk - from_ends
            pulled = jnp.transpose(later * state * through)
            grad_last = jnp.sum(from_ends + pulled, 0, keepdims=True)
            grad_log_forget = running_sum(upper, grad_log) + grad_last
            grad_keys = (
                grad_shrunk * shrink + grad_ends * trailing - grad_log_forget / (1.0 - keys)
            )
            grads_ref[:, spots[1]] = -grad_keys * keys * (1.0 - forget_gate)

        cols = halves(jnp.transpose(refs.normed_cols[...]))
        for index in range(count):
            part = grads_ref[:, index * width : (index + 1) * width]
            block_refs[index][...] += thin(cols, halves(part), 1, 0)

        @pl.when(step == chunks - 1)
        def _():
            total = 0.0
            for index in range(count):
                fetch(index).wait()
                total = total + weight_buf[index] * block_refs[index][...]
            ones = jnp.ones((8, width), BF16)
            high, low = halves(total)
            sums = product(ones, high, 1, 1) + product(ones, low, 1, 1)
            for index in range(X):
                refs.sums[index * 8 : (index + 1) * 8, :] = sums[
                    :, index * wide // X : (index + 1) * wide // X
                ]

        schedule(step, (0, 1, 2, 4, 6, 7), small.events())
        schedule(step, (0, 2, 3, 5, 7, 7), move.events())

    def by_chunk(size):
        return pl.BlockSpec((CHUNK, size), lambda step: (chunks - 1 - step, 0))

    return fused(
        dict(
            lengths=(lengths, pl.BlockSpec(memory_space=pltpu.SMEM)),
            projected=(projected, by_chunk(columns)),
            raw=(raw_rows, by_chunk(width)),
            states=(
                states,
                pl.BlockSpec((1, heads, HDIM, HDIM), lambda step: (chunks - 1 - step, 0, 0, 0)),
            ),
            grad_mixer=(grad_mixer, by_chunk(width)),
            normed_cols=(normed_cols, by_chunk(wide)),
            lower_bound=(lower_bound[None], WHOLE),
            group_gain=(group_gain[None], WHOLE),
            grad_residual=(grad_residual, WHOLE),
            second=(second, WHOLE),
            **{f"weight_{index}": (weight, ANY) for index, weight in enumerate(weights)},
        ),
        dict(
            grads=((rows, columns), by_chunk(columns)),
            group=((8, width), WHOLE),
            sums=((X * 8, wide // X), WHOLE),
            residual_cols=Columns.results([grad_residual])[0],
            second_cols=Columns.results([second])[0],
            **{f"block_{index}": ((wide, width), WHOLE) for index in range(count)},
        ),
        dict(
            work=[
                pltpu.VMEM((heads, HDIM, HDIM), F32),
                pltpu.VMEM((count, wide, width), F32),
                pltpu.SemaphoreType.DMA((count,)),
            ],
            columns=Columns.scratch([grad_residual]),
            small=Columns.scratch([second]),
        ),
        chunks,
        body,
        collective_id,
        far=True,
        flops=60 * rows * HDIM * width + 6 * rows * wide * columns,
    )


def fast_shards(
    tokens_in,
    cotangent,
    lengths,
    lower_bound,
    query_weight,
    forget_weight,
    input_weight,
    gate_weight,
    out_weight,
    swiglu_gate,
    swiglu_up,
    swiglu_down,
    first_gain,
    group_gain,
    second_gain,
):
    place = lax.axis_index("seq")
    z, x = place // X, place % X
    rows, model = tokens_in.shape
    wide = model // Z
    narrow = model // (Z * X)
    width = query_weight.shape[1] // X
    share_rows = rows // 4
    token_count = rows * Z * X

    def share(entries):
        return cut(entries, lax.axis_index("mp"), share_rows, 0)

    in_weights = (query_weight, forget_weight, input_weight, gate_weight)
    split = first_kernel(tokens_in, out_weight, swiglu_gate, swiglu_up, swiglu_down, 1)
    mixed = mixer_kernel(
        split.all,
        tokens_in,
        cotangent,
        lengths,
        lower_bound,
        in_weights,
        split,
        first_gain,
        group_gain,
        second_gain,
        2,
    )
    fed = feed_forward_kernel(
        mixed.normed_two, mixed.all_cotangent, mixed.grad_hidden, split, 3
    )

    def tiles(first, count):
        return partial(
            tile_parts,
            fed.all_normed_two,
            mixed.all_cotangent,
            mixed.grad_hidden,
            fed.late,
            split,
            swiglu_gate.shape[1],
            first,
            count,
        )

    early = 4
    late = pl.cdiv(swiglu_gate.shape[1], TILE) - early
    sent = residual_kernel(
        fed.grad,
        fed.ffn,
        mixed.residual,
        cotangent,
        second_gain,
        split,
        fed.all_normed_two,
        tiles(0, early),
        early,
        4,
    )
    grad_residual = sent.grad_residual
    output = share(mixed.residual) + sent.ffn_share
    back = backward_kernel(
        mixed.projected,
        mixed.raw,
        mixed.states,
        sent.all_grad_mixer,
        mixed.normed_cols,
        grad_residual,
        sent.second,
        in_weights,
        lower_bound,
        group_gain,
        lengths,
        5,
    )
    second_cols = jnp.sum(back.second_cols[:, :, 0], (0, 1))
    out_block = dot(back.residual_cols.reshape(token_count, wide), mixed.mixer, 0, 0)
    blocks = [*(back[f"block_{index}"] for index in range(4)), out_block]
    last = last_kernel(
        back.grads,
        back.group,
        blocks,
        back.sums,
        in_weights,
        sent.normed_high,
        sent.normed_low,
        tiles(early, late),
        late,
        6,
    )
    grad_group = in_order(x == 0, back.group[0], last.other_group[0], 0)
    *weight_grads, grad_outw = (
        in_order(x == 0, cut(block, x, narrow, 0), last[f"swapped_{index}"], 1)
        for index, block in enumerate(blocks)
    )
    grad_normed_one, first_sum = last.share, last.first_sum
    grad_sgate, grad_sup, grad_sdown = (
        jnp.concatenate([sent[name], last[name]], axis)
        for name, axis in (("grad_gate", 1), ("grad_up", 1), ("grad_down", 0))
    )
    tokens_share = share(tokens_in)
    scale_one = rms(tokens_share)
    pulled_one = grad_normed_one * first_gain
    grad_tokens = (
        share(grad_residual)
        + scale_one * pulled_one
        - tokens_share * scale_one**3 * jnp.mean(pulled_one * tokens_share, -1, keepdims=True)
    )
    return (
        output,
        grad_tokens,
        *weight_grads,
        jnp.transpose(grad_outw),
        grad_sgate,
        grad_sup,
        grad_sdown,
        first_sum[0] / cut(first_gain, place, narrow, 0),
        cut(grad_group, place, group_gain.shape[0] // (Z * X), 0),
        cut(second_cols, x, narrow, 0),
    )


def solution(mesh):
    in_specs = (
        P("seq", None),
        P("seq", None),
        P(),
        P("mp"),
        P(None, "mp"),
        P(None, "mp"),
        P(None, "mp"),
        P(None, "mp"),
        P("mp", None),
        P(None, "mp"),
        P(None, "mp"),
        P("mp", None),
        P(),
        P("mp"),
        P(),
    )
    out_specs = (
        P(("seq", "mp"), None),
        P(("seq", "mp"), None),
        P("seq", "mp"),
        P("seq", "mp"),
        P("seq", "mp"),
        P("seq", "mp"),
        P("mp", "seq"),
        P("seq", "mp"),
        P("seq", "mp"),
        P("mp", "seq"),
        P("seq"),
        P(("mp", "seq")),
        P("seq"),
    )
    small = (mesh.shape["seq"], mesh.shape["mp"]) == (Z * X, 4)
    body = fast_shards if small else shards
    return jax.shard_map(body, mesh=mesh, in_specs=in_specs, out_specs=out_specs, check_vma=False)
```
